32 devices in a mesh: groups: 2 (over x), row: 16 (over z, y, core).
Axes of the slice: x: 2, y: 2, z: 4, core: 2. Of those that a mesh axis runs over, the one named last changes fastest.
Arguments:
- inputs: bfloat16 [8192, 8192], P(('groups', 'row')), parts along dimension 0, may hold values from -6 to 6
- output_gradient: bfloat16 [8192, 512], P(('groups', 'row')), parts along dimension 0, may hold values from -1.5 to 1.5
- token_adapter: int32 [8192, 1], P(('groups', 'row')), parts along dimension 0, may hold values from 0 to 31; in each aligned block of 256 rows (0 to 255, 256 to 511, ...) at most 16 rows name the same one
- adapter_slot: int32 [32], replicated, may hold values from 0 to 31, each once
- frozen_key_weight: bfloat16 [8192, 512], P('row'), may hold values from -0.25 to 0.25
- adapter_down_weight: bfloat16 [32, 8192, 64], P('row'), may hold values from -0.0625 to 0.0625
- adapter_up_weight: bfloat16 [32, 64, 512], P('row'), may hold values from -0.125 to 0.125
Outputs:
- input_gradient: bfloat16 [8192, 8192], P(('groups', 'row')), parts along dimension 0
- grad_a: bfloat16 [64, 8192, 64], P(('groups', 'row')), parts along dimension 0
- grad_b: bfloat16 [64, 64, 512], P(('groups', 'row')), parts along dimension 0
The draws below stay inside these ranges and needn't reach their ends.
There are 2 independent parts, one for each index of `groups`. The reference program is written for one: setup_inputs(seed, part) draws one part's arguments, and reference() takes and returns one part's arrays. A program takes and returns all parts, laid end to end along the dimension named above; an argument that names none is the same for every part. Nothing has to cross between parts.
Inputs may be any that keep to these rules, and one draw needn't show every extreme that they name: `token_adapter`: among the 256 rows of one index of row, no adapter is named by more than 16 rows, a bound that some block reaches. A permutation: adapter_slot[a] is the slot of adapter a, and slot s belongs to index s // 2 of row.
All inputs are finite; a program needn't handle non-finite values.
Results may differ from the reference program's by a relative error of at most 0.005.
Values may be sent and summed in bfloat16 or wider, within the bound.
No kernel may reach another device: no remote copies, remote signals or barrier semaphores. Data moves between devices by JAX's collectives and lax.ppermute only.
A program may use at most 128 MiB of HBM per device.

```python
import math
import jax
import jax.numpy as jnp
import numpy as np
from jax import lax

MODEL_DIMENSION = 8192
KEY_OUTPUTS = 512
ADAPTER_RANK = 64
ADAPTER_COUNT = 32
TOK_DEV = 256
TOKEN_COUNT = 4096
MOST = 16
N_ROW = 16


def shard_levels(rng, shape, split, smallest, top_value):
    level, own = 1.0, jax.random.fold_in(rng, 6)
    for dim, blocks in split:
        draws = jnp.exp(jax.random.uniform(jax.random.fold_in(own, dim), (blocks,), jnp.float32, smallest / len(split), top_value / len(split)))
        level = level * jnp.repeat(draws, shape[dim] // blocks).reshape([-1 if axis == dim else 1 for axis in range(len(shape))])
    return level


def assign_block(own_key, own, number, rows, count, top, bound, skew):
    sequence = jax.random.permutation(own_key, count)
    heavy_load, common = portions_of(count, rows * top, bound, skew, True), portions_of(count, rows * top, bound, skew, False)
    places = jnp.arange(count)

    def named(tallies, offset_by):
        used = int((tallies > 0).sum())
        fixed = max(1, used // 4)
        moved = fixed + (places - fixed + offset_by * (used - fixed)) % max(1, count - fixed)
        return jnp.zeros((count,), jnp.int32).at[sequence[jnp.where(places < fixed, places, moved)]].set(jnp.asarray(tallies, jnp.int32))

    tallies = jnp.where(number % 4 == 0, named(heavy_load, number // 4), named(common, number - number // 4 - 1))
    mixed = jax.random.permutation(jax.random.fold_in(own, 3), count)
    source_of, receiver = mixed[0:count // 2 * 2:2], mixed[1:count // 2 * 2:2]
    room = jnp.minimum(tallies[source_of] - 1, bound - tallies[receiver]) // 2
    room = jnp.where((source_of == sequence[0]) | (receiver == sequence[0]) | (tallies[receiver] == 0), 0, jnp.maximum(room, 0))
    moved = jax.random.randint(jax.random.fold_in(own, 4), (count // 2,), 0, 1 << 20) % (room + 1)
    tallies = tallies.at[source_of].add(-moved).at[receiver].add(moved)
    labels = jnp.searchsorted(jnp.cumsum(tallies), jnp.arange(rows * top), side="right").astype(jnp.int32)
    listing = labels.reshape(top, rows).T
    listing = listing[jax.random.permutation(jax.random.fold_in(own, 1), rows)]
    offset_by = jax.random.randint(jax.random.fold_in(own, 2), (rows, 1), 0, top)
    return jnp.take_along_axis(listing, (jnp.arange(top)[None, :] + offset_by) % top, axis=1)


def portions_of(amount, total, reach, skew, full):
    portions = [(1 << 20) // math.isqrt(standing ** skew) + 1 for standing in range(1, amount + 1)]
    largest = reach if full else min(reach, max(-(-total // amount), total * portions[0] // sum(portions)))
    least = 1 if total - largest >= amount - 1 else 0
    given, surplus = [largest] + [least] * (amount - 1), total - largest - least * (amount - 1)
    while surplus > 0:
        free = [i for i in range(1, amount) if given[i] < largest] or [i for i in range(1, amount) if given[i] < reach]
        whole, remaining = sum([portions[i] for i in free]), surplus
        for i in free:
            more = min(reach - given[i], max(1, remaining * portions[i] // whole), surplus)
            given[i] = given[i] + more
            surplus = surplus - more
    return np.array(given)


def normal_values(rng, extent, deviation, bound, cuts=(), kind=jnp.bfloat16):
    values = jax.random.normal(rng, extent, jnp.float32) * deviation
    if len(cuts) > 0:
        values = shard_levels(rng, extent, cuts, -0.22, 0.18) * values
    return jnp.clip(values, min=-bound, max=bound).astype(kind)


def setup_inputs(seed: int = 0, part: int = 0) -> dict:
    arg_keys = jax.random.split(jax.random.key(seed), 8)
    part_keys = jax.random.split(jax.random.fold_in(arg_keys[7], part), 8)
    inputs = normal_values(part_keys[0], (TOKEN_COUNT, MODEL_DIMENSION), 1.0, 6.0, ((0, 16),))
    output_gradient = normal_values(part_keys[1], (TOKEN_COUNT, KEY_OUTPUTS), 0.25, 1.5, ((0, 16),))
    token_adapter_keys = jax.random.split(jax.random.fold_in(part_keys[2], 1), TOKEN_COUNT // TOK_DEV)
    token_adapter_turns = jax.random.permutation(jax.random.fold_in(part_keys[2], 3), TOKEN_COUNT // TOK_DEV)
    token_adapter = jax.vmap(lambda own, number: assign_block(jax.random.fold_in(part_keys[2], 2), own, number, TOK_DEV, ADAPTER_COUNT, 1, MOST, 2))(token_adapter_keys, token_adapter_turns).reshape((TOKEN_COUNT, 1))
    adapter_slot = jax.random.permutation(arg_keys[3], ADAPTER_COUNT).astype(jnp.int32)
    frozen_key_weight = normal_values(arg_keys[4], (MODEL_DIMENSION, KEY_OUTPUTS), KEY_OUTPUTS ** -0.5, 0.25, ((0, 16),))
    adapter_down_weight = normal_values(arg_keys[5], (ADAPTER_COUNT, MODEL_DIMENSION, ADAPTER_RANK), MODEL_DIMENSION ** -0.5, 0.0625, ((0, 16),))
    adapter_up_weight = normal_values(arg_keys[6], (ADAPTER_COUNT, ADAPTER_RANK, KEY_OUTPUTS), (4 * KEY_OUTPUTS) ** -0.5, 0.125, ((0, 16),))
    return {"inputs": inputs, "output_gradient": output_gradient, "token_adapter": token_adapter, "adapter_slot": adapter_slot, "frozen_key_weight": frozen_key_weight, "adapter_down_weight": adapter_down_weight, "adapter_up_weight": adapter_up_weight}


adapter_scale = 2.0


def reference(inputs, output_gradient, token_adapter, adapter_slot, frozen_key_weight, adapter_down_weight, adapter_up_weight):
    slot_index = adapter_slot[token_adapter[:, 0]].astype(jnp.int32)
    sorting_order = jnp.argsort(slot_index, stable=True)
    counts = jnp.zeros((ADAPTER_COUNT,), jnp.int32).at[slot_index].add(1)
    starts = (jnp.cumsum(counts) - counts).astype(jnp.int32)
    span = N_ROW * MOST
    sorted_rows = jnp.concatenate([inputs[sorting_order], jnp.zeros((span, MODEL_DIMENSION), inputs.dtype)], 0)
    sorted_grads = jnp.concatenate([output_gradient[sorting_order], jnp.zeros((span, KEY_OUTPUTS), output_gradient.dtype)], 0)
    offsets_local = jnp.arange(span, dtype=jnp.int32)

    def step(loop_carry, loop_index):
        begin_offset = starts[loop_index].astype(jnp.int32)
        live = (offsets_local < counts[loop_index])[:, None]
        input_rows = jnp.where(live, lax.dynamic_slice_in_dim(sorted_rows, begin_offset, span, 0), jnp.zeros((), inputs.dtype))
        gradient_rows = jnp.where(live, lax.dynamic_slice_in_dim(sorted_grads, begin_offset, span, 0), jnp.zeros((), output_gradient.dtype))
        down_weight = adapter_down_weight[loop_index]
        up_weight = adapter_up_weight[loop_index]
        reduced_hidden = jnp.dot(input_rows, down_weight, preferred_element_type=jnp.float32).astype(jnp.bfloat16)
        reduced_gradient = jnp.dot(gradient_rows, up_weight.T, preferred_element_type=jnp.float32).astype(jnp.bfloat16)
        down_portion = (adapter_scale * jnp.dot(input_rows.T, reduced_gradient, preferred_element_type=jnp.float32)).astype(jnp.bfloat16)
        up_portion = (adapter_scale * jnp.dot(reduced_hidden.T, gradient_rows, preferred_element_type=jnp.float32)).astype(jnp.bfloat16)
        adapter_rows = (adapter_scale * jnp.dot(reduced_gradient, down_weight.T, preferred_element_type=jnp.float32)).astype(jnp.bfloat16)
        current_slot = lax.dynamic_slice_in_dim(loop_carry, begin_offset, span, 0)
        loop_carry = lax.dynamic_update_slice_in_dim(loop_carry, current_slot + adapter_rows.astype(jnp.float32), begin_offset, 0)
        return loop_carry, (down_portion, up_portion)

    start_carry = jnp.zeros((TOKEN_COUNT + span, MODEL_DIMENSION), jnp.float32)
    loop_carry, parts = lax.scan(step, start_carry, jnp.arange(ADAPTER_COUNT, dtype=jnp.int32))
    grad_a, grad_b = parts
    adapter_tokens = jnp.zeros((TOKEN_COUNT, MODEL_DIMENSION), jnp.float32).at[sorting_order].set(loop_carry[:TOKEN_COUNT])
    base_offset = lax.dot_general(output_gradient, frozen_key_weight, (((1,), (1,)), ((), ())), preferred_element_type=jnp.float32)
    input_gradient = (base_offset + adapter_tokens).astype(jnp.bfloat16)
    return input_gradient, grad_a, grad_b
```

```python
import jax
import jax.numpy as jnp
from jax import lax
from jax.experimental import pallas as pl
from jax.experimental.pallas import tpu as pltpu
from jax.sharding import Mesh, PartitionSpec as P

adapter_scale = 2.0
cube = ("groups", "inner")
vmem_limit = 56 * 1024 * 1024
NT = (((1,), (1,)), ((), ()))


def grad_a_kernel(first, per_step, slot_ref, back_ref, x_ref, out_ref):
    base = first + pl.program_id(1) * per_step
    slots = slot_ref[0]
    back = back_ref[0]
    rows = [back * (slots == base + k).astype(jnp.bfloat16) for k in range(per_step)]
    masked = jnp.concatenate(rows, axis=0)
    out = jnp.dot(masked, x_ref[0], preferred_element_type=jnp.float32)
    out_ref[0] = out.astype(out_ref.dtype)


def grad_a_part(slot_row, back_t, x_cols, first, count, dtype):
    groups, tokens, width = x_cols.shape
    rank = back_t.shape[1]
    per_step = 4
    return pl.pallas_call(
        lambda *refs: grad_a_kernel(first, per_step, *refs),
        grid=(groups, count // per_step),
        in_specs=[
            pl.BlockSpec((1, 1, tokens), lambda g, s: (g, 0, 0)),
            pl.BlockSpec((1, rank, tokens), lambda g, s: (g, 0, 0)),
            pl.BlockSpec((1, tokens, width), lambda g, s: (g, 0, 0)),
        ],
        out_specs=pl.BlockSpec((1, per_step * rank, width), lambda g, s: (g, s, 0)),
        out_shape=jax.ShapeDtypeStruct((groups, count * rank, width), dtype),
        compiler_params=pltpu.CompilerParams(vmem_limit_bytes=vmem_limit),
        cost_estimate=pl.CostEstimate(
            flops=2 * groups * tokens * width * count * rank,
            bytes_accessed=2 * groups * (tokens + 2 * count * rank) * width,
            transcendentals=0,
        ),
        name="grad_a_part",
    )(slot_row, back_t, x_cols)


def token_kernel(chunk, rank, slot_ref, back_ref, g_ref, x_ref, a_ref, w_ref, out_ref, low_ref):
    slots = slot_ref[...]
    back = back_ref[...]
    x = x_ref[...]
    tile = x.shape[0]
    repeated = jnp.concatenate([back] * (chunk // rank), axis=1)
    lane_slot = lax.broadcasted_iota(jnp.int32, (tile, chunk), 1) // rank
    acc = jnp.zeros((tile, x.shape[1]), jnp.float32)
    low = jnp.zeros((tile, 2 * rank), jnp.float32)
    for c in range(a_ref.shape[0] // chunk):
        block = a_ref[c * chunk : (c + 1) * chunk, :]
        keep = lane_slot + c * (chunk // rank) == slots
        masked = jnp.where(keep, repeated, jnp.zeros((), jnp.float32)).astype(jnp.bfloat16)
        acc += jnp.dot(masked, block, preferred_element_type=jnp.float32)
        hidden = lax.dot_general(x, block, NT, preferred_element_type=jnp.float32)
        hidden = jnp.where(keep, hidden, 0.0)
        for k in range(chunk // (2 * rank)):
            low += hidden[:, k * 2 * rank : (k + 1) * 2 * rank]
    base = lax.dot_general(g_ref[...], w_ref[...], NT, preferred_element_type=jnp.float32)
    out_ref[...] = (base + adapter_scale * acc).astype(out_ref.dtype)
    low_ref[...] = low[:, :rank] + low[:, rank:]


def token_part(slot_col, back, g_all, x_cols, a_cols, w_cols):
    tokens, width = x_cols.shape
    outs = g_all.shape[1]
    rank = back.shape[1]
    depth = a_cols.shape[0]
    tile = 256
    return pl.pallas_call(
        lambda *refs: token_kernel(512, rank, *refs),
        grid=(tokens // tile,),
        in_specs=[
            pl.BlockSpec((tile, 1), lambda t: (t, 0)),
            pl.BlockSpec((tile, rank), lambda t: (t, 0)),
            pl.BlockSpec((tile, outs), lambda t: (t, 0)),
            pl.BlockSpec((tile, width), lambda t: (t, 0)),
            pl.BlockSpec((depth, width), lambda t: (0, 0)),
            pl.BlockSpec((width, outs), lambda t: (0, 0)),
        ],
        out_specs=[
            pl.BlockSpec((tile, width), lambda t: (t, 0)),
            pl.BlockSpec((tile, rank), lambda t: (t, 0)),
        ],
        out_shape=[
            jax.ShapeDtypeStruct((tokens, width), jnp.bfloat16),
            jax.ShapeDtypeStruct((tokens, rank), jnp.float32),
        ],
        compiler_params=pltpu.CompilerParams(vmem_limit_bytes=vmem_limit),
        cost_estimate=pl.CostEstimate(
            flops=2 * tokens * width * (2 * depth + outs),
            bytes_accessed=2 * (tokens * (2 * width + outs) + depth * width),
            transcendentals=0,
        ),
        name="token_part",
    )(slot_col, back, g_all, x_cols, a_cols, w_cols)


def body(x, g, tok, adapter_slot, w, a, b):
    groups, inner = lax.axis_size("groups"), lax.axis_size("inner")
    gi, hi, ji = lax.axis_index("groups"), lax.axis_index("half"), lax.axis_index("inner")
    size = groups * inner
    tokens, model = x.shape
    outs = g.shape[1]
    resident, _, rank = a.shape
    share = resident // groups
    slots_half = inner * resident
    slots_all = 2 * slots_half
    width = model // size
    swap = [(0, 1), (1, 0)]

    matches = tok == lax.broadcasted_iota(jnp.int32, (tokens, adapter_slot.shape[0]), 1)
    slot = jnp.sum(jnp.where(matches, adapter_slot[None, :], 0), axis=1)
    slot_cube = lax.all_gather(slot, cube, axis=0, tiled=True)

    a_t = jnp.swapaxes(a, 1, 2)
    a_mine = lax.dynamic_slice_in_dim(a_t, gi * share, share, 0)
    a_mine = a_mine.reshape(share * rank, size, width).swapaxes(0, 1)
    a_own = lax.all_to_all(a_mine, cube, 0, 0, tiled=True)
    a_other = lax.ppermute(a_own, "half", swap)
    a_cols = jnp.concatenate([a_own, a_other], axis=0).reshape(slots_all * rank, width)

    w_got = lax.ppermute(w, ("groups", "half"), [(0, 1), (3, 2)])
    w_cols = jnp.where(hi == gi, w, w_got)

    x_cols = lax.all_to_all(
        x.reshape(tokens, size, width).swapaxes(0, 1), cube, 0, 0, tiled=True
    ).reshape(groups, inner * tokens, width)
    g_all = lax.all_gather(g, cube, axis=0, tiled=True)

    b_mine = lax.dynamic_slice_in_dim(b, gi * share, share, 0)
    b_all = lax.all_gather(b_mine, ("groups", "half", "inner"), axis=0, tiled=True)
    owner, res = slot // resident, slot % resident
    slot_b = ((res // share) * 2 * inner + owner) * share + res % share
    wide = lax.dot_general(
        g, b_all.reshape(slots_all * rank, outs), NT, preferred_element_type=jnp.float32
    ).reshape(tokens, slots_all, rank)
    keep = slot_b[:, None] == jnp.arange(slots_all)[None, :]
    back = jnp.sum(jnp.where(keep[:, :, None], wide, 0.0), axis=1).astype(jnp.bfloat16)
    back_all = lax.all_gather(back, cube, axis=0, tiled=True)

    owner, res = slot_cube // resident, slot_cube % resident
    half_rel, owner_j = (owner // inner) ^ hi, owner % inner
    slot_p = (half_rel * inner + owner_j) * resident + res
    slot_a = ((half_rel * groups + res // share) * inner + owner_j) * share + res % share

    slot_row = slot_p.reshape(groups, 1, inner * tokens)
    back_t = jnp.swapaxes(back_all.reshape(groups, inner * tokens, rank), 1, 2)
    p_other = grad_a_part(slot_row, back_t, x_cols, slots_half, slots_half, jnp.bfloat16)
    p_got = lax.ppermute(p_other, "half", swap)
    p_own = grad_a_part(slot_row, back_t, x_cols, 0, slots_half, jnp.float32)
    p_sum = (adapter_scale * (p_own + p_got.astype(jnp.float32))).astype(jnp.bfloat16)
    p_sum = p_sum.reshape(size, resident * rank, width)
    p_back = lax.all_to_all(p_sum, cube, 0, 0, tiled=True)
    grad_a = p_back.swapaxes(0, 1).reshape(resident, rank, model).swapaxes(1, 2)

    out_cols, low_part = token_part(
        slot_a[:, None],
        back_all,
        g_all,
        x_cols.reshape(size * tokens, width),
        a_cols,
        w_cols,
    )
    out_back = lax.all_to_all(out_cols.reshape(size, tokens, width), cube, 0, 0, tiled=True)
    input_gradient = out_back.swapaxes(0, 1).reshape(tokens, model)

    low_all = lax.psum(low_part, cube).astype(jnp.bfloat16)
    count = inner * tokens
    low_mine = lax.dynamic_slice_in_dim(low_all, gi * count, count, 0)
    g_mine = lax.dynamic_slice_in_dim(g_all, gi * count, count, 0)
    slot_mine = lax.dynamic_slice_in_dim(slot_p, gi * count, count, 0)
    wanted = jnp.concatenate(
        [ji * resident + jnp.arange(resident), slots_half + ji * resident + jnp.arange(resident)]
    )
    keep = slot_mine[:, None] == wanted[None, :]
    low_wide = jnp.where(keep[:, :, None], low_mine[:, None, :], jnp.zeros((), jnp.bfloat16))
    q = lax.dot_general(
        low_wide.reshape(count, 2 * resident * rank),
        g_mine,
        (((0,), (0,)), ((), ())),
        preferred_element_type=jnp.float32,
    )
    q_own, q_other = q[: resident * rank], q[resident * rank :]
    q_got = lax.ppermute(q_other.astype(jnp.bfloat16), "half", swap)
    grad_b = (adapter_scale * (q_own + q_got.astype(jnp.float32))).astype(jnp.bfloat16)
    return input_gradient, grad_a, grad_b.reshape(resident, rank, outs)


def solution(mesh):
    groups, rows = mesh.shape["groups"], mesh.shape["row"]
    split = Mesh(mesh.devices.reshape(groups, 2, rows // 2), ("groups", "half", "inner"))
    every = ("groups", "half", "inner")
    row = ("half", "inner")
    return jax.shard_map(
        body,
        mesh=split,
        in_specs=(
            P(every, None),
            P(every, None),
            P(every, None),
            P(),
            P(row, None),
            P(row, None, None),
            P(row, None, None),
        ),
        out_specs=(P(every, None), P(every, None, None), P(every, None, None)),
        check_vma=False,
    )
```

```python
import jax
import jax.numpy as jnp
from jax import lax
from jax.experimental import pallas as pl
from jax.experimental.pallas import tpu as pltpu
from jax.sharding import Mesh, PartitionSpec as P

adapter_scale = 2.0
cube = ("groups", "inner")
every = ("groups", "inner", "half")
vmem_limit = 56 * 1024 * 1024
NT = (((1,), (1,)), ((), ()))


def call(kernel, place, grid, in_specs, out_specs, out_shape, flops, moved, name, *args):
    return pl.pallas_call(
        kernel,
        grid_spec=pltpu.PrefetchScalarGridSpec(
            num_scalar_prefetch=1, grid=grid, in_specs=in_specs, out_specs=out_specs
        ),
        out_shape=out_shape,
        compiler_params=pltpu.CompilerParams(vmem_limit_bytes=vmem_limit),
        cost_estimate=pl.CostEstimate(flops=flops, bytes_accessed=moved, transcendentals=0),
        name=name,
    )(place, *args)


def split_tokens(packed, rank):
    rows = packed.astype(jnp.float32).T
    return rows[:, :rank], rows[:, rank : rank + 1].astype(jnp.int32)


def grad_a_kernel(inner, resident, place_ref, packed_ref, x_ref, out_ref):
    devices, depth, tokens = packed_ref.shape
    rank = out_ref.shape[1] // (2 * resident)
    j = pl.program_id(1)
    wanted = [(h * inner + j) * resident + r for h in range(2) for r in range(resident)]
    wanted = [jnp.asarray(slot, jnp.int32).astype(jnp.float32) for slot in wanted]
    chunk = min(devices, 16)
    total = jnp.zeros(out_ref.shape[1:], jnp.float32)
    for c in range(devices // chunk):
        columns = []
        for d in range(c * chunk, (c + 1) * chunk):
            back = packed_ref[d, :rank, :]
            slots = packed_ref[d, rank : rank + 1, :].astype(jnp.float32)
            rows = [back * (slots == slot).astype(jnp.bfloat16) for slot in wanted]
            columns.append(jnp.concatenate(rows, axis=0))
        masked = jnp.concatenate(columns, axis=1)
        x = x_ref[c * chunk * tokens : (c + 1) * chunk * tokens, :]
        total += jnp.dot(masked, x, preferred_element_type=jnp.float32)
    out_ref[0] = (adapter_scale * total).astype(out_ref.dtype)


def grad_a_part(place, packed, x_cols, groups, inner, resident, rank):
    devices, depth, tokens = packed.shape
    width = x_cols.shape[1]
    local = devices // groups
    rows = 2 * resident * rank
    return call(
        lambda *refs: grad_a_kernel(inner, resident, *refs),
        place,
        (groups, inner),
        [
            pl.BlockSpec((local, depth, tokens), lambda g, s, place: (g, 0, 0)),
            pl.BlockSpec((local * tokens, width), lambda g, s, place: (g, 0)),
        ],
        pl.BlockSpec((1, rows, width), lambda g, s, place: (g * inner + s, 0, 0)),
        jax.ShapeDtypeStruct((groups * inner, rows, width), jnp.bfloat16),
        2 * devices * tokens * width * rows * inner,
        2 * (devices * tokens + groups * inner * rows) * width,
        "grad_a_part",
        packed,
        x_cols,
    )


def low_kernel(chunk, rank, place_ref, packed_ref, x_ref, a_ref, low_ref):
    _, slots = split_tokens(packed_ref[0], rank)
    x = x_ref[...]
    tile = x.shape[0]
    lane_slot = lax.broadcasted_iota(jnp.int32, (tile, chunk), 1) // rank
    low = jnp.zeros((tile, 2 * rank), jnp.float32)
    for c in range(a_ref.shape[0] // chunk):
        block = a_ref[c * chunk : (c + 1) * chunk, :]
        hidden = lax.dot_general(x, block, NT, preferred_element_type=jnp.float32)
        hidden = jnp.where(lane_slot + c * (chunk // rank) == slots, hidden, 0.0)
        for k in range(chunk // (2 * rank)):
            low += hidden[:, k * 2 * rank : (k + 1) * 2 * rank]
    low = low.T
    low_ref[0] = (low[:rank] + low[rank:]).astype(low_ref.dtype)


def low_part(place, packed, x_cols, a_cols, rank):
    devices, depth, tokens = packed.shape
    width = x_cols.shape[1]
    slots = a_cols.shape[0]
    return call(
        lambda *refs: low_kernel(512, rank, *refs),
        place,
        (devices,),
        [
            pl.BlockSpec((1, depth, tokens), lambda t, place: (t, 0, 0)),
            pl.BlockSpec((tokens, width), lambda t, place: (t, 0)),
            pl.BlockSpec((slots, width), lambda t, place: (0, 0)),
        ],
        pl.BlockSpec((1, rank, tokens), lambda t, place: (t, 0, 0)),
        jax.ShapeDtypeStruct((devices, rank, tokens), jnp.bfloat16),
        2 * devices * tokens * width * slots,
        2 * (devices * tokens + slots) * width,
        "low_part",
        packed,
        x_cols,
        a_cols,
    )


def out_kernel(chunk, rank, place_ref, packed_ref, g_ref, a_ref, w_ref, out_ref):
    back, slots = split_tokens(packed_ref[0], rank)
    tile = back.shape[0]
    repeated = jnp.concatenate([back] * (chunk // rank), axis=1)
    lane_slot = lax.broadcasted_iota(jnp.int32, (tile, chunk), 1) // rank
    acc = jnp.zeros((tile, a_ref.shape[1]), jnp.float32)
    for c in range(a_ref.shape[0] // chunk):
        keep = lane_slot + c * (chunk // rank) == slots
        masked = jnp.where(keep, repeated, 0.0).astype(jnp.bfloat16)
        acc += jnp.dot(
            masked, a_ref[c * chunk : (c + 1) * chunk, :], preferred_element_type=jnp.float32
        )
    base = lax.dot_general(g_ref[...], w_ref[...], NT, preferred_element_type=jnp.float32)
    out_ref[0] = (base + adapter_scale * acc).astype(out_ref.dtype)


def out_part(place, packed, g_all, a_cols, w_cols, rank):
    devices, depth, tokens = packed.shape
    outs = g_all.shape[1]
    slots, width = a_cols.shape
    return call(
        lambda *refs: out_kernel(512, rank, *refs),
        place,
        (devices // 2,),
        [
            pl.BlockSpec((1, depth, tokens), lambda t, place: (2 * t + place[1], 0, 0)),
            pl.BlockSpec((tokens, outs), lambda t, place: (t, 0)),
            pl.BlockSpec((slots, width), lambda t, place: (0, 0)),
            pl.BlockSpec((width, outs), lambda t, place: (0, 0)),
        ],
        pl.BlockSpec((1, tokens, width), lambda t, place: (t, 0, 0)),
        jax.ShapeDtypeStruct((devices // 2, tokens, width), jnp.bfloat16),
        devices * tokens * width * (slots + outs),
        devices * tokens * (width + outs) + 2 * slots * width,
        "out_part",
        packed,
        g_all,
        a_cols,
        w_cols,
    )


def grad_b_kernel(inner, resident, place_ref, packed_ref, low_ref, g_ref, own_ref, other_ref, acc):
    rank = low_ref.shape[1]
    step = pl.program_id(0)
    low = low_ref[0]
    slots = packed_ref[0, rank : rank + 1, :].astype(jnp.float32)
    rows = []
    for h in (place_ref[1], 1 - place_ref[1]):
        for r in range(resident):
            slot = ((h * inner + place_ref[2]) * resident + r).astype(jnp.float32)
            rows.append(low * (slots == slot).astype(jnp.bfloat16))
    term = jnp.dot(jnp.concatenate(rows, axis=0), g_ref[...], preferred_element_type=jnp.float32)

    @pl.when(step == 0)
    def _():
        acc[...] = term

    @pl.when(step > 0)
    def _():
        acc[...] += term

    @pl.when(step == inner - 1)
    def _():
        own_ref[...] = acc[: resident * rank]
        other_ref[...] = acc[resident * rank :].astype(jnp.bfloat16)


def grad_b_part(place, packed, low, g_all, inner, resident):
    _, depth, tokens = packed.shape
    outs = g_all.shape[1]
    rank = low.shape[1]
    rows = resident * rank
    return pl.pallas_call(
        lambda *refs: grad_b_kernel(inner, resident, *refs),
        grid_spec=pltpu.PrefetchScalarGridSpec(
            num_scalar_prefetch=1,
            grid=(inner,),
            in_specs=[
                pl.BlockSpec(
                    (1, depth, tokens),
                    lambda t, place: (2 * (place[0] * inner + t) + place[1], 0, 0),
                ),
                pl.BlockSpec((1, rank, tokens), lambda t, place: (t, 0, 0)),
                pl.BlockSpec((tokens, outs), lambda t, place: (place[0] * inner + t, 0)),
            ],
            out_specs=[
                pl.BlockSpec((rows, outs), lambda t, place: (0, 0)),
                pl.BlockSpec((rows, outs), lambda t, place: (0, 0)),
            ],
            scratch_shapes=[pltpu.VMEM((2 * rows, outs), jnp.float32)],
        ),
        out_shape=[
            jax.ShapeDtypeStruct((rows, outs), jnp.float32),
            jax.ShapeDtypeStruct((rows, outs), jnp.bfloat16),
        ],
        compiler_params=pltpu.CompilerParams(vmem_limit_bytes=vmem_limit),
        cost_estimate=pl.CostEstimate(
            flops=4 * inner * tokens * outs * rows,
            bytes_accessed=2 * inner * tokens * outs,
            transcendentals=0,
        ),
        name="grad_b_part",
    )(place, packed, low, g_all)


def body(x, g, tok, adapter_slot, w, a, b):
    groups, inner = lax.axis_size("groups"), lax.axis_size("inner")
    gi, hi, ji = lax.axis_index("groups"), lax.axis_index("half"), lax.axis_index("inner")
    place = jnp.stack([gi, hi, ji]).astype(jnp.int32)
    size = groups * inner
    tokens, model = x.shape
    outs = g.shape[1]
    resident, _, rank = a.shape
    share = resident // groups
    slots_all = 2 * inner * resident
    width = model // size
    part = width // 2
    swap = [(0, 1), (1, 0)]

    a_t = jnp.swapaxes(a, 1, 2)
    a_mine = lax.dynamic_slice_in_dim(a_t, gi * share, share, 0)
    a_mine = a_mine.reshape(share * rank, size, width).swapaxes(0, 1)
    a_own = lax.all_to_all(a_mine, cube, 0, 0, tiled=True)
    w_got = lax.ppermute(w, ("groups", "half"), [(0, 1), (3, 2)])
    w_cols = jnp.where(hi == gi, w, w_got)

    b_mine = lax.dynamic_slice_in_dim(b, gi * share, share, 0)
    b_all = lax.all_gather(b_mine, every, axis=0, tiled=True)
    g_all = lax.all_gather(g, cube, axis=0, tiled=True)

    x_send = x.reshape(tokens, 2 * size, part).swapaxes(0, 1)
    x_cols = lax.all_to_all(x_send, every, 0, 0, tiled=True).reshape(2 * size * tokens, part)

    a_other = lax.ppermute(a_own, "half", swap)
    a_cols = jnp.stack(
        [jnp.where(hi == 0, a_own, a_other), jnp.where(hi == 0, a_other, a_own)]
    ).reshape(2, groups, inner, share * rank, width)
    a_cols = a_cols.swapaxes(1, 2).reshape(slots_all * rank, width)

    matches = tok == lax.broadcasted_iota(jnp.int32, (tokens, adapter_slot.shape[0]), 1)
    slot = jnp.sum(jnp.where(matches, adapter_slot[None, :], 0), axis=1)
    owner, res = slot // resident, slot % resident
    slot_b = (((res // share) * inner + owner % inner) * 2 + owner // inner) * share + res % share
    wide = lax.dot_general(
        g, b_all.reshape(slots_all * rank, outs), NT, preferred_element_type=jnp.float32
    ).reshape(tokens, slots_all, rank)
    keep = slot_b[:, None] == jnp.arange(slots_all)[None, :]
    back = jnp.sum(jnp.where(keep[:, :, None], wide, 0.0), axis=1).astype(jnp.bfloat16)
    packed = jnp.concatenate(
        [back.T, jnp.broadcast_to(slot[None, :].astype(jnp.bfloat16), (16, tokens))], axis=0
    )
    packed = lax.all_gather(packed[None], every, axis=0, tiled=True)

    out_cols = out_part(place, packed, g_all, a_cols, w_cols, rank)
    out_back = lax.all_to_all(out_cols, cube, 0, 0, tiled=True)
    input_gradient = out_back.swapaxes(0, 1).reshape(tokens, model)

    x_cols, out_cols = lax.optimization_barrier((x_cols, out_cols))
    p = grad_a_part(place, packed, x_cols, groups, inner, resident, rank)
    p = p.reshape(2 * size, resident * rank, part)
    p_back = lax.all_to_all(p, every, 0, 0, tiled=True)
    grad_a = p_back.swapaxes(0, 1).reshape(resident, rank, model).swapaxes(1, 2)

    a_part = lax.dynamic_slice_in_dim(a_cols, hi * part, part, 1)
    low = low_part(place, packed, x_cols, a_part, rank)
    low = lax.all_to_all(low, every, 0, 0, tiled=True)
    low = jnp.sum(low.astype(jnp.float32), axis=0).astype(jnp.bfloat16)
    low = jnp.broadcast_to(low[None], (inner,) + low.shape)
    low = lax.all_to_all(low, "inner", 0, 0, tiled=True)
    q_own, q_other = grad_b_part(place, packed, low, g_all, inner, resident)
    q_got = lax.ppermute(q_other, "half", swap)
    grad_b = (adapter_scale * (q_own + q_got.astype(jnp.float32))).astype(jnp.bfloat16)
    return input_gradient, grad_a, grad_b.reshape(resident, rank, outs)


def solution(mesh):
    groups, rows = mesh.shape["groups"], mesh.shape["row"]
    split = Mesh(mesh.devices.reshape(groups, 2, rows // 2), ("groups", "half", "inner"))
    whole = ("groups", "half", "inner")
    row = ("half", "inner")
    return jax.shard_map(
        body,
        mesh=split,
        in_specs=(
            P(whole, None),
            P(whole, None),
            P(whole, None),
            P(),
            P(row, None),
            P(row, None, None),
            P(row, None, None),
        ),
        out_specs=(P(whole, None), P(whole, None, None), P(whole, None, None)),
        check_vma=False,
    )
```

```python
import jax
import jax.numpy as jnp
from jax import lax
from jax.experimental import pallas as pl
from jax.experimental.pallas import tpu as pltpu
from jax.sharding import Mesh, PartitionSpec as P

adapter_scale = 2.0
line_length = 4
plane = ("groups", "inner")
vmem_limit = 56 * 1024 * 1024
NT = (((1,), (1,)), ((), ()))


def call(kernel, place, grid, in_specs, out_specs, out_shape, flops, moved, name, args, scratch=()):
    return pl.pallas_call(
        kernel,
        grid_spec=pltpu.PrefetchScalarGridSpec(
            num_scalar_prefetch=1,
            grid=grid,
            in_specs=in_specs,
            out_specs=out_specs,
            scratch_shapes=scratch,
        ),
        out_shape=out_shape,
        compiler_params=pltpu.CompilerParams(vmem_limit_bytes=vmem_limit),
        cost_estimate=pl.CostEstimate(flops=flops, bytes_accessed=moved, transcendentals=0),
        name=name,
    )(place, *args)


def repeat(count, step, start):
    if count <= 4:
        for i in range(count):
            start = step(i, start)
        return start
    return lax.fori_loop(0, count, step, start)


def back_kernel(rank, rows_ref, slot_ref, b_ref, g_ref, out_ref):
    slots = slot_ref[0]
    chunk = 512

    def step(c, total):
        block = b_ref[pl.ds(pl.multiple_of(c * chunk, chunk), chunk), :]
        wide = jnp.dot(block, g_ref[0], preferred_element_type=jnp.float32)
        for v in range(chunk // rank):
            named = slots == c * (chunk // rank) + v
            total += jnp.where(named, wide[v * rank : (v + 1) * rank], 0.0)
        return total

    start = jnp.zeros((rank, slots.shape[1]), jnp.float32)
    out_ref[0] = repeat(b_ref.shape[0] // chunk, step, start)


def move_blocks(name, source, picks, out_shape, out_block, in_block, in_map, out_map, grid):
    def kernel(*refs):
        for i in range(len(source)):
            @pl.when(pl.program_id(1) == i if picks else True)
            def _(i=i):
                refs[-1][...] = refs[i][...].reshape(refs[-1].shape)

    moved = 2
    for n in out_shape:
        moved *= n
    return pl.pallas_call(
        kernel,
        grid=grid,
        in_specs=[pl.BlockSpec(in_block, in_map)] * len(source),
        out_specs=pl.BlockSpec(out_block, out_map),
        out_shape=jax.ShapeDtypeStruct(out_shape, jnp.bfloat16),
        compiler_params=pltpu.CompilerParams(vmem_limit_bytes=vmem_limit),
        cost_estimate=pl.CostEstimate(flops=0, bytes_accessed=2 * moved, transcendentals=0),
        name=name,
    )(*source)


def split_columns(x, c, groups, halves, inner, part):
    size, tokens = groups * inner, x.shape[0]
    if part % 128:
        x = x.reshape(tokens, groups, halves, inner, part)[:, :, c]
        return x.transpose(1, 2, 0, 3).reshape(size, tokens, part)
    return move_blocks(
        "split_columns", [x], False, (size, tokens, part), (1, tokens, part), (tokens, part),
        lambda g, j: (0, (g * halves + c) * inner + j),
        lambda g, j: (g * inner + j, 0, 0),
        (groups, inner),
    )


def join_rows(rows, groups, halves, inner, part):
    size, tokens = rows.shape[:2]
    if part % 128:
        rows = rows.reshape(groups, inner, tokens, halves, part)
        return rows.transpose(2, 0, 3, 1, 4).reshape(tokens, -1)
    return move_blocks(
        "join_rows", [rows], False, (tokens, size * halves * part), (tokens, part),
        (1, tokens, part),
        lambda s, c: (s, 0, c),
        lambda s, c: (0, ((s // inner) * halves + c) * inner + s % inner),
        (size, halves),
    )


def join_slots(parts, resident, groups, halves, inner, part):
    size, rows = parts[0].shape[:2]
    if part % 128:
        parts = [p.reshape(groups, inner, rows, part) for p in parts]
        joined = jnp.stack(parts, axis=1).transpose(3, 0, 1, 2, 4)
        return joined.reshape(resident, rows // resident, -1)
    return move_blocks(
        "join_slots", parts, True, (resident, rows // resident, size * halves * part),
        (resident, rows // resident, part), (1, rows, part),
        lambda s, c: (s, 0, 0),
        lambda s, c: (0, 0, ((s // inner) * halves + c) * inner + s % inner),
        (size, halves),
    )


def back_part(place, slot_b, b_cols, g_cols, rank):
    devices, depth, tokens = g_cols.shape
    rows = b_cols.shape[0]
    return call(
        lambda *refs: back_kernel(rank, *refs),
        place,
        (devices,),
        [
            pl.BlockSpec((1, 1, tokens), lambda t, place: (t, 0, 0)),
            pl.BlockSpec((rows, depth), lambda t, place: (0, 0)),
            pl.BlockSpec((1, depth, tokens), lambda t, place: (t, 0, 0)),
        ],
        pl.BlockSpec((1, rank, tokens), lambda t, place: (t, 0, 0)),
        jax.ShapeDtypeStruct((devices, rank, tokens), jnp.float32),
        2 * rows * depth * devices * tokens,
        devices * tokens * 4 * rank,
        "back_part",
        (slot_b, b_cols, g_cols),
    )


def slot_sums(packed_ref, x_ref, rank, first, count):
    devices, _, tokens = packed_ref.shape
    chunk = min(devices, 4)

    def step(c, total):
        columns = []
        for d in range(chunk):
            back = packed_ref[c * chunk + d, :rank, :]
            slots = packed_ref[c * chunk + d, rank : rank + 1, :].astype(jnp.float32)
            rows = [
                back * (slots == (first + i).astype(jnp.float32)).astype(jnp.bfloat16)
                for i in range(count)
            ]
            columns.append(jnp.concatenate(rows, axis=0))
        x = x_ref[pl.ds(c * chunk, chunk)].reshape(chunk * tokens, x_ref.shape[2])
        return total + jnp.dot(
            jnp.concatenate(columns, axis=1), x, preferred_element_type=jnp.float32
        )

    start = jnp.zeros((count * rank, x_ref.shape[2]), jnp.float32)
    return repeat(devices // chunk, step, start)


def send_kernel(slots_line, count, rank, away, place_ref, packed_ref, x_ref, *refs):
    line = place_ref[1]
    outs, got = refs[-2:], refs[:-2]
    targets = (jnp.minimum(line + away, line_length - 1), jnp.maximum(line - away, 0))
    for way, target in enumerate(targets):
        first = target * slots_line + pl.program_id(1) * count
        total = slot_sums(packed_ref, x_ref, rank, first, count)
        if got:
            total += got[way][0].astype(jnp.float32)
        outs[way][0] = total.astype(jnp.bfloat16)


def own_kernel(slots_line, count, rank, place_ref, packed_ref, x_ref, right_ref, left_ref, out_ref):
    first = place_ref[1] * slots_line + pl.program_id(1) * count
    total = slot_sums(packed_ref, x_ref, rank, first, count)
    total += right_ref[0].astype(jnp.float32) + left_ref[0].astype(jnp.float32)
    out_ref[0] = (adapter_scale * total).astype(jnp.bfloat16)


def grad_a_step(place, packed, x_cols, got, away, groups, slots_line, rank):
    devices, depth, tokens = packed.shape
    width = x_cols.shape[2]
    local = devices // groups
    count = 8
    rows = count * rank
    block = pl.BlockSpec((1, rows, width), lambda g, s, place: (g, s, 0))
    shape = jax.ShapeDtypeStruct((groups, slots_line * rank, width), jnp.bfloat16)
    ways = 1 if away == 0 else 2
    if away == 0:
        kernel = lambda *refs: own_kernel(slots_line, count, rank, *refs)
    else:
        kernel = lambda *refs: send_kernel(slots_line, count, rank, away, *refs)
    return call(
        kernel,
        place,
        (groups, slots_line // count),
        [
            pl.BlockSpec((local, depth, tokens), lambda g, s, place: (g, 0, 0)),
            pl.BlockSpec((local, tokens, width), lambda g, s, place: (g, 0, 0)),
        ]
        + [block] * len(got),
        block if away == 0 else [block, block],
        shape if away == 0 else [shape, shape],
        ways * 2 * devices * tokens * width * slots_line * rank,
        2 * devices * tokens * width + 2 * groups * slots_line * rank * width * (ways + len(got)),
        "grad_a_step" + str(away),
        (packed, x_cols, *got),
    )


def low_kernel(chunk, rank, place_ref, packed_ref, x0_ref, x1_ref, a_ref, low_ref):
    slots = packed_ref[0].astype(jnp.float32).T[:, rank + 1 : rank + 2].astype(jnp.int32)
    tile, width = x0_ref.shape[1:]
    lane_slot = lax.broadcasted_iota(jnp.int32, (tile, chunk), 1) // rank

    def step(c, low):
        part = pl.ds(pl.multiple_of(c * chunk, chunk), chunk)
        hidden = lax.dot_general(
            x0_ref[0], a_ref[part, :width], NT, preferred_element_type=jnp.float32
        )
        hidden += lax.dot_general(
            x1_ref[0], a_ref[part, width:], NT, preferred_element_type=jnp.float32
        )
        hidden = jnp.where(lane_slot + c * (chunk // rank) == slots, hidden, 0.0)
        for k in range(chunk // (2 * rank)):
            low += hidden[:, k * 2 * rank : (k + 1) * 2 * rank]
        return low

    start = jnp.zeros((tile, 2 * rank), jnp.float32)
    low = repeat(a_ref.shape[0] // chunk, step, start).T
    low_ref[0] = low[:rank] + low[rank:]


def low_part(place, packed, x0, x1, a_cols, rank):
    devices, depth, tokens = packed.shape
    width = x0.shape[2]
    slots = a_cols.shape[0]
    return call(
        lambda *refs: low_kernel(512, rank, *refs),
        place,
        (devices,),
        [
            pl.BlockSpec((1, depth, tokens), lambda t, place: (t, 0, 0)),
            pl.BlockSpec((1, tokens, width), lambda t, place: (t, 0, 0)),
            pl.BlockSpec((1, tokens, width), lambda t, place: (t, 0, 0)),
            pl.BlockSpec((slots, 2 * width), lambda t, place: (0, 0)),
        ],
        pl.BlockSpec((1, rank, tokens), lambda t, place: (t, 0, 0)),
        jax.ShapeDtypeStruct((devices, rank, tokens), jnp.float32),
        4 * devices * tokens * width * slots,
        4 * (devices * tokens + slots) * width,
        "low_part",
        (packed, x0, x1, a_cols),
    )


def out_kernel(chunk, rank, place_ref, packed_ref, g_ref, a_ref, w_ref, out_ref):
    rows = packed_ref[0].astype(jnp.float32).T
    back, slots = rows[:, :rank], rows[:, rank + 1 : rank + 2].astype(jnp.int32)
    tile = back.shape[0]
    repeated = jnp.concatenate([back] * (chunk // rank), axis=1)
    lane_slot = lax.broadcasted_iota(jnp.int32, (tile, chunk), 1) // rank

    def step(c, acc):
        keep = lane_slot + c * (chunk // rank) == slots
        masked = jnp.where(keep, repeated, 0.0).astype(jnp.bfloat16)
        block = a_ref[pl.ds(pl.multiple_of(c * chunk, chunk), chunk), :]
        return acc + jnp.dot(masked, block, preferred_element_type=jnp.float32)

    start = jnp.zeros((tile, a_ref.shape[1]), jnp.float32)
    acc = repeat(a_ref.shape[0] // chunk, step, start)
    base = lax.dot_general(g_ref[...], w_ref[...], NT, preferred_element_type=jnp.float32)
    out_ref[0] = (base + adapter_scale * acc).astype(out_ref.dtype)


def out_part(place, packed, g_all, a_cols, w_cols, rank):
    devices, depth, tokens = packed.shape
    outs = g_all.shape[1]
    slots, width = a_cols.shape
    return call(
        lambda *refs: out_kernel(512, rank, *refs),
        place,
        (devices,),
        [
            pl.BlockSpec((1, depth, tokens), lambda t, place: (t, 0, 0)),
            pl.BlockSpec((tokens, outs), lambda t, place: (t, 0)),
            pl.BlockSpec((slots, width), lambda t, place: (0, 0)),
            pl.BlockSpec((width, outs), lambda t, place: (0, 0)),
        ],
        pl.BlockSpec((1, tokens, width), lambda t, place: (t, 0, 0)),
        jax.ShapeDtypeStruct((devices, tokens, width), jnp.bfloat16),
        2 * devices * tokens * width * (slots + outs),
        2 * devices * tokens * (width + outs) + 2 * slots * width,
        "out_part",
        (packed, g_all, a_cols, w_cols),
    )


def grad_b_kernel(inner, resident, place_ref, packed_ref, low_ref, g_ref, out_ref, acc):
    rank = low_ref.shape[1]
    step = pl.program_id(0)
    low = low_ref[0]
    slots = packed_ref[0, rank : rank + 1, :].astype(jnp.float32)
    rows = []
    for line in range(line_length):
        for r in range(resident):
            slot = ((line * inner + place_ref[2]) * resident + r).astype(jnp.float32)
            rows.append(low * (slots == slot).astype(jnp.bfloat16))
    term = jnp.dot(jnp.concatenate(rows, axis=0), g_ref[...], preferred_element_type=jnp.float32)

    @pl.when(step == 0)
    def _():
        acc[...] = term

    @pl.when(step > 0)
    def _():
        acc[...] += term

    @pl.when(step == inner - 1)
    def _():
        out_ref[...] = acc[...].astype(jnp.bfloat16)


def grad_b_part(place, packed, low, g_all, inner, resident):
    _, depth, tokens = packed.shape
    outs = g_all.shape[1]
    rank = low.shape[1]
    rows = line_length * resident * rank
    return call(
        lambda *refs: grad_b_kernel(inner, resident, *refs),
        place,
        (inner,),
        [
            pl.BlockSpec((1, depth, tokens), lambda t, place: (place[0] * inner + t, 0, 0)),
            pl.BlockSpec((1, rank, tokens), lambda t, place: (t, 0, 0)),
            pl.BlockSpec((tokens, outs), lambda t, place: (place[0] * inner + t, 0)),
        ],
        pl.BlockSpec((rows, outs), lambda t, place: (0, 0)),
        jax.ShapeDtypeStruct((rows, outs), jnp.bfloat16),
        2 * inner * tokens * outs * rows,
        2 * inner * tokens * outs,
        "grad_b_part",
        (packed, low, g_all),
        [pltpu.VMEM((rows, outs), jnp.float32)],
    )


def body(x, g, tok, adapter_slot, w, a, b):
    groups, inner = lax.axis_size("groups"), lax.axis_size("inner")
    gi, li, ji = lax.axis_index("groups"), lax.axis_index("line"), lax.axis_index("inner")
    place = jnp.stack([gi, li, ji]).astype(jnp.int32)
    size = groups * inner
    tokens, model = x.shape
    outs = g.shape[1]
    resident, _, rank = a.shape
    share = resident // groups
    count = inner * resident
    halves = line_length // groups
    width = model // size
    part = width // halves
    depth = outs // size

    matches = tok == lax.broadcasted_iota(jnp.int32, (tokens, adapter_slot.shape[0]), 1)
    slot = jnp.sum(jnp.where(matches, adapter_slot[None, :], 0), axis=1)
    a_mine = lax.dynamic_slice_in_dim(jnp.swapaxes(a, 1, 2), gi * share, share, 0)
    a_mine = a_mine.reshape(share * rank, groups, halves, inner, part)
    a_mine = a_mine.transpose(1, 3, 0, 2, 4).reshape(size, share * rank, width)
    b_mine = lax.dynamic_slice_in_dim(b, gi * share, share, 0)
    b_mine = b_mine.reshape(share * rank, size, depth).swapaxes(0, 1)
    g_mine = g.T.reshape(size, depth, tokens)
    slot_rows = jnp.broadcast_to(slot.astype(jnp.bfloat16)[None, None, :], (size, 16, tokens))
    height = max(share * rank, depth + 16)

    def tall(rows):
        return jnp.pad(rows, ((0, 0), (0, height - rows.shape[1]), (0, -rows.shape[2] % 128)))

    first = jnp.concatenate(
        [tall(a_mine), tall(jnp.concatenate([slot_rows, g_mine], axis=1)), tall(b_mine)], axis=2
    )
    first = lax.all_to_all(first, plane, 0, 0, tiled=True)
    wide = width + -width % 128
    a_own = first[:, : share * rank, :width]
    slot_all = first[:, 0, wide : wide + tokens].astype(jnp.int32)
    g_cols = first[:, 16 : 16 + depth, wide : wide + tokens]
    b_own = first[:, : share * rank, wide + tokens : wide + tokens + depth]

    x_sends = [split_columns(x, c, groups, halves, inner, part) for c in range(halves)]
    x_send, first = lax.optimization_barrier((x_sends[0], first))
    x_cols = [lax.all_to_all(x_send, plane, 0, 0, tiled=True)]

    b_own = b_own.reshape(count * rank, depth)
    b_cols = [b_own]
    for away in range(1, line_length):
        pairs = [(i, (i + away) % line_length) for i in range(line_length)]
        b_cols.append(lax.ppermute(b_own, "line", pairs))
    b_cols = jnp.concatenate(b_cols, axis=0)
    a_cols = lax.all_gather(a_own, "line", axis=0).reshape(-1, width)
    w_line = lax.all_gather(w, "line", axis=0)
    w_cols = lax.dynamic_slice_in_dim(w_line, gi * halves, halves, 0).reshape(width, outs)
    g_all = lax.all_gather(g, plane, axis=0, tiled=True)

    def number(slot):
        owner, res = slot // resident, slot % resident
        return owner // inner, ((res // share) * inner + owner % inner) * share + res % share

    slot_line, slot_in = number(slot_all)
    slot_b = (((li - slot_line) % line_length) * count + slot_in)[:, None, :]
    back = back_part(place, slot_b, b_cols, g_cols, rank)
    back = lax.all_to_all(back, plane, 0, 0, tiled=True)
    back = jnp.sum(back, axis=0).astype(jnp.bfloat16)
    slot_line, slot_in = number(slot)
    slot_a = slot_line * count + slot_in
    names = jnp.stack([slot, slot_a] + [slot] * 14).astype(jnp.bfloat16)
    packed = jnp.concatenate([back, names], axis=0)
    packed = jnp.broadcast_to(packed[None], (size,) + packed.shape)
    packed = lax.all_to_all(packed, plane, 0, 0, tiled=True)

    x_send, packed = lax.optimization_barrier((x_sends[1], packed))
    x_cols.append(lax.all_to_all(x_send, plane, 0, 0, tiled=True))

    p_back = []
    for c in range(halves):
        got = ()
        for away in range(line_length - 1, 0, -1):
            right, left = grad_a_step(
                place, packed, x_cols[c], got, away, groups, count, rank
            )
            up = [(i, i + 1) for i in range(line_length - away)]
            down = [(i, i - 1) for i in range(away, line_length)]
            got = (lax.ppermute(right, "line", up), lax.ppermute(left, "line", down))
        p = grad_a_step(place, packed, x_cols[c], got, 0, groups, count, rank)
        p = p.reshape(size, resident * rank, part)
        p = lax.all_to_all(p, plane, 0, 0, tiled=True)
        p_back.append(p)
    grad_a = join_slots(p_back, resident, groups, halves, inner, part).swapaxes(1, 2)

    out_cols = out_part(place, packed, g_all, a_cols, w_cols, rank)
    out_back = lax.all_to_all(out_cols, plane, 0, 0, tiled=True)
    input_gradient = join_rows(out_back, groups, halves, inner, part)

    low = low_part(place, packed, x_cols[0], x_cols[1], a_cols, rank)
    low = lax.all_to_all(low, plane, 0, 0, tiled=True)
    low = jnp.sum(low, axis=0).astype(jnp.bfloat16)
    low = jnp.broadcast_to(low[None], (inner,) + low.shape)
    low = lax.all_to_all(low, "inner", 0, 0, tiled=True)
    q = grad_b_part(place, packed, low, g_all, inner, resident)
    q = lax.all_to_all(q.reshape(line_length, resident * rank, outs), "line", 0, 0, tiled=True)
    grad_b = (adapter_scale * jnp.sum(q.astype(jnp.float32), axis=0)).astype(jnp.bfloat16)
    return input_gradient, grad_a, grad_b.reshape(resident, rank, outs)


def solution(mesh):
    groups, rows = mesh.shape["groups"], mesh.shape["row"]
    whole = ("groups", "line", "inner")
    split = Mesh(mesh.devices.reshape(groups, line_length, rows // line_length), whole)
    row = ("line", "inner")
    return jax.shard_map(
        body,
        mesh=split,
        in_specs=(
            P(whole, None),
            P(whole, None),
            P(whole, None),
            P(),
            P(row, None),
            P(row, None, None),
            P(row, None, None),
        ),
        out_specs=(P(whole, None), P(whole, None, None), P(whole, None, None)),
        check_vma=False,
    )
```

```python
import jax
import jax.numpy as jnp
from jax import lax
from jax.experimental import pallas as pl
from jax.experimental.pallas import tpu as pltpu
from jax.sharding import Mesh, PartitionSpec as P

adapter_scale = 2.0
line_length = 4
plane = ("groups", "inner")
cube = ("groups", "pair", "inner")
vmem_limit = 56 * 1024 * 1024
NT = (((1,), (1,)), ((), ()))


def call(kernel, place, grid, in_specs, out_specs, out_shape, flops, moved, name, args, scratch=()):
    return pl.pallas_call(
        kernel,
        grid_spec=pltpu.PrefetchScalarGridSpec(
            num_scalar_prefetch=1,
            grid=grid,
            in_specs=in_specs,
            out_specs=out_specs,
            scratch_shapes=scratch,
        ),
        out_shape=out_shape,
        compiler_params=pltpu.CompilerParams(vmem_limit_bytes=vmem_limit),
        cost_estimate=pl.CostEstimate(flops=flops, bytes_accessed=moved, transcendentals=0),
        name=name,
    )(place, *args)


def repeat(count, step, start):
    if count <= 4:
        for i in range(count):
            start = step(i, start)
        return start
    return lax.fori_loop(0, count, step, start)


def back_kernel(rank, rows_ref, slot_ref, b_ref, g_ref, out_ref):
    slots = slot_ref[0]
    chunk = 512

    def step(c, total):
        block = b_ref[pl.ds(pl.multiple_of(c * chunk, chunk), chunk), :]
        wide = jnp.dot(block, g_ref[0], preferred_element_type=jnp.float32)
        for v in range(chunk // rank):
            named = slots == c * (chunk // rank) + v
            total += jnp.where(named, wide[v * rank : (v + 1) * rank], 0.0)
        return total

    start = jnp.zeros((rank, slots.shape[1]), jnp.float32)
    out_ref[0] = repeat(b_ref.shape[0] // chunk, step, start)


def move(name, sources, in_blocks, in_maps, outs, out_blocks, out_maps, grid, kernel, place):
    moved = 0
    for shape in outs:
        size = 4
        for n in shape:
            size *= n
        moved += size
    return call(
        kernel,
        place,
        grid,
        [pl.BlockSpec(block, index) for block, index in zip(in_blocks, in_maps)],
        [pl.BlockSpec(block, index) for block, index in zip(out_blocks, out_maps)],
        [jax.ShapeDtypeStruct(shape, jnp.bfloat16) for shape in outs],
        0,
        moved,
        name,
        sources,
    )


def split_columns(place, x, size, parts, width):
    tokens = x.shape[0]
    if width % 128:
        x = x.reshape(tokens, size, parts, width)
        return [x[:, :, c].swapaxes(0, 1) for c in range(parts)]
    tile = min(tokens, 64)

    def kernel(place_ref, x_ref, *out_refs):
        for q in range(size):
            for c in range(parts):
                first = (q * parts + c) * width
                out_refs[c][q] = x_ref[:, first : first + width]

    return move(
        "split_columns", [x], [(tile, x.shape[1])], [lambda t, place: (t, 0)],
        [(size, tokens, width)] * parts, [(size, tile, width)] * parts,
        [lambda t, place: (0, t, 0)] * parts, (tokens // tile,), kernel, place,
    )


def join_slots(place, parts, resident):
    size, rows, width = parts[0].shape
    count, rank = len(parts), rows // resident
    if width % 128:
        joined = jnp.stack(parts, axis=1).transpose(2, 0, 1, 3)
        return joined.reshape(resident, rank, -1)

    def kernel(place_ref, *refs):
        for q in range(size):
            for c in range(count):
                first = (q * count + c) * width
                refs[-1][0, :, first : first + width] = refs[c][q]

    return move(
        "join_slots", parts, [(size, rank, width)] * count, [lambda r, place: (0, r, 0)] * count,
        [(resident, rank, size * count * width)], [(1, rank, size * count * width)],
        [lambda r, place: (r, 0, 0)], (resident,), kernel, place,
    )[0]


def join_rows(place, pieces, groups, halves, inner, part):
    size, tokens = len(pieces), pieces[0].shape[0]
    if part % 128 or size > 8:
        rows = jnp.stack(pieces).reshape(size, tokens, halves, part)
        me = place[0] * inner + place[3]
        rows = rows[jnp.arange(size) ^ me].reshape(groups, inner, tokens, halves, part)
        return rows.transpose(2, 0, 3, 1, 4).reshape(tokens, -1)
    tile = min(tokens, 64)
    model = size * halves * part

    def kernel(place_ref, *refs):
        me = place_ref[0] * inner + place_ref[3]
        for m in range(size):
            device = me ^ m
            for c in range(halves):
                block = ((device // inner) * halves + c) * inner + device % inner
                first = pl.multiple_of(block * part, part)
                refs[-1][:, pl.ds(first, part)] = refs[m][:, c * part : (c + 1) * part]

    return move(
        "join_rows", pieces, [(tile, halves * part)] * size, [lambda t, place: (t, 0)] * size,
        [(tokens, model)], [(tile, model)], [lambda t, place: (t, 0)], (tokens // tile,),
        kernel, place,
    )[0]


def back_part(place, slot_b, b_cols, g_cols, rank):
    devices, depth, tokens = g_cols.shape
    rows = b_cols.shape[0]
    return call(
        lambda *refs: back_kernel(rank, *refs),
        place,
        (devices,),
        [
            pl.BlockSpec((1, 1, tokens), lambda t, place: (t, 0, 0)),
            pl.BlockSpec((rows, depth), lambda t, place: (0, 0)),
            pl.BlockSpec((1, depth, tokens), lambda t, place: (t, 0, 0)),
        ],
        pl.BlockSpec((1, rank, tokens), lambda t, place: (t, 0, 0)),
        jax.ShapeDtypeStruct((devices, rank, tokens), jnp.float32),
        2 * rows * depth * devices * tokens,
        devices * tokens * 4 * rank,
        "back_part",
        (slot_b, b_cols, g_cols),
    )


def slot_sums(packed_ref, x_ref, rank, first, count):
    devices, _, tokens = packed_ref.shape
    chunk = min(devices, 4)

    def step(c, total):
        columns = []
        for d in range(chunk):
            back = packed_ref[c * chunk + d, :rank, :]
            slots = packed_ref[c * chunk + d, rank : rank + 1, :].astype(jnp.float32)
            rows = [
                back * (slots == (first + i).astype(jnp.float32)).astype(jnp.bfloat16)
                for i in range(count)
            ]
            columns.append(jnp.concatenate(rows, axis=0))
        x = x_ref[pl.ds(c * chunk, chunk)].reshape(chunk * tokens, x_ref.shape[2])
        return total + jnp.dot(
            jnp.concatenate(columns, axis=1), x, preferred_element_type=jnp.float32
        )

    start = jnp.zeros((count * rank, x_ref.shape[2]), jnp.float32)
    return repeat(devices // chunk, step, start)


def grad_a_kernel(slots_half, count, rank, own, place_ref, packed_ref, x_ref, *refs):
    half = place_ref[1] if own else 1 - place_ref[1]
    first = half * slots_half + pl.program_id(1) * count
    total = slot_sums(packed_ref, x_ref, rank, first, count)
    if own:
        total = adapter_scale * (total + refs[0][0].astype(jnp.float32))
    refs[-1][0] = total.astype(jnp.bfloat16)


def grad_a_part(place, packed, x_cols, got, groups, slots_half, rank):
    devices, depth, tokens = packed.shape
    width = x_cols.shape[2]
    local = devices // groups
    count = 8
    rows = count * rank
    block = pl.BlockSpec((1, rows, width), lambda g, s, place: (g, s, 0))
    return call(
        lambda *refs: grad_a_kernel(slots_half, count, rank, len(got) > 0, *refs),
        place,
        (groups, slots_half // count),
        [
            pl.BlockSpec((local, depth, tokens), lambda g, s, place: (g, 0, 0)),
            pl.BlockSpec((local, tokens, width), lambda g, s, place: (g, 0, 0)),
        ]
        + [block] * len(got),
        block,
        jax.ShapeDtypeStruct((groups, slots_half * rank, width), jnp.bfloat16),
        2 * devices * tokens * width * slots_half * rank,
        2 * devices * tokens * width + 2 * groups * slots_half * rank * width * (1 + len(got)),
        "grad_a_own" if got else "grad_a_other",
        (packed, x_cols, *got),
    )


def in_line(slots, place_ref, total):
    slots -= (2 * place_ref[1] + place_ref[2]) * (total // line_length)
    return jnp.where(slots < 0, slots + total, slots)


def low_kernel(chunk, rank, place_ref, packed_ref, x0_ref, x1_ref, a_ref, low_ref):
    slots = packed_ref[0].astype(jnp.float32).T[:, rank + 1 : rank + 2].astype(jnp.int32)
    slots = in_line(slots, place_ref, a_ref.shape[0] // rank)
    tile, width = x0_ref.shape[1:]
    lane_slot = lax.broadcasted_iota(jnp.int32, (tile, chunk), 1) // rank

    def step(c, low):
        part = pl.ds(pl.multiple_of(c * chunk, chunk), chunk)
        hidden = lax.dot_general(
            x0_ref[0], a_ref[part, :width], NT, preferred_element_type=jnp.float32
        )
        hidden += lax.dot_general(
            x1_ref[0], a_ref[part, width:], NT, preferred_element_type=jnp.float32
        )
        hidden = jnp.where(lane_slot + c * (chunk // rank) == slots, hidden, 0.0)
        for k in range(chunk // (2 * rank)):
            low += hidden[:, k * 2 * rank : (k + 1) * 2 * rank]
        return low

    start = jnp.zeros((tile, 2 * rank), jnp.float32)
    low = repeat(a_ref.shape[0] // chunk, step, start).T
    low_ref[0] = low[:rank] + low[rank:]


def low_part(place, packed, x0, x1, a_cols, rank):
    devices, depth, tokens = packed.shape
    width = x0.shape[2]
    slots = a_cols.shape[0]
    if width % 64:
        a_cols = lax.dynamic_slice_in_dim(a_cols, place[2] * 2 * width, 2 * width, 1)
    column = lambda place: 0 if width % 64 else place[2]
    return call(
        lambda *refs: low_kernel(512, rank, *refs),
        place,
        (devices,),
        [
            pl.BlockSpec((1, depth, tokens), lambda t, place: (t, 0, 0)),
            pl.BlockSpec((1, tokens, width), lambda t, place: (t, 0, 0)),
            pl.BlockSpec((1, tokens, width), lambda t, place: (t, 0, 0)),
            pl.BlockSpec((slots, 2 * width), lambda t, place: (0, column(place))),
        ],
        pl.BlockSpec((1, rank, tokens), lambda t, place: (t, 0, 0)),
        jax.ShapeDtypeStruct((devices, rank, tokens), jnp.float32),
        4 * devices * tokens * width * slots,
        4 * (devices * tokens + slots) * width,
        "low_part",
        (packed, x0, x1, a_cols),
    )


def out_kernel(chunk, rank, place_ref, packed_ref, g_ref, a_ref, w_ref, out_ref):
    rows = packed_ref[0].astype(jnp.float32).T
    back, slots = rows[:, :rank], rows[:, rank + 1 : rank + 2].astype(jnp.int32)
    slots = in_line(slots, place_ref, a_ref.shape[0] // rank)
    tile = back.shape[0]
    repeated = jnp.concatenate([back] * (chunk // rank), axis=1)
    lane_slot = lax.broadcasted_iota(jnp.int32, (tile, chunk), 1) // rank

    def step(c, acc):
        keep = lane_slot + c * (chunk // rank) == slots
        masked = jnp.where(keep, repeated, 0.0).astype(jnp.bfloat16)
        block = a_ref[pl.ds(pl.multiple_of(c * chunk, chunk), chunk), :]
        return acc + jnp.dot(masked, block, preferred_element_type=jnp.float32)

    start = jnp.zeros((tile, a_ref.shape[1]), jnp.float32)
    acc = repeat(a_ref.shape[0] // chunk, step, start)
    base = lax.dot_general(g_ref[...], w_ref[...], NT, preferred_element_type=jnp.float32)
    out_ref[0] = (base + adapter_scale * acc).astype(out_ref.dtype)


def out_part(place, packed, g_all, a_cols, w_cols, inner, rank):
    _, depth, tokens = packed.shape
    devices = g_all.shape[0] // tokens
    outs = g_all.shape[1]
    slots, width = a_cols.shape
    return call(
        lambda *refs: out_kernel(512, rank, *refs),
        place,
        (devices,),
        [
            pl.BlockSpec(
                (1, depth, tokens),
                lambda t, place: (((t // inner) * 2 + place[2]) * inner + t % inner, 0, 0),
            ),
            pl.BlockSpec((tokens, outs), lambda t, place: (t, 0)),
            pl.BlockSpec((slots, width), lambda t, place: (0, 0)),
            pl.BlockSpec((width, outs), lambda t, place: (0, 0)),
        ],
        pl.BlockSpec((1, tokens, width), lambda t, place: (t, 0, 0)),
        jax.ShapeDtypeStruct((devices, tokens, width), jnp.bfloat16),
        2 * devices * tokens * width * (slots + outs),
        2 * devices * tokens * (width + outs) + 2 * slots * width,
        "out_part",
        (packed, g_all, a_cols, w_cols),
    )


def grad_b_kernel(inner, resident, place_ref, packed_ref, low_ref, g_ref, out_ref, acc):
    rank = low_ref.shape[1]
    step = pl.program_id(0)
    low = low_ref[0]
    slots = packed_ref[0, rank : rank + 1, :].astype(jnp.float32)
    rows = []
    for line in range(line_length):
        for r in range(resident):
            slot = ((line * inner + place_ref[3]) * resident + r).astype(jnp.float32)
            rows.append(low * (slots == slot).astype(jnp.bfloat16))
    term = jnp.dot(jnp.concatenate(rows, axis=0), g_ref[...], preferred_element_type=jnp.float32)

    @pl.when(step == 0)
    def _():
        acc[...] = term

    @pl.when(step > 0)
    def _():
        acc[...] += term

    @pl.when(step == inner - 1)
    def _():
        out_ref[...] = acc[...].astype(jnp.bfloat16)


def grad_b_part(place, packed, low, g_all, inner, resident):
    _, depth, tokens = packed.shape
    outs = g_all.shape[1]
    rank = low.shape[1]
    rows = line_length * resident * rank
    return call(
        lambda *refs: grad_b_kernel(inner, resident, *refs),
        place,
        (inner,),
        [
            pl.BlockSpec(
                (1, depth, tokens),
                lambda t, place: ((place[0] * 2 + place[2]) * inner + t, 0, 0),
            ),
            pl.BlockSpec((1, rank, tokens), lambda t, place: (t, 0, 0)),
            pl.BlockSpec((tokens, outs), lambda t, place: (place[0] * inner + t, 0)),
        ],
        pl.BlockSpec((rows, outs), lambda t, place: (0, 0)),
        jax.ShapeDtypeStruct((rows, outs), jnp.bfloat16),
        2 * inner * tokens * outs * rows,
        2 * inner * tokens * outs,
        "grad_b_part",
        (packed, low, g_all),
        [pltpu.VMEM((rows, outs), jnp.float32)],
    )


def body(x, g, tok, adapter_slot, w, a, b):
    groups, inner = lax.axis_size("groups"), lax.axis_size("inner")
    gi, hi, pi = lax.axis_index("groups"), lax.axis_index("half"), lax.axis_index("pair")
    ji = lax.axis_index("inner")
    place = jnp.stack([gi, hi, pi, ji]).astype(jnp.int32)
    li = 2 * hi + pi
    size = groups * inner
    tokens, model = x.shape
    outs = g.shape[1]
    resident, _, rank = a.shape
    share = resident // groups
    count = inner * resident
    halves = line_length // groups
    width = model // size
    part = width // halves
    depth = outs // size
    line = ("half", "pair")

    matches = tok == lax.broadcasted_iota(jnp.int32, (tokens, adapter_slot.shape[0]), 1)
    slot = jnp.sum(jnp.where(matches, adapter_slot[None, :], 0), axis=1)
    a_mine = lax.dynamic_slice_in_dim(jnp.swapaxes(a, 1, 2), gi * share, share, 0)
    a_mine = a_mine.reshape(share * rank, groups, halves, inner, part)
    a_mine = a_mine.transpose(1, 3, 0, 2, 4).reshape(size, share * rank, width)
    b_mine = lax.dynamic_slice_in_dim(b, gi * share, share, 0)
    b_mine = b_mine.reshape(share * rank, size, depth).swapaxes(0, 1)
    g_mine = g.T.reshape(size, depth, tokens)
    slot_rows = jnp.broadcast_to(slot.astype(jnp.bfloat16)[None, None, :], (size, 16, tokens))
    height = max(share * rank, depth + 16)

    def tall(rows):
        return jnp.pad(rows, ((0, 0), (0, height - rows.shape[1]), (0, -rows.shape[2] % 128)))

    first = jnp.concatenate(
        [tall(a_mine), tall(jnp.concatenate([slot_rows, g_mine], axis=1)), tall(b_mine)], axis=2
    )
    first = lax.all_to_all(first, plane, 0, 0, tiled=True)
    wide = width + -width % 128
    a_own = first[:, : share * rank, :width].reshape(count * rank, width)
    slot_all = first[:, 0, wide : wide + tokens].astype(jnp.int32)
    g_cols = first[:, 16 : 16 + depth, wide : wide + tokens]
    b_own = first[:, : share * rank, wide + tokens : wide + tokens + depth]

    x_sends = split_columns(place, x, 2 * size, 2, part // 2)
    x_send, first = lax.optimization_barrier((x_sends[0], first))
    x_cols = [lax.all_to_all(x_send, cube, 0, 0, tiled=True)]

    b_own = b_own.reshape(count * rank, depth)
    b_cols = [b_own]
    for away in range(1, line_length):
        pairs = [(i, (i - away) % line_length) for i in range(line_length)]
        b_cols.append(lax.ppermute(b_own, line, pairs))
    b_cols = jnp.concatenate(b_cols, axis=0)
    up = [(i, i + 1) for i in range(line_length - 1)]
    down = [(i + 1, i) for i in range(line_length - 1)]
    from_left, from_right = [a_own], [a_own]
    for away in range(1, line_length):
        from_left.append(lax.ppermute(from_left[-1], line, up[away - 1 :]))
        from_right.append(lax.ppermute(from_right[-1], line, down[: line_length - away]))
    w_line = lax.all_gather(w, line, axis=0)
    w_cols = lax.dynamic_slice_in_dim(w_line, gi * halves, halves, 0).reshape(width, outs)
    g_all = lax.all_gather(g, plane, axis=0, tiled=True)

    def number(slot):
        owner, res = slot // resident, slot % resident
        return owner // inner, ((res // share) * inner + owner % inner) * share + res % share

    slot_line, slot_in = number(slot_all)
    slot_b = (((slot_line - li) % line_length) * count + slot_in)[:, None, :]
    back = back_part(place, slot_b, b_cols, g_cols, rank)
    back, x_first = lax.optimization_barrier((back, x_cols[0]))
    back = lax.all_to_all(back, plane, 0, 0, tiled=True)
    back = jnp.sum(back, axis=0).astype(jnp.bfloat16)
    slot_line, slot_in = number(slot)
    slot_a = slot_line * count + slot_in
    names = jnp.stack([slot, slot_a] + [slot] * 14).astype(jnp.bfloat16)
    packed = jnp.concatenate([back, names], axis=0)
    packed = jnp.broadcast_to(packed[None], (2 * size,) + packed.shape)
    packed = lax.all_to_all(packed, cube, 0, 0, tiled=True)

    x_send, packed = lax.optimization_barrier((x_sends[1], packed))
    x_cols = [x_first, lax.all_to_all(x_send, cube, 0, 0, tiled=True)]

    swap = [(0, 1), (1, 0)]
    got = []
    for c in range(2):
        other = grad_a_part(place, packed, x_cols[c], (), groups, 2 * count, rank)
        got.append(lax.ppermute(other, "half", swap))

    a_cols = [a_own] + [
        from_right[k] + from_left[line_length - k] for k in range(1, line_length)
    ]
    a_cols = jnp.concatenate(a_cols, axis=0)
    a_cols, other = lax.optimization_barrier((a_cols, other))
    out_cols = out_part(place, packed, g_all, a_cols, w_cols, inner, rank)
    me = gi * inner + ji
    if size > 8:
        out_back = lax.all_to_all(out_cols, plane, 0, 0, tiled=True)
        pieces = [out_back[me ^ m] for m in range(size)]
    else:
        pieces = [lax.dynamic_index_in_dim(out_cols, me, 0, keepdims=False)]
        for m in range(1, size):
            piece = lax.dynamic_index_in_dim(out_cols, me ^ m, 0, keepdims=False)
            pieces.append(lax.ppermute(piece, plane, [(i, i ^ m) for i in range(size)]))
    input_gradient = join_rows(place, pieces, groups, halves, inner, part)

    p_back = []
    x_own, out_cols = lax.optimization_barrier((x_cols[0], out_cols))
    for c in range(2):
        p = grad_a_part(place, packed, x_own if c == 0 else x_cols[1], (got[c],), groups, 2 * count, rank)
        p = p.reshape(2 * size, resident * rank, part // 2)
        p_back.append(lax.all_to_all(p, cube, 0, 0, tiled=True))
    grad_a = join_slots(place, p_back, resident).swapaxes(1, 2)

    low = low_part(place, packed, x_cols[0], x_cols[1], a_cols, rank)
    low = lax.all_to_all(low, cube, 0, 0, tiled=True)
    low = jnp.sum(low, axis=0).astype(jnp.bfloat16)
    low = jnp.broadcast_to(low[None], (inner,) + low.shape)
    low = lax.all_to_all(low, "inner", 0, 0, tiled=True)
    q = grad_b_part(place, packed, low, g_all, inner, resident)
    q = lax.all_to_all(q.reshape(line_length, resident * rank, outs), line, 0, 0, tiled=True)
    grad_b = (adapter_scale * jnp.sum(q.astype(jnp.float32), axis=0)).astype(jnp.bfloat16)
    return input_gradient, grad_a, grad_b.reshape(resident, rank, outs)


def solution(mesh):
    groups, rows = mesh.shape["groups"], mesh.shape["row"]
    whole = ("groups", "half", "pair", "inner")
    split = Mesh(mesh.devices.reshape(groups, 2, 2, rows // line_length), whole)
    row = ("half", "pair", "inner")
    return jax.shard_map(
        body,
        mesh=split,
        in_specs=(
            P(whole, None),
            P(whole, None),
            P(whole, None),
            P(),
            P(row, None),
            P(row, None, None),
            P(row, None, None),
        ),
        out_specs=(P(whole, None), P(whole, None, None), P(whole, None, None)),
        check_vma=False,
    )
```

```python
import jax
import jax.numpy as jnp
from jax import lax
from jax.experimental import pallas as pl
from jax.experimental.pallas import tpu as pltpu
from jax.sharding import Mesh, PartitionSpec as P

adapter_scale = 2.0
line_length = 4
plane = ("groups", "inner")
cube = ("groups", "pair", "inner")
vmem_limit = 56 * 1024 * 1024
NT = (((1,), (1,)), ((), ()))


def call(kernel, place, grid, in_specs, out_specs, out_shape, flops, moved, name, args, scratch=()):
    return pl.pallas_call(
        kernel,
        grid_spec=pltpu.PrefetchScalarGridSpec(
            num_scalar_prefetch=1,
            grid=grid,
            in_specs=in_specs,
            out_specs=out_specs,
            scratch_shapes=scratch,
        ),
        out_shape=out_shape,
        compiler_params=pltpu.CompilerParams(vmem_limit_bytes=vmem_limit),
        cost_estimate=pl.CostEstimate(flops=flops, bytes_accessed=moved, transcendentals=0),
        name=name,
    )(place, *args)


def repeat(count, step, start):
    if count <= 4:
        for i in range(count):
            start = step(i, start)
        return start
    return lax.fori_loop(0, count, step, start)


def back_kernel(rank, place_ref, slot_ref, b_ref, g_ref, out_ref):
    slots = slot_ref[0]
    devices, rows, _ = b_ref.shape
    depth = g_ref.shape[1]
    share = rows // rank
    total = jnp.zeros((rank, slots.shape[1]), jnp.float32)
    chunk = min(devices, 8)
    for k in range(line_length):

        def step(c, total):
            block = b_ref[pl.ds(c * chunk, chunk), :, k * depth : (k + 1) * depth]
            block = block.reshape(chunk * rows, depth)
            wide = jnp.dot(block, g_ref[0], preferred_element_type=jnp.float32)
            first = (k * devices + c * chunk) * share
            for v in range(chunk * share):
                total += jnp.where(slots == first + v, wide[v * rank : (v + 1) * rank], 0.0)
            return total

        total = repeat(devices // chunk, step, total)
    out_ref[0] = total


def move(name, sources, in_blocks, in_maps, outs, out_blocks, out_maps, grid, kernel, place):
    moved = 0
    for shape in outs:
        size = 4
        for n in shape:
            size *= n
        moved += size
    return call(
        kernel,
        place,
        grid,
        [pl.BlockSpec(block, index) for block, index in zip(in_blocks, in_maps)],
        [pl.BlockSpec(block, index) for block, index in zip(out_blocks, out_maps)],
        [jax.ShapeDtypeStruct(shape, jnp.bfloat16) for shape in outs],
        0,
        moved,
        name,
        sources,
    )


def split_columns(place, x, size, parts, width):
    tokens = x.shape[0]
    if width % 128:
        x = x.reshape(tokens, size, parts, width)
        return [x[:, :, c].swapaxes(0, 1) for c in range(parts)]
    tile = min(tokens, 64)

    def kernel(place_ref, x_ref, *out_refs):
        for q in range(size):
            for c in range(parts):
                first = (q * parts + c) * width
                out_refs[c][q] = x_ref[:, first : first + width]

    return move(
        "split_columns", [x], [(tile, x.shape[1])], [lambda t, place: (t, 0)],
        [(size, tokens, width)] * parts, [(size, tile, width)] * parts,
        [lambda t, place: (0, t, 0)] * parts, (tokens // tile,), kernel, place,
    )


def join_slots(place, parts, resident):
    size, rows, width = parts[0].shape
    count, rank = len(parts), rows // resident
    if width % 128:
        joined = jnp.stack(parts, axis=1).transpose(2, 0, 1, 3)
        return joined.reshape(resident, rank, -1)

    def kernel(place_ref, *refs):
        for q in range(size):
            for c in range(count):
                first = (q * count + c) * width
                refs[-1][0, :, first : first + width] = refs[c][q]

    return move(
        "join_slots", parts, [(size, rank, width)] * count, [lambda r, place: (0, r, 0)] * count,
        [(resident, rank, size * count * width)], [(1, rank, size * count * width)],
        [lambda r, place: (r, 0, 0)], (resident,), kernel, place,
    )[0]


def join_rows(place, pieces, groups, halves, inner, part):
    size, tokens = len(pieces), pieces[0].shape[0]
    if part % 128 or size > 8:
        rows = jnp.stack(pieces).reshape(size, tokens, halves, part)
        me = place[0] * inner + place[3]
        rows = rows[jnp.arange(size) ^ me].reshape(groups, inner, tokens, halves, part)
        return rows.transpose(2, 0, 3, 1, 4).reshape(tokens, -1)
    tile = min(tokens, 64)
    model = size * halves * part

    def kernel(place_ref, *refs):
        me = place_ref[0] * inner + place_ref[3]
        for m in range(size):
            device = me ^ m
            for c in range(halves):
                block = ((device // inner) * halves + c) * inner + device % inner
                first = pl.multiple_of(block * part, part)
                refs[-1][:, pl.ds(first, part)] = refs[m][:, c * part : (c + 1) * part]

    return move(
        "join_rows", pieces, [(tile, halves * part)] * size, [lambda t, place: (t, 0)] * size,
        [(tokens, model)], [(tile, model)], [lambda t, place: (t, 0)], (tokens // tile,),
        kernel, place,
    )[0]


def back_part(place, slot_b, b_cols, g_cols, rank):
    devices, depth, tokens = g_cols.shape
    return call(
        lambda *refs: back_kernel(rank, *refs),
        place,
        (devices,),
        [
            pl.BlockSpec((1, 1, tokens), lambda t, place: (t, 0, 0)),
            pl.BlockSpec(b_cols.shape, lambda t, place: (0, 0, 0)),
            pl.BlockSpec((1, depth, tokens), lambda t, place: (t, 0, 0)),
        ],
        pl.BlockSpec((1, rank, tokens), lambda t, place: (t, 0, 0)),
        jax.ShapeDtypeStruct((devices, rank, tokens), jnp.float32),
        2 * b_cols.size * devices * tokens,
        devices * tokens * 4 * rank,
        "back_part",
        (slot_b, b_cols, g_cols),
    )


def slot_sums(packed_ref, x_ref, rank, first, count):
    devices, _, tokens = packed_ref.shape
    chunk = min(devices, 4)

    def step(c, total):
        columns = []
        for d in range(chunk):
            back = packed_ref[c * chunk + d, :rank, :]
            slots = packed_ref[c * chunk + d, rank : rank + 1, :].astype(jnp.float32)
            rows = [
                back * (slots == (first + i).astype(jnp.float32)).astype(jnp.bfloat16)
                for i in range(count)
            ]
            columns.append(jnp.concatenate(rows, axis=0))
        x = x_ref[pl.ds(c * chunk, chunk)].reshape(chunk * tokens, x_ref.shape[2])
        return total + jnp.dot(
            jnp.concatenate(columns, axis=1), x, preferred_element_type=jnp.float32
        )

    start = jnp.zeros((count * rank, x_ref.shape[2]), jnp.float32)
    return repeat(devices // chunk, step, start)


def grad_a_kernel(slots_half, count, rank, own, place_ref, packed_ref, x_ref, *refs):
    half = place_ref[1] if own else 1 - place_ref[1]
    first = half * slots_half + pl.program_id(1) * count
    total = slot_sums(packed_ref, x_ref, rank, first, count)
    if own:
        total = adapter_scale * (total + refs[0][0].astype(jnp.float32))
    refs[-1][0] = total.astype(jnp.bfloat16)


def grad_a_part(place, packed, x_cols, got, groups, slots_half, rank):
    devices, depth, tokens = packed.shape
    width = x_cols.shape[2]
    local = devices // groups
    count = 8
    rows = count * rank
    block = pl.BlockSpec((1, rows, width), lambda g, s, place: (g, s, 0))
    return call(
        lambda *refs: grad_a_kernel(slots_half, count, rank, len(got) > 0, *refs),
        place,
        (groups, slots_half // count),
        [
            pl.BlockSpec((local, depth, tokens), lambda g, s, place: (g, 0, 0)),
            pl.BlockSpec((local, tokens, width), lambda g, s, place: (g, 0, 0)),
        ]
        + [block] * len(got),
        block,
        jax.ShapeDtypeStruct((groups, slots_half * rank, width), jnp.bfloat16),
        2 * devices * tokens * width * slots_half * rank,
        2 * devices * tokens * width + 2 * groups * slots_half * rank * width * (1 + len(got)),
        "grad_a_own" if got else "grad_a_other",
        (packed, x_cols, *got),
    )


def in_line(slots, place_ref, total):
    slots -= (2 * place_ref[1] + place_ref[2]) * (total // line_length)
    return jnp.where(slots < 0, slots + total, slots)


def put_together(pieces, a_ref):
    @pl.when(pl.program_id(0) == 0)
    def _():
        rows = pieces[0].shape[0]
        a_ref[:rows] = pieces[0][...]
        for k in range(1, line_length):
            left, right = pieces[line_length - k], pieces[line_length - 1 + k]
            a_ref[k * rows : (k + 1) * rows] = left[...] + right[...]


def low_kernel(chunk, rank, place_ref, packed_ref, x0_ref, x1_ref, *refs):
    *pieces, low_ref, a_ref = refs
    put_together(pieces, a_ref)
    slots = packed_ref[0].astype(jnp.float32).T[:, rank + 1 : rank + 2].astype(jnp.int32)
    slots = in_line(slots, place_ref, a_ref.shape[0] // rank)
    tile, width = x0_ref.shape[1:]
    lane_slot = lax.broadcasted_iota(jnp.int32, (tile, chunk), 1) // rank

    def step(c, low):
        part = pl.ds(pl.multiple_of(c * chunk, chunk), chunk)
        hidden = lax.dot_general(
            x0_ref[0], a_ref[part, :width], NT, preferred_element_type=jnp.float32
        )
        hidden += lax.dot_general(
            x1_ref[0], a_ref[part, width:], NT, preferred_element_type=jnp.float32
        )
        hidden = jnp.where(lane_slot + c * (chunk // rank) == slots, hidden, 0.0)
        for k in range(chunk // (2 * rank)):
            low += hidden[:, k * 2 * rank : (k + 1) * 2 * rank]
        return low

    start = jnp.zeros((tile, 2 * rank), jnp.float32)
    low = repeat(a_ref.shape[0] // chunk, step, start).T
    low_ref[0] = low[:rank] + low[rank:]


def low_part(place, packed, x0, x1, a_pieces, rank):
    devices, depth, tokens = packed.shape
    width = x0.shape[2]
    rows = a_pieces[0].shape[0]
    slots = line_length * rows
    if width % 64:
        a_pieces = [
            lax.dynamic_slice_in_dim(a, place[2] * 2 * width, 2 * width, 1) for a in a_pieces
        ]
    column = lambda place: 0 if width % 64 else place[2]
    return call(
        lambda *refs: low_kernel(512, rank, *refs),
        place,
        (devices,),
        [
            pl.BlockSpec((1, depth, tokens), lambda t, place: (t, 0, 0)),
            pl.BlockSpec((1, tokens, width), lambda t, place: (t, 0, 0)),
            pl.BlockSpec((1, tokens, width), lambda t, place: (t, 0, 0)),
        ]
        + [pl.BlockSpec((rows, 2 * width), lambda t, place: (0, column(place)))] * len(a_pieces),
        pl.BlockSpec((1, rank, tokens), lambda t, place: (t, 0, 0)),
        jax.ShapeDtypeStruct((devices, rank, tokens), jnp.float32),
        4 * devices * tokens * width * slots,
        4 * (devices * tokens + slots) * width,
        "low_part",
        (packed, x0, x1, *a_pieces),
        [pltpu.VMEM((slots, 2 * width), jnp.bfloat16)],
    )


def out_kernel(chunk, rank, place_ref, packed_ref, g_ref, w_ref, *refs):
    *pieces, out_ref, a_ref = refs
    put_together(pieces, a_ref)
    rows = packed_ref[0].astype(jnp.float32).T
    back, slots = rows[:, :rank], rows[:, rank + 1 : rank + 2].astype(jnp.int32)
    slots = in_line(slots, place_ref, a_ref.shape[0] // rank)
    tile = back.shape[0]
    repeated = jnp.concatenate([back] * (chunk // rank), axis=1)
    lane_slot = lax.broadcasted_iota(jnp.int32, (tile, chunk), 1) // rank

    def step(c, acc):
        keep = lane_slot + c * (chunk // rank) == slots
        masked = jnp.where(keep, repeated, 0.0).astype(jnp.bfloat16)
        block = a_ref[pl.ds(pl.multiple_of(c * chunk, chunk), chunk), :]
        return acc + jnp.dot(masked, block, preferred_element_type=jnp.float32)

    start = jnp.zeros((tile, a_ref.shape[1]), jnp.float32)
    acc = repeat(a_ref.shape[0] // chunk, step, start)
    base = lax.dot_general(g_ref[...], w_ref[...], NT, preferred_element_type=jnp.float32)
    out_ref[0] = (base + adapter_scale * acc).astype(out_ref.dtype)


def out_part(place, packed, g_all, w_cols, a_pieces, inner, rank):
    _, depth, tokens = packed.shape
    devices = g_all.shape[0] // tokens
    outs = g_all.shape[1]
    rows, width = a_pieces[0].shape
    slots = line_length * rows
    return call(
        lambda *refs: out_kernel(512, rank, *refs),
        place,
        (devices,),
        [
            pl.BlockSpec(
                (1, depth, tokens),
                lambda t, place: (((t // inner) * 2 + place[2]) * inner + t % inner, 0, 0),
            ),
            pl.BlockSpec((tokens, outs), lambda t, place: (t, 0)),
            pl.BlockSpec((width, outs), lambda t, place: (0, 0)),
        ]
        + [pl.BlockSpec((rows, width), lambda t, place: (0, 0))] * len(a_pieces),
        pl.BlockSpec((1, tokens, width), lambda t, place: (t, 0, 0)),
        jax.ShapeDtypeStruct((devices, tokens, width), jnp.bfloat16),
        2 * devices * tokens * width * (slots + outs),
        2 * devices * tokens * (width + outs) + 2 * slots * width,
        "out_part",
        (packed, g_all, w_cols, *a_pieces),
        [pltpu.VMEM((slots, width), jnp.bfloat16)],
    )


def grad_b_kernel(inner, resident, place_ref, packed_ref, low_ref, g_ref, out_ref, acc):
    rank = low_ref.shape[1]
    step = pl.program_id(0)
    low = low_ref[0]
    slots = packed_ref[0, rank : rank + 1, :].astype(jnp.float32)
    rows = []
    for line in range(line_length):
        for r in range(resident):
            slot = ((line * inner + place_ref[3]) * resident + r).astype(jnp.float32)
            rows.append(low * (slots == slot).astype(jnp.bfloat16))
    term = jnp.dot(jnp.concatenate(rows, axis=0), g_ref[...], preferred_element_type=jnp.float32)

    @pl.when(step == 0)
    def _():
        acc[...] = term

    @pl.when(step > 0)
    def _():
        acc[...] += term

    @pl.when(step == inner - 1)
    def _():
        out_ref[...] = acc[...].astype(jnp.bfloat16)


def grad_b_part(place, packed, low, g_all, inner, resident):
    _, depth, tokens = packed.shape
    outs = g_all.shape[1]
    rank = low.shape[1]
    rows = line_length * resident * rank
    return call(
        lambda *refs: grad_b_kernel(inner, resident, *refs),
        place,
        (inner,),
        [
            pl.BlockSpec(
                (1, depth, tokens),
                lambda t, place: ((place[0] * 2 + place[2]) * inner + t, 0, 0),
            ),
            pl.BlockSpec((1, rank, tokens), lambda t, place: (t, 0, 0)),
            pl.BlockSpec((tokens, outs), lambda t, place: (place[0] * inner + t, 0)),
        ],
        pl.BlockSpec((rows, outs), lambda t, place: (0, 0)),
        jax.ShapeDtypeStruct((rows, outs), jnp.bfloat16),
        2 * inner * tokens * outs * rows,
        2 * inner * tokens * outs,
        "grad_b_part",
        (packed, low, g_all),
        [pltpu.VMEM((rows, outs), jnp.float32)],
    )


def body(x, g, tok, adapter_slot, w, a, b):
    groups, inner = lax.axis_size("groups"), lax.axis_size("inner")
    gi, hi, pi = lax.axis_index("groups"), lax.axis_index("half"), lax.axis_index("pair")
    ji = lax.axis_index("inner")
    place = jnp.stack([gi, hi, pi, ji]).astype(jnp.int32)
    li = 2 * hi + pi
    size = groups * inner
    tokens, model = x.shape
    outs = g.shape[1]
    resident, _, rank = a.shape
    share = resident // groups
    count = inner * resident
    halves = line_length // groups
    width = model // size
    part = width // halves
    depth = outs // size
    line = ("half", "pair")

    b_mine = lax.dynamic_slice_in_dim(b, gi * share, share, 0)
    b_mine = b_mine.reshape(share * rank, outs)
    b_line = [b_mine]
    for away in range(1, line_length):
        pairs = [(i, (i - away) % line_length) for i in range(line_length)]
        b_line.append(lax.ppermute(b_mine, line, pairs))
    b_line = jnp.stack(b_line, axis=1).reshape(share * rank, line_length, size, depth)
    b_line = b_line.transpose(2, 0, 1, 3).reshape(size, share * rank, line_length * depth)
    matches = tok == lax.broadcasted_iota(jnp.int32, (tokens, adapter_slot.shape[0]), 1)
    slot = jnp.sum(jnp.where(matches, adapter_slot[None, :], 0), axis=1)
    a_mine = lax.dynamic_slice_in_dim(jnp.swapaxes(a, 1, 2), gi * share, share, 0)
    a_mine = a_mine.reshape(share * rank, groups, halves, inner, part)
    a_mine = a_mine.transpose(1, 3, 0, 2, 4).reshape(size, share * rank, width)
    g_mine = g.T.reshape(size, depth, tokens)
    slot_rows = jnp.broadcast_to(slot.astype(jnp.bfloat16)[None, None, :], (size, 16, tokens))
    height = max(share * rank, depth + 16)

    def tall(rows):
        return jnp.pad(rows, ((0, 0), (0, height - rows.shape[1]), (0, -rows.shape[2] % 128)))

    first = jnp.concatenate(
        [tall(a_mine), tall(jnp.concatenate([slot_rows, g_mine], axis=1)), tall(b_line)], axis=2
    )
    first = lax.all_to_all(first, plane, 0, 0, tiled=True)
    wide = width + -width % 128
    a_own = first[:, : share * rank, :width].reshape(count * rank, width)
    slot_all = first[:, 0, wide : wide + tokens].astype(jnp.int32)
    g_cols = first[:, 16 : 16 + depth, wide : wide + tokens]
    b_cols = first[:, : share * rank, wide + tokens : wide + tokens + line_length * depth]

    x_sends = split_columns(place, x, 2 * size, 2, part // 2)
    x_send, first = lax.optimization_barrier((x_sends[0], first))
    x_first = lax.all_to_all(x_send, cube, 0, 0, tiled=True)

    up = [(i, i + 1) for i in range(line_length - 1)]
    down = [(i + 1, i) for i in range(line_length - 1)]

    def hop(pieces, away):
        left, right = pieces
        return [
            lax.ppermute(left, line, up[away - 1 :]),
            lax.ppermute(right, line, down[: line_length - away]),
        ]

    hops = [hop((a_own, a_own), 1)]
    w_line = lax.all_gather(w, line, axis=0)
    g_all = lax.all_gather(g, plane, axis=0, tiled=True)

    def number(slot):
        owner, res = slot // resident, slot % resident
        return owner // inner, ((res // share) * inner + owner % inner) * share + res % share

    slot_line, slot_in = number(slot_all)
    slot_b = (((slot_line - li) % line_length) * count + slot_in)[:, None, :]
    back = back_part(place, slot_b, b_cols, g_cols, rank)
    back, x_first, hops[0], w_line = lax.optimization_barrier((back, x_first, hops[0], w_line))
    w_cols = lax.dynamic_slice_in_dim(w_line, gi * halves, halves, 0).reshape(width, outs)
    hops.append(hop(hops[0], 2))
    back = lax.all_to_all(back, plane, 0, 0, tiled=True)
    back = jnp.sum(back, axis=0).astype(jnp.bfloat16)
    slot_line, slot_in = number(slot)
    slot_a = slot_line * count + slot_in
    names = jnp.stack([slot, slot_a] + [slot] * 14).astype(jnp.bfloat16)
    packed = jnp.concatenate([back, names], axis=0)
    packed = jnp.broadcast_to(packed[None], (2 * size,) + packed.shape)
    packed = lax.all_to_all(packed, cube, 0, 0, tiled=True)

    x_send, packed = lax.optimization_barrier((x_sends[1], packed))
    x_second = lax.all_to_all(x_send, cube, 0, 0, tiled=True)

    swap = [(0, 1), (1, 0)]
    packed, hops[1], g_all = lax.optimization_barrier((packed, hops[1], g_all))
    hops.append(hop(hops[1], 3))
    other = grad_a_part(place, packed, x_first, (), groups, 2 * count, rank)
    got = [lax.ppermute(other, "half", swap)]
    x_second, hops[2] = lax.optimization_barrier((x_second, hops[2]))
    other = grad_a_part(place, packed, x_second, (), groups, 2 * count, rank)

    a_pieces = [a_own] + [h[0] for h in hops] + [h[1] for h in hops]
    a_pieces, other = lax.optimization_barrier((a_pieces, other))
    low = low_part(place, packed, x_first, x_second, a_pieces, rank)

    a_pieces, low = lax.optimization_barrier((a_pieces, low))
    low = lax.all_to_all(low, cube, 0, 0, tiled=True)
    out_cols = out_part(place, packed, g_all, w_cols, a_pieces, inner, rank)
    other, got[0], out_cols = lax.optimization_barrier((other, got[0], out_cols))
    got.append(lax.ppermute(other, "half", swap))
    me = gi * inner + ji
    if size > 8:
        out_back = lax.all_to_all(out_cols, plane, 0, 0, tiled=True)
        pieces = [out_back[me ^ m] for m in range(size)]
    else:
        pieces = [lax.dynamic_index_in_dim(out_cols, me, 0, keepdims=False)]
        for m in range(1, size):
            piece = lax.dynamic_index_in_dim(out_cols, me ^ m, 0, keepdims=False)
            pieces.append(lax.ppermute(piece, plane, [(i, i ^ m) for i in range(size)]))

    def own(x_cols, got):
        p = grad_a_part(place, packed, x_cols, (got,), groups, 2 * count, rank)
        return lax.all_to_all(
            p.reshape(2 * size, resident * rank, part // 2), cube, 0, 0, tiled=True
        )

    p_back = [own(x_first, got[0])]
    low = jnp.sum(low, axis=0).astype(jnp.bfloat16)
    low = jnp.broadcast_to(low[None], (inner,) + low.shape)
    low = lax.all_to_all(low, "inner", 0, 0, tiled=True)
    q = grad_b_part(place, packed, low, g_all, inner, resident)
    q = lax.all_to_all(q.reshape(line_length, resident * rank, outs), line, 0, 0, tiled=True)
    q, got[1], pieces = lax.optimization_barrier((q, got[1], pieces))
    grad_b = (adapter_scale * jnp.sum(q.astype(jnp.float32), axis=0)).astype(jnp.bfloat16)
    p_back.append(own(x_second, got[1]))
    input_gradient = join_rows(place, pieces, groups, halves, inner, part)
    grad_a = join_slots(place, p_back, resident).swapaxes(1, 2)
    return input_gradient, grad_a, grad_b.reshape(resident, rank, outs)


def solution(mesh):
    groups, rows = mesh.shape["groups"], mesh.shape["row"]
    whole = ("groups", "half", "pair", "inner")
    split = Mesh(mesh.devices.reshape(groups, 2, 2, rows // line_length), whole)
    row = ("half", "pair", "inner")
    return jax.shard_map(
        body,
        mesh=split,
        in_specs=(
            P(whole, None),
            P(whole, None),
            P(whole, None),
            P(),
            P(row, None),
            P(row, None, None),
            P(row, None, None),
        ),
        out_specs=(P(whole, None), P(whole, None, None), P(whole, None, None)),
        check_vma=False,
    )
```

```python
import jax
import jax.numpy as jnp
from jax import lax
from jax.experimental import pallas as pl
from jax.experimental.pallas import tpu as pltpu
from jax.sharding import Mesh, PartitionSpec as P

adapter_scale = 2.0
line_length = 4
plane = ("groups", "inner")
row = ("line", "inner")
vmem_limit = 56 * 1024 * 1024
NT = (((1,), (1,)), ((), ()))


def call(kernel, place, grid, in_specs, out_specs, out_shape, flops, moved, name, args, scratch=()):
    return pl.pallas_call(
        kernel,
        grid_spec=pltpu.PrefetchScalarGridSpec(
            num_scalar_prefetch=1,
            grid=grid,
            in_specs=in_specs,
            out_specs=out_specs,
            scratch_shapes=scratch,
        ),
        out_shape=out_shape,
        compiler_params=pltpu.CompilerParams(vmem_limit_bytes=vmem_limit),
        cost_estimate=pl.CostEstimate(flops=flops, bytes_accessed=moved, transcendentals=0),
        name=name,
    )(place, *args)


def repeat(count, step, start):
    if count <= 4:
        for i in range(count):
            start = step(i, start)
        return start
    return lax.fori_loop(0, count, step, start)


def move(name, sources, in_blocks, in_maps, outs, out_blocks, out_maps, grid, kernel, place):
    moved = 0
    for shape in outs:
        size = 4
        for n in shape:
            size *= n
        moved += size
    return call(
        kernel,
        place,
        grid,
        [pl.BlockSpec(block, index) for block, index in zip(in_blocks, in_maps)],
        [pl.BlockSpec(block, index) for block, index in zip(out_blocks, out_maps)],
        [jax.ShapeDtypeStruct(shape, jnp.bfloat16) for shape in outs],
        0,
        moved,
        name,
        sources,
    )


def columns_of(q, c, halves, inner):
    return ((q // inner) * halves + c) * inner + q % inner


def split_columns(place, x, groups, halves, inner, width):
    size, tokens = groups * inner, x.shape[0]
    if width % 128:
        x = x.reshape(tokens, groups, halves, inner, width)
        return [
            x[:, :, c].transpose(1, 2, 0, 3).reshape(size, tokens, width) for c in range(halves)
        ]
    tile = min(tokens, 64)

    def kernel(place_ref, x_ref, *out_refs):
        for q in range(size):
            for c in range(halves):
                first = columns_of(q, c, halves, inner) * width
                out_refs[c][q] = x_ref[:, first : first + width]

    return move(
        "split_columns", [x], [(tile, x.shape[1])], [lambda t, place: (t, 0)],
        [(size, tokens, width)] * halves, [(size, tile, width)] * halves,
        [lambda t, place: (0, t, 0)] * halves, (tokens // tile,), kernel, place,
    )


def join_slots(place, parts, resident, groups, inner):
    size, rows, width = parts[0].shape
    halves, rank = len(parts), rows // resident
    if width % 128:
        parts = [p.reshape(groups, inner, rows, width) for p in parts]
        joined = jnp.stack(parts, axis=1).transpose(3, 0, 1, 2, 4)
        return joined.reshape(resident, rank, -1)

    def kernel(place_ref, *refs):
        for q in range(size):
            for c in range(halves):
                first = columns_of(q, c, halves, inner) * width
                refs[-1][0, :, first : first + width] = refs[c][q]

    return move(
        "join_slots", parts, [(size, rank, width)] * halves, [lambda r, place: (0, r, 0)] * halves,
        [(resident, rank, size * halves * width)], [(1, rank, size * halves * width)],
        [lambda r, place: (r, 0, 0)], (resident,), kernel, place,
    )[0]


def join_rows(place, rows, groups, halves, inner, part):
    size, tokens = rows.shape[:2]
    if part % 128:
        rows = rows.reshape(groups, inner, tokens, halves, part)
        return rows.transpose(2, 0, 3, 1, 4).reshape(tokens, -1)
    tile = min(tokens, 64)
    model = size * halves * part

    def kernel(place_ref, rows_ref, out_ref):
        for q in range(size):
            for c in range(halves):
                first = columns_of(q, c, halves, inner) * part
                out_ref[:, first : first + part] = rows_ref[q, :, c * part : (c + 1) * part]

    return move(
        "join_rows", [rows], [(size, tile, halves * part)], [lambda t, place: (0, t, 0)],
        [(tokens, model)], [(tile, model)], [lambda t, place: (t, 0)], (tokens // tile,),
        kernel, place,
    )[0]


def slot_sums(packed_ref, x_ref, rank, first, count):
    devices, _, tokens = packed_ref.shape
    chunk = min(devices, 4)

    def step(c, total):
        columns = []
        for d in range(chunk):
            back = packed_ref[c * chunk + d, :rank, :]
            slots = packed_ref[c * chunk + d, rank : rank + 1, :].astype(jnp.float32)
            rows = [
                back * (slots == (first + i).astype(jnp.float32)).astype(jnp.bfloat16)
                for i in range(count)
            ]
            columns.append(jnp.concatenate(rows, axis=0))
        x = x_ref[pl.ds(c * chunk, chunk)].reshape(chunk * tokens, x_ref.shape[2])
        return total + jnp.dot(
            jnp.concatenate(columns, axis=1), x, preferred_element_type=jnp.float32
        )

    start = jnp.zeros((count * rank, x_ref.shape[2]), jnp.float32)
    return repeat(devices // chunk, step, start)


def send_kernel(slots_line, count, rank, away, place_ref, packed_ref, x_ref, *refs):
    line = place_ref[1]
    outs, got = refs[-2:], refs[:-2]
    ways = ((line + away < line_length, line + away), (line >= away, line - away))
    for way, (inside, target) in enumerate(ways):

        @pl.when(inside)
        def _(way=way, target=target):
            first = target * slots_line + pl.program_id(1) * count
            total = slot_sums(packed_ref, x_ref, rank, first, count)
            if got:
                total += got[way][0].astype(jnp.float32)
            outs[way][0] = total.astype(jnp.bfloat16)


def own_kernel(slots_line, count, rank, place_ref, packed_ref, x_ref, right_ref, left_ref, out_ref):
    first = place_ref[1] * slots_line + pl.program_id(1) * count
    total = slot_sums(packed_ref, x_ref, rank, first, count)
    total += right_ref[0].astype(jnp.float32) + left_ref[0].astype(jnp.float32)
    out_ref[0] = (adapter_scale * total).astype(jnp.bfloat16)


def grad_a_step(place, packed, x_cols, got, away, groups, slots_line, rank):
    devices, depth, tokens = packed.shape
    width = x_cols.shape[2]
    local = devices // groups
    count = 8
    rows = count * rank
    block = pl.BlockSpec((1, rows, width), lambda g, s, place: (g, s, 0))
    shape = jax.ShapeDtypeStruct((groups, slots_line * rank, width), jnp.bfloat16)
    ways = 1 if away == 0 else 2
    if away == 0:
        kernel = lambda *refs: own_kernel(slots_line, count, rank, *refs)
    else:
        kernel = lambda *refs: send_kernel(slots_line, count, rank, away, *refs)
    return call(
        kernel,
        place,
        (groups, slots_line // count),
        [
            pl.BlockSpec((local, depth, tokens), lambda g, s, place: (g, 0, 0)),
            pl.BlockSpec((local, tokens, width), lambda g, s, place: (g, 0, 0)),
        ]
        + [block] * len(got),
        block if away == 0 else [block, block],
        shape if away == 0 else [shape, shape],
        ways * 2 * devices * tokens * width * slots_line * rank,
        2 * devices * tokens * width + 2 * groups * slots_line * rank * width * (ways + len(got)),
        "grad_a_step" + str(away),
        (packed, x_cols, *got),
    )


def in_line(slots, place_ref, total):
    slots -= place_ref[1] * (total // line_length)
    return jnp.where(slots < 0, slots + total, slots)


def put_together(pieces, a_ref):
    @pl.when(pl.program_id(0) == 0)
    def _():
        rows = pieces[0].shape[0]
        a_ref[:rows] = pieces[0][...]
        for k in range(1, line_length):
            left, right = pieces[line_length - k], pieces[line_length - 1 + k]
            a_ref[k * rows : (k + 1) * rows] = left[...] + right[...]


def low_kernel(chunk, rank, place_ref, packed_ref, x0_ref, x1_ref, *refs):
    *pieces, low_ref, a_ref = refs
    put_together(pieces, a_ref)
    slots = packed_ref[0].astype(jnp.float32).T[:, rank + 1 : rank + 2].astype(jnp.int32)
    slots = in_line(slots, place_ref, a_ref.shape[0] // rank)
    tile, width = x0_ref.shape[1:]
    lane_slot = lax.broadcasted_iota(jnp.int32, (tile, chunk), 1) // rank

    def step(c, low):
        part = pl.ds(pl.multiple_of(c * chunk, chunk), chunk)
        hidden = lax.dot_general(
            x0_ref[0], a_ref[part, :width], NT, preferred_element_type=jnp.float32
        )
        hidden += lax.dot_general(
            x1_ref[0], a_ref[part, width:], NT, preferred_element_type=jnp.float32
        )
        hidden = jnp.where(lane_slot + c * (chunk // rank) == slots, hidden, 0.0)
        for k in range(chunk // (2 * rank)):
            low += hidden[:, k * 2 * rank : (k + 1) * 2 * rank]
        return low

    start = jnp.zeros((tile, 2 * rank), jnp.float32)
    low = repeat(a_ref.shape[0] // chunk, step, start).T
    low_ref[0] = low[:rank] + low[rank:]


def low_part(place, packed, x0, x1, a_pieces, rank):
    devices, depth, tokens = packed.shape
    width = x0.shape[2]
    rows = a_pieces[0].shape[0]
    slots = line_length * rows
    return call(
        lambda *refs: low_kernel(512, rank, *refs),
        place,
        (devices,),
        [
            pl.BlockSpec((1, depth, tokens), lambda t, place: (t, 0, 0)),
            pl.BlockSpec((1, tokens, width), lambda t, place: (t, 0, 0)),
            pl.BlockSpec((1, tokens, width), lambda t, place: (t, 0, 0)),
        ]
        + [pl.BlockSpec((rows, 2 * width), lambda t, place: (0, 0))] * len(a_pieces),
        pl.BlockSpec((1, rank, tokens), lambda t, place: (t, 0, 0)),
        jax.ShapeDtypeStruct((devices, rank, tokens), jnp.float32),
        4 * devices * tokens * width * slots,
        4 * (devices * tokens + slots) * width,
        "low_part",
        (packed, x0, x1, *a_pieces),
        [pltpu.VMEM((slots, 2 * width), jnp.bfloat16)],
    )


def out_kernel(chunk, rank, place_ref, packed_ref, g_ref, w_ref, *refs):
    *pieces, out_ref, a_ref = refs
    put_together(pieces, a_ref)
    rows = packed_ref[0].astype(jnp.float32).T
    back, slots = rows[:, :rank], rows[:, rank + 1 : rank + 2].astype(jnp.int32)
    slots = in_line(slots, place_ref, a_ref.shape[0] // rank)
    tile = back.shape[0]
    repeated = jnp.concatenate([back] * (chunk // rank), axis=1)
    lane_slot = lax.broadcasted_iota(jnp.int32, (tile, chunk), 1) // rank

    def step(c, acc):
        keep = lane_slot + c * (chunk // rank) == slots
        masked = jnp.where(keep, repeated, 0.0).astype(jnp.bfloat16)
        block = a_ref[pl.ds(pl.multiple_of(c * chunk, chunk), chunk), :]
        return acc + jnp.dot(masked, block, preferred_element_type=jnp.float32)

    start = jnp.zeros((tile, a_ref.shape[1]), jnp.float32)
    acc = repeat(a_ref.shape[0] // chunk, step, start)
    base = lax.dot_general(g_ref[...], w_ref[...], NT, preferred_element_type=jnp.float32)
    out_ref[0] = (base + adapter_scale * acc).astype(out_ref.dtype)


def out_part(place, packed, g_all, w_cols, a_pieces, rank):
    _, depth, tokens = packed.shape
    devices = g_all.shape[0] // tokens
    outs = g_all.shape[1]
    rows, width = a_pieces[0].shape
    slots = line_length * rows
    return call(
        lambda *refs: out_kernel(512, rank, *refs),
        place,
        (devices,),
        [
            pl.BlockSpec((1, depth, tokens), lambda t, place: (t, 0, 0)),
            pl.BlockSpec((tokens, outs), lambda t, place: (t, 0)),
            pl.BlockSpec((width, outs), lambda t, place: (0, 0)),
        ]
        + [pl.BlockSpec((rows, width), lambda t, place: (0, 0))] * len(a_pieces),
        pl.BlockSpec((1, tokens, width), lambda t, place: (t, 0, 0)),
        jax.ShapeDtypeStruct((devices, tokens, width), jnp.bfloat16),
        2 * devices * tokens * width * (slots + outs),
        2 * devices * tokens * (width + outs) + 2 * slots * width,
        "out_part",
        (packed, g_all, w_cols, *a_pieces),
        [pltpu.VMEM((slots, width), jnp.bfloat16)],
    )


def body(x, g, tok, adapter_slot, w, a, b):
    groups, inner = lax.axis_size("groups"), lax.axis_size("inner")
    gi, li, ji = lax.axis_index("groups"), lax.axis_index("line"), lax.axis_index("inner")
    place = jnp.stack([gi, li, ji]).astype(jnp.int32)
    size = groups * inner
    devices = line_length * inner
    tokens, model = x.shape
    outs = g.shape[1]
    resident, _, rank = a.shape
    share = resident // groups
    count = inner * resident
    halves = line_length // groups
    width = model // size
    part = width // halves
    adapters = adapter_slot.shape[0]
    capacity = max(2, 2 * tokens // adapters)

    step = ("groups", "line")
    w_mate = lax.ppermute(w, step, [(0, 1), (1, 0), (6, 7), (7, 6)])
    odd = li % 2 == 1
    w_both = jnp.concatenate([jnp.where(odd, w_mate, w), jnp.where(odd, w, w_mate)], axis=0)
    w_near = lax.ppermute(w_both, step, [(1, 2), (6, 5)])
    w_far = lax.ppermute(w_near, step, [(2, 3), (5, 4)])

    a_mine = lax.dynamic_slice_in_dim(jnp.swapaxes(a, 1, 2), gi * share, share, 0)
    a_mine = a_mine.reshape(share * rank, groups, halves, inner, part)
    a_mine = a_mine.transpose(1, 3, 0, 2, 4).reshape(size, share * rank, width)
    a_own = lax.all_to_all(a_mine, plane, 0, 0, tiled=True).reshape(count * rank, width)

    matches = tok == lax.broadcasted_iota(jnp.int32, (tokens, adapters), 1)
    slot = jnp.sum(jnp.where(matches, adapter_slot[None, :], 0), axis=1)
    running = jnp.cumsum(matches.astype(jnp.int32), axis=0)
    within = jnp.sum(jnp.where(matches, running - 1, 0), axis=1)
    position = slot * capacity + within
    at = lax.broadcasted_iota(jnp.int32, (adapters * capacity, tokens), 0) == position[None, :]
    at = at.astype(jnp.bfloat16)

    def route(rows):
        rows = rows.reshape(devices, resident * capacity, rows.shape[1])
        rows = lax.all_to_all(rows, row, 0, 0, tiled=True)
        return rows.reshape(devices, resident, capacity, rows.shape[2])

    g_send = jnp.dot(at, g, preferred_element_type=jnp.float32).astype(jnp.bfloat16)
    g_send, a_own = lax.optimization_barrier((g_send, a_own))
    g_rows = route(g_send)
    back = jnp.einsum("hjct,jrt->hjcr", g_rows, b, preferred_element_type=jnp.float32)
    back = back.astype(jnp.bfloat16).reshape(devices, resident * capacity, rank)

    x_sends = split_columns(place, x, groups, halves, inner, part)
    x_send, g_rows = lax.optimization_barrier((x_sends[0], g_rows))
    x_cols = [lax.all_to_all(x_send, plane, 0, 0, tiled=True)]

    up = [(i, i + 1) for i in range(line_length - 1)]
    down = [(i + 1, i) for i in range(line_length - 1)]

    def hop(pieces, away):
        left, right = pieces
        return [
            lax.ppermute(left, "line", up[away - 1 :]),
            lax.ppermute(right, "line", down[: line_length - away]),
        ]

    hops = [hop((a_own, a_own), 1)]
    back, x_cols[0], hops[0] = lax.optimization_barrier((back, x_cols[0], hops[0]))
    hops.append(hop(hops[0], 2))
    back = lax.all_to_all(back, row, 0, 0, tiled=True).reshape(adapters * capacity, rank)
    back = lax.dot_general(
        back, at, (((0,), (0,)), ((), ())), preferred_element_type=jnp.float32
    ).astype(jnp.bfloat16)
    owner, res = slot // resident, slot % resident
    slot_a = (owner // inner) * count + ((res // share) * inner + owner % inner) * share + res % share
    names = jnp.stack([slot, slot_a] + [slot] * 14).astype(jnp.bfloat16)
    packed = jnp.concatenate([back, names], axis=0)
    packed = jnp.broadcast_to(packed[None], (size,) + packed.shape)
    packed = lax.all_to_all(packed, plane, 0, 0, tiled=True)

    x_send, packed, hops[1] = lax.optimization_barrier((x_sends[1], packed, hops[1]))
    hops.append(hop(hops[1], 3))
    x_cols.append(lax.all_to_all(x_send, plane, 0, 0, tiled=True))
    g_send, x_cols[1] = lax.optimization_barrier((g, x_cols[1]))
    g_all = jnp.broadcast_to(g_send[None], (size, tokens, outs))
    g_all = lax.all_to_all(g_all, plane, 0, 0, tiled=True).reshape(size * tokens, outs)

    def send(c, got, away):
        sums = grad_a_step(place, packed, x_cols[c], got, away, groups, count, rank)
        ahead = [(i, i + 1) for i in range(line_length - away)]
        behind = [(i, i - 1) for i in range(away, line_length)]
        moved = (lax.ppermute(sums[0], "line", ahead), lax.ppermute(sums[1], "line", behind))
        return moved, sums[0]

    def own(c, got):
        p = grad_a_step(place, packed, x_cols[c], got, 0, groups, count, rank)
        return lax.all_to_all(
            p.reshape(size, resident * rank, part), plane, 0, 0, tiled=True
        )

    first, second = (send(c, (), 3)[0] for c in range(2))
    first, done = send(0, first, 2)

    a_pieces = [a_own] + [h[0] for h in hops] + [h[1] for h in hops]
    a_pieces, done = lax.optimization_barrier((a_pieces, done))
    low = low_part(place, packed, x_cols[0], x_cols[1], a_pieces, rank)
    second, low = lax.optimization_barrier((second, low))
    second, done = send(1, second, 2)
    first, done = lax.optimization_barrier((first, done))
    first, done = send(0, first, 1)
    low = lax.all_to_all(low, plane, 0, 0, tiled=True)

    w_cols = jnp.where(li // 2 == gi, w_both, w_near + w_far)
    a_pieces, w_cols, low, done = lax.optimization_barrier((a_pieces, w_cols, low, done))
    out_cols = out_part(place, packed, g_all, w_cols, a_pieces, rank)
    second, out_cols = lax.optimization_barrier((second, out_cols))
    out_back = lax.all_to_all(out_cols, plane, 0, 0, tiled=True)
    second, done = send(1, second, 1)
    first, done = lax.optimization_barrier((first, done))
    p_back = [own(0, first), own(1, second)]

    low = jnp.sum(low, axis=0).astype(jnp.bfloat16)
    low = lax.dot_general(at, low, NT, preferred_element_type=jnp.float32).astype(jnp.bfloat16)
    low, out_back, done = lax.optimization_barrier((low, out_back, done))
    low = route(low)
    grad_b = jnp.einsum("hjcr,hjco->jro", low, g_rows, preferred_element_type=jnp.float32)
    grad_b = (adapter_scale * grad_b).astype(jnp.bfloat16)
    input_gradient = join_rows(place, out_back, groups, halves, inner, part)
    grad_a = join_slots(place, p_back, resident, groups, inner).swapaxes(1, 2)
    return input_gradient, grad_a, grad_b


def solution(mesh):
    groups, rows = mesh.shape["groups"], mesh.shape["row"]
    whole = ("groups", "line", "inner")
    split = Mesh(mesh.devices.reshape(groups, line_length, rows // line_length), whole)
    return jax.shard_map(
        body,
        mesh=split,
        in_specs=(
            P(whole, None),
            P(whole, None),
            P(whole, None),
            P(),
            P(row, None),
            P(row, None, None),
            P(row, None, None),
        ),
        out_specs=(P(whole, None), P(whole, None, None), P(whole, None, None)),
        check_vma=False,
    )
```

```python
import jax
import jax.numpy as jnp
from jax import lax
from jax.experimental import pallas as pl
from jax.experimental.pallas import tpu as pltpu
from jax.sharding import Mesh, PartitionSpec as P

adapter_scale = 2.0
line_length = 4
plane = ("groups", "inner")
row = ("line", "inner")
vmem_limit = 56 * 1024 * 1024
NT = (((1,), (1,)), ((), ()))


def call(kernel, place, grid, in_specs, out_specs, out_shape, flops, moved, name, args, scratch=()):
    return pl.pallas_call(
        kernel,
        grid_spec=pltpu.PrefetchScalarGridSpec(
            num_scalar_prefetch=1,
            grid=grid,
            in_specs=in_specs,
            out_specs=out_specs,
            scratch_shapes=scratch,
        ),
        out_shape=out_shape,
        compiler_params=pltpu.CompilerParams(vmem_limit_bytes=vmem_limit),
        cost_estimate=pl.CostEstimate(flops=flops, bytes_accessed=moved, transcendentals=0),
        name=name,
    )(place, *args)


def repeat(count, step, start):
    if count <= 4:
        for i in range(count):
            start = step(i, start)
        return start
    return lax.fori_loop(0, count, step, start)


def move(name, sources, in_blocks, in_maps, outs, out_blocks, out_maps, grid, kernel, place):
    moved = 0
    for shape in outs:
        size = 4
        for n in shape:
            size *= n
        moved += size
    return call(
        kernel,
        place,
        grid,
        [pl.BlockSpec(block, index) for block, index in zip(in_blocks, in_maps)],
        [pl.BlockSpec(block, index) for block, index in zip(out_blocks, out_maps)],
        [jax.ShapeDtypeStruct(shape, jnp.bfloat16) for shape in outs],
        0,
        moved,
        name,
        sources,
    )


def columns_of(q, c, halves, inner):
    return ((q // inner) * halves + c) * inner + q % inner


def split_columns(place, x, groups, halves, inner, width):
    size, tokens = groups * inner, x.shape[0]
    if width % 128:
        x = x.reshape(tokens, groups, halves, inner, width)
        return [
            x[:, :, c].transpose(1, 2, 0, 3).reshape(size, tokens, width) for c in range(halves)
        ]
    tile = min(tokens, 64)

    def kernel(place_ref, x_ref, *out_refs):
        for q in range(size):
            for c in range(halves):
                first = columns_of(q, c, halves, inner) * width
                out_refs[c][q] = x_ref[:, first : first + width]

    return move(
        "split_columns", [x], [(tile, x.shape[1])], [lambda t, place: (t, 0)],
        [(size, tokens, width)] * halves, [(size, tile, width)] * halves,
        [lambda t, place: (0, t, 0)] * halves, (tokens // tile,), kernel, place,
    )


def split_maps(place, maps, groups, halves, inner, width):
    slots, rank, model = maps.shape
    size, share = groups * inner, slots // groups
    if width % 128:
        mine = lax.dynamic_slice_in_dim(maps, place[0] * share, share, 0)
        mine = mine.reshape(share * rank, groups, halves, inner, width)
        return mine.transpose(1, 3, 0, 2, 4).reshape(size, share * rank, halves * width)

    def kernel(place_ref, maps_ref, out_ref):
        for q in range(size):
            for c in range(halves):
                first = columns_of(q, c, halves, inner) * width
                out_ref[q, :, c * width : (c + 1) * width] = maps_ref[0, :, first : first + width]

    tile = min(rank, 32)
    steps = rank // tile
    return move(
        "split_maps", [maps], [(1, tile, model)],
        [lambda s, r, place: (place[0] * share + s, r, 0)],
        [(size, share * rank, halves * width)], [(size, tile, halves * width)],
        [lambda s, r, place: (0, s * steps + r, 0)], (share, steps), kernel, place,
    )[0]


def join_slots(place, parts, resident, groups, inner):
    size, rows, width = parts[0].shape
    halves, rank = len(parts), rows // resident
    if width % 128:
        parts = [p.reshape(groups, inner, rows, width) for p in parts]
        joined = jnp.stack(parts, axis=1).transpose(3, 0, 1, 2, 4)
        return joined.reshape(resident, rank, -1)

    def kernel(place_ref, *refs):
        for q in range(size):
            for c in range(halves):
                first = columns_of(q, c, halves, inner) * width
                refs[-1][0, :, first : first + width] = refs[c][q]

    return move(
        "join_slots", parts, [(size, rank, width)] * halves, [lambda r, place: (0, r, 0)] * halves,
        [(resident, rank, size * halves * width)], [(1, rank, size * halves * width)],
        [lambda r, place: (r, 0, 0)], (resident,), kernel, place,
    )[0]


def join_rows(place, rows, groups, halves, inner, part):
    size, tokens = rows.shape[:2]
    if part % 128:
        rows = rows.reshape(groups, inner, tokens, halves, part)
        return rows.transpose(2, 0, 3, 1, 4).reshape(tokens, -1)
    tile = min(tokens, 64)
    model = size * halves * part

    def kernel(place_ref, rows_ref, out_ref):
        for q in range(size):
            for c in range(halves):
                first = columns_of(q, c, halves, inner) * part
                out_ref[:, first : first + part] = rows_ref[q, :, c * part : (c + 1) * part]

    return move(
        "join_rows", [rows], [(size, tile, halves * part)], [lambda t, place: (0, t, 0)],
        [(tokens, model)], [(tile, model)], [lambda t, place: (t, 0)], (tokens // tile,),
        kernel, place,
    )[0]


def slot_sums(packed_ref, x_ref, rank, first, count):
    devices, _, tokens = packed_ref.shape
    chunk = min(devices, 4)

    def step(c, total):
        columns = []
        for d in range(chunk):
            back = packed_ref[c * chunk + d, :rank, :]
            slots = packed_ref[c * chunk + d, rank : rank + 1, :].astype(jnp.float32)
            rows = [
                back * (slots == (first + i).astype(jnp.float32)).astype(jnp.bfloat16)
                for i in range(count)
            ]
            columns.append(jnp.concatenate(rows, axis=0))
        x = x_ref[pl.ds(c * chunk, chunk)].reshape(chunk * tokens, x_ref.shape[2])
        return total + jnp.dot(
            jnp.concatenate(columns, axis=1), x, preferred_element_type=jnp.float32
        )

    start = jnp.zeros((count * rank, x_ref.shape[2]), jnp.float32)
    return repeat(devices // chunk, step, start)


def send_kernel(slots_line, count, rank, away, place_ref, packed_ref, x_ref, *refs):
    line = place_ref[1]
    outs, got = refs[-2:], refs[:-2]
    ways = ((line + away < line_length, line + away), (line >= away, line - away))
    for way, (inside, target) in enumerate(ways):

        @pl.when(inside)
        def _(way=way, target=target):
            first = target * slots_line + pl.program_id(1) * count
            total = slot_sums(packed_ref, x_ref, rank, first, count)
            if got:
                total += got[way][0].astype(jnp.float32)
            outs[way][0] = total.astype(jnp.bfloat16)


def own_kernel(slots_line, count, rank, place_ref, packed_ref, x_ref, right_ref, left_ref, out_ref):
    first = place_ref[1] * slots_line + pl.program_id(1) * count
    total = slot_sums(packed_ref, x_ref, rank, first, count)
    total += right_ref[0].astype(jnp.float32) + left_ref[0].astype(jnp.float32)
    out_ref[0] = (adapter_scale * total).astype(jnp.bfloat16)


def grad_a_step(place, packed, x_cols, got, away, groups, slots_line, rank):
    devices, depth, tokens = packed.shape
    width = x_cols.shape[2]
    local = devices // groups
    count = 8
    rows = count * rank
    block = pl.BlockSpec((1, rows, width), lambda g, s, place: (g, s, 0))
    shape = jax.ShapeDtypeStruct((groups, slots_line * rank, width), jnp.bfloat16)
    ways = 1 if away == 0 else 2
    if away == 0:
        kernel = lambda *refs: own_kernel(slots_line, count, rank, *refs)
    else:
        kernel = lambda *refs: send_kernel(slots_line, count, rank, away, *refs)
    return call(
        kernel,
        place,
        (groups, slots_line // count),
        [
            pl.BlockSpec((local, depth, tokens), lambda g, s, place: (g, 0, 0)),
            pl.BlockSpec((local, tokens, width), lambda g, s, place: (g, 0, 0)),
        ]
        + [block] * len(got),
        block if away == 0 else [block, block],
        shape if away == 0 else [shape, shape],
        ways * 2 * devices * tokens * width * slots_line * rank,
        2 * devices * tokens * width + 2 * groups * slots_line * rank * width * (ways + len(got)),
        "grad_a_step" + str(away),
        (packed, x_cols, *got),
    )


def in_line(slots, place_ref, total):
    slots -= place_ref[1] * (total // line_length)
    return jnp.where(slots < 0, slots + total, slots)


def put_together(pieces, a_ref):
    @pl.when(pl.program_id(0) == 0)
    def _():
        rows = pieces[0].shape[0]
        a_ref[:rows] = pieces[0][...]
        for k in range(1, line_length):
            left, right = pieces[line_length - k], pieces[line_length - 1 + k]
            a_ref[k * rows : (k + 1) * rows] = left[...] + right[...]


def low_kernel(chunk, rank, place_ref, packed_ref, x0_ref, x1_ref, *refs):
    *pieces, low_ref, a_ref = refs
    put_together(pieces, a_ref)
    slots = packed_ref[0].astype(jnp.float32).T[:, rank + 1 : rank + 2].astype(jnp.int32)
    slots = in_line(slots, place_ref, a_ref.shape[0] // rank)
    tile, width = x0_ref.shape[1:]
    lane_slot = lax.broadcasted_iota(jnp.int32, (tile, chunk), 1) // rank

    def step(c, low):
        part = pl.ds(pl.multiple_of(c * chunk, chunk), chunk)
        hidden = lax.dot_general(
            x0_ref[0], a_ref[part, :width], NT, preferred_element_type=jnp.float32
        )
        hidden += lax.dot_general(
            x1_ref[0], a_ref[part, width:], NT, preferred_element_type=jnp.float32
        )
        hidden = jnp.where(lane_slot + c * (chunk // rank) == slots, hidden, 0.0)
        for k in range(chunk // (2 * rank)):
            low += hidden[:, k * 2 * rank : (k + 1) * 2 * rank]
        return low

    start = jnp.zeros((tile, 2 * rank), jnp.float32)
    low = repeat(a_ref.shape[0] // chunk, step, start).T
    low_ref[0] = low[:rank] + low[rank:]


def low_part(place, packed, x0, x1, a_pieces, rank):
    devices, depth, tokens = packed.shape
    width = x0.shape[2]
    rows = a_pieces[0].shape[0]
    slots = line_length * rows
    return call(
        lambda *refs: low_kernel(512, rank, *refs),
        place,
        (devices,),
        [
            pl.BlockSpec((1, depth, tokens), lambda t, place: (t, 0, 0)),
            pl.BlockSpec((1, tokens, width), lambda t, place: (t, 0, 0)),
            pl.BlockSpec((1, tokens, width), lambda t, place: (t, 0, 0)),
        ]
        + [pl.BlockSpec((rows, 2 * width), lambda t, place: (0, 0))] * len(a_pieces),
        pl.BlockSpec((1, rank, tokens), lambda t, place: (t, 0, 0)),
        jax.ShapeDtypeStruct((devices, rank, tokens), jnp.float32),
        4 * devices * tokens * width * slots,
        4 * (devices * tokens + slots) * width,
        "low_part",
        (packed, x0, x1, *a_pieces),
        [pltpu.VMEM((slots, 2 * width), jnp.bfloat16)],
    )


def out_kernel(chunk, rank, place_ref, packed_ref, g_ref, w_ref, *refs):
    *pieces, out_ref, a_ref = refs
    put_together(pieces, a_ref)
    rows = packed_ref[0].astype(jnp.float32).T
    back, slots = rows[:, :rank], rows[:, rank + 1 : rank + 2].astype(jnp.int32)
    slots = in_line(slots, place_ref, a_ref.shape[0] // rank)
    tile = back.shape[0]
    repeated = jnp.concatenate([back] * (chunk // rank), axis=1)
    lane_slot = lax.broadcasted_iota(jnp.int32, (tile, chunk), 1) // rank

    def step(c, acc):
        keep = lane_slot + c * (chunk // rank) == slots
        masked = jnp.where(keep, repeated, 0.0).astype(jnp.bfloat16)
        block = a_ref[pl.ds(pl.multiple_of(c * chunk, chunk), chunk), :]
        return acc + jnp.dot(masked, block, preferred_element_type=jnp.float32)

    start = jnp.zeros((tile, a_ref.shape[1]), jnp.float32)
    acc = repeat(a_ref.shape[0] // chunk, step, start)
    base = lax.dot_general(g_ref[...], w_ref[...], NT, preferred_element_type=jnp.float32)
    out_ref[0] = (base + adapter_scale * acc).astype(out_ref.dtype)


def out_part(place, packed, g_all, w_cols, a_pieces, rank):
    _, depth, tokens = packed.shape
    devices = g_all.shape[0] // tokens
    outs = g_all.shape[1]
    rows, width = a_pieces[0].shape
    slots = line_length * rows
    return call(
        lambda *refs: out_kernel(512, rank, *refs),
        place,
        (devices,),
        [
            pl.BlockSpec((1, depth, tokens), lambda t, place: (t, 0, 0)),
            pl.BlockSpec((tokens, outs), lambda t, place: (t, 0)),
            pl.BlockSpec((width, outs), lambda t, place: (0, 0)),
        ]
        + [pl.BlockSpec((rows, width), lambda t, place: (0, 0))] * len(a_pieces),
        pl.BlockSpec((1, tokens, width), lambda t, place: (t, 0, 0)),
        jax.ShapeDtypeStruct((devices, tokens, width), jnp.bfloat16),
        2 * devices * tokens * width * (slots + outs),
        2 * devices * tokens * (width + outs) + 2 * slots * width,
        "out_part",
        (packed, g_all, w_cols, *a_pieces),
        [pltpu.VMEM((slots, width), jnp.bfloat16)],
    )


def body(x, g, tok, adapter_slot, w, a, b):
    groups, inner = lax.axis_size("groups"), lax.axis_size("inner")
    gi, li, ji = lax.axis_index("groups"), lax.axis_index("line"), lax.axis_index("inner")
    place = jnp.stack([gi, li, ji]).astype(jnp.int32)
    size = groups * inner
    devices = line_length * inner
    tokens, model = x.shape
    outs = g.shape[1]
    resident, _, rank = a.shape
    share = resident // groups
    count = inner * resident
    halves = line_length // groups
    width = model // size
    part = width // halves
    adapters = adapter_slot.shape[0]
    capacity = max(2, 2 * tokens // adapters)

    step = ("groups", "line")
    w_mate = lax.ppermute(w, step, [(0, 1), (1, 0), (6, 7), (7, 6)])

    a_mine = split_maps(place, jnp.swapaxes(a, 1, 2), groups, halves, inner, part)
    a_own = lax.all_to_all(a_mine, plane, 0, 0, tiled=True).reshape(count * rank, width)

    matches = tok == lax.broadcasted_iota(jnp.int32, (tokens, adapters), 1)
    slot = jnp.sum(jnp.where(matches, adapter_slot[None, :], 0), axis=1)
    running = jnp.cumsum(matches.astype(jnp.int32), axis=0)
    within = jnp.sum(jnp.where(matches, running - 1, 0), axis=1)
    position = slot * capacity + within
    at = lax.broadcasted_iota(jnp.int32, (adapters * capacity, tokens), 0) == position[None, :]
    at = at.astype(jnp.bfloat16)

    def route(rows):
        rows = rows.reshape(devices, resident * capacity, rows.shape[1])
        rows = lax.all_to_all(rows, row, 0, 0, tiled=True)
        return rows.reshape(devices, resident, capacity, rows.shape[2])

    g_send = jnp.dot(at, g, preferred_element_type=jnp.float32).astype(jnp.bfloat16)
    g_send, a_own, w_mate = lax.optimization_barrier((g_send, a_own, w_mate))
    odd = li % 2 == 1
    w_both = jnp.concatenate([jnp.where(odd, w_mate, w), jnp.where(odd, w, w_mate)], axis=0)
    w_near = lax.ppermute(w_both, step, [(1, 2), (6, 5)])
    g_rows = route(g_send)
    back = jnp.einsum("hjct,jrt->hjcr", g_rows, b, preferred_element_type=jnp.float32)
    back = back.astype(jnp.bfloat16).reshape(devices, resident * capacity, rank)

    up = [(i, i + 1) for i in range(line_length - 1)]
    down = [(i + 1, i) for i in range(line_length - 1)]

    def hop(pieces, away):
        left, right = pieces
        return [
            lax.ppermute(left, "line", up[away - 1 :]),
            lax.ppermute(right, "line", down[: line_length - away]),
        ]

    hops = [hop((a_own, a_own), 1)]

    x_sends = split_columns(place, x, groups, halves, inner, part)
    x_send, back = lax.optimization_barrier((x_sends[0], back))
    x_cols = [lax.all_to_all(x_send, plane, 0, 0, tiled=True)]
    back, x_cols[0], hops[0], w_near = lax.optimization_barrier(
        (back, x_cols[0], hops[0], w_near)
    )
    back = lax.all_to_all(back, row, 0, 0, tiled=True).reshape(adapters * capacity, rank)
    back, hops[0], w_near = lax.optimization_barrier((back, hops[0], w_near))
    hops.append(hop(hops[0], 2))
    w_far = lax.ppermute(w_near, step, [(2, 3), (5, 4)])
    back = lax.dot_general(
        back, at, (((0,), (0,)), ((), ())), preferred_element_type=jnp.float32
    ).astype(jnp.bfloat16)
    owner, res = slot // resident, slot % resident
    slot_a = (owner // inner) * count + ((res // share) * inner + owner % inner) * share + res % share
    names = jnp.stack([slot, slot_a] + [slot] * 14).astype(jnp.bfloat16)
    packed = jnp.concatenate([back, names], axis=0)
    packed = jnp.broadcast_to(packed[None], (size,) + packed.shape)
    packed = lax.all_to_all(packed, plane, 0, 0, tiled=True)
    x_send, packed = lax.optimization_barrier((x_sends[1], packed))
    x_cols.append(lax.all_to_all(x_send, plane, 0, 0, tiled=True))
    g_all = lax.all_gather(g, plane, axis=0, tiled=True)

    def send(c, got, away):
        sums = grad_a_step(place, packed, x_cols[c], got, away, groups, count, rank)
        ahead = [(i, i + 1) for i in range(line_length - away)]
        behind = [(i, i - 1) for i in range(away, line_length)]
        moved = (lax.ppermute(sums[0], "line", ahead), lax.ppermute(sums[1], "line", behind))
        return moved, sums[0]

    def own(c, got):
        p = grad_a_step(place, packed, x_cols[c], got, 0, groups, count, rank)
        return p.reshape(size, resident * rank, part)

    first, done = send(0, (), 3)
    hops[1], w_far, done = lax.optimization_barrier((hops[1], w_far, done))
    hops.append(hop(hops[1], 3))
    second = send(1, (), 3)[0]
    first, done = send(0, first, 2)

    a_pieces = [a_own] + [h[0] for h in hops] + [h[1] for h in hops]
    w_cols = jnp.where(li // 2 == gi, w_both, w_near + w_far)
    a_pieces, w_cols, done = lax.optimization_barrier((a_pieces, w_cols, done))
    out_cols = out_part(place, packed, g_all, w_cols, a_pieces, rank)
    out_back = lax.all_to_all(out_cols, plane, 0, 0, tiled=True)
    second, out_cols = lax.optimization_barrier((second, out_cols))
    second, done = send(1, second, 2)
    first, done = lax.optimization_barrier((first, done))
    first, done = send(0, first, 1)

    a_pieces, done = lax.optimization_barrier((a_pieces, done))
    low = low_part(place, packed, x_cols[0], x_cols[1], a_pieces, rank)
    second, low = lax.optimization_barrier((second, low))
    second, done = send(1, second, 1)
    first, done = lax.optimization_barrier((first, done))
    p_back = [own(0, first)]
    low, out_back = lax.optimization_barrier((low, out_back))
    low = lax.all_to_all(low, plane, 0, 0, tiled=True)
    low, p_back[0] = lax.optimization_barrier((low, p_back[0]))
    p_back[0] = lax.all_to_all(p_back[0], plane, 0, 0, tiled=True)
    low = jnp.sum(low, axis=0).astype(jnp.bfloat16)
    low = lax.dot_general(at, low, NT, preferred_element_type=jnp.float32).astype(jnp.bfloat16)
    low, p_back[0] = lax.optimization_barrier((low, p_back[0]))
    low = route(low)
    p_second, low = lax.optimization_barrier((own(1, second), low))
    p_back.append(lax.all_to_all(p_second, plane, 0, 0, tiled=True))

    grad_b = jnp.einsum("hjcr,hjco->jro", low, g_rows, preferred_element_type=jnp.float32)
    grad_b = (adapter_scale * grad_b).astype(jnp.bfloat16)
    input_gradient = join_rows(place, out_back, groups, halves, inner, part)
    grad_a = join_slots(place, p_back, resident, groups, inner).swapaxes(1, 2)
    return input_gradient, grad_a, grad_b


def solution(mesh):
    groups, rows = mesh.shape["groups"], mesh.shape["row"]
    whole = ("groups", "line", "inner")
    split = Mesh(mesh.devices.reshape(groups, line_length, rows // line_length), whole)
    return jax.shard_map(
        body,
        mesh=split,
        in_specs=(
            P(whole, None),
            P(whole, None),
            P(whole, None),
            P(),
            P(row, None),
            P(row, None, None),
            P(row, None, None),
        ),
        out_specs=(P(whole, None), P(whole, None, None), P(whole, None, None)),
        check_vma=False,
    )
```

```python
import jax
import jax.numpy as jnp
from jax import lax
from jax.experimental import pallas as pl
from jax.experimental.pallas import tpu as pltpu
from jax.sharding import Mesh, PartitionSpec as P

adapter_scale = 2.0
line_length = 4
plane = ("groups", "inner")
row = ("line", "inner")
vmem_limit = 56 * 1024 * 1024
NT = (((1,), (1,)), ((), ()))


def call(kernel, place, grid, in_specs, out_specs, out_shape, flops, moved, name, args, scratch=()):
    return pl.pallas_call(
        kernel,
        grid_spec=pltpu.PrefetchScalarGridSpec(
            num_scalar_prefetch=1,
            grid=grid,
            in_specs=in_specs,
            out_specs=out_specs,
            scratch_shapes=scratch,
        ),
        out_shape=out_shape,
        compiler_params=pltpu.CompilerParams(vmem_limit_bytes=vmem_limit),
        cost_estimate=pl.CostEstimate(flops=flops, bytes_accessed=moved, transcendentals=0),
        name=name,
    )(place, *args)


def repeat(count, step, start):
    if count <= 4:
        for i in range(count):
            start = step(i, start)
        return start
    return lax.fori_loop(0, count, step, start)


def move(name, sources, in_blocks, in_maps, outs, out_blocks, out_maps, grid, kernel, place):
    moved = 0
    for shape in outs:
        size = 4
        for n in shape:
            size *= n
        moved += size
    return call(
        kernel,
        place,
        grid,
        [pl.BlockSpec(block, index) for block, index in zip(in_blocks, in_maps)],
        [pl.BlockSpec(block, index) for block, index in zip(out_blocks, out_maps)],
        [jax.ShapeDtypeStruct(shape, jnp.bfloat16) for shape in outs],
        0,
        moved,
        name,
        sources,
    )


def columns_of(q, c, halves, inner):
    return ((q // inner) * halves + c) * inner + q % inner


def split_columns(place, rows, groups, halves, inner, width):
    slots, rank, model = rows.shape
    size, share = groups * inner, max(1, slots // groups)
    group = lambda place: place[0] if slots >= groups else 0
    if width % 128:
        mine = lax.dynamic_slice_in_dim(rows, group(place) * share, share, 0)
        mine = mine.reshape(share * rank, groups, halves, inner, width)
        return mine.transpose(1, 3, 0, 2, 4).reshape(size, share * rank, halves * width)

    def kernel(place_ref, rows_ref, out_ref):
        for q in range(size):
            for c in range(halves):
                first = columns_of(q, c, halves, inner) * width
                out_ref[q, :, c * width : (c + 1) * width] = rows_ref[0, :, first : first + width]

    tile = min(rank, 64)
    steps = rank // tile
    return move(
        "split_columns", [rows], [(1, tile, model)],
        [lambda s, r, place: (group(place) * share + s, r, 0)],
        [(size, share * rank, halves * width)], [(size, tile, halves * width)],
        [lambda s, r, place: (0, s * steps + r, 0)], (share, steps), kernel, place,
    )[0]


def join_slots(place, parts, resident, groups, inner):
    size, rows, width = parts[0].shape
    halves, rank = len(parts), rows // resident
    if width % 128:
        parts = [p.reshape(groups, inner, rows, width) for p in parts]
        joined = jnp.stack(parts, axis=1).transpose(3, 0, 1, 2, 4)
        return joined.reshape(resident, rank, -1)

    def kernel(place_ref, *refs):
        for q in range(size):
            for c in range(halves):
                first = columns_of(q, c, halves, inner) * width
                refs[-1][0, :, first : first + width] = refs[c][q]

    return move(
        "join_slots", parts, [(size, rank, width)] * halves, [lambda r, place: (0, r, 0)] * halves,
        [(resident, rank, size * halves * width)], [(1, rank, size * halves * width)],
        [lambda r, place: (r, 0, 0)], (resident,), kernel, place,
    )[0]


def join_rows(place, rows, groups, halves, inner, part):
    size, tokens = rows.shape[:2]
    if part % 128:
        rows = rows.reshape(groups, inner, tokens, halves, part)
        return rows.transpose(2, 0, 3, 1, 4).reshape(tokens, -1)
    tile = min(tokens, 64)
    model = size * halves * part

    def kernel(place_ref, rows_ref, out_ref):
        for q in range(size):
            for c in range(halves):
                first = columns_of(q, c, halves, inner) * part
                out_ref[:, first : first + part] = rows_ref[q, :, c * part : (c + 1) * part]

    return move(
        "join_rows", [rows], [(size, tile, halves * part)], [lambda t, place: (0, t, 0)],
        [(tokens, model)], [(tile, model)], [lambda t, place: (t, 0)], (tokens // tile,),
        kernel, place,
    )[0]


def slot_sums(packed_ref, x_ref, rank, first, count):
    devices, _, tokens = packed_ref.shape
    chunk = min(devices, 4)

    def step(c, total):
        columns = []
        for d in range(chunk):
            back = packed_ref[c * chunk + d, :rank, :]
            slots = packed_ref[c * chunk + d, rank : rank + 1, :].astype(jnp.float32)
            rows = [
                back * (slots == (first + i).astype(jnp.float32)).astype(jnp.bfloat16)
                for i in range(count)
            ]
            columns.append(jnp.concatenate(rows, axis=0))
        x = x_ref[pl.ds(c * chunk, chunk)].reshape(chunk * tokens, x_ref.shape[2])
        return total + jnp.dot(
            jnp.concatenate(columns, axis=1), x, preferred_element_type=jnp.float32
        )

    start = jnp.zeros((count * rank, x_ref.shape[2]), jnp.float32)
    return repeat(devices // chunk, step, start)


def send_kernel(slots_line, count, rank, away, place_ref, packed_ref, x_ref, *refs):
    line = place_ref[1]
    outs, got = refs[-2:], refs[:-2]
    ways = ((line + away < line_length, line + away), (line >= away, line - away))
    for way, (inside, target) in enumerate(ways):

        @pl.when(inside)
        def _(way=way, target=target):
            first = target * slots_line + pl.program_id(1) * count
            total = slot_sums(packed_ref, x_ref, rank, first, count)
            if got:
                total += got[way][0].astype(jnp.float32)
            outs[way][0] = total.astype(jnp.bfloat16)


def own_kernel(slots_line, count, rank, place_ref, packed_ref, x_ref, right_ref, left_ref, out_ref):
    first = place_ref[1] * slots_line + pl.program_id(1) * count
    total = slot_sums(packed_ref, x_ref, rank, first, count)
    total += right_ref[0].astype(jnp.float32) + left_ref[0].astype(jnp.float32)
    out_ref[0] = (adapter_scale * total).astype(jnp.bfloat16)


def grad_a_step(place, packed, x_cols, half, got, away, groups, slots_line, rank):
    devices, depth, tokens = packed.shape
    width = x_cols.shape[2] // 2
    if width % 128:
        x_cols, half = x_cols[:, :, half * width : (half + 1) * width], 0
    local = devices // groups
    count = 8
    rows = count * rank
    block = pl.BlockSpec((1, rows, width), lambda g, s, place: (g, s, 0))
    shape = jax.ShapeDtypeStruct((groups, slots_line * rank, width), jnp.bfloat16)
    ways = 1 if away == 0 else 2
    if away == 0:
        kernel = lambda *refs: own_kernel(slots_line, count, rank, *refs)
    else:
        kernel = lambda *refs: send_kernel(slots_line, count, rank, away, *refs)
    return call(
        kernel,
        place,
        (groups, slots_line // count),
        [
            pl.BlockSpec((local, depth, tokens), lambda g, s, place: (g, 0, 0)),
            pl.BlockSpec((local, tokens, width), lambda g, s, place: (g, 0, half)),
        ]
        + [block] * len(got),
        block if away == 0 else [block, block],
        shape if away == 0 else [shape, shape],
        ways * 2 * devices * tokens * width * slots_line * rank,
        2 * devices * tokens * width + 2 * groups * slots_line * rank * width * (ways + len(got)),
        "grad_a_step" + str(away),
        (packed, x_cols, *got),
    )


def in_line(slots, place_ref, total):
    slots -= place_ref[1] * (total // line_length)
    return jnp.where(slots < 0, slots + total, slots)


def put_together(pieces, a_ref):
    @pl.when(pl.program_id(0) == 0)
    def _():
        rows = pieces[0].shape[0]
        a_ref[:rows] = pieces[0][...]
        for k in range(1, line_length):
            left, right = pieces[line_length - k], pieces[line_length - 1 + k]
            a_ref[k * rows : (k + 1) * rows] = left[...] + right[...]


def low_kernel(chunk, rank, place_ref, packed_ref, x_ref, *refs):
    *pieces, low_ref, a_ref = refs
    put_together(pieces, a_ref)
    slots = packed_ref[0].astype(jnp.float32).T[:, rank + 1 : rank + 2].astype(jnp.int32)
    slots = in_line(slots, place_ref, a_ref.shape[0] // rank)
    tile = x_ref.shape[1]
    lane_slot = lax.broadcasted_iota(jnp.int32, (tile, chunk), 1) // rank

    def step(c, low):
        part = pl.ds(pl.multiple_of(c * chunk, chunk), chunk)
        hidden = lax.dot_general(x_ref[0], a_ref[part], NT, preferred_element_type=jnp.float32)
        hidden = jnp.where(lane_slot + c * (chunk // rank) == slots, hidden, 0.0)
        for k in range(chunk // (2 * rank)):
            low += hidden[:, k * 2 * rank : (k + 1) * 2 * rank]
        return low

    start = jnp.zeros((tile, 2 * rank), jnp.float32)
    low = repeat(a_ref.shape[0] // chunk, step, start).T
    low_ref[0] = low[:rank] + low[rank:]


def low_part(place, packed, x_cols, a_pieces, rank):
    devices, depth, tokens = packed.shape
    width = x_cols.shape[2]
    rows = a_pieces[0].shape[0]
    slots = line_length * rows
    return call(
        lambda *refs: low_kernel(512, rank, *refs),
        place,
        (devices,),
        [
            pl.BlockSpec((1, depth, tokens), lambda t, place: (t, 0, 0)),
            pl.BlockSpec((1, tokens, width), lambda t, place: (t, 0, 0)),
        ]
        + [pl.BlockSpec((rows, width), lambda t, place: (0, 0))] * len(a_pieces),
        pl.BlockSpec((1, rank, tokens), lambda t, place: (t, 0, 0)),
        jax.ShapeDtypeStruct((devices, rank, tokens), jnp.float32),
        2 * devices * tokens * width * slots,
        2 * (devices * tokens + slots) * width,
        "low_part",
        (packed, x_cols, *a_pieces),
        [pltpu.VMEM((slots, width), jnp.bfloat16)],
    )


def out_kernel(chunk, rank, place_ref, packed_ref, g_ref, w_ref, *refs):
    *pieces, out_ref, a_ref = refs
    put_together(pieces, a_ref)
    rows = packed_ref[0].astype(jnp.float32).T
    back, slots = rows[:, :rank], rows[:, rank + 1 : rank + 2].astype(jnp.int32)
    slots = in_line(slots, place_ref, a_ref.shape[0] // rank)
    tile = back.shape[0]
    repeated = jnp.concatenate([back] * (chunk // rank), axis=1)
    lane_slot = lax.broadcasted_iota(jnp.int32, (tile, chunk), 1) // rank

    def step(c, acc):
        keep = lane_slot + c * (chunk // rank) == slots
        masked = jnp.where(keep, repeated, 0.0).astype(jnp.bfloat16)
        block = a_ref[pl.ds(pl.multiple_of(c * chunk, chunk), chunk), :]
        return acc + jnp.dot(masked, block, preferred_element_type=jnp.float32)

    start = jnp.zeros((tile, a_ref.shape[1]), jnp.float32)
    acc = repeat(a_ref.shape[0] // chunk, step, start)
    base = lax.dot_general(g_ref[...], w_ref[...], NT, preferred_element_type=jnp.float32)
    out_ref[0] = (base + adapter_scale * acc).astype(out_ref.dtype)


def out_part(place, packed, g_all, w_cols, a_pieces, rank):
    _, depth, tokens = packed.shape
    devices = g_all.shape[0] // tokens
    outs = g_all.shape[1]
    rows, width = a_pieces[0].shape
    slots = line_length * rows
    return call(
        lambda *refs: out_kernel(512, rank, *refs),
        place,
        (devices,),
        [
            pl.BlockSpec((1, depth, tokens), lambda t, place: (t, 0, 0)),
            pl.BlockSpec((tokens, outs), lambda t, place: (t, 0)),
            pl.BlockSpec((width, outs), lambda t, place: (0, 0)),
        ]
        + [pl.BlockSpec((rows, width), lambda t, place: (0, 0))] * len(a_pieces),
        pl.BlockSpec((1, tokens, width), lambda t, place: (t, 0, 0)),
        jax.ShapeDtypeStruct((devices, tokens, width), jnp.bfloat16),
        2 * devices * tokens * width * (slots + outs),
        2 * devices * tokens * (width + outs) + 2 * slots * width,
        "out_part",
        (packed, g_all, w_cols, *a_pieces),
        [pltpu.VMEM((slots, width), jnp.bfloat16)],
    )


def body(x, g, tok, adapter_slot, w, a, b):
    groups, inner = lax.axis_size("groups"), lax.axis_size("inner")
    gi, li, ji = lax.axis_index("groups"), lax.axis_index("line"), lax.axis_index("inner")
    place = jnp.stack([gi, li, ji]).astype(jnp.int32)
    size = groups * inner
    devices = line_length * inner
    tokens, model = x.shape
    outs = g.shape[1]
    resident, _, rank = a.shape
    share = resident // groups
    count = inner * resident
    halves = line_length // groups
    width = model // size
    part = width // halves
    adapters = adapter_slot.shape[0]
    capacity = max(2, 2 * tokens // adapters)

    step = ("groups", "line")
    w_mate = lax.ppermute(w, step, [(0, 1), (1, 0), (6, 7), (7, 6)])

    a_mine = split_columns(place, jnp.swapaxes(a, 1, 2), groups, halves, inner, part)
    a_own = lax.all_to_all(a_mine, plane, 0, 0, tiled=True).reshape(count * rank, width)

    matches = tok == lax.broadcasted_iota(jnp.int32, (tokens, adapters), 1)
    slot = jnp.sum(jnp.where(matches, adapter_slot[None, :], 0), axis=1)
    running = jnp.cumsum(matches.astype(jnp.int32), axis=0)
    within = jnp.sum(jnp.where(matches, running - 1, 0), axis=1)
    position = slot * capacity + within
    at = lax.broadcasted_iota(jnp.int32, (adapters * capacity, tokens), 0) == position[None, :]
    at = at.astype(jnp.bfloat16)

    def route(rows):
        rows = rows.reshape(devices, resident * capacity, rows.shape[1])
        rows = lax.all_to_all(rows, row, 0, 0, tiled=True)
        return rows.reshape(devices, resident, capacity, rows.shape[2])

    g_send = jnp.dot(at, g, preferred_element_type=jnp.float32).astype(jnp.bfloat16)
    g_send, a_own, w_mate = lax.optimization_barrier((g_send, a_own, w_mate))
    g_rows = route(g_send)
    back = jnp.einsum("hjct,jrt->hjcr", g_rows, b, preferred_element_type=jnp.float32)
    back = back.astype(jnp.bfloat16).reshape(devices, resident * capacity, rank)

    up = [(i, i + 1) for i in range(line_length - 1)]
    down = [(i + 1, i) for i in range(line_length - 1)]

    def hop(pieces, away):
        left, right = pieces
        return [
            lax.ppermute(left, "line", up[away - 1 :]),
            lax.ppermute(right, "line", down[: line_length - away]),
        ]

    hops = [hop((a_own, a_own), 1)]
    back, hops[0] = lax.optimization_barrier((back, hops[0]))
    back = lax.all_to_all(back, row, 0, 0, tiled=True).reshape(adapters * capacity, rank)
    back, hops[0] = lax.optimization_barrier((back, hops[0]))
    hops.append(hop(hops[0], 2))
    back = lax.dot_general(
        back, at, (((0,), (0,)), ((), ())), preferred_element_type=jnp.float32
    ).astype(jnp.bfloat16)
    owner, res = slot // resident, slot % resident
    slot_a = (owner // inner) * count + ((res // share) * inner + owner % inner) * share + res % share
    names = jnp.stack([slot, slot_a] + [slot] * 14).astype(jnp.bfloat16)
    packed = jnp.concatenate([back, names], axis=0)
    packed = jnp.broadcast_to(packed[None], (size,) + packed.shape)
    packed = lax.all_to_all(packed, plane, 0, 0, tiled=True)

    x_send = split_columns(place, x[None], groups, halves, inner, part)
    x_send, packed, hops[1], w_mate = lax.optimization_barrier((x_send, packed, hops[1], w_mate))
    x_cols = lax.all_to_all(x_send, plane, 0, 0, tiled=True)
    hops.append(hop(hops[1], 3))
    odd = li % 2 == 1
    w_both = jnp.concatenate([jnp.where(odd, w_mate, w), jnp.where(odd, w, w_mate)], axis=0)
    w_near = lax.ppermute(w_both, step, [(1, 2), (6, 5)])
    x_cols, hops[2], w_near = lax.optimization_barrier((x_cols, hops[2], w_near))
    w_far = lax.ppermute(w_near, step, [(2, 3), (5, 4)])
    g_all = lax.all_gather(g, plane, axis=0, tiled=True)

    def send(c, got, away):
        sums = grad_a_step(place, packed, x_cols, c, got, away, groups, count, rank)
        ahead = [(i, i + 1) for i in range(line_length - away)]
        behind = [(i, i - 1) for i in range(away, line_length)]
        moved = (lax.ppermute(sums[0], "line", ahead), lax.ppermute(sums[1], "line", behind))
        return moved, sums[0]

    def own(c, got):
        p = grad_a_step(place, packed, x_cols, c, got, 0, groups, count, rank)
        return p.reshape(size, resident * rank, part)

    first, done = send(0, (), 3)
    packed, done = lax.optimization_barrier((packed, done))
    second, done = send(1, (), 3)

    a_pieces = [a_own] + [h[0] for h in hops] + [h[1] for h in hops]
    w_cols = jnp.where(li // 2 == gi, w_both, w_near + w_far)
    a_pieces, w_cols, done = lax.optimization_barrier((a_pieces, w_cols, done))
    out_cols = out_part(place, packed, g_all, w_cols, a_pieces, rank)
    out_back = lax.all_to_all(out_cols, plane, 0, 0, tiled=True)
    first, out_cols = lax.optimization_barrier((first, out_cols))
    first, done = send(0, first, 2)
    second, done = lax.optimization_barrier((second, done))
    second, done = send(1, second, 2)

    a_pieces, done = lax.optimization_barrier((a_pieces, done))
    low = low_part(place, packed, x_cols, a_pieces, rank)
    first, low = lax.optimization_barrier((first, low))
    first, done = send(0, first, 1)
    second, done = lax.optimization_barrier((second, done))
    second, done = send(1, second, 1)
    first, done = lax.optimization_barrier((first, done))
    p_back = [own(0, first)]
    low, out_back = lax.optimization_barrier((low, out_back))
    low = lax.all_to_all(low, plane, 0, 0, tiled=True)
    low, p_back[0] = lax.optimization_barrier((low, p_back[0]))
    p_back[0] = lax.all_to_all(p_back[0], plane, 0, 0, tiled=True)
    low = jnp.sum(low, axis=0).astype(jnp.bfloat16)
    low = lax.dot_general(at, low, NT, preferred_element_type=jnp.float32).astype(jnp.bfloat16)
    low, p_back[0] = lax.optimization_barrier((low, p_back[0]))
    low = route(low)
    p_second, low = lax.optimization_barrier((own(1, second), low))
    p_back.append(lax.all_to_all(p_second, plane, 0, 0, tiled=True))

    grad_b = jnp.einsum("hjcr,hjco->jro", low, g_rows, preferred_element_type=jnp.float32)
    grad_b = (adapter_scale * grad_b).astype(jnp.bfloat16)
    input_gradient = join_rows(place, out_back, groups, halves, inner, part)
    grad_a = join_slots(place, p_back, resident, groups, inner).swapaxes(1, 2)
    return input_gradient, grad_a, grad_b


def solution(mesh):
    groups, rows = mesh.shape["groups"], mesh.shape["row"]
    whole = ("groups", "line", "inner")
    split = Mesh(mesh.devices.reshape(groups, line_length, rows // line_length), whole)
    return jax.shard_map(
        body,
        mesh=split,
        in_specs=(
            P(whole, None),
            P(whole, None),
            P(whole, None),
            P(),
            P(row, None),
            P(row, None, None),
            P(row, None, None),
        ),
        out_specs=(P(whole, None), P(whole, None, None), P(whole, None, None)),
        check_vma=False,
    )
```

```python
import jax
import jax.numpy as jnp
from jax import lax
from jax.experimental import pallas as pl
from jax.experimental.pallas import tpu as pltpu
from jax.sharding import Mesh, PartitionSpec as P

adapter_scale = 2.0
line_length = 4
plane = ("groups", "inner")
row = ("line", "inner")
vmem_limit = 56 * 1024 * 1024
NT = (((1,), (1,)), ((), ()))


def call(kernel, place, grid, in_specs, out_specs, out_shape, flops, moved, name, args, scratch=()):
    return pl.pallas_call(
        kernel,
        grid_spec=pltpu.PrefetchScalarGridSpec(
            num_scalar_prefetch=1,
            grid=grid,
            in_specs=in_specs,
            out_specs=out_specs,
            scratch_shapes=scratch,
        ),
        out_shape=out_shape,
        compiler_params=pltpu.CompilerParams(vmem_limit_bytes=vmem_limit),
        cost_estimate=pl.CostEstimate(flops=flops, bytes_accessed=moved, transcendentals=0),
        name=name,
    )(place, *args)


def repeat(count, step, start):
    if count <= 4:
        for i in range(count):
            start = step(i, start)
        return start
    return lax.fori_loop(0, count, step, start)


def move(name, sources, in_blocks, in_maps, outs, out_blocks, out_maps, grid, kernel, place):
    moved = 0
    for shape in outs:
        size = 4
        for n in shape:
            size *= n
        moved += size
    return call(
        kernel,
        place,
        grid,
        [pl.BlockSpec(block, index) for block, index in zip(in_blocks, in_maps)],
        [pl.BlockSpec(block, index) for block, index in zip(out_blocks, out_maps)],
        [jax.ShapeDtypeStruct(shape, jnp.bfloat16) for shape in outs],
        0,
        moved,
        name,
        sources,
    )


def columns_of(q, c, halves, inner):
    return ((q // inner) * halves + c) * inner + q % inner


def split_columns(place, rows, groups, halves, inner, width):
    slots, rank, model = rows.shape
    size, share = groups * inner, max(1, slots // groups)
    group = lambda place: place[0] if slots >= groups else 0
    if width % 128:
        mine = lax.dynamic_slice_in_dim(rows, group(place) * share, share, 0)
        mine = mine.reshape(share * rank, groups, halves, inner, width)
        return mine.transpose(1, 3, 0, 2, 4).reshape(size, share * rank, halves * width)

    def kernel(place_ref, rows_ref, out_ref):
        for q in range(size):
            for c in range(halves):
                first = columns_of(q, c, halves, inner) * width
                out_ref[q, :, c * width : (c + 1) * width] = rows_ref[0, :, first : first + width]

    tile = min(rank, 64)
    steps = rank // tile
    return move(
        "split_columns", [rows], [(1, tile, model)],
        [lambda s, r, place: (group(place) * share + s, r, 0)],
        [(size, share * rank, halves * width)], [(size, tile, halves * width)],
        [lambda s, r, place: (0, s * steps + r, 0)], (share, steps), kernel, place,
    )[0]


def split_pieces(place, rows, groups, halves, inner, width):
    count, model = rows.shape
    size = groups * inner
    tile = min(count, 64)

    def kernel(place_ref, rows_ref, *out_refs):
        me = place_ref[0] * inner + place_ref[2]
        for m in range(size):
            for c in range(halves):
                first = pl.multiple_of(columns_of(me ^ m, c, halves, inner) * width, width)
                out_refs[m][:, c * width : (c + 1) * width] = rows_ref[:, pl.ds(first, width)]

    return move(
        "split_pieces", [rows], [(tile, model)], [lambda t, place: (t, 0)],
        [(count, halves * width)] * size, [(tile, halves * width)] * size,
        [lambda t, place: (t, 0)] * size, (count // tile,), kernel, place,
    )


def join_slots(place, parts, resident, groups, inner):
    size, rows, width = parts[0].shape
    halves, rank = len(parts), rows // resident
    if width % 128:
        parts = [p.reshape(groups, inner, rows, width) for p in parts]
        joined = jnp.stack(parts, axis=1).transpose(3, 0, 1, 2, 4)
        return joined.reshape(resident, rank, -1)

    def kernel(place_ref, *refs):
        for q in range(size):
            for c in range(halves):
                first = columns_of(q, c, halves, inner) * width
                refs[-1][0, :, first : first + width] = refs[c][q]

    return move(
        "join_slots", parts, [(size, rank, width)] * halves, [lambda r, place: (0, r, 0)] * halves,
        [(resident, rank, size * halves * width)], [(1, rank, size * halves * width)],
        [lambda r, place: (r, 0, 0)], (resident,), kernel, place,
    )[0]


def join_rows(place, rows, groups, halves, inner, part):
    size, tokens = rows.shape[:2]
    if part % 128:
        rows = rows.reshape(groups, inner, tokens, halves, part)
        return rows.transpose(2, 0, 3, 1, 4).reshape(tokens, -1)
    tile = min(tokens, 64)
    model = size * halves * part

    def kernel(place_ref, rows_ref, out_ref):
        for q in range(size):
            for c in range(halves):
                first = columns_of(q, c, halves, inner) * part
                out_ref[:, first : first + part] = rows_ref[q, :, c * part : (c + 1) * part]

    return move(
        "join_rows", [rows], [(size, tile, halves * part)], [lambda t, place: (0, t, 0)],
        [(tokens, model)], [(tile, model)], [lambda t, place: (t, 0)], (tokens // tile,),
        kernel, place,
    )[0]


def slot_sums(packed_ref, x_ref, me, rank, first, count):
    devices, _, tokens = packed_ref.shape
    chunk = min(devices, 4)

    def step(c, total):
        columns = []
        for d in range(chunk):
            device = (c * chunk + d) ^ me
            back = packed_ref[device, :rank, :]
            slots = packed_ref[device, rank : rank + 1, :].astype(jnp.float32)
            rows = [
                back * (slots == (first + i).astype(jnp.float32)).astype(jnp.bfloat16)
                for i in range(count)
            ]
            columns.append(jnp.concatenate(rows, axis=0))
        x = x_ref[pl.ds(c * chunk, chunk)].reshape(chunk * tokens, x_ref.shape[2])
        return total + jnp.dot(
            jnp.concatenate(columns, axis=1), x, preferred_element_type=jnp.float32
        )

    start = jnp.zeros((count * rank, x_ref.shape[2]), jnp.float32)
    return repeat(devices // chunk, step, start)


def send_kernel(slots_line, count, rank, away, place_ref, packed_ref, x_ref, *refs):
    line = place_ref[1]
    outs, got = refs[-2:], refs[:-2]
    ways = ((line + away < line_length, line + away), (line >= away, line - away))
    for way, (inside, target) in enumerate(ways):

        @pl.when(inside)
        def _(way=way, target=target):
            first = target * slots_line + pl.program_id(1) * count
            total = slot_sums(packed_ref, x_ref, place_ref[2], rank, first, count)
            if got:
                total += got[way][0].astype(jnp.float32)
            outs[way][0] = total.astype(jnp.bfloat16)


def own_kernel(slots_line, count, rank, place_ref, packed_ref, x_ref, right_ref, left_ref, out_ref):
    first = place_ref[1] * slots_line + pl.program_id(1) * count
    total = slot_sums(packed_ref, x_ref, place_ref[2], rank, first, count)
    total += right_ref[0].astype(jnp.float32) + left_ref[0].astype(jnp.float32)
    out_ref[0] = (adapter_scale * total).astype(jnp.bfloat16)


def grad_a_step(place, packed, x_cols, half, got, away, groups, slots_line, rank):
    devices, depth, tokens = packed.shape
    width = x_cols.shape[2] // 2
    if width % 128:
        x_cols, half = x_cols[:, :, half * width : (half + 1) * width], 0
    local = devices // groups
    count = 8
    rows = count * rank
    block = pl.BlockSpec((1, rows, width), lambda g, s, place: (g, s, 0))
    final = pl.BlockSpec((1, rows, width), lambda g, s, place: (g ^ place[0], s, 0))
    shape = jax.ShapeDtypeStruct((groups, slots_line * rank, width), jnp.bfloat16)
    ways = 1 if away == 0 else 2
    if away == 0:
        kernel = lambda *refs: own_kernel(slots_line, count, rank, *refs)
    else:
        kernel = lambda *refs: send_kernel(slots_line, count, rank, away, *refs)
    return call(
        kernel,
        place,
        (groups, slots_line // count),
        [
            pl.BlockSpec((local, depth, tokens), lambda g, s, place: (g ^ place[0], 0, 0)),
            pl.BlockSpec((local, tokens, width), lambda g, s, place: (g, 0, half)),
        ]
        + [block] * len(got),
        final if away == 0 else [block, block],
        shape if away == 0 else [shape, shape],
        ways * 2 * devices * tokens * width * slots_line * rank,
        2 * devices * tokens * width + 2 * groups * slots_line * rank * width * (ways + len(got)),
        "grad_a_step" + str(away),
        (packed, x_cols, *got),
    )


def in_line(slots, place_ref, total):
    slots -= place_ref[1] * (total // line_length)
    return jnp.where(slots < 0, slots + total, slots)


def put_together(pieces, a_ref):
    @pl.when(pl.program_id(0) == 0)
    def _():
        rows = pieces[0].shape[0]
        a_ref[:rows] = pieces[0][...]
        for k in range(1, line_length):
            left, right = pieces[line_length - k], pieces[line_length - 1 + k]
            a_ref[k * rows : (k + 1) * rows] = left[...] + right[...]


def low_kernel(chunk, rank, place_ref, packed_ref, x_ref, *refs):
    *pieces, low_ref, a_ref = refs
    put_together(pieces, a_ref)
    slots = packed_ref[0].astype(jnp.float32).T[:, rank + 1 : rank + 2].astype(jnp.int32)
    slots = in_line(slots, place_ref, a_ref.shape[0] // rank)
    tile = x_ref.shape[1]
    lane_slot = lax.broadcasted_iota(jnp.int32, (tile, chunk), 1) // rank

    def step(c, low):
        part = pl.ds(pl.multiple_of(c * chunk, chunk), chunk)
        hidden = lax.dot_general(x_ref[0], a_ref[part], NT, preferred_element_type=jnp.float32)
        hidden = jnp.where(lane_slot + c * (chunk // rank) == slots, hidden, 0.0)
        for k in range(chunk // (2 * rank)):
            low += hidden[:, k * 2 * rank : (k + 1) * 2 * rank]
        return low

    start = jnp.zeros((tile, 2 * rank), jnp.float32)
    low = repeat(a_ref.shape[0] // chunk, step, start).T
    low_ref[0] = low[:rank] + low[rank:]


def low_part(place, packed, x_cols, a_pieces, inner, rank):
    devices, depth, tokens = packed.shape
    width = x_cols.shape[2]
    rows = a_pieces[0].shape[0]
    slots = line_length * rows
    mate = lambda t, place: (t ^ (place[0] * inner + place[2]), 0, 0)
    return call(
        lambda *refs: low_kernel(512, rank, *refs),
        place,
        (devices,),
        [
            pl.BlockSpec((1, depth, tokens), mate),
            pl.BlockSpec((1, tokens, width), lambda t, place: (t, 0, 0)),
        ]
        + [pl.BlockSpec((rows, width), lambda t, place: (0, 0))] * len(a_pieces),
        pl.BlockSpec((1, rank, tokens), mate),
        jax.ShapeDtypeStruct((devices, rank, tokens), jnp.float32),
        2 * devices * tokens * width * slots,
        2 * (devices * tokens + slots) * width,
        "low_part",
        (packed, x_cols, *a_pieces),
        [pltpu.VMEM((slots, width), jnp.bfloat16)],
    )


def out_kernel(chunk, rank, place_ref, packed_ref, g_ref, w_ref, *refs):
    *pieces, out_ref, a_ref = refs
    put_together(pieces, a_ref)
    rows = packed_ref[0].astype(jnp.float32).T
    back, slots = rows[:, :rank], rows[:, rank + 1 : rank + 2].astype(jnp.int32)
    slots = in_line(slots, place_ref, a_ref.shape[0] // rank)
    tile = back.shape[0]
    repeated = jnp.concatenate([back] * (chunk // rank), axis=1)
    lane_slot = lax.broadcasted_iota(jnp.int32, (tile, chunk), 1) // rank

    def step(c, acc):
        keep = lane_slot + c * (chunk // rank) == slots
        masked = jnp.where(keep, repeated, 0.0).astype(jnp.bfloat16)
        block = a_ref[pl.ds(pl.multiple_of(c * chunk, chunk), chunk), :]
        return acc + jnp.dot(masked, block, preferred_element_type=jnp.float32)

    start = jnp.zeros((tile, a_ref.shape[1]), jnp.float32)
    acc = repeat(a_ref.shape[0] // chunk, step, start)
    base = lax.dot_general(g_ref[...], w_ref[...], NT, preferred_element_type=jnp.float32)
    out_ref[0] = (base + adapter_scale * acc).astype(out_ref.dtype)


def out_part(place, packed, g_all, w_cols, a_pieces, rank):
    _, depth, tokens = packed.shape
    devices = g_all.shape[0] // tokens
    outs = g_all.shape[1]
    rows, width = a_pieces[0].shape
    slots = line_length * rows
    return call(
        lambda *refs: out_kernel(512, rank, *refs),
        place,
        (devices,),
        [
            pl.BlockSpec((1, depth, tokens), lambda t, place: (t, 0, 0)),
            pl.BlockSpec((tokens, outs), lambda t, place: (t, 0)),
            pl.BlockSpec((width, outs), lambda t, place: (0, 0)),
        ]
        + [pl.BlockSpec((rows, width), lambda t, place: (0, 0))] * len(a_pieces),
        pl.BlockSpec((1, tokens, width), lambda t, place: (t, 0, 0)),
        jax.ShapeDtypeStruct((devices, tokens, width), jnp.bfloat16),
        2 * devices * tokens * width * (slots + outs),
        2 * devices * tokens * (width + outs) + 2 * slots * width,
        "out_part",
        (packed, g_all, w_cols, *a_pieces),
        [pltpu.VMEM((slots, width), jnp.bfloat16)],
    )


def body(x, g, tok, adapter_slot, w, a, b):
    groups, inner = lax.axis_size("groups"), lax.axis_size("inner")
    gi, li, ji = lax.axis_index("groups"), lax.axis_index("line"), lax.axis_index("inner")
    place = jnp.stack([gi, li, ji]).astype(jnp.int32)
    size = groups * inner
    devices = line_length * inner
    tokens, model = x.shape
    outs = g.shape[1]
    resident, _, rank = a.shape
    share = resident // groups
    count = inner * resident
    halves = line_length // groups
    width = model // size
    part = width // halves
    adapters = adapter_slot.shape[0]
    capacity = max(2, 2 * tokens // adapters)

    step = ("groups", "line")
    w_mate = lax.ppermute(w, step, [(0, 1), (1, 0), (6, 7), (7, 6)])

    a_mine = split_columns(place, jnp.swapaxes(a, 1, 2), groups, halves, inner, part)
    a_own = lax.all_to_all(a_mine, plane, 0, 0, tiled=True).reshape(count * rank, width)

    def meet(pieces, m):
        return lax.ppermute(pieces[m], plane, [(i, i ^ m) for i in range(size)])

    direct = size <= 8 and part % 128 == 0
    if direct:
        x_sends = split_pieces(place, x, groups, halves, inner, part)
        x_near = [x_sends[0]] + [meet(x_sends, m) for m in range(1, 4)]
    else:
        x_far = split_columns(place, x[None], groups, halves, inner, part)
        x_far = lax.all_to_all(x_far, plane, 0, 0, tiled=True)
        x_far, x_near = [x_far[jnp.arange(size) ^ (gi * inner + ji)]], []

    matches = tok == lax.broadcasted_iota(jnp.int32, (tokens, adapters), 1)
    slot = jnp.sum(jnp.where(matches, adapter_slot[None, :], 0), axis=1)
    running = jnp.cumsum(matches.astype(jnp.int32), axis=0)
    within = jnp.sum(jnp.where(matches, running - 1, 0), axis=1)
    position = slot * capacity + within
    at = lax.broadcasted_iota(jnp.int32, (adapters * capacity, tokens), 0) == position[None, :]
    at = at.astype(jnp.bfloat16)

    def route(rows):
        rows = rows.reshape(devices, resident * capacity, rows.shape[1])
        rows = lax.all_to_all(rows, row, 0, 0, tiled=True)
        return rows.reshape(devices, resident, capacity, rows.shape[2])

    g_send = jnp.dot(at, g, preferred_element_type=jnp.float32).astype(jnp.bfloat16)
    g_send, a_own, w_mate, x_near = lax.optimization_barrier((g_send, a_own, w_mate, x_near))
    if direct:
        x_far = [meet(x_sends, m) for m in range(4, size)]
    g_rows = route(g_send)
    back = jnp.einsum("hjct,jrt->hjcr", g_rows, b, preferred_element_type=jnp.float32)
    back = back.astype(jnp.bfloat16).reshape(devices, resident * capacity, rank)

    up = [(i, i + 1) for i in range(line_length - 1)]
    down = [(i + 1, i) for i in range(line_length - 1)]

    def hop(pieces, away):
        left, right = pieces
        return [
            lax.ppermute(left, "line", up[away - 1 :]),
            lax.ppermute(right, "line", down[: line_length - away]),
        ]

    hops = [hop((a_own, a_own), 1)]
    back, hops[0], x_far = lax.optimization_barrier((back, hops[0], x_far))
    back = lax.all_to_all(back, row, 0, 0, tiled=True).reshape(adapters * capacity, rank)
    back, hops[0] = lax.optimization_barrier((back, hops[0]))
    hops.append(hop(hops[0], 2))
    g_own, x_far = lax.optimization_barrier((g, x_far))
    g_all = lax.all_gather(g_own, plane, axis=0, tiled=True)
    x_cols = jnp.stack(x_near + x_far) if direct else x_far[0]
    back = lax.dot_general(
        back, at, (((0,), (0,)), ((), ())), preferred_element_type=jnp.float32
    ).astype(jnp.bfloat16)
    owner, res = slot // resident, slot % resident
    slot_a = (owner // inner) * count + ((res // share) * inner + owner % inner) * share + res % share
    names = jnp.stack([slot, slot_a] + [slot] * 14).astype(jnp.bfloat16)
    packed = jnp.concatenate([back, names], axis=0)
    packed = jnp.broadcast_to(packed[None], (size,) + packed.shape)
    packed = lax.all_to_all(packed, plane, 0, 0, tiled=True)

    packed, hops[1], x_cols = lax.optimization_barrier((packed, hops[1], x_cols))
    hops.append(hop(hops[1], 3))
    odd = li % 2 == 1
    w_both = jnp.concatenate([jnp.where(odd, w_mate, w), jnp.where(odd, w, w_mate)], axis=0)
    w_near = lax.ppermute(w_both, step, [(1, 2), (6, 5)])
    w_far = lax.ppermute(w_near, step, [(2, 3), (5, 4)])

    def send(c, got, away):
        sums = grad_a_step(place, packed, x_cols, c, got, away, groups, count, rank)
        ahead = [(i, i + 1) for i in range(line_length - away)]
        behind = [(i, i - 1) for i in range(away, line_length)]
        moved = (lax.ppermute(sums[0], "line", ahead), lax.ppermute(sums[1], "line", behind))
        return moved, sums[0]

    def own(c, got):
        p = grad_a_step(place, packed, x_cols, c, got, 0, groups, count, rank)
        return p.reshape(size, resident * rank, part)

    first, done = send(0, (), 3)
    packed, done = lax.optimization_barrier((packed, done))
    second, done = send(1, (), 3)

    a_pieces = [a_own] + [h[0] for h in hops] + [h[1] for h in hops]
    w_cols = jnp.where(li // 2 == gi, w_both, w_near + w_far)
    a_pieces, w_cols, done = lax.optimization_barrier((a_pieces, w_cols, done))
    out_cols = out_part(place, packed, g_all, w_cols, a_pieces, rank)
    first, out_cols = lax.optimization_barrier((first, out_cols))
    first, done = send(0, first, 2)
    second, done = lax.optimization_barrier((second, done))
    second, done = send(1, second, 2)
    out_cols, done = lax.optimization_barrier((out_cols, done))
    out_back = lax.all_to_all(out_cols, plane, 0, 0, tiled=True)

    a_pieces, done = lax.optimization_barrier((a_pieces, done))
    low = low_part(place, packed, x_cols, a_pieces, inner, rank)
    first, low = lax.optimization_barrier((first, low))
    first, done = send(0, first, 1)
    second, done = lax.optimization_barrier((second, done))
    second, done = send(1, second, 1)
    first, done = lax.optimization_barrier((first, done))
    p_back = [own(0, first)]
    low, out_back = lax.optimization_barrier((low, out_back))
    low = lax.all_to_all(low, plane, 0, 0, tiled=True)
    low, p_back[0] = lax.optimization_barrier((low, p_back[0]))
    p_back[0] = lax.all_to_all(p_back[0], plane, 0, 0, tiled=True)
    low = jnp.sum(low, axis=0).astype(jnp.bfloat16)
    low = lax.dot_general(at, low, NT, preferred_element_type=jnp.float32).astype(jnp.bfloat16)
    low, p_back[0] = lax.optimization_barrier((low, p_back[0]))
    low = route(low)
    p_second, low = lax.optimization_barrier((own(1, second), low))
    p_back.append(lax.all_to_all(p_second, plane, 0, 0, tiled=True))

    grad_b = jnp.einsum("hjcr,hjco->jro", low, g_rows, preferred_element_type=jnp.float32)
    grad_b = (adapter_scale * grad_b).astype(jnp.bfloat16)
    input_gradient = join_rows(place, out_back, groups, halves, inner, part)
    grad_a = join_slots(place, p_back, resident, groups, inner).swapaxes(1, 2)
    return input_gradient, grad_a, grad_b


def solution(mesh):
    groups, rows = mesh.shape["groups"], mesh.shape["row"]
    whole = ("groups", "line", "inner")
    split = Mesh(mesh.devices.reshape(groups, line_length, rows // line_length), whole)
    return jax.shard_map(
        body,
        mesh=split,
        in_specs=(
            P(whole, None),
            P(whole, None),
            P(whole, None),
            P(),
            P(row, None),
            P(row, None, None),
            P(row, None, None),
        ),
        out_specs=(P(whole, None), P(whole, None, None), P(whole, None, None)),
        check_vma=False,
    )
```

```python
import jax
import jax.numpy as jnp
from jax import lax
from jax.experimental import pallas as pl
from jax.experimental.pallas import tpu as pltpu
from jax.sharding import Mesh, PartitionSpec as P

adapter_scale = 2.0
cube = ("groups", "inner")
row = ("half", "inner")
vmem_limit = 56 * 1024 * 1024
NT = (((1,), (1,)), ((), ()))


def call(kernel, place, grid, in_specs, out_specs, out_shape, flops, moved, name, args, scratch=()):
    return pl.pallas_call(
        kernel,
        grid_spec=pltpu.PrefetchScalarGridSpec(
            num_scalar_prefetch=1,
            grid=grid,
            in_specs=in_specs,
            out_specs=out_specs,
            scratch_shapes=scratch,
        ),
        out_shape=out_shape,
        compiler_params=pltpu.CompilerParams(vmem_limit_bytes=vmem_limit),
        cost_estimate=pl.CostEstimate(flops=flops, bytes_accessed=moved, transcendentals=0),
        name=name,
    )(place, *args)


def repeat(count, step, start):
    if count <= 4:
        for i in range(count):
            start = step(i, start)
        return start
    return lax.fori_loop(0, count, step, start)


def move(name, sources, in_blocks, in_maps, outs, out_blocks, out_maps, grid, kernel, place):
    moved = 0
    for shape in outs:
        size = 4
        for n in shape:
            size *= n
        moved += size
    return call(
        kernel,
        place,
        grid,
        [pl.BlockSpec(block, index) for block, index in zip(in_blocks, in_maps)],
        [pl.BlockSpec(block, index) for block, index in zip(out_blocks, out_maps)],
        [jax.ShapeDtypeStruct(shape, jnp.bfloat16) for shape in outs],
        0,
        moved,
        name,
        sources,
    )


def split_columns(place, rows, groups, size):
    slots, rank, model = rows.shape
    share, width = max(1, slots // groups), model // size
    group = lambda place: place[0] if slots >= groups else 0
    if width % 128:
        mine = lax.dynamic_slice_in_dim(rows, group(place) * share, share, 0)
        return mine.reshape(share * rank, size, width).swapaxes(0, 1)

    def kernel(place_ref, rows_ref, out_ref):
        for q in range(size):
            out_ref[q] = rows_ref[0, :, q * width : (q + 1) * width]

    tile = min(rank, 64)
    steps = rank // tile
    return move(
        "split_columns", [rows], [(1, tile, model)],
        [lambda s, r, place: (group(place) * share + s, r, 0)],
        [(size, share * rank, width)], [(size, tile, width)],
        [lambda s, r, place: (0, s * steps + r, 0)], (share, steps), kernel, place,
    )[0]


def join_slots(place, parts, resident):
    size, rows, width = parts[0].shape
    count, rank = len(parts), rows // resident
    if width % 128:
        joined = jnp.stack(parts, axis=1).transpose(2, 0, 1, 3)
        return joined.reshape(resident, rank, -1)

    def kernel(place_ref, *refs):
        for q in range(size):
            for c in range(count):
                first = (q * count + c) * width
                refs[-1][0, :, first : first + width] = refs[c][q]

    return move(
        "join_slots", parts, [(size, rank, width)] * count, [lambda r, place: (0, r, 0)] * count,
        [(resident, rank, size * count * width)], [(1, rank, size * count * width)],
        [lambda r, place: (r, 0, 0)], (resident,), kernel, place,
    )[0]


def join_rows(place, rows):
    size, tokens, width = rows.shape
    if width % 128:
        return rows.swapaxes(0, 1).reshape(tokens, size * width)
    tile = min(tokens, 64)

    def kernel(place_ref, rows_ref, out_ref):
        for q in range(size):
            out_ref[:, q * width : (q + 1) * width] = rows_ref[q]

    return move(
        "join_rows", [rows], [(size, tile, width)], [lambda t, place: (0, t, 0)],
        [(tokens, size * width)], [(tile, size * width)], [lambda t, place: (t, 0)],
        (tokens // tile,), kernel, place,
    )[0]


def slot_sums(packed_ref, x_ref, rank, first, count):
    devices, _, tokens = packed_ref.shape
    chunk = min(devices, 4)

    def step(c, total):
        columns = []
        for d in range(chunk):
            device = c * chunk + d
            back = packed_ref[device, :rank, :]
            slots = packed_ref[device, rank : rank + 1, :].astype(jnp.float32)
            rows = [
                back * (slots == (first + i).astype(jnp.float32)).astype(jnp.bfloat16)
                for i in range(count)
            ]
            columns.append(jnp.concatenate(rows, axis=0))
        x = x_ref[pl.ds(c * chunk, chunk)].reshape(chunk * tokens, x_ref.shape[2])
        return total + jnp.dot(
            jnp.concatenate(columns, axis=1), x, preferred_element_type=jnp.float32
        )

    start = jnp.zeros((count * rank, x_ref.shape[2]), jnp.float32)
    return repeat(devices // chunk, step, start)


def grad_a_kernel(slots_half, count, rank, own, place_ref, packed_ref, x_ref, *refs):
    half = place_ref[1] if own else 1 - place_ref[1]
    first = half * slots_half + pl.program_id(1) * count
    total = slot_sums(packed_ref, x_ref, rank, first, count)
    if own:
        total = adapter_scale * (total + refs[0][0].astype(jnp.float32))
    refs[-1][0] = total.astype(jnp.bfloat16)


def grad_a_part(place, packed, x_cols, part, got, groups, slots_half, rank):
    devices, depth, tokens = packed.shape
    width = x_cols.shape[2] // 2
    if width % 128:
        x_cols, part = x_cols[:, :, part * width : (part + 1) * width], 0
    local = devices // groups
    count = 8
    rows = count * rank
    block = pl.BlockSpec((1, rows, width), lambda g, s, place: (g, s, 0))
    return call(
        lambda *refs: grad_a_kernel(slots_half, count, rank, len(got) > 0, *refs),
        place,
        (groups, slots_half // count),
        [
            pl.BlockSpec((local, depth, tokens), lambda g, s, place: (g, 0, 0)),
            pl.BlockSpec((local, tokens, width), lambda g, s, place: (g, 0, part)),
        ]
        + [block] * len(got),
        block,
        jax.ShapeDtypeStruct((groups, slots_half * rank, width), jnp.bfloat16),
        2 * devices * tokens * width * slots_half * rank,
        2 * devices * tokens * width + 2 * groups * slots_half * rank * width * (1 + len(got)),
        "grad_a_own" if got else "grad_a_other",
        (packed, x_cols, *got),
    )


def from_here(slots, place_ref, total):
    slots -= place_ref[1] * (total // 2)
    return jnp.where(slots < 0, slots + total, slots)


def each_piece(pieces, chunk, step, start):
    first = 0
    for piece in pieces:
        count = piece.shape[0] // chunk

        def one(c, total, piece=piece, first=first):
            block = piece[pl.ds(pl.multiple_of(c * chunk, chunk), chunk), :]
            return step(block, first + c * chunk, total)

        start = repeat(count, one, start)
        first += piece.shape[0]
    return start


def low_kernel(chunk, rank, place_ref, packed_ref, x_ref, *refs):
    *pieces, low_ref = refs
    total = sum(piece.shape[0] for piece in pieces)
    slots = packed_ref[0].astype(jnp.float32).T[:, rank + 1 : rank + 2].astype(jnp.int32)
    slots = from_here(slots, place_ref, total // rank)
    tile = x_ref.shape[1]
    lane_slot = lax.broadcasted_iota(jnp.int32, (tile, chunk), 1) // rank

    def step(block, first, low):
        hidden = lax.dot_general(x_ref[0], block, NT, preferred_element_type=jnp.float32)
        hidden = jnp.where(lane_slot + first // rank == slots, hidden, 0.0)
        for k in range(chunk // (2 * rank)):
            low += hidden[:, k * 2 * rank : (k + 1) * 2 * rank]
        return low

    low = each_piece(pieces, chunk, step, jnp.zeros((tile, 2 * rank), jnp.float32)).T
    low_ref[0] = low[:rank] + low[rank:]


def low_part(place, packed, x_cols, a_pieces, rank):
    devices, depth, tokens = packed.shape
    width = x_cols.shape[2]
    slots = sum(piece.shape[0] for piece in a_pieces)
    return call(
        lambda *refs: low_kernel(512, rank, *refs),
        place,
        (devices,),
        [
            pl.BlockSpec((1, depth, tokens), lambda t, place: (t, 0, 0)),
            pl.BlockSpec((1, tokens, width), lambda t, place: (t, 0, 0)),
        ]
        + [pl.BlockSpec(piece.shape, lambda t, place: (0, 0)) for piece in a_pieces],
        pl.BlockSpec((1, rank, tokens), lambda t, place: (t, 0, 0)),
        jax.ShapeDtypeStruct((devices, rank, tokens), jnp.float32),
        2 * devices * tokens * width * slots,
        2 * (devices * tokens + slots) * width,
        "low_part",
        (packed, x_cols, *a_pieces),
    )


def out_kernel(chunk, rank, place_ref, packed_ref, g_ref, w_ref, *refs):
    *pieces, out_ref = refs
    total = sum(piece.shape[0] for piece in pieces)
    rows = packed_ref[0].astype(jnp.float32).T
    back, slots = rows[:, :rank], rows[:, rank + 1 : rank + 2].astype(jnp.int32)
    slots = from_here(slots, place_ref, total // rank)
    tile = back.shape[0]
    repeated = jnp.concatenate([back] * (chunk // rank), axis=1)
    lane_slot = lax.broadcasted_iota(jnp.int32, (tile, chunk), 1) // rank

    def step(block, first, acc):
        keep = lane_slot + first // rank == slots
        masked = jnp.where(keep, repeated, 0.0).astype(jnp.bfloat16)
        return acc + jnp.dot(masked, block, preferred_element_type=jnp.float32)

    acc = each_piece(pieces, chunk, step, jnp.zeros((tile, w_ref.shape[0]), jnp.float32))
    base = lax.dot_general(g_ref[...], w_ref[...], NT, preferred_element_type=jnp.float32)
    out_ref[0] = (base + adapter_scale * acc).astype(out_ref.dtype)


def out_part(place, packed, g_all, w_cols, a_pieces, rank):
    devices, depth, tokens = packed.shape
    outs = g_all.shape[1]
    width = w_cols.shape[0]
    slots = sum(piece.shape[0] for piece in a_pieces)
    return call(
        lambda *refs: out_kernel(512, rank, *refs),
        place,
        (devices,),
        [
            pl.BlockSpec((1, depth, tokens), lambda t, place: (t, 0, 0)),
            pl.BlockSpec((tokens, outs), lambda t, place: (t, 0)),
            pl.BlockSpec((width, outs), lambda t, place: (0, 0)),
        ]
        + [pl.BlockSpec(piece.shape, lambda t, place: (0, 0)) for piece in a_pieces],
        pl.BlockSpec((1, tokens, width), lambda t, place: (t, 0, 0)),
        jax.ShapeDtypeStruct((devices, tokens, width), jnp.bfloat16),
        2 * devices * tokens * width * (slots + outs),
        2 * devices * tokens * (width + outs) + 2 * slots * width,
        "out_part",
        (packed, g_all, w_cols, *a_pieces),
    )


def body(x, g, tok, adapter_slot, w, a, b):
    groups, inner = lax.axis_size("groups"), lax.axis_size("inner")
    gi, hi, ji = lax.axis_index("groups"), lax.axis_index("half"), lax.axis_index("inner")
    place = jnp.stack([gi, hi, ji]).astype(jnp.int32)
    size = groups * inner
    devices = 2 * inner
    tokens, model = x.shape
    outs = g.shape[1]
    resident, _, rank = a.shape
    share = resident // groups
    count = inner * resident
    width = model // size
    adapters = adapter_slot.shape[0]
    capacity = max(2, 2 * tokens // adapters)
    swap = [(0, 1), (1, 0)]

    w_other = lax.ppermute(w, "half", swap)

    a_mine = split_columns(place, jnp.swapaxes(a, 1, 2), groups, size)
    a_own = lax.all_to_all(a_mine, cube, 0, 0, tiled=True).reshape(count * rank, width)

    matches = tok == lax.broadcasted_iota(jnp.int32, (tokens, adapters), 1)
    slot = jnp.sum(jnp.where(matches, adapter_slot[None, :], 0), axis=1)
    running = jnp.cumsum(matches.astype(jnp.int32), axis=0)
    within = jnp.sum(jnp.where(matches, running - 1, 0), axis=1)
    position = slot * capacity + within
    at = lax.broadcasted_iota(jnp.int32, (adapters * capacity, tokens), 0) == position[None, :]
    at = at.astype(jnp.bfloat16)

    def route(rows):
        rows = rows.reshape(devices, resident * capacity, rows.shape[1])
        rows = lax.all_to_all(rows, row, 0, 0, tiled=True)
        return rows.reshape(devices, resident, capacity, rows.shape[2])

    g_send = jnp.dot(at, g, preferred_element_type=jnp.float32).astype(jnp.bfloat16)
    g_send, a_own, w_other = lax.optimization_barrier((g_send, a_own, w_other))
    w_cols = jnp.where(hi == gi, w, w_other)
    g_rows = route(g_send)
    back = jnp.einsum("hjct,jrt->hjcr", g_rows, b, preferred_element_type=jnp.float32)
    back = back.astype(jnp.bfloat16).reshape(devices, resident * capacity, rank)
    a_half = count * rank // 2
    a_first = lax.ppermute(a_own[:a_half], "half", swap)
    back, a_first = lax.optimization_barrier((back, a_first))
    back = lax.all_to_all(back, row, 0, 0, tiled=True).reshape(adapters * capacity, rank)
    a_own, a_first = lax.optimization_barrier((a_own, a_first))
    a_second = lax.ppermute(a_own[a_half:], "half", swap)
    back = lax.dot_general(
        back, at, (((0,), (0,)), ((), ())), preferred_element_type=jnp.float32
    ).astype(jnp.bfloat16)
    owner, res = slot // resident, slot % resident
    slot_a = (owner // inner) * count + ((res // share) * inner + owner % inner) * share + res % share
    names = jnp.stack([slot, slot_a] + [slot] * 14).astype(jnp.bfloat16)
    packed = jnp.concatenate([back, names], axis=0)
    packed = jnp.broadcast_to(packed[None], (size,) + packed.shape)
    packed = lax.all_to_all(packed, cube, 0, 0, tiled=True)

    g_all = lax.all_gather(g, cube, axis=0, tiled=True)
    x_send = split_columns(place, x[None], groups, size)
    x_send, packed, a_second, g_all = lax.optimization_barrier((x_send, packed, a_second, g_all))
    x_cols = lax.all_to_all(x_send, cube, 0, 0, tiled=True)

    def other(part):
        return grad_a_part(place, packed, x_cols, part, (), groups, count, rank)

    def own(part, got):
        p = grad_a_part(place, packed, x_cols, part, (got,), groups, count, rank)
        return p.reshape(size, resident * rank, width // 2)

    first = other(0)
    got = [lax.ppermute(first, "half", swap)]
    packed, first = lax.optimization_barrier((packed, first))
    second = other(1)
    got.append(lax.ppermute(second, "half", swap))

    a_pieces = [a_own, a_first, a_second]
    a_pieces, second = lax.optimization_barrier((a_pieces, second))
    out_cols = out_part(place, packed, g_all, w_cols, a_pieces, rank)
    a_pieces, out_cols = lax.optimization_barrier((a_pieces, out_cols))
    out_back = lax.all_to_all(out_cols, cube, 0, 0, tiled=True)

    low = low_part(place, packed, x_cols, a_pieces, rank)
    got[0], low = lax.optimization_barrier((got[0], low))
    p_back = [own(0, got[0])]
    low, out_back = lax.optimization_barrier((low, out_back))
    low = lax.all_to_all(low, cube, 0, 0, tiled=True)
    low, p_back[0] = lax.optimization_barrier((low, p_back[0]))
    p_back[0] = lax.all_to_all(p_back[0], cube, 0, 0, tiled=True)
    low = jnp.sum(low, axis=0).astype(jnp.bfloat16)
    low = lax.dot_general(at, low, NT, preferred_element_type=jnp.float32).astype(jnp.bfloat16)
    low, p_back[0] = lax.optimization_barrier((low, p_back[0]))
    low = route(low)
    p_second, low = lax.optimization_barrier((own(1, got[1]), low))
    p_back.append(lax.all_to_all(p_second, cube, 0, 0, tiled=True))

    grad_b = jnp.einsum("hjcr,hjco->jro", low, g_rows, preferred_element_type=jnp.float32)
    grad_b = (adapter_scale * grad_b).astype(jnp.bfloat16)
    input_gradient = join_rows(place, out_back)
    grad_a = join_slots(place, p_back, resident).swapaxes(1, 2)
    return input_gradient, grad_a, grad_b


def solution(mesh):
    groups, rows = mesh.shape["groups"], mesh.shape["row"]
    whole = ("groups", "half", "inner")
    split = Mesh(mesh.devices.reshape(groups, 2, rows // 2), whole)
    return jax.shard_map(
        body,
        mesh=split,
        in_specs=(
            P(whole, None),
            P(whole, None),
            P(whole, None),
            P(),
            P(row, None),
            P(row, None, None),
            P(row, None, None),
        ),
        out_specs=(P(whole, None), P(whole, None, None), P(whole, None, None)),
        check_vma=False,
    )
```

```python
import jax
import jax.numpy as jnp
from jax import lax
from jax.experimental import pallas as pl
from jax.experimental.pallas import tpu as pltpu
from jax.sharding import Mesh, PartitionSpec as P

adapter_scale = 2.0
line_length = 4
plane = ("groups", "inner")
row = ("line", "inner")
vmem_limit = 56 * 1024 * 1024
NT = (((1,), (1,)), ((), ()))


def call(kernel, place, grid, in_specs, out_specs, out_shape, flops, moved, name, args, scratch=()):
    return pl.pallas_call(
        kernel,
        grid_spec=pltpu.PrefetchScalarGridSpec(
            num_scalar_prefetch=1,
            grid=grid,
            in_specs=in_specs,
            out_specs=out_specs,
            scratch_shapes=scratch,
        ),
        out_shape=out_shape,
        compiler_params=pltpu.CompilerParams(vmem_limit_bytes=vmem_limit),
        cost_estimate=pl.CostEstimate(flops=flops, bytes_accessed=moved, transcendentals=0),
        name=name,
    )(place, *args)


def repeat(count, step, start):
    if count <= 4:
        for i in range(count):
            start = step(i, start)
        return start
    return lax.fori_loop(0, count, step, start)


def move(name, sources, in_blocks, in_maps, outs, out_blocks, out_maps, grid, kernel, place):
    moved = 0
    for shape in outs:
        size = 4
        for n in shape:
            size *= n
        moved += size
    return call(
        kernel,
        place,
        grid,
        [pl.BlockSpec(block, index) for block, index in zip(in_blocks, in_maps)],
        [pl.BlockSpec(block, index) for block, index in zip(out_blocks, out_maps)],
        [jax.ShapeDtypeStruct(shape, jnp.bfloat16) for shape in outs],
        0,
        moved,
        name,
        sources,
    )


def columns_of(q, c, halves, inner):
    return ((q // inner) * halves + c) * inner + q % inner


def split_columns(place, rows, groups, halves, inner, width):
    slots, rank, model = rows.shape
    size, share = groups * inner, max(1, slots // groups)
    group = lambda place: place[0] if slots >= groups else 0
    if width % 128:
        mine = lax.dynamic_slice_in_dim(rows, group(place) * share, share, 0)
        mine = mine.reshape(share * rank, groups, halves, inner, width)
        return mine.transpose(1, 3, 0, 2, 4).reshape(size, share * rank, halves * width)

    def kernel(place_ref, rows_ref, out_ref):
        for q in range(size):
            for c in range(halves):
                first = columns_of(q, c, halves, inner) * width
                out_ref[q, :, c * width : (c + 1) * width] = rows_ref[0, :, first : first + width]

    tile = min(rank, 64)
    steps = rank // tile
    return move(
        "split_columns", [rows], [(1, tile, model)],
        [lambda s, r, place: (group(place) * share + s, r, 0)],
        [(size, share * rank, halves * width)], [(size, tile, halves * width)],
        [lambda s, r, place: (0, s * steps + r, 0)], (share, steps), kernel, place,
    )[0]


def split_pieces(place, rows, groups, halves, inner, width):
    count, model = rows.shape
    size = groups * inner
    tile = min(count, 64)

    def kernel(place_ref, rows_ref, *out_refs):
        me = place_ref[0] * inner + place_ref[2]
        for m in range(size):
            for c in range(halves):
                first = pl.multiple_of(columns_of(me ^ m, c, halves, inner) * width, width)
                out_refs[m][:, c * width : (c + 1) * width] = rows_ref[:, pl.ds(first, width)]

    return move(
        "split_pieces", [rows], [(tile, model)], [lambda t, place: (t, 0)],
        [(count, halves * width)] * size, [(tile, halves * width)] * size,
        [lambda t, place: (t, 0)] * size, (count // tile,), kernel, place,
    )


def join_slots(place, parts, resident, groups, inner):
    size, rows, width = parts[0].shape
    halves, rank = len(parts), rows // resident
    if width % 128:
        parts = [p.reshape(groups, inner, rows, width) for p in parts]
        joined = jnp.stack(parts, axis=1).transpose(3, 0, 1, 2, 4)
        return joined.reshape(resident, rank, -1)

    def kernel(place_ref, *refs):
        for q in range(size):
            for c in range(halves):
                first = columns_of(q, c, halves, inner) * width
                refs[-1][0, :, first : first + width] = refs[c][q]

    return move(
        "join_slots", parts, [(size, rank, width)] * halves, [lambda r, place: (0, r, 0)] * halves,
        [(resident, rank, size * halves * width)], [(1, rank, size * halves * width)],
        [lambda r, place: (r, 0, 0)], (resident,), kernel, place,
    )[0]


def join_rows(place, rows, groups, halves, inner, part):
    size, tokens = rows.shape[:2]
    if part % 128:
        rows = rows.reshape(groups, inner, tokens, halves, part)
        return rows.transpose(2, 0, 3, 1, 4).reshape(tokens, -1)
    tile = min(tokens, 64)
    model = size * halves * part

    def kernel(place_ref, rows_ref, out_ref):
        for q in range(size):
            for c in range(halves):
                first = columns_of(q, c, halves, inner) * part
                out_ref[:, first : first + part] = rows_ref[q, :, c * part : (c + 1) * part]

    return move(
        "join_rows", [rows], [(size, tile, halves * part)], [lambda t, place: (0, t, 0)],
        [(tokens, model)], [(tile, model)], [lambda t, place: (t, 0)], (tokens // tile,),
        kernel, place,
    )[0]


def slot_sums(packed_ref, x_refs, me, rank, first, count):
    devices, _, tokens = packed_ref.shape
    width = x_refs[0].shape[-1]
    chunk = min(devices, 4)

    def step(c, total):
        columns = []
        for d in range(chunk):
            device = (c * chunk + d) ^ me
            back = packed_ref[device, :rank, :]
            slots = packed_ref[device, rank : rank + 1, :].astype(jnp.float32)
            rows = [
                back * (slots == (first + i).astype(jnp.float32)).astype(jnp.bfloat16)
                for i in range(count)
            ]
            columns.append(jnp.concatenate(rows, axis=0))
        if len(x_refs) > 1:
            x = jnp.concatenate([x_ref[...] for x_ref in x_refs], axis=0)
        else:
            x = x_refs[0][pl.ds(c * chunk, chunk)].reshape(chunk * tokens, width)
        return total + jnp.dot(
            jnp.concatenate(columns, axis=1), x, preferred_element_type=jnp.float32
        )

    return repeat(devices // chunk, step, jnp.zeros((count * rank, width), jnp.float32))


def by_group(x_refs, groups, use):
    if len(x_refs) == 1:
        use(x_refs)
        return
    local = len(x_refs) // groups
    for g in range(groups):

        @pl.when(pl.program_id(0) == g)
        def _(g=g):
            use(x_refs[g * local : (g + 1) * local])


def send_kernel(groups, number, slots_line, count, rank, away, place_ref, packed_ref, *refs):
    line = place_ref[1]
    x_refs, got, outs = refs[:number], refs[number:-2], refs[-2:]
    ways = ((line + away < line_length, line + away), (line >= away, line - away))
    for way, (inside, target) in enumerate(ways):

        def use(x_refs, way=way, target=target):
            first = target * slots_line + pl.program_id(1) * count
            total = slot_sums(packed_ref, x_refs, place_ref[2], rank, first, count)
            if got:
                total += got[way][0].astype(jnp.float32)
            outs[way][0] = total.astype(jnp.bfloat16)

        @pl.when(inside)
        def _(use=use):
            by_group(x_refs, groups, use)


def own_kernel(groups, number, slots_line, count, rank, place_ref, packed_ref, *refs):
    x_refs, (right_ref, left_ref, out_ref) = refs[:number], refs[number:]

    def use(x_refs):
        first = place_ref[1] * slots_line + pl.program_id(1) * count
        total = slot_sums(packed_ref, x_refs, place_ref[2], rank, first, count)
        total += right_ref[0].astype(jnp.float32) + left_ref[0].astype(jnp.float32)
        out_ref[0] = (adapter_scale * total).astype(jnp.bfloat16)

    by_group(x_refs, groups, use)


def grad_a_step(place, packed, x_cols, half, got, away, groups, slots_line, rank):
    devices, depth, tokens = packed.shape
    width = x_cols[0].shape[-1] // 2
    local = devices // groups
    count = 8
    rows = count * rank
    number = len(x_cols)
    if number > 1:
        x_specs = [pl.BlockSpec((tokens, width), lambda g, s, place: (0, half))] * number
    else:
        if width % 128:
            x_cols, half = [x_cols[0][:, :, half * width : (half + 1) * width]], 0
        x_specs = [pl.BlockSpec((local, tokens, width), lambda g, s, place: (g, 0, half))]
    block = pl.BlockSpec((1, rows, width), lambda g, s, place: (g, s, 0))
    final = pl.BlockSpec((1, rows, width), lambda g, s, place: (g ^ place[0], s, 0))
    shape = jax.ShapeDtypeStruct((groups, slots_line * rank, width), jnp.bfloat16)
    ways = 1 if away == 0 else 2
    if away == 0:
        kernel = lambda *refs: own_kernel(groups, number, slots_line, count, rank, *refs)
    else:
        kernel = lambda *refs: send_kernel(groups, number, slots_line, count, rank, away, *refs)
    return call(
        kernel,
        place,
        (groups, slots_line // count),
        [pl.BlockSpec((local, depth, tokens), lambda g, s, place: (g ^ place[0], 0, 0))]
        + x_specs
        + [block] * len(got),
        final if away == 0 else [block, block],
        shape if away == 0 else [shape, shape],
        ways * 2 * devices * tokens * width * slots_line * rank,
        2 * devices * tokens * width + 2 * groups * slots_line * rank * width * (ways + len(got)),
        "grad_a_step" + str(away),
        (packed, *x_cols, *got),
    )


def in_line(slots, place_ref, total):
    slots -= place_ref[1] * (total // line_length)
    return jnp.where(slots < 0, slots + total, slots)


def put_together(pieces, a_ref):
    @pl.when(pl.program_id(0) == 0)
    def _():
        rows = pieces[0].shape[0]
        a_ref[:rows] = pieces[0][...]
        for k in range(1, line_length):
            left, right = pieces[line_length - k], pieces[line_length - 1 + k]
            a_ref[k * rows : (k + 1) * rows] = left[...] + right[...]


def low_kernel(chunk, rank, number, place_ref, packed_ref, *refs):
    x_refs, pieces, (low_ref, a_ref) = refs[:number], refs[number:-2], refs[-2:]
    put_together(pieces, a_ref)
    slots = packed_ref[0].astype(jnp.float32).T[:, rank + 1 : rank + 2].astype(jnp.int32)
    slots = in_line(slots, place_ref, a_ref.shape[0] // rank)
    tile = slots.shape[0]
    lane_slot = lax.broadcasted_iota(jnp.int32, (tile, chunk), 1) // rank

    def use(x):
        def step(c, low):
            part = pl.ds(pl.multiple_of(c * chunk, chunk), chunk)
            hidden = lax.dot_general(x, a_ref[part], NT, preferred_element_type=jnp.float32)
            hidden = jnp.where(lane_slot + c * (chunk // rank) == slots, hidden, 0.0)
            for k in range(chunk // (2 * rank)):
                low += hidden[:, k * 2 * rank : (k + 1) * 2 * rank]
            return low

        start = jnp.zeros((tile, 2 * rank), jnp.float32)
        low = repeat(a_ref.shape[0] // chunk, step, start).T
        low_ref[0] = low[:rank] + low[rank:]

    if number == 1:
        use(x_refs[0][0])
    else:
        for m in range(number):

            @pl.when(pl.program_id(0) == m)
            def _(m=m):
                use(x_refs[m][...])


def low_part(place, packed, x_cols, a_pieces, inner, rank):
    devices, depth, tokens = packed.shape
    width = x_cols[0].shape[-1]
    rows = a_pieces[0].shape[0]
    slots = line_length * rows
    number = len(x_cols)
    mate = lambda t, place: (t ^ (place[0] * inner + place[2]), 0, 0)
    if number > 1:
        x_specs = [pl.BlockSpec((tokens, width), lambda t, place: (0, 0))] * number
    else:
        x_specs = [pl.BlockSpec((1, tokens, width), lambda t, place: (t, 0, 0))]
    return call(
        lambda *refs: low_kernel(512, rank, number, *refs),
        place,
        (devices,),
        [pl.BlockSpec((1, depth, tokens), mate)]
        + x_specs
        + [pl.BlockSpec((rows, width), lambda t, place: (0, 0))] * len(a_pieces),
        pl.BlockSpec((1, rank, tokens), mate),
        jax.ShapeDtypeStruct((devices, rank, tokens), jnp.float32),
        2 * devices * tokens * width * slots,
        2 * (devices * tokens + slots) * width,
        "low_part",
        (packed, *x_cols, *a_pieces),
        [pltpu.VMEM((slots, width), jnp.bfloat16)],
    )


def out_kernel(chunk, rank, place_ref, packed_ref, g_ref, w_ref, *refs):
    *pieces, out_ref, a_ref = refs
    put_together(pieces, a_ref)
    rows = jnp.concatenate([p.astype(jnp.float32).T for p in packed_ref[...]], axis=0)
    back, slots = rows[:, :rank], rows[:, rank + 1 : rank + 2].astype(jnp.int32)
    slots = in_line(slots, place_ref, a_ref.shape[0] // rank)
    tile = back.shape[0]
    repeated = jnp.concatenate([back] * (chunk // rank), axis=1)
    lane_slot = lax.broadcasted_iota(jnp.int32, (tile, chunk), 1) // rank

    def step(c, acc):
        keep = lane_slot + c * (chunk // rank) == slots
        masked = jnp.where(keep, repeated, 0.0).astype(jnp.bfloat16)
        block = a_ref[pl.ds(pl.multiple_of(c * chunk, chunk), chunk), :]
        return acc + jnp.dot(masked, block, preferred_element_type=jnp.float32)

    start = jnp.zeros((tile, a_ref.shape[1]), jnp.float32)
    acc = repeat(a_ref.shape[0] // chunk, step, start)
    base = lax.dot_general(g_ref[...], w_ref[...], NT, preferred_element_type=jnp.float32)
    out = (base + adapter_scale * acc).astype(out_ref.dtype)
    out_ref[...] = out.reshape(out_ref.shape)


def out_part(place, packed, g_all, w_cols, a_pieces, rank):
    devices, depth, tokens = packed.shape
    outs = g_all.shape[1]
    rows, width = a_pieces[0].shape
    slots = line_length * rows
    both = 2
    return call(
        lambda *refs: out_kernel(512, rank, *refs),
        place,
        (devices // both,),
        [
            pl.BlockSpec((both, depth, tokens), lambda t, place: (t, 0, 0)),
            pl.BlockSpec((both * tokens, outs), lambda t, place: (t, 0)),
            pl.BlockSpec((width, outs), lambda t, place: (0, 0)),
        ]
        + [pl.BlockSpec((rows, width), lambda t, place: (0, 0))] * len(a_pieces),
        pl.BlockSpec((both, tokens, width), lambda t, place: (t, 0, 0)),
        jax.ShapeDtypeStruct((devices, tokens, width), jnp.bfloat16),
        2 * devices * tokens * width * (slots + outs),
        2 * devices * tokens * (width + outs) + 2 * slots * width,
        "out_part",
        (packed, g_all, w_cols, *a_pieces),
        [pltpu.VMEM((slots, width), jnp.bfloat16)],
    )


def body(x, g, tok, adapter_slot, w, a, b):
    groups, inner = lax.axis_size("groups"), lax.axis_size("inner")
    gi, li, ji = lax.axis_index("groups"), lax.axis_index("line"), lax.axis_index("inner")
    place = jnp.stack([gi, li, ji]).astype(jnp.int32)
    size = groups * inner
    devices = line_length * inner
    tokens, model = x.shape
    outs = g.shape[1]
    resident, _, rank = a.shape
    share = resident // groups
    count = inner * resident
    halves = line_length // groups
    width = model // size
    part = width // halves
    adapters = adapter_slot.shape[0]
    capacity = max(2, 2 * tokens // adapters)

    a_mine = split_columns(place, jnp.swapaxes(a, 1, 2), groups, halves, inner, part)
    a_own = lax.all_to_all(a_mine, plane, 0, 0, tiled=True).reshape(count * rank, width)

    def meet(m):
        return lax.ppermute(x_sends[m], plane, [(i, i ^ m) for i in range(size)])

    direct = size == 8 and part % 128 == 0
    x_cols = {}
    if direct:
        x_sends = split_pieces(place, x, groups, halves, inner, part)
        x_cols = {0: x_sends[0], 1: meet(1), 2: meet(2), 4: meet(4)}
    else:
        x_far = split_columns(place, x[None], groups, halves, inner, part)
        x_far = lax.all_to_all(x_far, plane, 0, 0, tiled=True)
        x_cols = {0: x_far[jnp.arange(size) ^ (gi * inner + ji)]}

    matches = tok == lax.broadcasted_iota(jnp.int32, (tokens, adapters), 1)
    slot = jnp.sum(jnp.where(matches, adapter_slot[None, :], 0), axis=1)
    running = jnp.cumsum(matches.astype(jnp.int32), axis=0)
    within = jnp.sum(jnp.where(matches, running - 1, 0), axis=1)
    position = slot * capacity + within
    at = lax.broadcasted_iota(jnp.int32, (adapters * capacity, tokens), 0) == position[None, :]
    at = at.astype(jnp.bfloat16)

    def route(rows):
        rows = rows.reshape(devices, resident * capacity, rows.shape[1])
        rows = lax.all_to_all(rows, row, 0, 0, tiled=True)
        return rows.reshape(devices, resident, capacity, rows.shape[2])

    g_send = jnp.dot(at, g, preferred_element_type=jnp.float32).astype(jnp.bfloat16)
    g_send, a_own, x_cols = lax.optimization_barrier((g_send, a_own, x_cols))
    g_rows = route(g_send)
    back = jnp.einsum("hjct,jrt->hjcr", g_rows, b, preferred_element_type=jnp.float32)
    back = back.astype(jnp.bfloat16).reshape(devices, resident * capacity, rank)
    w_line = lax.all_gather(w, "line", axis=0)
    g_all = lax.all_gather(g, plane, axis=0, tiled=True)

    up = [(i, i + 1) for i in range(line_length - 1)]
    down = [(i + 1, i) for i in range(line_length - 1)]

    def hop(pieces, away):
        left, right = pieces
        return [
            lax.ppermute(left, "line", up[away - 1 :]),
            lax.ppermute(right, "line", down[: line_length - away]),
        ]

    hops = [hop((a_own, a_own), 1)]
    if direct:
        x_cols.update({3: meet(3), 5: meet(5)})
    back, hops, x_cols = lax.optimization_barrier((back, hops, x_cols))
    hops.append(hop(hops[0], 2))
    if direct:
        x_sends, hops[0] = lax.optimization_barrier((x_sends, hops[0]))
        x_cols.update({6: meet(6), 7: meet(7)})
    back, x_cols, w_line = lax.optimization_barrier((back, x_cols, w_line))
    back = lax.all_to_all(back, row, 0, 0, tiled=True).reshape(adapters * capacity, rank)
    back, hops[1] = lax.optimization_barrier((back, hops[1]))
    hops.append(hop(hops[1], 3))
    back = lax.dot_general(
        back, at, (((0,), (0,)), ((), ())), preferred_element_type=jnp.float32
    ).astype(jnp.bfloat16)
    owner, res = slot // resident, slot % resident
    slot_a = (owner // inner) * count + ((res // share) * inner + owner % inner) * share + res % share
    names = jnp.stack([slot, slot_a] + [slot] * 14).astype(jnp.bfloat16)
    packed = jnp.concatenate([back, names], axis=0)
    packed = jnp.broadcast_to(packed[None], (size,) + packed.shape)
    packed = lax.all_to_all(packed, plane, 0, 0, tiled=True)
    x_cols = [x_cols[m] for m in range(len(x_cols))]

    a_pieces = [a_own] + [h[0] for h in hops] + [h[1] for h in hops]
    w_cols = lax.dynamic_slice_in_dim(w_line, gi * halves, halves, 0).reshape(width, outs)
    out_cols = out_part(place, packed, g_all, w_cols, a_pieces, rank)
    packed, out_cols = lax.optimization_barrier((packed, out_cols))
    out_back = lax.all_to_all(out_cols, plane, 0, 0, tiled=True)

    def send(c, got, away):
        sums = grad_a_step(place, packed, x_cols, c, got, away, groups, count, rank)
        ahead = [(i, i + 1) for i in range(line_length - away)]
        behind = [(i, i - 1) for i in range(away, line_length)]
        moved = (lax.ppermute(sums[0], "line", ahead), lax.ppermute(sums[1], "line", behind))
        return moved, sums[0]

    def own(c, got):
        p = grad_a_step(place, packed, x_cols, c, got, 0, groups, count, rank)
        return p.reshape(size, resident * rank, part)

    first, done = send(0, (), 3)
    packed, done = lax.optimization_barrier((packed, done))
    second, done = send(1, (), 3)

    first, done = send(0, first, 2)
    second, done = lax.optimization_barrier((second, done))
    second, done = send(1, second, 2)

    a_pieces, done = lax.optimization_barrier((a_pieces, done))
    low = low_part(place, packed, x_cols, a_pieces, inner, rank)
    first, low = lax.optimization_barrier((first, low))
    first, done = send(0, first, 1)
    second, done = lax.optimization_barrier((second, done))
    second, done = send(1, second, 1)
    first, done = lax.optimization_barrier((first, done))
    p_back = [own(0, first)]
    low, out_back = lax.optimization_barrier((low, out_back))
    low = lax.all_to_all(low, plane, 0, 0, tiled=True)
    low, p_back[0] = lax.optimization_barrier((low, p_back[0]))
    p_back[0] = lax.all_to_all(p_back[0], plane, 0, 0, tiled=True)
    low = jnp.sum(low, axis=0).astype(jnp.bfloat16)
    low = lax.dot_general(at, low, NT, preferred_element_type=jnp.float32).astype(jnp.bfloat16)
    low, p_back[0] = lax.optimization_barrier((low, p_back[0]))
    low = route(low)
    p_second, low = lax.optimization_barrier((own(1, second), low))
    p_back.append(lax.all_to_all(p_second, plane, 0, 0, tiled=True))

    grad_b = jnp.einsum("hjcr,hjco->jro", low, g_rows, preferred_element_type=jnp.float32)
    grad_b = (adapter_scale * grad_b).astype(jnp.bfloat16)
    input_gradient = join_rows(place, out_back, groups, halves, inner, part)
    grad_a = join_slots(place, p_back, resident, groups, inner).swapaxes(1, 2)
    return input_gradient, grad_a, grad_b


def solution(mesh):
    groups, rows = mesh.shape["groups"], mesh.shape["row"]
    whole = ("groups", "line", "inner")
    split = Mesh(mesh.devices.reshape(groups, line_length, rows // line_length), whole)
    return jax.shard_map(
        body,
        mesh=split,
        in_specs=(
            P(whole, None),
            P(whole, None),
            P(whole, None),
            P(),
            P(row, None),
            P(row, None, None),
            P(row, None, None),
        ),
        out_specs=(P(whole, None), P(whole, None, None), P(whole, None, None)),
        check_vma=False,
    )
```

```python
import jax
import jax.numpy as jnp
from jax import lax
from jax.experimental import pallas as pl
from jax.experimental.pallas import tpu as pltpu
from jax.sharding import Mesh, PartitionSpec as P

adapter_scale = 2.0
line_length = 4
plane = ("groups", "inner")
row = ("line", "inner")
vmem_limit = 56 * 1024 * 1024
NT = (((1,), (1,)), ((), ()))


def call(kernel, place, grid, in_specs, out_specs, out_shape, flops, moved, name, args, scratch=()):
    return pl.pallas_call(
        kernel,
        grid_spec=pltpu.PrefetchScalarGridSpec(
            num_scalar_prefetch=1,
            grid=grid,
            in_specs=in_specs,
            out_specs=out_specs,
            scratch_shapes=scratch,
        ),
        out_shape=out_shape,
        compiler_params=pltpu.CompilerParams(vmem_limit_bytes=vmem_limit),
        cost_estimate=pl.CostEstimate(flops=flops, bytes_accessed=moved, transcendentals=0),
        name=name,
    )(place, *args)


def repeat(count, step, start):
    if count <= 4:
        for i in range(count):
            start = step(i, start)
        return start
    return lax.fori_loop(0, count, step, start)


def move(name, sources, in_blocks, in_maps, outs, out_blocks, out_maps, grid, kernel, place):
    moved = 0
    for shape in outs:
        size = 4
        for n in shape:
            size *= n
        moved += size
    return call(
        kernel,
        place,
        grid,
        [pl.BlockSpec(block, index) for block, index in zip(in_blocks, in_maps)],
        [pl.BlockSpec(block, index) for block, index in zip(out_blocks, out_maps)],
        [jax.ShapeDtypeStruct(shape, jnp.bfloat16) for shape in outs],
        0,
        moved,
        name,
        sources,
    )


def columns_of(q, c, halves, inner):
    return ((q // inner) * halves + c) * inner + q % inner


def split_columns(place, rows, groups, halves, inner, width):
    slots, rank, model = rows.shape
    size, share = groups * inner, max(1, slots // groups)
    group = lambda place: place[0] if slots >= groups else 0
    if width % 128:
        mine = lax.dynamic_slice_in_dim(rows, group(place) * share, share, 0)
        mine = mine.reshape(share * rank, groups, halves, inner, width)
        return mine.transpose(1, 3, 0, 2, 4).reshape(size, share * rank, halves * width)

    def kernel(place_ref, rows_ref, out_ref):
        for q in range(size):
            for c in range(halves):
                first = columns_of(q, c, halves, inner) * width
                out_ref[q, :, c * width : (c + 1) * width] = rows_ref[0, :, first : first + width]

    tile = min(rank, 64)
    steps = rank // tile
    return move(
        "split_columns", [rows], [(1, tile, model)],
        [lambda s, r, place: (group(place) * share + s, r, 0)],
        [(size, share * rank, halves * width)], [(size, tile, halves * width)],
        [lambda s, r, place: (0, s * steps + r, 0)], (share, steps), kernel, place,
    )[0]


def split_pieces(place, rows, groups, halves, inner, width):
    count, model = rows.shape
    size = groups * inner
    tile = min(count, 64)

    def kernel(place_ref, rows_ref, *out_refs):
        me = place_ref[0] * inner + place_ref[2]
        for m in range(size):
            for c in range(halves):
                first = pl.multiple_of(columns_of(me ^ m, c, halves, inner) * width, width)
                out_refs[m][:, c * width : (c + 1) * width] = rows_ref[:, pl.ds(first, width)]

    return move(
        "split_pieces", [rows], [(tile, model)], [lambda t, place: (t, 0)],
        [(count, halves * width)] * size, [(tile, halves * width)] * size,
        [lambda t, place: (t, 0)] * size, (count // tile,), kernel, place,
    )


def join_slots(place, parts, resident, groups, inner):
    size, rows, width = parts[0].shape
    halves, rank = len(parts), rows // resident
    if width % 128:
        parts = [p.reshape(groups, inner, rows, width) for p in parts]
        joined = jnp.stack(parts, axis=1).transpose(3, 0, 1, 2, 4)
        return joined.reshape(resident, rank, -1)

    def kernel(place_ref, *refs):
        for q in range(size):
            for c in range(halves):
                first = columns_of(q, c, halves, inner) * width
                refs[-1][0, :, first : first + width] = refs[c][q]

    return move(
        "join_slots", parts, [(size, rank, width)] * halves, [lambda r, place: (0, r, 0)] * halves,
        [(resident, rank, size * halves * width)], [(1, rank, size * halves * width)],
        [lambda r, place: (r, 0, 0)], (resident,), kernel, place,
    )[0]


def join_rows(place, rows, groups, halves, inner, part):
    size, tokens = rows.shape[:2]
    if part % 128:
        rows = rows.reshape(groups, inner, tokens, halves, part)
        return rows.transpose(2, 0, 3, 1, 4).reshape(tokens, -1)
    tile = min(tokens, 64)
    model = size * halves * part

    def kernel(place_ref, rows_ref, out_ref):
        for q in range(size):
            for c in range(halves):
                first = columns_of(q, c, halves, inner) * part
                out_ref[:, first : first + part] = rows_ref[q, :, c * part : (c + 1) * part]

    return move(
        "join_rows", [rows], [(size, tile, halves * part)], [lambda t, place: (0, t, 0)],
        [(tokens, model)], [(tile, model)], [lambda t, place: (t, 0)], (tokens // tile,),
        kernel, place,
    )[0]


def slot_sums(packed_ref, x_refs, me, rank, first, count):
    devices, _, tokens = packed_ref.shape
    width = x_refs[0].shape[-1]
    chunk = min(devices, 4)

    def step(c, total):
        columns = []
        for d in range(chunk):
            device = (c * chunk + d) ^ me
            back = packed_ref[device, :rank, :]
            slots = packed_ref[device, rank : rank + 1, :].astype(jnp.float32)
            rows = [
                back * (slots == (first + i).astype(jnp.float32)).astype(jnp.bfloat16)
                for i in range(count)
            ]
            columns.append(jnp.concatenate(rows, axis=0))
        if len(x_refs) > 1:
            x = jnp.concatenate([x_ref[...] for x_ref in x_refs], axis=0)
        else:
            x = x_refs[0][pl.ds(c * chunk, chunk)].reshape(chunk * tokens, width)
        return total + jnp.dot(
            jnp.concatenate(columns, axis=1), x, preferred_element_type=jnp.float32
        )

    return repeat(devices // chunk, step, jnp.zeros((count * rank, width), jnp.float32))


def by_group(x_refs, groups, use):
    if len(x_refs) == 1:
        use(x_refs)
        return
    local = len(x_refs) // groups
    for g in range(groups):

        @pl.when(pl.program_id(0) == g)
        def _(g=g):
            use(x_refs[g * local : (g + 1) * local])


def send_kernel(groups, number, slots_line, count, rank, away, place_ref, packed_ref, *refs):
    line = place_ref[1]
    x_refs, got, outs = refs[:number], refs[number:-2], refs[-2:]
    ways = ((line + away < line_length, line + away), (line >= away, line - away))
    for way, (inside, target) in enumerate(ways):

        def use(x_refs, way=way, target=target):
            first = target * slots_line + pl.program_id(1) * count
            total = slot_sums(packed_ref, x_refs, place_ref[2], rank, first, count)
            if got:
                total += got[way][0].astype(jnp.float32)
            outs[way][0] = total.astype(jnp.bfloat16)

        @pl.when(inside)
        def _(use=use):
            by_group(x_refs, groups, use)


def own_kernel(groups, number, slots_line, count, rank, place_ref, packed_ref, *refs):
    x_refs, (right_ref, left_ref, out_ref) = refs[:number], refs[number:]

    def use(x_refs):
        first = place_ref[1] * slots_line + pl.program_id(1) * count
        total = slot_sums(packed_ref, x_refs, place_ref[2], rank, first, count)
        total += right_ref[0].astype(jnp.float32) + left_ref[0].astype(jnp.float32)
        out_ref[0] = (adapter_scale * total).astype(jnp.bfloat16)

    by_group(x_refs, groups, use)


def grad_a_step(place, packed, x_cols, half, got, away, groups, slots_line, rank):
    devices, depth, tokens = packed.shape
    width = x_cols[0].shape[-1] // 2
    local = devices // groups
    count = 8
    rows = count * rank
    number = len(x_cols)
    if number > 1:
        x_specs = [pl.BlockSpec((tokens, width), lambda g, s, place: (0, half))] * number
    else:
        if width % 128:
            x_cols, half = [x_cols[0][:, :, half * width : (half + 1) * width]], 0
        x_specs = [pl.BlockSpec((local, tokens, width), lambda g, s, place: (g, 0, half))]
    block = pl.BlockSpec((1, rows, width), lambda g, s, place: (g, s, 0))
    final = pl.BlockSpec((1, rows, width), lambda g, s, place: (g ^ place[0], s, 0))
    shape = jax.ShapeDtypeStruct((groups, slots_line * rank, width), jnp.bfloat16)
    ways = 1 if away == 0 else 2
    if away == 0:
        kernel = lambda *refs: own_kernel(groups, number, slots_line, count, rank, *refs)
    else:
        kernel = lambda *refs: send_kernel(groups, number, slots_line, count, rank, away, *refs)
    return call(
        kernel,
        place,
        (groups, slots_line // count),
        [pl.BlockSpec((local, depth, tokens), lambda g, s, place: (g ^ place[0], 0, 0))]
        + x_specs
        + [block] * len(got),
        final if away == 0 else [block, block],
        shape if away == 0 else [shape, shape],
        ways * 2 * devices * tokens * width * slots_line * rank,
        2 * devices * tokens * width + 2 * groups * slots_line * rank * width * (ways + len(got)),
        "grad_a_step" + str(away),
        (packed, *x_cols, *got),
    )


def in_line(slots, place_ref, total):
    slots -= place_ref[1] * (total // line_length)
    return jnp.where(slots < 0, slots + total, slots)


def put_together(pieces, a_ref):
    @pl.when(pl.program_id(0) == 0)
    def _():
        rows = pieces[0].shape[0]
        a_ref[:rows] = pieces[0][...]
        for k in range(1, line_length):
            left, right = pieces[line_length - k], pieces[line_length - 1 + k]
            a_ref[k * rows : (k + 1) * rows] = left[...] + right[...]


def low_kernel(chunk, rank, number, place_ref, packed_ref, *refs):
    x_refs, pieces, (low_ref, a_ref) = refs[:number], refs[number:-2], refs[-2:]
    put_together(pieces, a_ref)
    slots = packed_ref[0].astype(jnp.float32).T[:, rank + 1 : rank + 2].astype(jnp.int32)
    slots = in_line(slots, place_ref, a_ref.shape[0] // rank)
    tile = slots.shape[0]
    lane_slot = lax.broadcasted_iota(jnp.int32, (tile, chunk), 1) // rank

    def use(x):
        def step(c, low):
            part = pl.ds(pl.multiple_of(c * chunk, chunk), chunk)
            hidden = lax.dot_general(x, a_ref[part], NT, preferred_element_type=jnp.float32)
            hidden = jnp.where(lane_slot + c * (chunk // rank) == slots, hidden, 0.0)
            for k in range(chunk // (2 * rank)):
                low += hidden[:, k * 2 * rank : (k + 1) * 2 * rank]
            return low

        start = jnp.zeros((tile, 2 * rank), jnp.float32)
        low = repeat(a_ref.shape[0] // chunk, step, start).T
        low_ref[0] = low[:rank] + low[rank:]

    if number == 1:
        use(x_refs[0][0])
    else:
        for m in range(number):

            @pl.when(pl.program_id(0) == m)
            def _(m=m):
                use(x_refs[m][...])


def low_part(place, packed, x_cols, a_pieces, inner, rank):
    devices, depth, tokens = packed.shape
    width = x_cols[0].shape[-1]
    rows = a_pieces[0].shape[0]
    slots = line_length * rows
    number = len(x_cols)
    mate = lambda t, place: (t ^ (place[0] * inner + place[2]), 0, 0)
    if number > 1:
        x_specs = [pl.BlockSpec((tokens, width), lambda t, place: (0, 0))] * number
    else:
        x_specs = [pl.BlockSpec((1, tokens, width), lambda t, place: (t, 0, 0))]
    return call(
        lambda *refs: low_kernel(512, rank, number, *refs),
        place,
        (devices,),
        [pl.BlockSpec((1, depth, tokens), mate)]
        + x_specs
        + [pl.BlockSpec((rows, width), lambda t, place: (0, 0))] * len(a_pieces),
        pl.BlockSpec((1, rank, tokens), mate),
        jax.ShapeDtypeStruct((devices, rank, tokens), jnp.float32),
        2 * devices * tokens * width * slots,
        2 * (devices * tokens + slots) * width,
        "low_part",
        (packed, *x_cols, *a_pieces),
        [pltpu.VMEM((slots, width), jnp.bfloat16)],
    )


def out_kernel(chunk, rank, groups, place_ref, packed_ref, g_ref, *refs):
    number = 2 * line_length - 1
    a_pieces, w_pieces, (out_ref, a_ref, w_ref) = refs[:number], refs[number:-3], refs[-3:]
    put_together(a_pieces, a_ref)
    put_together(w_pieces, w_ref)
    rows = jnp.concatenate([p.astype(jnp.float32).T for p in packed_ref[...]], axis=0)
    back, slots = rows[:, :rank], rows[:, rank + 1 : rank + 2].astype(jnp.int32)
    total = a_ref.shape[0]
    slots = in_line(slots, place_ref, total // rank)
    tile = back.shape[0]
    repeated = jnp.concatenate([back] * (chunk // rank), axis=1)
    lane_slot = lax.broadcasted_iota(jnp.int32, (tile, chunk), 1) // rank

    def masked(c):
        keep = lane_slot + c * (chunk // rank) == slots
        return jnp.where(keep, repeated, 0.0).astype(jnp.bfloat16)

    if total // chunk <= 4:
        wide = jnp.concatenate([masked(c) for c in range(total // chunk)], axis=1)
        acc = jnp.dot(wide, a_ref[...], preferred_element_type=jnp.float32)
    else:

        def step(c, acc):
            block = a_ref[pl.ds(pl.multiple_of(c * chunk, chunk), chunk), :]
            return acc + jnp.dot(masked(c), block, preferred_element_type=jnp.float32)

        acc = repeat(total // chunk, step, jnp.zeros((tile, a_ref.shape[1]), jnp.float32))
    base = []
    count = w_pieces[0].shape[0]
    halves = line_length // groups
    for c in range(halves):
        at = (place_ref[0] * halves + c - place_ref[1] + line_length) % line_length
        w = w_ref[pl.ds(pl.multiple_of(at * count, count), count), :]
        base.append(lax.dot_general(g_ref[...], w, NT, preferred_element_type=jnp.float32))
    out = jnp.concatenate(base, axis=1) + adapter_scale * acc
    out_ref[...] = out.astype(out_ref.dtype).reshape(out_ref.shape)


def out_part(place, packed, g_all, w_pieces, a_pieces, groups, rank):
    devices, depth, tokens = packed.shape
    outs = g_all.shape[1]
    rows, width = a_pieces[0].shape
    slots = line_length * rows
    both = 2
    pieces = [*a_pieces, *w_pieces]
    return call(
        lambda *refs: out_kernel(512, rank, groups, *refs),
        place,
        (devices // both,),
        [
            pl.BlockSpec((both, depth, tokens), lambda t, place: (t, 0, 0)),
            pl.BlockSpec((both * tokens, outs), lambda t, place: (t, 0)),
        ]
        + [pl.BlockSpec(piece.shape, lambda t, place: (0, 0)) for piece in pieces],
        pl.BlockSpec((both, tokens, width), lambda t, place: (t, 0, 0)),
        jax.ShapeDtypeStruct((devices, tokens, width), jnp.bfloat16),
        2 * devices * tokens * width * (slots + outs),
        2 * devices * tokens * (width + outs) + 2 * slots * width,
        "out_part",
        (packed, g_all, *pieces),
        [
            pltpu.VMEM((slots, width), jnp.bfloat16),
            pltpu.VMEM((line_length * w_pieces[0].shape[0], outs), jnp.bfloat16),
        ],
    )


def body(x, g, tok, adapter_slot, w, a, b):
    groups, inner = lax.axis_size("groups"), lax.axis_size("inner")
    gi, li, ji = lax.axis_index("groups"), lax.axis_index("line"), lax.axis_index("inner")
    place = jnp.stack([gi, li, ji]).astype(jnp.int32)
    size = groups * inner
    devices = line_length * inner
    tokens, model = x.shape
    outs = g.shape[1]
    resident, _, rank = a.shape
    share = resident // groups
    count = inner * resident
    halves = line_length // groups
    width = model // size
    part = width // halves
    adapters = adapter_slot.shape[0]
    capacity = max(2, 2 * tokens // adapters)

    up = [(i, i + 1) for i in range(line_length - 1)]
    down = [(i + 1, i) for i in range(line_length - 1)]

    def hop(pieces, away):
        left, right = pieces
        return [
            lax.ppermute(left, "line", up[away - 1 :]),
            lax.ppermute(right, "line", down[: line_length - away]),
        ]

    w_hops = [hop((w, w), 1)]
    w_hops.append(hop(w_hops[0], 2))

    a_mine = split_columns(place, jnp.swapaxes(a, 1, 2), groups, halves, inner, part)
    a_own = lax.all_to_all(a_mine, plane, 0, 0, tiled=True).reshape(count * rank, width)

    def meet(m):
        return lax.ppermute(x_sends[m], plane, [(i, i ^ m) for i in range(size)])

    direct = size == 8 and part % 128 == 0
    x_cols = {}
    if direct:
        x_sends = split_pieces(place, x, groups, halves, inner, part)
        x_cols = {0: x_sends[0], 1: meet(1), 2: meet(2), 4: meet(4)}
    else:
        x_far = split_columns(place, x[None], groups, halves, inner, part)
        x_far = lax.all_to_all(x_far, plane, 0, 0, tiled=True)
        x_cols = {0: x_far[jnp.arange(size) ^ (gi * inner + ji)]}

    matches = tok == lax.broadcasted_iota(jnp.int32, (tokens, adapters), 1)
    slot = jnp.sum(jnp.where(matches, adapter_slot[None, :], 0), axis=1)
    running = jnp.cumsum(matches.astype(jnp.int32), axis=0)
    within = jnp.sum(jnp.where(matches, running - 1, 0), axis=1)
    position = slot * capacity + within
    at = lax.broadcasted_iota(jnp.int32, (adapters * capacity, tokens), 0) == position[None, :]
    at = at.astype(jnp.bfloat16)

    def route(rows):
        rows = rows.reshape(devices, resident * capacity, rows.shape[1])
        rows = lax.all_to_all(rows, row, 0, 0, tiled=True)
        return rows.reshape(devices, resident, capacity, rows.shape[2])

    g_send = jnp.dot(at, g, preferred_element_type=jnp.float32).astype(jnp.bfloat16)
    g_send, a_own, x_cols, w_hops = lax.optimization_barrier((g_send, a_own, x_cols, w_hops))
    w_hops.append(hop(w_hops[1], 3))
    g_rows = route(g_send)
    back = jnp.einsum("hjct,jrt->hjcr", g_rows, b, preferred_element_type=jnp.float32)
    back = back.astype(jnp.bfloat16).reshape(devices, resident * capacity, rank)
    hops = [hop((a_own, a_own), 1)]
    if direct:
        x_cols.update({3: meet(3), 5: meet(5)})
    back, x_cols = lax.optimization_barrier((back, x_cols))
    if direct:
        x_cols.update({6: meet(6), 7: meet(7)})
    back = lax.all_to_all(back, row, 0, 0, tiled=True).reshape(adapters * capacity, rank)
    back = lax.dot_general(
        back, at, (((0,), (0,)), ((), ())), preferred_element_type=jnp.float32
    ).astype(jnp.bfloat16)
    owner, res = slot // resident, slot % resident
    slot_a = (owner // inner) * count + ((res // share) * inner + owner % inner) * share + res % share
    names = jnp.stack([slot, slot_a] + [slot] * 14).astype(jnp.bfloat16)
    packed = jnp.concatenate([back, names], axis=0)
    packed, x_cols, hops, w_hops = lax.optimization_barrier((packed, x_cols, hops, w_hops))
    packed = jnp.broadcast_to(packed[None], (size,) + packed.shape)
    packed = lax.all_to_all(packed, plane, 0, 0, tiled=True)
    x_cols = [x_cols[m] for m in range(len(x_cols))]
    g_own, x_cols = lax.optimization_barrier((g, x_cols))
    g_all = lax.all_gather(g_own, plane, axis=0, tiled=True)

    hops.append(hop(hops[0], 2))

    def send(c, got, away):
        sums = grad_a_step(place, packed, x_cols, c, got, away, groups, count, rank)
        ahead = [(i, i + 1) for i in range(line_length - away)]
        behind = [(i, i - 1) for i in range(away, line_length)]
        moved = (lax.ppermute(sums[0], "line", ahead), lax.ppermute(sums[1], "line", behind))
        return moved, sums[0]

    def own(c, got):
        p = grad_a_step(place, packed, x_cols, c, got, 0, groups, count, rank)
        return p.reshape(size, resident * rank, part)

    first, done = send(0, (), 3)
    packed, done = lax.optimization_barrier((packed, done))
    second, done = send(1, (), 3)

    first, hops[1], done = lax.optimization_barrier((first, hops[1], done))
    hops.append(hop(hops[1], 3))
    first, done = send(0, first, 2)
    second, done = lax.optimization_barrier((second, done))
    second, done = send(1, second, 2)

    a_pieces = [a_own] + [h[0] for h in hops] + [h[1] for h in hops]
    w_pieces = [w] + [h[0] for h in w_hops] + [h[1] for h in w_hops]
    a_pieces, done = lax.optimization_barrier((a_pieces, done))
    out_cols = out_part(place, packed, g_all, w_pieces, a_pieces, groups, rank)
    first, out_cols = lax.optimization_barrier((first, out_cols))
    first, done = send(0, first, 1)
    out_back = lax.all_to_all(out_cols, plane, 0, 0, tiled=True)

    a_pieces, done = lax.optimization_barrier((a_pieces, done))
    low = low_part(place, packed, x_cols, a_pieces, inner, rank)
    second, low = lax.optimization_barrier((second, low))
    second, done = send(1, second, 1)
    first, done = lax.optimization_barrier((first, done))
    p_back = [own(0, first)]
    low, out_back = lax.optimization_barrier((low, out_back))
    low = lax.all_to_all(low, plane, 0, 0, tiled=True)
    low, p_back[0] = lax.optimization_barrier((low, p_back[0]))
    p_back[0] = lax.all_to_all(p_back[0], plane, 0, 0, tiled=True)
    low = jnp.sum(low, axis=0).astype(jnp.bfloat16)
    low = lax.dot_general(at, low, NT, preferred_element_type=jnp.float32).astype(jnp.bfloat16)
    low, p_back[0] = lax.optimization_barrier((low, p_back[0]))
    low = route(low)
    p_second, low = lax.optimization_barrier((own(1, second), low))
    p_back.append(lax.all_to_all(p_second, plane, 0, 0, tiled=True))

    grad_b = jnp.einsum("hjcr,hjco->jro", low, g_rows, preferred_element_type=jnp.float32)
    grad_b = (adapter_scale * grad_b).astype(jnp.bfloat16)
    input_gradient = join_rows(place, out_back, groups, halves, inner, part)
    grad_a = join_slots(place, p_back, resident, groups, inner).swapaxes(1, 2)
    return input_gradient, grad_a, grad_b


def solution(mesh):
    groups, rows = mesh.shape["groups"], mesh.shape["row"]
    whole = ("groups", "line", "inner")
    split = Mesh(mesh.devices.reshape(groups, line_length, rows // line_length), whole)
    return jax.shard_map(
        body,
        mesh=split,
        in_specs=(
            P(whole, None),
            P(whole, None),
            P(whole, None),
            P(),
            P(row, None),
            P(row, None, None),
            P(row, None, None),
        ),
        out_specs=(P(whole, None), P(whole, None, None), P(whole, None, None)),
        check_vma=False,
    )
```

```python
import jax
import jax.numpy as jnp
from jax import lax
from jax.experimental import pallas as pl
from jax.experimental.pallas import tpu as pltpu
from jax.sharding import Mesh, PartitionSpec as P

adapter_scale = 2.0
line_length = 4
plane = ("groups", "inner")
row = ("line", "inner")
vmem_limit = 56 * 1024 * 1024
NT = (((1,), (1,)), ((), ()))


def call(kernel, place, grid, in_specs, out_specs, out_shape, flops, moved, name, args, scratch=()):
    return pl.pallas_call(
        kernel,
        grid_spec=pltpu.PrefetchScalarGridSpec(
            num_scalar_prefetch=1,
            grid=grid,
            in_specs=in_specs,
            out_specs=out_specs,
            scratch_shapes=scratch,
        ),
        out_shape=out_shape,
        compiler_params=pltpu.CompilerParams(vmem_limit_bytes=vmem_limit),
        cost_estimate=pl.CostEstimate(flops=flops, bytes_accessed=moved, transcendentals=0),
        name=name,
    )(place, *args)


def repeat(count, step, start):
    if count <= 4:
        for i in range(count):
            start = step(i, start)
        return start
    return lax.fori_loop(0, count, step, start)


def move(name, sources, in_blocks, in_maps, outs, out_blocks, out_maps, grid, kernel, place):
    moved = 0
    for shape in outs:
        size = 4
        for n in shape:
            size *= n
        moved += size
    return call(
        kernel,
        place,
        grid,
        [pl.BlockSpec(block, index) for block, index in zip(in_blocks, in_maps)],
        [pl.BlockSpec(block, index) for block, index in zip(out_blocks, out_maps)],
        [jax.ShapeDtypeStruct(shape, jnp.bfloat16) for shape in outs],
        0,
        moved,
        name,
        sources,
    )


def columns_of(q, c, halves, inner):
    return ((q // inner) * halves + c) * inner + q % inner


def split_columns(place, rows, groups, halves, inner, width):
    slots, rank, model = rows.shape
    size, share = groups * inner, max(1, slots // groups)
    group = lambda place: place[0] if slots >= groups else 0
    if width % 128:
        mine = lax.dynamic_slice_in_dim(rows, group(place) * share, share, 0)
        mine = mine.reshape(share * rank, groups, halves, inner, width)
        return mine.transpose(1, 3, 0, 2, 4).reshape(size, share * rank, halves * width)

    def kernel(place_ref, rows_ref, out_ref):
        for q in range(size):
            for c in range(halves):
                first = columns_of(q, c, halves, inner) * width
                out_ref[q, :, c * width : (c + 1) * width] = rows_ref[0, :, first : first + width]

    tile = min(rank, 64)
    steps = rank // tile
    return move(
        "split_columns", [rows], [(1, tile, model)],
        [lambda s, r, place: (group(place) * share + s, r, 0)],
        [(size, share * rank, halves * width)], [(size, tile, halves * width)],
        [lambda s, r, place: (0, s * steps + r, 0)], (share, steps), kernel, place,
    )[0]


def split_pieces(place, rows, groups, halves, inner, width):
    count, model = rows.shape
    size = groups * inner
    tile = min(count, 64)

    def kernel(place_ref, rows_ref, *out_refs):
        me = place_ref[0] * inner + place_ref[2]
        for m in range(size):
            for c in range(halves):
                first = pl.multiple_of(columns_of(me ^ m, c, halves, inner) * width, width)
                out_refs[m][:, c * width : (c + 1) * width] = rows_ref[:, pl.ds(first, width)]

    return move(
        "split_pieces", [rows], [(tile, model)], [lambda t, place: (t, 0)],
        [(count, halves * width)] * size, [(tile, halves * width)] * size,
        [lambda t, place: (t, 0)] * size, (count // tile,), kernel, place,
    )


def join_slots(place, parts, resident, groups, inner):
    size, rows, width = parts[0].shape
    halves, rank = len(parts), rows // resident
    if width % 128:
        parts = [p.reshape(groups, inner, rows, width) for p in parts]
        joined = jnp.stack(parts, axis=1).transpose(3, 0, 1, 2, 4)
        return joined.reshape(resident, rank, -1)

    def kernel(place_ref, *refs):
        for q in range(size):
            for c in range(halves):
                first = columns_of(q, c, halves, inner) * width
                refs[-1][0, :, first : first + width] = refs[c][q]

    return move(
        "join_slots", parts, [(size, rank, width)] * halves, [lambda r, place: (0, r, 0)] * halves,
        [(resident, rank, size * halves * width)], [(1, rank, size * halves * width)],
        [lambda r, place: (r, 0, 0)], (resident,), kernel, place,
    )[0]


def join_rows(place, rows, groups, halves, inner, part):
    size, tokens = rows.shape[:2]
    if part % 128:
        rows = rows.reshape(groups, inner, tokens, halves, part)
        return rows.transpose(2, 0, 3, 1, 4).reshape(tokens, -1)
    tile = min(tokens, 64)
    model = size * halves * part

    def kernel(place_ref, rows_ref, out_ref):
        for q in range(size):
            for c in range(halves):
                first = columns_of(q, c, halves, inner) * part
                out_ref[:, first : first + part] = rows_ref[q, :, c * part : (c + 1) * part]

    return move(
        "join_rows", [rows], [(size, tile, halves * part)], [lambda t, place: (0, t, 0)],
        [(tokens, model)], [(tile, model)], [lambda t, place: (t, 0)], (tokens // tile,),
        kernel, place,
    )[0]


def slot_sums(packed_ref, x_refs, me, rank, first, count):
    devices, _, tokens = packed_ref.shape
    width = x_refs[0].shape[-1]
    chunk = min(devices, 4)

    def step(c, total):
        columns = []
        for d in range(chunk):
            device = (c * chunk + d) ^ me
            back = packed_ref[device, :rank, :]
            slots = packed_ref[device, rank : rank + 1, :].astype(jnp.float32)
            rows = [
                back * (slots == (first + i).astype(jnp.float32)).astype(jnp.bfloat16)
                for i in range(count)
            ]
            columns.append(jnp.concatenate(rows, axis=0))
        if len(x_refs) > 1:
            x = jnp.concatenate([x_ref[...] for x_ref in x_refs], axis=0)
        else:
            x = x_refs[0][pl.ds(c * chunk, chunk)].reshape(chunk * tokens, width)
        return total + jnp.dot(
            jnp.concatenate(columns, axis=1), x, preferred_element_type=jnp.float32
        )

    return repeat(devices // chunk, step, jnp.zeros((count * rank, width), jnp.float32))


def by_group(x_refs, groups, use):
    if len(x_refs) == 1:
        use(x_refs)
        return
    local = len(x_refs) // groups
    for g in range(groups):

        @pl.when(pl.program_id(0) == g)
        def _(g=g):
            use(x_refs[g * local : (g + 1) * local])


def send_kernel(groups, number, slots_line, count, rank, away, place_ref, packed_ref, *refs):
    line = place_ref[1]
    x_refs, got, outs = refs[:number], refs[number:-2], refs[-2:]
    ways = ((line + away < line_length, line + away), (line >= away, line - away))
    for way, (inside, target) in enumerate(ways):

        def use(x_refs, way=way, target=target):
            first = target * slots_line + pl.program_id(1) * count
            total = slot_sums(packed_ref, x_refs, place_ref[2], rank, first, count)
            if got:
                total += got[way][0].astype(jnp.float32)
            outs[way][0] = total.astype(jnp.bfloat16)

        @pl.when(inside)
        def _(use=use):
            by_group(x_refs, groups, use)


def own_kernel(groups, number, slots_line, count, rank, place_ref, packed_ref, *refs):
    x_refs, (right_ref, left_ref, out_ref) = refs[:number], refs[number:]

    def use(x_refs):
        first = place_ref[1] * slots_line + pl.program_id(1) * count
        total = slot_sums(packed_ref, x_refs, place_ref[2], rank, first, count)
        total += right_ref[0].astype(jnp.float32) + left_ref[0].astype(jnp.float32)
        out_ref[0] = (adapter_scale * total).astype(jnp.bfloat16)

    by_group(x_refs, groups, use)


def grad_a_step(place, packed, x_cols, half, got, away, groups, slots_line, rank):
    devices, depth, tokens = packed.shape
    width = x_cols[0].shape[-1] // 2
    local = devices // groups
    count = 8
    rows = count * rank
    number = len(x_cols)
    if number > 1:
        x_specs = [pl.BlockSpec((tokens, width), lambda g, s, place: (0, half))] * number
    else:
        if width % 128:
            x_cols, half = [x_cols[0][:, :, half * width : (half + 1) * width]], 0
        x_specs = [pl.BlockSpec((local, tokens, width), lambda g, s, place: (g, 0, half))]
    block = pl.BlockSpec((1, rows, width), lambda g, s, place: (g, s, 0))
    final = pl.BlockSpec((1, rows, width), lambda g, s, place: (g ^ place[0], s, 0))
    shape = jax.ShapeDtypeStruct((groups, slots_line * rank, width), jnp.bfloat16)
    ways = 1 if away == 0 else 2
    if away == 0:
        kernel = lambda *refs: own_kernel(groups, number, slots_line, count, rank, *refs)
    else:
        kernel = lambda *refs: send_kernel(groups, number, slots_line, count, rank, away, *refs)
    return call(
        kernel,
        place,
        (groups, slots_line // count),
        [pl.BlockSpec((local, depth, tokens), lambda g, s, place: (g ^ place[0], 0, 0))]
        + x_specs
        + [block] * len(got),
        final if away == 0 else [block, block],
        shape if away == 0 else [shape, shape],
        ways * 2 * devices * tokens * width * slots_line * rank,
        2 * devices * tokens * width + 2 * groups * slots_line * rank * width * (ways + len(got)),
        "grad_a_step" + str(away),
        (packed, *x_cols, *got),
    )


def in_line(slots, place_ref, total):
    slots -= place_ref[1] * (total // line_length)
    return jnp.where(slots < 0, slots + total, slots)


def put_together(pieces, a_ref):
    @pl.when(pl.program_id(0) == 0)
    def _():
        rows = pieces[0].shape[0]
        a_ref[:rows] = pieces[0][...]
        for k in range(1, line_length):
            left, right = pieces[line_length - k], pieces[line_length - 1 + k]
            a_ref[k * rows : (k + 1) * rows] = left[...] + right[...]


def low_kernel(chunk, rank, number, place_ref, packed_ref, *refs):
    x_refs, pieces, (low_ref, a_ref) = refs[:number], refs[number:-2], refs[-2:]
    put_together(pieces, a_ref)
    slots = packed_ref[0].astype(jnp.float32).T[:, rank + 1 : rank + 2].astype(jnp.int32)
    slots = in_line(slots, place_ref, a_ref.shape[0] // rank)
    tile = slots.shape[0]
    lane_slot = lax.broadcasted_iota(jnp.int32, (tile, chunk), 1) // rank

    def use(x):
        def step(c, low):
            part = pl.ds(pl.multiple_of(c * chunk, chunk), chunk)
            hidden = lax.dot_general(x, a_ref[part], NT, preferred_element_type=jnp.float32)
            hidden = jnp.where(lane_slot + c * (chunk // rank) == slots, hidden, 0.0)
            for k in range(chunk // (2 * rank)):
                low += hidden[:, k * 2 * rank : (k + 1) * 2 * rank]
            return low

        start = jnp.zeros((tile, 2 * rank), jnp.float32)
        low = repeat(a_ref.shape[0] // chunk, step, start).T
        low_ref[0] = low[:rank] + low[rank:]

    if number == 1:
        use(x_refs[0][0])
    else:
        for m in range(number):

            @pl.when(pl.program_id(0) == m)
            def _(m=m):
                use(x_refs[m][...])


def low_part(place, packed, x_cols, a_pieces, inner, rank):
    devices, depth, tokens = packed.shape
    width = x_cols[0].shape[-1]
    rows = a_pieces[0].shape[0]
    slots = line_length * rows
    number = len(x_cols)
    mate = lambda t, place: (t ^ (place[0] * inner + place[2]), 0, 0)
    if number > 1:
        x_specs = [pl.BlockSpec((tokens, width), lambda t, place: (0, 0))] * number
    else:
        x_specs = [pl.BlockSpec((1, tokens, width), lambda t, place: (t, 0, 0))]
    return call(
        lambda *refs: low_kernel(512, rank, number, *refs),
        place,
        (devices,),
        [pl.BlockSpec((1, depth, tokens), mate)]
        + x_specs
        + [pl.BlockSpec((rows, width), lambda t, place: (0, 0))] * len(a_pieces),
        pl.BlockSpec((1, rank, tokens), mate),
        jax.ShapeDtypeStruct((devices, rank, tokens), jnp.float32),
        2 * devices * tokens * width * slots,
        2 * (devices * tokens + slots) * width,
        "low_part",
        (packed, *x_cols, *a_pieces),
        [pltpu.VMEM((slots, width), jnp.bfloat16)],
    )


def out_kernel(chunk, rank, groups, place_ref, packed_ref, g_ref, *refs):
    number = 2 * line_length - 1
    a_pieces, w_pieces, (out_ref, a_ref, w_ref) = refs[:number], refs[number:-3], refs[-3:]
    put_together(a_pieces, a_ref)
    put_together(w_pieces, w_ref)
    rows = jnp.concatenate([p.astype(jnp.float32).T for p in packed_ref[...]], axis=0)
    back, slots = rows[:, :rank], rows[:, rank + 1 : rank + 2].astype(jnp.int32)
    total = a_ref.shape[0]
    slots = in_line(slots, place_ref, total // rank)
    tile = back.shape[0]
    repeated = jnp.concatenate([back] * (chunk // rank), axis=1)
    lane_slot = lax.broadcasted_iota(jnp.int32, (tile, chunk), 1) // rank

    def masked(c):
        keep = lane_slot + c * (chunk // rank) == slots
        return jnp.where(keep, repeated, 0.0).astype(jnp.bfloat16)

    if total // chunk <= 4:
        wide = jnp.concatenate([masked(c) for c in range(total // chunk)], axis=1)
        acc = jnp.dot(wide, a_ref[...], preferred_element_type=jnp.float32)
    else:

        def step(c, acc):
            block = a_ref[pl.ds(pl.multiple_of(c * chunk, chunk), chunk), :]
            return acc + jnp.dot(masked(c), block, preferred_element_type=jnp.float32)

        acc = repeat(total // chunk, step, jnp.zeros((tile, a_ref.shape[1]), jnp.float32))
    base = []
    count = w_pieces[0].shape[0]
    halves = line_length // groups
    for c in range(halves):
        at = (place_ref[0] * halves + c - place_ref[1] + line_length) % line_length
        w = w_ref[pl.ds(pl.multiple_of(at * count, count), count), :]
        base.append(lax.dot_general(g_ref[...], w, NT, preferred_element_type=jnp.float32))
    out = jnp.concatenate(base, axis=1) + adapter_scale * acc
    out_ref[...] = out.astype(out_ref.dtype).reshape(out_ref.shape)


def out_part(place, packed, g_all, w_pieces, a_pieces, groups, rank):
    devices, depth, tokens = packed.shape
    outs = g_all.shape[1]
    rows, width = a_pieces[0].shape
    slots = line_length * rows
    both = 2
    pieces = [*a_pieces, *w_pieces]
    return call(
        lambda *refs: out_kernel(512, rank, groups, *refs),
        place,
        (devices // both,),
        [
            pl.BlockSpec((both, depth, tokens), lambda t, place: (t, 0, 0)),
            pl.BlockSpec((both * tokens, outs), lambda t, place: (t, 0)),
        ]
        + [pl.BlockSpec(piece.shape, lambda t, place: (0, 0)) for piece in pieces],
        pl.BlockSpec((both, tokens, width), lambda t, place: (t, 0, 0)),
        jax.ShapeDtypeStruct((devices, tokens, width), jnp.bfloat16),
        2 * devices * tokens * width * (slots + outs),
        2 * devices * tokens * (width + outs) + 2 * slots * width,
        "out_part",
        (packed, g_all, *pieces),
        [
            pltpu.VMEM((slots, width), jnp.bfloat16),
            pltpu.VMEM((line_length * w_pieces[0].shape[0], outs), jnp.bfloat16),
        ],
    )


def body(x, g, tok, adapter_slot, w, a, b):
    groups, inner = lax.axis_size("groups"), lax.axis_size("inner")
    gi, li, ji = lax.axis_index("groups"), lax.axis_index("line"), lax.axis_index("inner")
    place = jnp.stack([gi, li, ji]).astype(jnp.int32)
    size = groups * inner
    devices = line_length * inner
    tokens, model = x.shape
    outs = g.shape[1]
    resident, _, rank = a.shape
    share = resident // groups
    count = inner * resident
    halves = line_length // groups
    width = model // size
    part = width // halves
    adapters = adapter_slot.shape[0]
    capacity = max(2, 2 * tokens // adapters)

    up = [(i, i + 1) for i in range(line_length - 1)]
    down = [(i + 1, i) for i in range(line_length - 1)]

    def hop(pieces, away):
        left, right = pieces
        return [
            lax.ppermute(left, "line", up[away - 1 :]),
            lax.ppermute(right, "line", down[: line_length - away]),
        ]

    w_hops = [hop((w, w), 1)]

    a_mine = split_columns(place, jnp.swapaxes(a, 1, 2), groups, halves, inner, part)
    a_own = lax.all_to_all(a_mine, plane, 0, 0, tiled=True).reshape(count * rank, width)

    def meet(m):
        return lax.ppermute(x_sends[m], plane, [(i, i ^ m) for i in range(size)])

    direct = size == 8 and part % 128 == 0
    x_cols = {}
    if direct:
        x_sends = split_pieces(place, x, groups, halves, inner, part)
        x_cols = {0: x_sends[0], 1: meet(1), 2: meet(2)}
    else:
        x_far = split_columns(place, x[None], groups, halves, inner, part)
        x_far = lax.all_to_all(x_far, plane, 0, 0, tiled=True)
        x_cols = {0: x_far[jnp.arange(size) ^ (gi * inner + ji)]}

    matches = tok == lax.broadcasted_iota(jnp.int32, (tokens, adapters), 1)
    slot = jnp.sum(jnp.where(matches, adapter_slot[None, :], 0), axis=1)
    running = jnp.cumsum(matches.astype(jnp.int32), axis=0)
    within = jnp.sum(jnp.where(matches, running - 1, 0), axis=1)
    position = slot * capacity + within
    at = lax.broadcasted_iota(jnp.int32, (adapters * capacity, tokens), 0) == position[None, :]
    at = at.astype(jnp.bfloat16)

    def route(rows):
        rows = rows.reshape(devices, resident * capacity, rows.shape[1])
        rows = lax.all_to_all(rows, row, 0, 0, tiled=True)
        return rows.reshape(devices, resident, capacity, rows.shape[2])

    g_send = jnp.dot(at, g, preferred_element_type=jnp.float32).astype(jnp.bfloat16)
    g_send, a_own, x_cols, w_hops = lax.optimization_barrier((g_send, a_own, x_cols, w_hops))
    w_hops.append(hop(w_hops[0], 2))
    g_rows = route(g_send)
    back = jnp.einsum("hjct,jrt->hjcr", g_rows, b, preferred_element_type=jnp.float32)
    back = back.astype(jnp.bfloat16).reshape(devices, resident * capacity, rank)
    hops = [hop((a_own, a_own), 1)]
    if direct:
        x_cols.update({4: meet(4), 3: meet(3)})
    back, x_cols, hops, w_hops = lax.optimization_barrier((back, x_cols, hops, w_hops))
    w_hops.append(hop(w_hops[1], 3))
    if direct:
        x_cols.update({5: meet(5), 6: meet(6), 7: meet(7)})
    back = lax.all_to_all(back, row, 0, 0, tiled=True).reshape(adapters * capacity, rank)
    back = lax.dot_general(
        back, at, (((0,), (0,)), ((), ())), preferred_element_type=jnp.float32
    ).astype(jnp.bfloat16)
    owner, res = slot // resident, slot % resident
    slot_a = (owner // inner) * count + ((res // share) * inner + owner % inner) * share + res % share
    names = jnp.stack([slot, slot_a] + [slot] * 14).astype(jnp.bfloat16)
    packed = jnp.concatenate([back, names], axis=0)
    packed, x_cols = lax.optimization_barrier((packed, x_cols))
    packed = jnp.broadcast_to(packed[None], (size,) + packed.shape)
    packed = lax.all_to_all(packed, plane, 0, 0, tiled=True)
    x_cols = [x_cols[m] for m in range(len(x_cols))]
    g_own, x_cols = lax.optimization_barrier((g, x_cols))
    g_all = lax.all_gather(g_own, plane, axis=0, tiled=True)

    hops.append(hop(hops[0], 2))

    def send(c, got, away):
        sums = grad_a_step(place, packed, x_cols, c, got, away, groups, count, rank)
        ahead = [(i, i + 1) for i in range(line_length - away)]
        behind = [(i, i - 1) for i in range(away, line_length)]
        moved = (lax.ppermute(sums[0], "line", ahead), lax.ppermute(sums[1], "line", behind))
        return moved, sums[0]

    def own(c, got):
        p = grad_a_step(place, packed, x_cols, c, got, 0, groups, count, rank)
        return p.reshape(size, resident * rank, part)

    first, done = send(0, (), 3)
    packed, done = lax.optimization_barrier((packed, done))
    second, done = send(1, (), 3)

    first, hops[1], done = lax.optimization_barrier((first, hops[1], done))
    hops.append(hop(hops[1], 3))
    first, done = send(0, first, 2)
    second, done = lax.optimization_barrier((second, done))
    second, done = send(1, second, 2)

    a_pieces = [a_own] + [h[0] for h in hops] + [h[1] for h in hops]
    w_pieces = [w] + [h[0] for h in w_hops] + [h[1] for h in w_hops]
    a_pieces, done = lax.optimization_barrier((a_pieces, done))
    out_cols = out_part(place, packed, g_all, w_pieces, a_pieces, groups, rank)
    first, out_cols = lax.optimization_barrier((first, out_cols))
    first, done = send(0, first, 1)
    out_back = lax.all_to_all(out_cols, plane, 0, 0, tiled=True)

    second, done = lax.optimization_barrier((second, done))
    second, done = send(1, second, 1)

    a_pieces, done = lax.optimization_barrier((a_pieces, done))
    low = low_part(place, packed, x_cols, a_pieces, inner, rank)
    low, out_back = lax.optimization_barrier((low, out_back))
    low = lax.all_to_all(low, plane, 0, 0, tiled=True)
    p_first, low = lax.optimization_barrier((own(0, first), low))
    p_back = [lax.all_to_all(p_first, plane, 0, 0, tiled=True)]
    p_second, p_back[0] = lax.optimization_barrier((own(1, second), p_back[0]))
    p_back.append(lax.all_to_all(p_second, plane, 0, 0, tiled=True))
    low = jnp.sum(low, axis=0).astype(jnp.bfloat16)
    low = lax.dot_general(at, low, NT, preferred_element_type=jnp.float32).astype(jnp.bfloat16)
    low, p_back = lax.optimization_barrier((low, p_back))
    low = route(low)

    grad_b = jnp.einsum("hjcr,hjco->jro", low, g_rows, preferred_element_type=jnp.float32)
    grad_b = (adapter_scale * grad_b).astype(jnp.bfloat16)
    input_gradient = join_rows(place, out_back, groups, halves, inner, part)
    grad_a = join_slots(place, p_back, resident, groups, inner).swapaxes(1, 2)
    return input_gradient, grad_a, grad_b


def solution(mesh):
    groups, rows = mesh.shape["groups"], mesh.shape["row"]
    whole = ("groups", "line", "inner")
    split = Mesh(mesh.devices.reshape(groups, line_length, rows // line_length), whole)
    return jax.shard_map(
        body,
        mesh=split,
        in_specs=(
            P(whole, None),
            P(whole, None),
            P(whole, None),
            P(),
            P(row, None),
            P(row, None, None),
            P(row, None, None),
        ),
        out_specs=(P(whole, None), P(whole, None, None), P(whole, None, None)),
        check_vma=False,
    )
```

```python
import jax
import jax.numpy as jnp
from jax import lax
from jax.experimental import pallas as pl
from jax.experimental.pallas import tpu as pltpu
from jax.sharding import Mesh, PartitionSpec as P

adapter_scale = 2.0
line_length = 4
plane = ("groups", "inner")
row = ("line", "inner")
vmem_limit = 56 * 1024 * 1024
NT = (((1,), (1,)), ((), ()))


def call(kernel, place, grid, in_specs, out_specs, out_shape, flops, moved, name, args, scratch=()):
    return pl.pallas_call(
        kernel,
        grid_spec=pltpu.PrefetchScalarGridSpec(
            num_scalar_prefetch=1,
            grid=grid,
            in_specs=in_specs,
            out_specs=out_specs,
            scratch_shapes=scratch,
        ),
        out_shape=out_shape,
        compiler_params=pltpu.CompilerParams(vmem_limit_bytes=vmem_limit),
        cost_estimate=pl.CostEstimate(flops=1024, bytes_accessed=1024, transcendentals=0),
        name=name,
    )(place, *args)


def repeat(count, step, start):
    if count <= 4:
        for i in range(count):
            start = step(i, start)
        return start
    return lax.fori_loop(0, count, step, start)


def move(name, sources, in_blocks, in_maps, outs, out_blocks, out_maps, grid, kernel, place):
    moved = 0
    for shape in outs:
        size = 4
        for n in shape:
            size *= n
        moved += size
    return call(
        kernel,
        place,
        grid,
        [pl.BlockSpec(block, index) for block, index in zip(in_blocks, in_maps)],
        [pl.BlockSpec(block, index) for block, index in zip(out_blocks, out_maps)],
        [jax.ShapeDtypeStruct(shape, jnp.bfloat16) for shape in outs],
        0,
        moved,
        name,
        sources,
    )


def columns_of(q, c, halves, inner):
    return ((q // inner) * halves + c) * inner + q % inner


def split_columns(place, rows, groups, halves, inner, width):
    slots, rank, model = rows.shape
    size, share = groups * inner, max(1, slots // groups)
    group = lambda place: place[0] if slots >= groups else 0
    if width % 128:
        mine = lax.dynamic_slice_in_dim(rows, group(place) * share, share, 0)
        mine = mine.reshape(share * rank, groups, halves, inner, width)
        return mine.transpose(1, 3, 0, 2, 4).reshape(size, share * rank, halves * width)

    def kernel(place_ref, rows_ref, out_ref):
        for q in range(size):
            for c in range(halves):
                first = columns_of(q, c, halves, inner) * width
                out_ref[q, :, c * width : (c + 1) * width] = rows_ref[0, :, first : first + width]

    tile = min(rank, 64)
    steps = rank // tile
    return move(
        "split_columns", [rows], [(1, tile, model)],
        [lambda s, r, place: (group(place) * share + s, r, 0)],
        [(size, share * rank, halves * width)], [(size, tile, halves * width)],
        [lambda s, r, place: (0, s * steps + r, 0)], (share, steps), kernel, place,
    )[0]


def split_pieces(place, rows, groups, halves, inner, width):
    count, model = rows.shape
    size = groups * inner
    tile = min(count, 64)

    def kernel(place_ref, rows_ref, *out_refs):
        me = place_ref[0] * inner + place_ref[2]
        for m in range(size):
            for c in range(halves):
                first = pl.multiple_of(columns_of(me ^ m, c, halves, inner) * width, width)
                out_refs[m][:, c * width : (c + 1) * width] = rows_ref[:, pl.ds(first, width)]

    return move(
        "split_pieces", [rows], [(tile, model)], [lambda t, place: (t, 0)],
        [(count, halves * width)] * size, [(tile, halves * width)] * size,
        [lambda t, place: (t, 0)] * size, (count // tile,), kernel, place,
    )


def join_slots(place, parts, resident, groups, inner):
    size, rows, width = parts[0].shape
    halves, rank = len(parts), rows // resident
    if width % 128:
        parts = [p.reshape(groups, inner, rows, width) for p in parts]
        joined = jnp.stack(parts, axis=1).transpose(3, 0, 1, 2, 4)
        return joined.reshape(resident, rank, -1)

    def kernel(place_ref, *refs):
        for q in range(size):
            for c in range(halves):
                first = columns_of(q, c, halves, inner) * width
                refs[-1][0, :, first : first + width] = refs[c][q]

    return move(
        "join_slots", parts, [(size, rank, width)] * halves, [lambda r, place: (0, r, 0)] * halves,
        [(resident, rank, size * halves * width)], [(1, rank, size * halves * width)],
        [lambda r, place: (r, 0, 0)], (resident,), kernel, place,
    )[0]


def join_rows(place, rows, groups, halves, inner, part):
    size, tokens = rows.shape[:2]
    if part % 128:
        rows = rows.reshape(groups, inner, tokens, halves, part)
        return rows.transpose(2, 0, 3, 1, 4).reshape(tokens, -1)
    tile = min(tokens, 64)
    model = size * halves * part

    def kernel(place_ref, rows_ref, out_ref):
        for q in range(size):
            for c in range(halves):
                first = columns_of(q, c, halves, inner) * part
                out_ref[:, first : first + part] = rows_ref[q, :, c * part : (c + 1) * part]

    return move(
        "join_rows", [rows], [(size, tile, halves * part)], [lambda t, place: (0, t, 0)],
        [(tokens, model)], [(tile, model)], [lambda t, place: (t, 0)], (tokens // tile,),
        kernel, place,
    )[0]


def slot_sums(packed_ref, x_refs, me, rank, first, count):
    devices, _, tokens = packed_ref.shape
    width = x_refs[0].shape[-1]
    chunk = min(devices, 4)

    def step(c, total):
        columns = []
        for d in range(chunk):
            device = (c * chunk + d) ^ me
            back = packed_ref[device, :rank, :]
            slots = packed_ref[device, rank : rank + 1, :].astype(jnp.float32)
            rows = [
                back * (slots == (first + i).astype(jnp.float32)).astype(jnp.bfloat16)
                for i in range(count)
            ]
            columns.append(jnp.concatenate(rows, axis=0))
        if len(x_refs) > 1:
            x = jnp.concatenate([x_ref[...] for x_ref in x_refs], axis=0)
        else:
            x = x_refs[0][pl.ds(c * chunk, chunk)].reshape(chunk * tokens, width)
        return total + jnp.dot(
            jnp.concatenate(columns, axis=1), x, preferred_element_type=jnp.float32
        )

    return repeat(devices // chunk, step, jnp.zeros((count * rank, width), jnp.float32))


def by_group(x_refs, groups, use):
    if len(x_refs) == 1:
        use(x_refs)
        return
    local = len(x_refs) // groups
    for g in range(groups):

        @pl.when(pl.program_id(0) == g)
        def _(g=g):
            use(x_refs[g * local : (g + 1) * local])


def send_kernel(groups, number, slots_line, count, rank, away, place_ref, packed_ref, *refs):
    line = place_ref[1]
    x_refs, got, outs = refs[:number], refs[number:-2], refs[-2:]
    ways = ((line + away < line_length, line + away), (line >= away, line - away))
    for way, (inside, target) in enumerate(ways):

        def use(x_refs, way=way, target=target):
            first = target * slots_line + pl.program_id(1) * count
            total = slot_sums(packed_ref, x_refs, place_ref[2], rank, first, count)
            if got:
                total += got[way][0].astype(jnp.float32)
            outs[way][0] = total.astype(jnp.bfloat16)

        @pl.when(inside)
        def _(use=use):
            by_group(x_refs, groups, use)


def own_kernel(groups, number, slots_line, count, rank, place_ref, packed_ref, *refs):
    x_refs, (right_ref, left_ref, out_ref) = refs[:number], refs[number:]

    def use(x_refs):
        first = place_ref[1] * slots_line + pl.program_id(1) * count
        total = slot_sums(packed_ref, x_refs, place_ref[2], rank, first, count)
        total += right_ref[0].astype(jnp.float32) + left_ref[0].astype(jnp.float32)
        out_ref[0] = (adapter_scale * total).astype(jnp.bfloat16)

    by_group(x_refs, groups, use)


def grad_a_step(place, packed, x_cols, half, got, away, groups, slots_line, rank):
    devices, depth, tokens = packed.shape
    width = x_cols[0].shape[-1] // 2
    local = devices // groups
    count = 8
    rows = count * rank
    number = len(x_cols)
    if number > 1:
        x_specs = [pl.BlockSpec((tokens, width), lambda g, s, place: (0, half))] * number
    else:
        if width % 128:
            x_cols, half = [x_cols[0][:, :, half * width : (half + 1) * width]], 0
        x_specs = [pl.BlockSpec((local, tokens, width), lambda g, s, place: (g, 0, half))]
    block = pl.BlockSpec((1, rows, width), lambda g, s, place: (g, s, 0))
    final = pl.BlockSpec((1, rows, width), lambda g, s, place: (g ^ place[0], s, 0))
    shape = jax.ShapeDtypeStruct((groups, slots_line * rank, width), jnp.bfloat16)
    ways = 1 if away == 0 else 2
    if away == 0:
        kernel = lambda *refs: own_kernel(groups, number, slots_line, count, rank, *refs)
    else:
        kernel = lambda *refs: send_kernel(groups, number, slots_line, count, rank, away, *refs)
    return call(
        kernel,
        place,
        (groups, slots_line // count),
        [pl.BlockSpec((local, depth, tokens), lambda g, s, place: (g ^ place[0], 0, 0))]
        + x_specs
        + [block] * len(got),
        final if away == 0 else [block, block],
        shape if away == 0 else [shape, shape],
        ways * 2 * devices * tokens * width * slots_line * rank,
        2 * devices * tokens * width + 2 * groups * slots_line * rank * width * (ways + len(got)),
        "grad_a_step" + str(away),
        (packed, *x_cols, *got),
    )


def in_line(slots, place_ref, total):
    slots -= place_ref[1] * (total // line_length)
    return jnp.where(slots < 0, slots + total, slots)


def put_together(pieces, a_ref):
    @pl.when(pl.program_id(0) == 0)
    def _():
        rows = pieces[0].shape[0]
        a_ref[:rows] = pieces[0][...]
        for k in range(1, line_length):
            left, right = pieces[line_length - k], pieces[line_length - 1 + k]
            a_ref[k * rows : (k + 1) * rows] = left[...] + right[...]


def low_kernel(chunk, rank, number, place_ref, packed_ref, *refs):
    x_refs, pieces, (low_ref, a_ref) = refs[:number], refs[number:-2], refs[-2:]
    put_together(pieces, a_ref)
    slots = packed_ref[0].astype(jnp.float32).T[:, rank + 1 : rank + 2].astype(jnp.int32)
    slots = in_line(slots, place_ref, a_ref.shape[0] // rank)
    tile = slots.shape[0]
    lane_slot = lax.broadcasted_iota(jnp.int32, (tile, chunk), 1) // rank

    def use(x):
        def step(c, low):
            part = pl.ds(pl.multiple_of(c * chunk, chunk), chunk)
            hidden = lax.dot_general(x, a_ref[part], NT, preferred_element_type=jnp.float32)
            hidden = jnp.where(lane_slot + c * (chunk // rank) == slots, hidden, 0.0)
            for k in range(chunk // (2 * rank)):
                low += hidden[:, k * 2 * rank : (k + 1) * 2 * rank]
            return low

        start = jnp.zeros((tile, 2 * rank), jnp.float32)
        low = repeat(a_ref.shape[0] // chunk, step, start).T
        low_ref[0] = low[:rank] + low[rank:]

    if number == 1:
        use(x_refs[0][0])
    else:
        for m in range(number):

            @pl.when(pl.program_id(0) == m)
            def _(m=m):
                use(x_refs[m][...])


def low_part(place, packed, x_cols, a_pieces, inner, rank):
    devices, depth, tokens = packed.shape
    width = x_cols[0].shape[-1]
    rows = a_pieces[0].shape[0]
    slots = line_length * rows
    number = len(x_cols)
    mate = lambda t, place: (t ^ (place[0] * inner + place[2]), 0, 0)
    if number > 1:
        x_specs = [pl.BlockSpec((tokens, width), lambda t, place: (0, 0))] * number
    else:
        x_specs = [pl.BlockSpec((1, tokens, width), lambda t, place: (t, 0, 0))]
    return call(
        lambda *refs: low_kernel(512, rank, number, *refs),
        place,
        (devices,),
        [pl.BlockSpec((1, depth, tokens), mate)]
        + x_specs
        + [pl.BlockSpec((rows, width), lambda t, place: (0, 0))] * len(a_pieces),
        pl.BlockSpec((1, rank, tokens), mate),
        jax.ShapeDtypeStruct((devices, rank, tokens), jnp.float32),
        2 * devices * tokens * width * slots,
        2 * (devices * tokens + slots) * width,
        "low_part",
        (packed, *x_cols, *a_pieces),
        [pltpu.VMEM((slots, width), jnp.bfloat16)],
    )


def out_kernel(chunk, rank, groups, place_ref, packed_ref, g_ref, *refs):
    number = 2 * line_length - 1
    a_pieces, w_pieces, (out_ref, a_ref, w_ref) = refs[:number], refs[number:-3], refs[-3:]
    put_together(a_pieces, a_ref)
    put_together(w_pieces, w_ref)
    rows = jnp.concatenate([p.astype(jnp.float32).T for p in packed_ref[...]], axis=0)
    back, slots = rows[:, :rank], rows[:, rank + 1 : rank + 2].astype(jnp.int32)
    total = a_ref.shape[0]
    slots = in_line(slots, place_ref, total // rank)
    tile = back.shape[0]
    repeated = jnp.concatenate([back] * (chunk // rank), axis=1)
    lane_slot = lax.broadcasted_iota(jnp.int32, (tile, chunk), 1) // rank

    def masked(c):
        keep = lane_slot + c * (chunk // rank) == slots
        return jnp.where(keep, repeated, 0.0).astype(jnp.bfloat16)

    if total // chunk <= 4:
        wide = jnp.concatenate([masked(c) for c in range(total // chunk)], axis=1)
        acc = jnp.dot(wide, a_ref[...], preferred_element_type=jnp.float32)
    else:

        def step(c, acc):
            block = a_ref[pl.ds(pl.multiple_of(c * chunk, chunk), chunk), :]
            return acc + jnp.dot(masked(c), block, preferred_element_type=jnp.float32)

        acc = repeat(total // chunk, step, jnp.zeros((tile, a_ref.shape[1]), jnp.float32))
    base = []
    count = w_pieces[0].shape[0]
    halves = line_length // groups
    for c in range(halves):
        at = (place_ref[0] * halves + c - place_ref[1] + line_length) % line_length
        w = w_ref[pl.ds(pl.multiple_of(at * count, count), count), :]
        base.append(lax.dot_general(g_ref[...], w, NT, preferred_element_type=jnp.float32))
    out = jnp.concatenate(base, axis=1) + adapter_scale * acc
    out_ref[...] = out.astype(out_ref.dtype).reshape(out_ref.shape)


def out_part(place, packed, g_all, w_pieces, a_pieces, groups, rank):
    devices, depth, tokens = packed.shape
    outs = g_all.shape[1]
    rows, width = a_pieces[0].shape
    slots = line_length * rows
    both = 2
    pieces = [*a_pieces, *w_pieces]
    return call(
        lambda *refs: out_kernel(512, rank, groups, *refs),
        place,
        (devices // both,),
        [
            pl.BlockSpec((both, depth, tokens), lambda t, place: (t, 0, 0)),
            pl.BlockSpec((both * tokens, outs), lambda t, place: (t, 0)),
        ]
        + [pl.BlockSpec(piece.shape, lambda t, place: (0, 0)) for piece in pieces],
        pl.BlockSpec((both, tokens, width), lambda t, place: (t, 0, 0)),
        jax.ShapeDtypeStruct((devices, tokens, width), jnp.bfloat16),
        2 * devices * tokens * width * (slots + outs),
        2 * devices * tokens * (width + outs) + 2 * slots * width,
        "out_part",
        (packed, g_all, *pieces),
        [
            pltpu.VMEM((slots, width), jnp.bfloat16),
            pltpu.VMEM((line_length * w_pieces[0].shape[0], outs), jnp.bfloat16),
        ],
    )


def body(x, g, tok, adapter_slot, w, a, b):
    groups, inner = lax.axis_size("groups"), lax.axis_size("inner")
    gi, li, ji = lax.axis_index("groups"), lax.axis_index("line"), lax.axis_index("inner")
    place = jnp.stack([gi, li, ji]).astype(jnp.int32)
    size = groups * inner
    devices = line_length * inner
    tokens, model = x.shape
    outs = g.shape[1]
    resident, _, rank = a.shape
    share = resident // groups
    count = inner * resident
    halves = line_length // groups
    width = model // size
    part = width // halves
    adapters = adapter_slot.shape[0]
    capacity = max(2, 2 * tokens // adapters)

    up = [(i, i + 1) for i in range(line_length - 1)]
    down = [(i + 1, i) for i in range(line_length - 1)]

    def hop(pieces, away):
        left, right = pieces
        return [
            lax.ppermute(left, "line", up[away - 1 :]),
            lax.ppermute(right, "line", down[: line_length - away]),
        ]

    w_hops = [hop((w, w), 1)]
    w_hops.append(hop(w_hops[0], 2))

    a_mine = split_columns(place, jnp.swapaxes(a, 1, 2), groups, halves, inner, part)
    a_own = lax.all_to_all(a_mine, plane, 0, 0, tiled=True).reshape(count * rank, width)

    def meet(m):
        return lax.ppermute(x_sends[m], plane, [(i, i ^ m) for i in range(size)])

    direct = size == 8 and part % 128 == 0
    x_cols = {}
    if direct:
        x_sends = split_pieces(place, x, groups, halves, inner, part)
        x_cols = {0: x_sends[0], 1: meet(1), 2: meet(2), 4: meet(4)}
    else:
        x_far = split_columns(place, x[None], groups, halves, inner, part)
        x_far = lax.all_to_all(x_far, plane, 0, 0, tiled=True)
        x_cols = {0: x_far[jnp.arange(size) ^ (gi * inner + ji)]}

    matches = tok == lax.broadcasted_iota(jnp.int32, (tokens, adapters), 1)
    slot = jnp.sum(jnp.where(matches, adapter_slot[None, :], 0), axis=1)
    running = jnp.cumsum(matches.astype(jnp.int32), axis=0)
    within = jnp.sum(jnp.where(matches, running - 1, 0), axis=1)
    position = slot * capacity + within
    at = lax.broadcasted_iota(jnp.int32, (adapters * capacity, tokens), 0) == position[None, :]
    at = at.astype(jnp.bfloat16)

    def route(rows):
        rows = rows.reshape(devices, resident * capacity, rows.shape[1])
        rows = lax.all_to_all(rows, row, 0, 0, tiled=True)
        return rows.reshape(devices, resident, capacity, rows.shape[2])

    g_send = jnp.dot(at, g, preferred_element_type=jnp.float32).astype(jnp.bfloat16)
    g_send, a_own, x_cols, w_hops = lax.optimization_barrier((g_send, a_own, x_cols, w_hops))
    w_hops.append(hop(w_hops[1], 3))
    g_rows = route(g_send)
    back = jnp.einsum("hjct,jrt->hjcr", g_rows, b, preferred_element_type=jnp.float32)
    back = back.astype(jnp.bfloat16).reshape(devices, resident * capacity, rank)
    hops = [hop((a_own, a_own), 1)]
    if direct:
        x_cols.update({3: meet(3), 5: meet(5), 6: meet(6), 7: meet(7)})
    back = lax.all_to_all(back, row, 0, 0, tiled=True).reshape(adapters * capacity, rank)
    back = lax.dot_general(
        back, at, (((0,), (0,)), ((), ())), preferred_element_type=jnp.float32
    ).astype(jnp.bfloat16)
    owner, res = slot // resident, slot % resident
    slot_a = (owner // inner) * count + ((res // share) * inner + owner % inner) * share + res % share
    names = jnp.stack([slot, slot_a] + [slot] * 14).astype(jnp.bfloat16)
    packed = jnp.concatenate([back, names], axis=0)
    packed, x_cols, hops, w_hops = lax.optimization_barrier((packed, x_cols, hops, w_hops))
    packed = jnp.broadcast_to(packed[None], (size,) + packed.shape)
    packed = lax.all_to_all(packed, plane, 0, 0, tiled=True)
    x_cols = [x_cols[m] for m in range(len(x_cols))]
    g_own, x_cols = lax.optimization_barrier((g, x_cols))
    g_all = lax.all_gather(g_own, plane, axis=0, tiled=True)

    hops.append(hop(hops[0], 2))

    def send(c, got, away):
        sums = grad_a_step(place, packed, x_cols, c, got, away, groups, count, rank)
        ahead = [(i, i + 1) for i in range(line_length - away)]
        behind = [(i, i - 1) for i in range(away, line_length)]
        moved = (lax.ppermute(sums[0], "line", ahead), lax.ppermute(sums[1], "line", behind))
        return moved, sums[0]

    def own(c, got):
        p = grad_a_step(place, packed, x_cols, c, got, 0, groups, count, rank)
        return p.reshape(size, resident * rank, part)

    first, done = send(0, (), 3)
    packed, done = lax.optimization_barrier((packed, done))
    second, done = send(1, (), 3)

    first, hops[1], done = lax.optimization_barrier((first, hops[1], done))
    hops.append(hop(hops[1], 3))
    first, done = send(0, first, 2)
    second, done = lax.optimization_barrier((second, done))
    second, done = send(1, second, 2)

    a_pieces = [a_own] + [h[0] for h in hops] + [h[1] for h in hops]
    w_pieces = [w] + [h[0] for h in w_hops] + [h[1] for h in w_hops]
    a_pieces, done = lax.optimization_barrier((a_pieces, done))
    out_cols = out_part(place, packed, g_all, w_pieces, a_pieces, groups, rank)
    first, out_cols = lax.optimization_barrier((first, out_cols))
    first, done = send(0, first, 1)
    out_back = lax.all_to_all(out_cols, plane, 0, 0, tiled=True)

    second, done = lax.optimization_barrier((second, done))
    second, done = send(1, second, 1)

    a_pieces, done = lax.optimization_barrier((a_pieces, done))
    low = low_part(place, packed, x_cols, a_pieces, inner, rank)
    low, out_back = lax.optimization_barrier((low, out_back))
    low = lax.all_to_all(low, plane, 0, 0, tiled=True)
    p_first, low = lax.optimization_barrier((own(0, first), low))
    p_back = [lax.all_to_all(p_first, plane, 0, 0, tiled=True)]
    p_second, p_back[0] = lax.optimization_barrier((own(1, second), p_back[0]))
    p_back.append(lax.all_to_all(p_second, plane, 0, 0, tiled=True))
    low = jnp.sum(low, axis=0).astype(jnp.bfloat16)
    low = lax.dot_general(at, low, NT, preferred_element_type=jnp.float32).astype(jnp.bfloat16)
    low, p_back = lax.optimization_barrier((low, p_back))
    low = route(low)

    grad_b = jnp.einsum("hjcr,hjco->jro", low, g_rows, preferred_element_type=jnp.float32)
    grad_b = (adapter_scale * grad_b).astype(jnp.bfloat16)
    input_gradient = join_rows(place, out_back, groups, halves, inner, part)
    grad_a = join_slots(place, p_back, resident, groups, inner).swapaxes(1, 2)
    return input_gradient, grad_a, grad_b


def solution(mesh):
    groups, rows = mesh.shape["groups"], mesh.shape["row"]
    whole = ("groups", "line", "inner")
    split = Mesh(mesh.devices.reshape(groups, line_length, rows // line_length), whole)
    return jax.shard_map(
        body,
        mesh=split,
        in_specs=(
            P(whole, None),
            P(whole, None),
            P(whole, None),
            P(),
            P(row, None),
            P(row, None, None),
            P(row, None, None),
        ),
        out_specs=(P(whole, None), P(whole, None, None), P(whole, None, None)),
        check_vma=False,
    )
```

```python
import jax
import jax.numpy as jnp
from jax import lax
from jax.experimental import pallas as pl
from jax.experimental.pallas import tpu as pltpu
from jax.sharding import Mesh, PartitionSpec as P

adapter_scale = 2.0
line_length = 4
plane = ("groups", "inner")
row = ("line", "inner")
vmem_limit = 56 * 1024 * 1024
NT = (((1,), (1,)), ((), ()))


def call(kernel, place, grid, in_specs, out_specs, out_shape, flops, moved, name, args, scratch=()):
    return pl.pallas_call(
        kernel,
        grid_spec=pltpu.PrefetchScalarGridSpec(
            num_scalar_prefetch=1,
            grid=grid,
            in_specs=in_specs,
            out_specs=out_specs,
            scratch_shapes=scratch,
        ),
        out_shape=out_shape,
        compiler_params=pltpu.CompilerParams(vmem_limit_bytes=vmem_limit),
        cost_estimate=pl.CostEstimate(flops=flops, bytes_accessed=moved, transcendentals=0),
        name=name,
    )(place, *args)


def repeat(count, step, start):
    if count <= 4:
        for i in range(count):
            start = step(i, start)
        return start
    return lax.fori_loop(0, count, step, start)


def move(name, sources, in_blocks, in_maps, outs, out_blocks, out_maps, grid, kernel, place):
    moved = 0
    for shape in outs:
        size = 4
        for n in shape:
            size *= n
        moved += size
    return call(
        kernel,
        place,
        grid,
        [pl.BlockSpec(block, index) for block, index in zip(in_blocks, in_maps)],
        [pl.BlockSpec(block, index) for block, index in zip(out_blocks, out_maps)],
        [jax.ShapeDtypeStruct(shape, jnp.bfloat16) for shape in outs],
        0,
        moved,
        name,
        sources,
    )


def columns_of(q, c, halves, inner):
    return ((q // inner) * halves + c) * inner + q % inner


def split_columns(place, rows, groups, halves, inner, width):
    slots, rank, model = rows.shape
    size, share = groups * inner, max(1, slots // groups)
    group = lambda place: place[0] if slots >= groups else 0
    if width % 128:
        mine = lax.dynamic_slice_in_dim(rows, group(place) * share, share, 0)
        mine = mine.reshape(share * rank, groups, halves, inner, width)
        return mine.transpose(1, 3, 0, 2, 4).reshape(size, share * rank, halves * width)

    def kernel(place_ref, rows_ref, out_ref):
        for q in range(size):
            for c in range(halves):
                first = columns_of(q, c, halves, inner) * width
                out_ref[q, :, c * width : (c + 1) * width] = rows_ref[0, :, first : first + width]

    tile = min(rank, 64)
    steps = rank // tile
    return move(
        "split_columns", [rows], [(1, tile, model)],
        [lambda s, r, place: (group(place) * share + s, r, 0)],
        [(size, share * rank, halves * width)], [(size, tile, halves * width)],
        [lambda s, r, place: (0, s * steps + r, 0)], (share, steps), kernel, place,
    )[0]


def join_slots(place, parts, resident, groups, inner):
    size, rows, width = parts[0].shape
    halves, rank = len(parts), rows // resident
    if width % 128:
        parts = [p.reshape(groups, inner, rows, width) for p in parts]
        joined = jnp.stack(parts, axis=1).transpose(3, 0, 1, 2, 4)
        return joined.reshape(resident, rank, -1)

    def kernel(place_ref, *refs):
        for q in range(size):
            for c in range(halves):
                first = columns_of(q, c, halves, inner) * width
                refs[-1][0, :, first : first + width] = refs[c][q]

    return move(
        "join_slots", parts, [(size, rank, width)] * halves, [lambda r, place: (0, r, 0)] * halves,
        [(resident, rank, size * halves * width)], [(1, rank, size * halves * width)],
        [lambda r, place: (r, 0, 0)], (resident,), kernel, place,
    )[0]


def join_rows(place, rows, groups, halves, inner, part):
    size, tokens = rows.shape[:2]
    if part % 128:
        rows = rows.reshape(groups, inner, tokens, halves, part)
        return rows.transpose(2, 0, 3, 1, 4).reshape(tokens, -1)
    tile = min(tokens, 64)
    model = size * halves * part

    def kernel(place_ref, rows_ref, out_ref):
        for q in range(size):
            for c in range(halves):
                first = columns_of(q, c, halves, inner) * part
                out_ref[:, first : first + part] = rows_ref[q, :, c * part : (c + 1) * part]

    return move(
        "join_rows", [rows], [(size, tile, halves * part)], [lambda t, place: (0, t, 0)],
        [(tokens, model)], [(tile, model)], [lambda t, place: (t, 0)], (tokens // tile,),
        kernel, place,
    )[0]


def slot_sums(packed_ref, x_ref, rank, first, count):
    devices, _, tokens = packed_ref.shape
    width = x_ref.shape[2]
    chunk = min(devices, 4)

    def step(c, total):
        columns = []
        for d in range(chunk):
            back = packed_ref[c * chunk + d, :rank, :]
            slots = packed_ref[c * chunk + d, rank : rank + 1, :].astype(jnp.float32)
            rows = [
                back * (slots == (first + i).astype(jnp.float32)).astype(jnp.bfloat16)
                for i in range(count)
            ]
            columns.append(jnp.concatenate(rows, axis=0))
        x = x_ref[pl.ds(c * chunk, chunk)].reshape(chunk * tokens, width)
        return total + jnp.dot(
            jnp.concatenate(columns, axis=1), x, preferred_element_type=jnp.float32
        )

    return repeat(devices // chunk, step, jnp.zeros((count * rank, width), jnp.float32))


def send_kernel(slots_line, count, rank, away, place_ref, packed_ref, x_ref, *refs):
    line = place_ref[1]
    got, outs = refs[:-2], refs[-2:]
    ways = ((line + away < line_length, line + away), (line >= away, line - away))
    for way, (inside, target) in enumerate(ways):

        @pl.when(inside)
        def _(way=way, target=target):
            first = target * slots_line + pl.program_id(1) * count
            total = slot_sums(packed_ref, x_ref, rank, first, count)
            if got:
                total += got[way][0].astype(jnp.float32)
            outs[way][0] = total.astype(jnp.bfloat16)


def own_kernel(slots_line, count, rank, place_ref, packed_ref, x_ref, right_ref, left_ref, out_ref):
    first = place_ref[1] * slots_line + pl.program_id(1) * count
    total = slot_sums(packed_ref, x_ref, rank, first, count)
    total += right_ref[0].astype(jnp.float32) + left_ref[0].astype(jnp.float32)
    out_ref[0] = (adapter_scale * total).astype(jnp.bfloat16)


def grad_a_step(place, packed, x_cols, half, got, away, groups, slots_line, rank):
    devices, depth, tokens = packed.shape
    width = x_cols.shape[2] // 2
    if width % 128:
        x_cols, half = x_cols[:, :, half * width : (half + 1) * width], 0
    local = devices // groups
    count = 8
    rows = count * rank
    block = pl.BlockSpec((1, rows, width), lambda g, s, place: (g, s, 0))
    shape = jax.ShapeDtypeStruct((groups, slots_line * rank, width), jnp.bfloat16)
    ways = 1 if away == 0 else 2
    if away == 0:
        kernel = lambda *refs: own_kernel(slots_line, count, rank, *refs)
    else:
        kernel = lambda *refs: send_kernel(slots_line, count, rank, away, *refs)
    return call(
        kernel,
        place,
        (groups, slots_line // count),
        [
            pl.BlockSpec((local, depth, tokens), lambda g, s, place: (g, 0, 0)),
            pl.BlockSpec((local, tokens, width), lambda g, s, place: (g, 0, half)),
        ]
        + [block] * len(got),
        block if away == 0 else [block, block],
        shape if away == 0 else [shape, shape],
        ways * 2 * devices * tokens * width * slots_line * rank,
        2 * devices * tokens * width + 2 * groups * slots_line * rank * width * (ways + len(got)),
        "grad_a_step" + str(away),
        (packed, x_cols, *got),
    )


def in_line(slots, place_ref, total):
    slots -= place_ref[1] * (total // line_length)
    return jnp.where(slots < 0, slots + total, slots)


def put_together(pieces, a_ref):
    @pl.when(pl.program_id(0) == 0)
    def _():
        rows = pieces[0].shape[0]
        a_ref[:rows] = pieces[0][...]
        for k in range(1, line_length):
            left, right = pieces[line_length - k], pieces[line_length - 1 + k]
            a_ref[k * rows : (k + 1) * rows] = left[...] + right[...]


def low_kernel(chunk, rank, place_ref, packed_ref, x_ref, *refs):
    pieces, (low_ref, a_ref) = refs[:-2], refs[-2:]
    put_together(pieces, a_ref)
    slots = packed_ref[0].astype(jnp.float32).T[:, rank + 1 : rank + 2].astype(jnp.int32)
    slots = in_line(slots, place_ref, a_ref.shape[0] // rank)
    tile = slots.shape[0]
    lane_slot = lax.broadcasted_iota(jnp.int32, (tile, chunk), 1) // rank

    def step(c, low):
        part = pl.ds(pl.multiple_of(c * chunk, chunk), chunk)
        hidden = lax.dot_general(x_ref[0], a_ref[part], NT, preferred_element_type=jnp.float32)
        hidden = jnp.where(lane_slot + c * (chunk // rank) == slots, hidden, 0.0)
        for k in range(chunk // (2 * rank)):
            low += hidden[:, k * 2 * rank : (k + 1) * 2 * rank]
        return low

    low = repeat(a_ref.shape[0] // chunk, step, jnp.zeros((tile, 2 * rank), jnp.float32)).T
    low_ref[0] = low[:rank] + low[rank:]


def low_part(place, packed, x_cols, a_pieces, rank):
    devices, depth, tokens = packed.shape
    width = x_cols.shape[2]
    rows = a_pieces[0].shape[0]
    slots = line_length * rows
    return call(
        lambda *refs: low_kernel(512, rank, *refs),
        place,
        (devices,),
        [
            pl.BlockSpec((1, depth, tokens), lambda t, place: (t, 0, 0)),
            pl.BlockSpec((1, tokens, width), lambda t, place: (t, 0, 0)),
        ]
        + [pl.BlockSpec((rows, width), lambda t, place: (0, 0))] * len(a_pieces),
        pl.BlockSpec((1, rank, tokens), lambda t, place: (t, 0, 0)),
        jax.ShapeDtypeStruct((devices, rank, tokens), jnp.float32),
        2 * devices * tokens * width * slots,
        2 * (devices * tokens + slots) * width,
        "low_part",
        (packed, x_cols, *a_pieces),
        [pltpu.VMEM((slots, width), jnp.bfloat16)],
    )


def out_kernel(chunk, rank, groups, place_ref, packed_ref, g_ref, *refs):
    number = 2 * line_length - 1
    a_pieces, w_pieces, (out_ref, a_ref, w_ref) = refs[:number], refs[number:-3], refs[-3:]
    put_together(a_pieces, a_ref)
    put_together(w_pieces, w_ref)
    rows = jnp.concatenate([p.astype(jnp.float32).T for p in packed_ref[...]], axis=0)
    back, slots = rows[:, :rank], rows[:, rank + 1 : rank + 2].astype(jnp.int32)
    total = a_ref.shape[0]
    slots = in_line(slots, place_ref, total // rank)
    tile = back.shape[0]
    repeated = jnp.concatenate([back] * (chunk // rank), axis=1)
    lane_slot = lax.broadcasted_iota(jnp.int32, (tile, chunk), 1) // rank

    def masked(c):
        keep = lane_slot + c * (chunk // rank) == slots
        return jnp.where(keep, repeated, 0.0).astype(jnp.bfloat16)

    if total // chunk <= 4:
        wide = jnp.concatenate([masked(c) for c in range(total // chunk)], axis=1)
        acc = jnp.dot(wide, a_ref[...], preferred_element_type=jnp.float32)
    else:

        def step(c, acc):
            block = a_ref[pl.ds(pl.multiple_of(c * chunk, chunk), chunk), :]
            return acc + jnp.dot(masked(c), block, preferred_element_type=jnp.float32)

        acc = repeat(total // chunk, step, jnp.zeros((tile, a_ref.shape[1]), jnp.float32))
    base = []
    count = w_pieces[0].shape[0]
    halves = line_length // groups
    for c in range(halves):
        at = (place_ref[0] * halves + c - place_ref[1] + line_length) % line_length
        w = w_ref[pl.ds(pl.multiple_of(at * count, count), count), :]
        base.append(lax.dot_general(g_ref[...], w, NT, preferred_element_type=jnp.float32))
    out = jnp.concatenate(base, axis=1) + adapter_scale * acc
    out_ref[...] = out.astype(out_ref.dtype).reshape(out_ref.shape)


def out_part(place, packed, g_all, w_pieces, a_pieces, groups, rank):
    devices, depth, tokens = packed.shape
    outs = g_all.shape[1]
    rows, width = a_pieces[0].shape
    slots = line_length * rows
    both = 2
    pieces = [*a_pieces, *w_pieces]
    return call(
        lambda *refs: out_kernel(512, rank, groups, *refs),
        place,
        (devices // both,),
        [
            pl.BlockSpec((both, depth, tokens), lambda t, place: (t, 0, 0)),
            pl.BlockSpec((both * tokens, outs), lambda t, place: (t, 0)),
        ]
        + [pl.BlockSpec(piece.shape, lambda t, place: (0, 0)) for piece in pieces],
        pl.BlockSpec((both, tokens, width), lambda t, place: (t, 0, 0)),
        jax.ShapeDtypeStruct((devices, tokens, width), jnp.bfloat16),
        2 * devices * tokens * width * (slots + outs),
        2 * devices * tokens * (width + outs) + 2 * slots * width,
        "out_part",
        (packed, g_all, *pieces),
        [
            pltpu.VMEM((slots, width), jnp.bfloat16),
            pltpu.VMEM((line_length * w_pieces[0].shape[0], outs), jnp.bfloat16),
        ],
    )


def body(x, g, tok, adapter_slot, w, a, b):
    groups, inner = lax.axis_size("groups"), lax.axis_size("inner")
    gi, li, ji = lax.axis_index("groups"), lax.axis_index("line"), lax.axis_index("inner")
    place = jnp.stack([gi, li, ji]).astype(jnp.int32)
    size = groups * inner
    devices = line_length * inner
    tokens, model = x.shape
    outs = g.shape[1]
    resident, _, rank = a.shape
    share = resident // groups
    count = inner * resident
    halves = line_length // groups
    width = model // size
    part = width // halves
    adapters = adapter_slot.shape[0]
    capacity = max(2, 2 * tokens // adapters)

    up = [(i, i + 1) for i in range(line_length - 1)]
    down = [(i + 1, i) for i in range(line_length - 1)]

    def hop(pieces, away):
        left, right = pieces
        return [
            lax.ppermute(left, "line", up[away - 1 :]),
            lax.ppermute(right, "line", down[: line_length - away]),
        ]

    w_hops = [hop((w, w), 1)]
    w_hops.append(hop(w_hops[0], 2))

    a_mine = split_columns(place, jnp.swapaxes(a, 1, 2), groups, halves, inner, part)
    a_own = lax.all_to_all(a_mine, plane, 0, 0, tiled=True).reshape(count * rank, width)

    x_send = split_columns(place, x[None], groups, halves, inner, part)
    x_send, a_own = lax.optimization_barrier((x_send, a_own))
    x_cols = lax.all_to_all(x_send, plane, 0, 0, tiled=True)
    hops = [hop((a_own, a_own), 1)]
    hops.append(hop(hops[0], 2))

    matches = tok == lax.broadcasted_iota(jnp.int32, (tokens, adapters), 1)
    slot = jnp.sum(jnp.where(matches, adapter_slot[None, :], 0), axis=1)
    running = jnp.cumsum(matches.astype(jnp.int32), axis=0)
    within = jnp.sum(jnp.where(matches, running - 1, 0), axis=1)
    position = slot * capacity + within
    at = lax.broadcasted_iota(jnp.int32, (adapters * capacity, tokens), 0) == position[None, :]
    at = at.astype(jnp.bfloat16)

    def route(rows):
        rows = rows.reshape(devices, resident * capacity, rows.shape[1])
        rows = lax.all_to_all(rows, row, 0, 0, tiled=True)
        return rows.reshape(devices, resident, capacity, rows.shape[2])

    g_send = jnp.dot(at, g, preferred_element_type=jnp.float32).astype(jnp.bfloat16)
    g_send, x_cols, hops, w_hops, g = lax.optimization_barrier((g_send, x_cols, hops, w_hops, g))
    hops.append(hop(hops[1], 3))
    w_hops.append(hop(w_hops[1], 3))
    g_all = lax.all_gather(g, plane, axis=0, tiled=True)
    g_rows = route(g_send)
    back = jnp.einsum("hjct,jrt->hjcr", g_rows, b, preferred_element_type=jnp.float32)
    back = back.astype(jnp.bfloat16).reshape(devices, resident * capacity, rank)
    back = lax.all_to_all(back, row, 0, 0, tiled=True).reshape(adapters * capacity, rank)
    back = lax.dot_general(
        back, at, (((0,), (0,)), ((), ())), preferred_element_type=jnp.float32
    ).astype(jnp.bfloat16)
    owner, res = slot // resident, slot % resident
    slot_a = (owner // inner) * count + ((res // share) * inner + owner % inner) * share + res % share
    names = jnp.stack([slot, slot_a] + [slot] * 14).astype(jnp.bfloat16)
    packed = jnp.concatenate([back, names], axis=0)
    packed = jnp.broadcast_to(packed[None], (size,) + packed.shape)
    packed = lax.all_to_all(packed, plane, 0, 0, tiled=True)

    def send(c, got, away):
        sums = grad_a_step(place, packed, x_cols, c, got, away, groups, count, rank)
        ahead = [(i, i + 1) for i in range(line_length - away)]
        behind = [(i, i - 1) for i in range(away, line_length)]
        moved = (lax.ppermute(sums[0], "line", ahead), lax.ppermute(sums[1], "line", behind))
        return moved, sums[0]

    def own(c, got):
        p = grad_a_step(place, packed, x_cols, c, got, 0, groups, count, rank)
        return p.reshape(size, resident * rank, part)

    first, done = send(0, (), 3)
    packed, done = lax.optimization_barrier((packed, done))
    second, done = send(1, (), 3)


    a_pieces = [a_own] + [h[0] for h in hops] + [h[1] for h in hops]
    w_pieces = [w] + [h[0] for h in w_hops] + [h[1] for h in w_hops]
    a_pieces, done = lax.optimization_barrier((a_pieces, done))
    out_cols = out_part(place, packed, g_all, w_pieces, a_pieces, groups, rank)
    first, out_cols = lax.optimization_barrier((first, out_cols))
    out_back = lax.all_to_all(out_cols, plane, 0, 0, tiled=True)

    first, done = send(0, first, 2)
    second, done = lax.optimization_barrier((second, done))
    second, done = send(1, second, 2)
    first, done = lax.optimization_barrier((first, done))
    first, done = send(0, first, 1)
    second, done = lax.optimization_barrier((second, done))
    second, done = send(1, second, 1)

    a_pieces, done = lax.optimization_barrier((a_pieces, done))
    low = low_part(place, packed, x_cols, a_pieces, rank)
    low = lax.all_to_all(low, plane, 0, 0, tiled=True)
    low = jnp.sum(low, axis=0).astype(jnp.bfloat16)
    low = lax.dot_general(at, low, NT, preferred_element_type=jnp.float32).astype(jnp.bfloat16)
    low = route(low)
    p_back = [
        lax.all_to_all(own(c, got), plane, 0, 0, tiled=True) for c, got in enumerate((first, second))
    ]

    grad_b = jnp.einsum("hjcr,hjco->jro", low, g_rows, preferred_element_type=jnp.float32)
    grad_b = (adapter_scale * grad_b).astype(jnp.bfloat16)
    input_gradient = join_rows(place, out_back, groups, halves, inner, part)
    grad_a = join_slots(place, p_back, resident, groups, inner).swapaxes(1, 2)
    return input_gradient, grad_a, grad_b


def solution(mesh):
    groups, rows = mesh.shape["groups"], mesh.shape["row"]
    whole = ("groups", "line", "inner")
    split = Mesh(mesh.devices.reshape(groups, line_length, rows // line_length), whole)
    return jax.shard_map(
        body,
        mesh=split,
        in_specs=(
            P(whole, None),
            P(whole, None),
            P(whole, None),
            P(),
            P(row, None),
            P(row, None, None),
            P(row, None, None),
        ),
        out_specs=(P(whole, None), P(whole, None, None), P(whole, None, None)),
        check_vma=False,
    )
```

```python
import jax
import jax.numpy as jnp
from jax import lax
from jax.experimental import pallas as pl
from jax.experimental.pallas import tpu as pltpu
from jax.sharding import Mesh, PartitionSpec as P

adapter_scale = 2.0
line_length = 4
plane = ("groups", "inner")
row = ("line", "inner")
vmem_limit = 56 * 1024 * 1024
NT = (((1,), (1,)), ((), ()))


def call(kernel, place, grid, in_specs, out_specs, out_shape, flops, moved, name, args, scratch=()):
    return pl.pallas_call(
        kernel,
        grid_spec=pltpu.PrefetchScalarGridSpec(
            num_scalar_prefetch=1,
            grid=grid,
            in_specs=in_specs,
            out_specs=out_specs,
            scratch_shapes=scratch,
        ),
        out_shape=out_shape,
        compiler_params=pltpu.CompilerParams(vmem_limit_bytes=vmem_limit),
        cost_estimate=pl.CostEstimate(flops=flops, bytes_accessed=moved, transcendentals=0),
        name=name,
    )(place, *args)


def repeat(count, step, start):
    if count <= 4:
        for i in range(count):
            start = step(i, start)
        return start
    return lax.fori_loop(0, count, step, start)


def move(name, sources, in_blocks, in_maps, outs, out_blocks, out_maps, grid, kernel, place):
    moved = 0
    for shape in outs:
        size = 4
        for n in shape:
            size *= n
        moved += size
    return call(
        kernel,
        place,
        grid,
        [pl.BlockSpec(block, index) for block, index in zip(in_blocks, in_maps)],
        [pl.BlockSpec(block, index) for block, index in zip(out_blocks, out_maps)],
        [jax.ShapeDtypeStruct(shape, jnp.bfloat16) for shape in outs],
        0,
        moved,
        name,
        sources,
    )


def columns_of(q, c, halves, inner):
    return ((q // inner) * halves + c) * inner + q % inner


def split_columns(place, rows, groups, halves, inner, width):
    slots, rank, model = rows.shape
    size, share = groups * inner, max(1, slots // groups)
    group = lambda place: place[0] if slots >= groups else 0
    if width % 128:
        mine = lax.dynamic_slice_in_dim(rows, group(place) * share, share, 0)
        mine = mine.reshape(share * rank, groups, halves, inner, width)
        return mine.transpose(1, 3, 0, 2, 4).reshape(size, share * rank, halves * width)

    def kernel(place_ref, rows_ref, out_ref):
        for q in range(size):
            for c in range(halves):
                first = columns_of(q, c, halves, inner) * width
                out_ref[q, :, c * width : (c + 1) * width] = rows_ref[0, :, first : first + width]

    tile = min(rank, 64)
    steps = rank // tile
    return move(
        "split_columns", [rows], [(1, tile, model)],
        [lambda s, r, place: (group(place) * share + s, r, 0)],
        [(size, share * rank, halves * width)], [(size, tile, halves * width)],
        [lambda s, r, place: (0, s * steps + r, 0)], (share, steps), kernel, place,
    )[0]


def join_slots(place, parts, resident, groups, inner):
    size, rows, width = parts[0].shape
    halves, rank = len(parts), rows // resident
    if width % 128:
        parts = [p.reshape(groups, inner, rows, width) for p in parts]
        joined = jnp.stack(parts, axis=1).transpose(3, 0, 1, 2, 4)
        return joined.reshape(resident, rank, -1)

    def kernel(place_ref, *refs):
        for q in range(size):
            for c in range(halves):
                first = columns_of(q, c, halves, inner) * width
                refs[-1][0, :, first : first + width] = refs[c][q]

    return move(
        "join_slots", parts, [(size, rank, width)] * halves, [lambda r, place: (0, r, 0)] * halves,
        [(resident, rank, size * halves * width)], [(1, rank, size * halves * width)],
        [lambda r, place: (r, 0, 0)], (resident,), kernel, place,
    )[0]


def join_rows(place, rows, groups, halves, inner, part):
    size, tokens = rows.shape[:2]
    if part % 128:
        rows = rows.reshape(groups, inner, tokens, halves, part)
        return rows.transpose(2, 0, 3, 1, 4).reshape(tokens, -1)
    tile = min(tokens, 64)
    model = size * halves * part

    def kernel(place_ref, rows_ref, out_ref):
        for q in range(size):
            for c in range(halves):
                first = columns_of(q, c, halves, inner) * part
                out_ref[:, first : first + part] = rows_ref[q, :, c * part : (c + 1) * part]

    return move(
        "join_rows", [rows], [(size, tile, halves * part)], [lambda t, place: (0, t, 0)],
        [(tokens, model)], [(tile, model)], [lambda t, place: (t, 0)], (tokens // tile,),
        kernel, place,
    )[0]


def slot_sums(packed_ref, x_ref, rank, first, count):
    devices, _, tokens = packed_ref.shape
    width = x_ref.shape[2]
    chunk = min(devices, 4)

    def step(c, total):
        columns = []
        for d in range(chunk):
            back = packed_ref[c * chunk + d, :rank, :]
            slots = packed_ref[c * chunk + d, rank : rank + 1, :].astype(jnp.float32)
            rows = [
                back * (slots == (first + i).astype(jnp.float32)).astype(jnp.bfloat16)
                for i in range(count)
            ]
            columns.append(jnp.concatenate(rows, axis=0))
        x = x_ref[pl.ds(c * chunk, chunk)].reshape(chunk * tokens, width)
        return total + jnp.dot(
            jnp.concatenate(columns, axis=1), x, preferred_element_type=jnp.float32
        )

    return repeat(devices // chunk, step, jnp.zeros((count * rank, width), jnp.float32))


def send_kernel(slots_line, count, rank, away, place_ref, packed_ref, x_ref, *refs):
    line = place_ref[1]
    got, outs = refs[:-2], refs[-2:]
    ways = ((line + away < line_length, line + away), (line >= away, line - away))
    for way, (inside, target) in enumerate(ways):

        @pl.when(inside)
        def _(way=way, target=target):
            first = target * slots_line + pl.program_id(1) * count
            total = slot_sums(packed_ref, x_ref, rank, first, count)
            if got:
                total += got[way][0].astype(jnp.float32)
            outs[way][0] = total.astype(jnp.bfloat16)


def own_kernel(slots_line, count, rank, place_ref, packed_ref, x_ref, right_ref, left_ref, out_ref):
    first = place_ref[1] * slots_line + pl.program_id(1) * count
    total = slot_sums(packed_ref, x_ref, rank, first, count)
    total += right_ref[0].astype(jnp.float32) + left_ref[0].astype(jnp.float32)
    out_ref[0] = (adapter_scale * total).astype(jnp.bfloat16)


def grad_a_step(place, packed, x_cols, half, got, away, groups, slots_line, rank):
    devices, depth, tokens = packed.shape
    width = x_cols.shape[2] // 2
    if width % 128:
        x_cols, half = x_cols[:, :, half * width : (half + 1) * width], 0
    local = devices // groups
    count = 8
    rows = count * rank
    block = pl.BlockSpec((1, rows, width), lambda g, s, place: (g, s, 0))
    shape = jax.ShapeDtypeStruct((groups, slots_line * rank, width), jnp.bfloat16)
    ways = 1 if away == 0 else 2
    if away == 0:
        kernel = lambda *refs: own_kernel(slots_line, count, rank, *refs)
    else:
        kernel = lambda *refs: send_kernel(slots_line, count, rank, away, *refs)
    return call(
        kernel,
        place,
        (groups, slots_line // count),
        [
            pl.BlockSpec((local, depth, tokens), lambda g, s, place: (g, 0, 0)),
            pl.BlockSpec((local, tokens, width), lambda g, s, place: (g, 0, half)),
        ]
        + [block] * len(got),
        block if away == 0 else [block, block],
        shape if away == 0 else [shape, shape],
        ways * 2 * devices * tokens * width * slots_line * rank,
        2 * devices * tokens * width + 2 * groups * slots_line * rank * width * (ways + len(got)),
        "grad_a_step" + str(away),
        (packed, x_cols, *got),
    )


def in_line(slots, place_ref, total):
    slots -= place_ref[1] * (total // line_length)
    return jnp.where(slots < 0, slots + total, slots)


def put_together(pieces, a_ref):
    @pl.when(pl.program_id(0) == 0)
    def _():
        rows = pieces[0].shape[0]
        a_ref[:rows] = pieces[0][...]
        for k in range(1, line_length):
            left, right = pieces[line_length - k], pieces[line_length - 1 + k]
            a_ref[k * rows : (k + 1) * rows] = left[...] + right[...]


def low_kernel(chunk, rank, place_ref, packed_ref, x_ref, *refs):
    pieces, (low_ref, a_ref) = refs[:-2], refs[-2:]
    put_together(pieces, a_ref)
    slots = packed_ref[0].astype(jnp.float32).T[:, rank + 1 : rank + 2].astype(jnp.int32)
    slots = in_line(slots, place_ref, a_ref.shape[0] // rank)
    tile = slots.shape[0]
    lane_slot = lax.broadcasted_iota(jnp.int32, (tile, chunk), 1) // rank

    def step(c, low):
        part = pl.ds(pl.multiple_of(c * chunk, chunk), chunk)
        hidden = lax.dot_general(x_ref[0], a_ref[part], NT, preferred_element_type=jnp.float32)
        hidden = jnp.where(lane_slot + c * (chunk // rank) == slots, hidden, 0.0)
        for k in range(chunk // (2 * rank)):
            low += hidden[:, k * 2 * rank : (k + 1) * 2 * rank]
        return low

    low = repeat(a_ref.shape[0] // chunk, step, jnp.zeros((tile, 2 * rank), jnp.float32)).T
    low_ref[0] = low[:rank] + low[rank:]


def low_part(place, packed, x_cols, a_pieces, rank):
    devices, depth, tokens = packed.shape
    width = x_cols.shape[2]
    rows = a_pieces[0].shape[0]
    slots = line_length * rows
    return call(
        lambda *refs: low_kernel(512, rank, *refs),
        place,
        (devices,),
        [
            pl.BlockSpec((1, depth, tokens), lambda t, place: (t, 0, 0)),
            pl.BlockSpec((1, tokens, width), lambda t, place: (t, 0, 0)),
        ]
        + [pl.BlockSpec((rows, width), lambda t, place: (0, 0))] * len(a_pieces),
        pl.BlockSpec((1, rank, tokens), lambda t, place: (t, 0, 0)),
        jax.ShapeDtypeStruct((devices, rank, tokens), jnp.float32),
        2 * devices * tokens * width * slots,
        2 * (devices * tokens + slots) * width,
        "low_part",
        (packed, x_cols, *a_pieces),
        [pltpu.VMEM((slots, width), jnp.bfloat16)],
    )


def out_kernel(chunk, rank, groups, place_ref, packed_ref, g_ref, *refs):
    number = 2 * line_length - 1
    a_pieces, w_pieces, (out_ref, a_ref, w_ref) = refs[:number], refs[number:-3], refs[-3:]
    put_together(a_pieces, a_ref)
    put_together(w_pieces, w_ref)
    rows = jnp.concatenate([p.astype(jnp.float32).T for p in packed_ref[...]], axis=0)
    back, slots = rows[:, :rank], rows[:, rank + 1 : rank + 2].astype(jnp.int32)
    total = a_ref.shape[0]
    slots = in_line(slots, place_ref, total // rank)
    tile = back.shape[0]
    repeated = jnp.concatenate([back] * (chunk // rank), axis=1)
    lane_slot = lax.broadcasted_iota(jnp.int32, (tile, chunk), 1) // rank

    def masked(c):
        keep = lane_slot + c * (chunk // rank) == slots
        return jnp.where(keep, repeated, 0.0).astype(jnp.bfloat16)

    if total // chunk <= 4:
        wide = jnp.concatenate([masked(c) for c in range(total // chunk)], axis=1)
        acc = jnp.dot(wide, a_ref[...], preferred_element_type=jnp.float32)
    else:

        def step(c, acc):
            block = a_ref[pl.ds(pl.multiple_of(c * chunk, chunk), chunk), :]
            return acc + jnp.dot(masked(c), block, preferred_element_type=jnp.float32)

        acc = repeat(total // chunk, step, jnp.zeros((tile, a_ref.shape[1]), jnp.float32))
    base = []
    count = w_pieces[0].shape[0]
    halves = line_length // groups
    for c in range(halves):
        at = (place_ref[0] * halves + c - place_ref[1] + line_length) % line_length
        w = w_ref[pl.ds(pl.multiple_of(at * count, count), count), :]
        base.append(lax.dot_general(g_ref[...], w, NT, preferred_element_type=jnp.float32))
    out = jnp.concatenate(base, axis=1) + adapter_scale * acc
    out_ref[...] = out.astype(out_ref.dtype).reshape(out_ref.shape)


def out_part(place, packed, g_all, w_pieces, a_pieces, groups, rank):
    devices, depth, tokens = packed.shape
    outs = g_all.shape[1]
    rows, width = a_pieces[0].shape
    slots = line_length * rows
    both = 2
    pieces = [*a_pieces, *w_pieces]
    return call(
        lambda *refs: out_kernel(512, rank, groups, *refs),
        place,
        (devices // both,),
        [
            pl.BlockSpec((both, depth, tokens), lambda t, place: (t, 0, 0)),
            pl.BlockSpec((both * tokens, outs), lambda t, place: (t, 0)),
        ]
        + [pl.BlockSpec(piece.shape, lambda t, place: (0, 0)) for piece in pieces],
        pl.BlockSpec((both, tokens, width), lambda t, place: (t, 0, 0)),
        jax.ShapeDtypeStruct((devices, tokens, width), jnp.bfloat16),
        2 * devices * tokens * width * (slots + outs),
        2 * devices * tokens * (width + outs) + 2 * slots * width,
        "out_part",
        (packed, g_all, *pieces),
        [
            pltpu.VMEM((slots, width), jnp.bfloat16),
            pltpu.VMEM((line_length * w_pieces[0].shape[0], outs), jnp.bfloat16),
        ],
    )


def body(x, g, tok, adapter_slot, w, a, b):
    groups, inner = lax.axis_size("groups"), lax.axis_size("inner")
    gi, li, ji = lax.axis_index("groups"), lax.axis_index("line"), lax.axis_index("inner")
    place = jnp.stack([gi, li, ji]).astype(jnp.int32)
    size = groups * inner
    devices = line_length * inner
    tokens, model = x.shape
    outs = g.shape[1]
    resident, _, rank = a.shape
    share = resident // groups
    count = inner * resident
    halves = line_length // groups
    width = model // size
    part = width // halves
    adapters = adapter_slot.shape[0]
    capacity = max(2, 2 * tokens // adapters)

    up = [(i, i + 1) for i in range(line_length - 1)]
    down = [(i + 1, i) for i in range(line_length - 1)]

    def hop(pieces, away):
        left, right = pieces
        return [
            lax.ppermute(left, "line", up[away - 1 :]),
            lax.ppermute(right, "line", down[: line_length - away]),
        ]

    w_hops = [hop((w, w), 1)]
    w_hops.append(hop(w_hops[0], 2))

    a_mine = split_columns(place, jnp.swapaxes(a, 1, 2), groups, halves, inner, part)
    a_own = lax.all_to_all(a_mine, plane, 0, 0, tiled=True).reshape(count * rank, width)

    x_send = split_columns(place, x[None], groups, halves, inner, part)
    g_all = lax.all_gather(g, plane, axis=0, tiled=True)
    x_send, a_own, w_hops, g_all = lax.optimization_barrier((x_send, a_own, w_hops, g_all))
    w_hops.append(hop(w_hops[1], 3))
    x_cols = lax.all_to_all(x_send, plane, 0, 0, tiled=True)
    hops = [hop((a_own, a_own), 1)]
    hops.append(hop(hops[0], 2))

    matches = tok == lax.broadcasted_iota(jnp.int32, (tokens, adapters), 1)
    slot = jnp.sum(jnp.where(matches, adapter_slot[None, :], 0), axis=1)
    running = jnp.cumsum(matches.astype(jnp.int32), axis=0)
    within = jnp.sum(jnp.where(matches, running - 1, 0), axis=1)
    position = slot * capacity + within
    at = lax.broadcasted_iota(jnp.int32, (adapters * capacity, tokens), 0) == position[None, :]
    at = at.astype(jnp.bfloat16)

    def route(rows):
        rows = rows.reshape(devices, resident * capacity, rows.shape[1])
        rows = lax.all_to_all(rows, row, 0, 0, tiled=True)
        return rows.reshape(devices, resident, capacity, rows.shape[2])

    g_send = jnp.dot(at, g, preferred_element_type=jnp.float32).astype(jnp.bfloat16)
    g_send, x_cols, hops, w_hops = lax.optimization_barrier((g_send, x_cols, hops, w_hops))
    hops.append(hop(hops[1], 3))
    g_rows = route(g_send)
    back = jnp.einsum("hjct,jrt->hjcr", g_rows, b, preferred_element_type=jnp.float32)
    back = back.astype(jnp.bfloat16).reshape(devices, resident * capacity, rank)
    back = lax.all_to_all(back, row, 0, 0, tiled=True).reshape(adapters * capacity, rank)
    back = lax.dot_general(
        back, at, (((0,), (0,)), ((), ())), preferred_element_type=jnp.float32
    ).astype(jnp.bfloat16)
    owner, res = slot // resident, slot % resident
    slot_a = (owner // inner) * count + ((res // share) * inner + owner % inner) * share + res % share
    names = jnp.stack([slot, slot_a] + [slot] * 14).astype(jnp.bfloat16)
    packed = jnp.concatenate([back, names], axis=0)
    packed = jnp.broadcast_to(packed[None], (size,) + packed.shape)
    packed = lax.all_to_all(packed, plane, 0, 0, tiled=True)

    def send(c, got, away):
        sums = grad_a_step(place, packed, x_cols, c, got, away, groups, count, rank)
        ahead = [(i, i + 1) for i in range(line_length - away)]
        behind = [(i, i - 1) for i in range(away, line_length)]
        moved = (lax.ppermute(sums[0], "line", ahead), lax.ppermute(sums[1], "line", behind))
        return moved, sums[0]

    def own(c, got):
        p = grad_a_step(place, packed, x_cols, c, got, 0, groups, count, rank)
        return p.reshape(size, resident * rank, part)

    first, done = send(0, (), 3)
    packed, done = lax.optimization_barrier((packed, done))
    second, done = send(1, (), 3)


    a_pieces = [a_own] + [h[0] for h in hops] + [h[1] for h in hops]
    w_pieces = [w] + [h[0] for h in w_hops] + [h[1] for h in w_hops]
    a_pieces, done = lax.optimization_barrier((a_pieces, done))
    out_cols = out_part(place, packed, g_all, w_pieces, a_pieces, groups, rank)
    first, out_cols = lax.optimization_barrier((first, out_cols))
    out_back = lax.all_to_all(out_cols, plane, 0, 0, tiled=True)

    first, done = send(0, first, 2)
    second, done = lax.optimization_barrier((second, done))
    second, done = send(1, second, 2)
    first, done = lax.optimization_barrier((first, done))
    first, done = send(0, first, 1)
    second, done = lax.optimization_barrier((second, done))
    second, done = send(1, second, 1)

    a_pieces, done = lax.optimization_barrier((a_pieces, done))
    low = low_part(place, packed, x_cols, a_pieces, rank)
    low, out_back = lax.optimization_barrier((low, out_back))
    low = lax.all_to_all(low, plane, 0, 0, tiled=True)
    low = jnp.sum(low, axis=0).astype(jnp.bfloat16)
    low = lax.dot_general(at, low, NT, preferred_element_type=jnp.float32).astype(jnp.bfloat16)
    low = route(low)
    p_first = own(0, first)
    second, p_first = lax.optimization_barrier((second, p_first))
    p_back = [
        lax.all_to_all(p, plane, 0, 0, tiled=True) for p in (p_first, own(1, second))
    ]

    grad_b = jnp.einsum("hjcr,hjco->jro", low, g_rows, preferred_element_type=jnp.float32)
    grad_b = (adapter_scale * grad_b).astype(jnp.bfloat16)
    input_gradient = join_rows(place, out_back, groups, halves, inner, part)
    grad_a = join_slots(place, p_back, resident, groups, inner).swapaxes(1, 2)
    return input_gradient, grad_a, grad_b


def solution(mesh):
    groups, rows = mesh.shape["groups"], mesh.shape["row"]
    whole = ("groups", "line", "inner")
    split = Mesh(mesh.devices.reshape(groups, line_length, rows // line_length), whole)
    return jax.shard_map(
        body,
        mesh=split,
        in_specs=(
            P(whole, None),
            P(whole, None),
            P(whole, None),
            P(),
            P(row, None),
            P(row, None, None),
            P(row, None, None),
        ),
        out_specs=(P(whole, None), P(whole, None, None), P(whole, None, None)),
        check_vma=False,
    )
```

```python
import jax
import jax.numpy as jnp
from jax import lax
from jax.experimental import pallas as pl
from jax.experimental.pallas import tpu as pltpu
from jax.sharding import Mesh, PartitionSpec as P

adapter_scale = 2.0
line_length = 4
plane = ("groups", "inner")
row = ("line", "inner")
vmem_limit = 56 * 1024 * 1024
NT = (((1,), (1,)), ((), ()))


def call(kernel, place, grid, in_specs, out_specs, out_shape, flops, moved, name, args, scratch=()):
    return pl.pallas_call(
        kernel,
        grid_spec=pltpu.PrefetchScalarGridSpec(
            num_scalar_prefetch=1,
            grid=grid,
            in_specs=in_specs,
            out_specs=out_specs,
            scratch_shapes=scratch,
        ),
        out_shape=out_shape,
        compiler_params=pltpu.CompilerParams(vmem_limit_bytes=vmem_limit),
        cost_estimate=pl.CostEstimate(flops=flops, bytes_accessed=moved, transcendentals=0),
        name=name,
    )(place, *args)


def repeat(count, step, start):
    if count <= 4:
        for i in range(count):
            start = step(i, start)
        return start
    return lax.fori_loop(0, count, step, start)


def move(name, sources, in_blocks, in_maps, outs, out_blocks, out_maps, grid, kernel, place):
    moved = 0
    for shape in outs:
        size = 4
        for n in shape:
            size *= n
        moved += size
    return call(
        kernel,
        place,
        grid,
        [pl.BlockSpec(block, index) for block, index in zip(in_blocks, in_maps)],
        [pl.BlockSpec(block, index) for block, index in zip(out_blocks, out_maps)],
        [jax.ShapeDtypeStruct(shape, jnp.bfloat16) for shape in outs],
        0,
        moved,
        name,
        sources,
    )


def columns_of(q, c, halves, inner):
    return ((q // inner) * halves + c) * inner + q % inner


def split_columns(place, rows, groups, halves, inner, width):
    slots, rank, model = rows.shape
    size, share = groups * inner, max(1, slots // groups)
    group = lambda place: place[0] if slots >= groups else 0
    if width % 128:
        mine = lax.dynamic_slice_in_dim(rows, group(place) * share, share, 0)
        mine = mine.reshape(share * rank, groups, halves, inner, width)
        return mine.transpose(1, 3, 0, 2, 4).reshape(size, share * rank, halves * width)

    def kernel(place_ref, rows_ref, out_ref):
        for q in range(size):
            for c in range(halves):
                first = columns_of(q, c, halves, inner) * width
                out_ref[q, :, c * width : (c + 1) * width] = rows_ref[0, :, first : first + width]

    tile = min(rank, 64)
    steps = rank // tile
    return move(
        "split_columns", [rows], [(1, tile, model)],
        [lambda s, r, place: (group(place) * share + s, r, 0)],
        [(size, share * rank, halves * width)], [(size, tile, halves * width)],
        [lambda s, r, place: (0, s * steps + r, 0)], (share, steps), kernel, place,
    )[0]


def split_pieces(place, rows, groups, halves, inner, width):
    count, model = rows.shape
    size = groups * inner
    tile = min(count, 64)

    def kernel(place_ref, rows_ref, *out_refs):
        me = place_ref[0] * inner + place_ref[2]
        for m in range(size):
            for c in range(halves):
                first = pl.multiple_of(columns_of(me ^ m, c, halves, inner) * width, width)
                out_refs[m][:, c * width : (c + 1) * width] = rows_ref[:, pl.ds(first, width)]

    return move(
        "split_pieces", [rows], [(tile, model)], [lambda t, place: (t, 0)],
        [(count, halves * width)] * size, [(tile, halves * width)] * size,
        [lambda t, place: (t, 0)] * size, (count // tile,), kernel, place,
    )


def join_slots(place, parts, resident, groups, inner):
    size, rows, width = parts[0].shape
    halves, rank = len(parts), rows // resident
    if width % 128:
        parts = [p.reshape(groups, inner, rows, width) for p in parts]
        joined = jnp.stack(parts, axis=1).transpose(3, 0, 1, 2, 4)
        return joined.reshape(resident, rank, -1)

    def kernel(place_ref, *refs):
        for q in range(size):
            for c in range(halves):
                first = columns_of(q, c, halves, inner) * width
                refs[-1][0, :, first : first + width] = refs[c][q]

    return move(
        "join_slots", parts, [(size, rank, width)] * halves, [lambda r, place: (0, r, 0)] * halves,
        [(resident, rank, size * halves * width)], [(1, rank, size * halves * width)],
        [lambda r, place: (r, 0, 0)], (resident,), kernel, place,
    )[0]


def join_rows(place, rows, groups, halves, inner, part):
    size, tokens = rows.shape[:2]
    if part % 128:
        rows = rows.reshape(groups, inner, tokens, halves, part)
        return rows.transpose(2, 0, 3, 1, 4).reshape(tokens, -1)
    tile = min(tokens, 64)
    model = size * halves * part

    def kernel(place_ref, rows_ref, out_ref):
        for q in range(size):
            for c in range(halves):
                first = columns_of(q, c, halves, inner) * part
                out_ref[:, first : first + part] = rows_ref[q, :, c * part : (c + 1) * part]

    return move(
        "join_rows", [rows], [(size, tile, halves * part)], [lambda t, place: (0, t, 0)],
        [(tokens, model)], [(tile, model)], [lambda t, place: (t, 0)], (tokens // tile,),
        kernel, place,
    )[0]


def slot_sums(packed_ref, x_refs, me, rank, first, count):
    devices, _, tokens = packed_ref.shape
    width = x_refs[0].shape[-1]
    chunk = min(devices, 4)

    def step(c, total):
        columns = []
        for d in range(chunk):
            device = (c * chunk + d) ^ me
            back = packed_ref[device, :rank, :]
            slots = packed_ref[device, rank : rank + 1, :].astype(jnp.float32)
            rows = [
                back * (slots == (first + i).astype(jnp.float32)).astype(jnp.bfloat16)
                for i in range(count)
            ]
            columns.append(jnp.concatenate(rows, axis=0))
        if len(x_refs) > 1:
            x = jnp.concatenate([x_ref[...] for x_ref in x_refs], axis=0)
        else:
            x = x_refs[0][pl.ds(c * chunk, chunk)].reshape(chunk * tokens, width)
        return total + jnp.dot(
            jnp.concatenate(columns, axis=1), x, preferred_element_type=jnp.float32
        )

    return repeat(devices // chunk, step, jnp.zeros((count * rank, width), jnp.float32))


def by_group(x_refs, groups, use):
    if len(x_refs) == 1:
        use(x_refs)
        return
    local = len(x_refs) // groups
    for g in range(groups):

        @pl.when(pl.program_id(0) == g)
        def _(g=g):
            use(x_refs[g * local : (g + 1) * local])


def send_kernel(groups, number, slots_line, count, rank, away, place_ref, packed_ref, *refs):
    line = place_ref[1]
    x_refs, got, outs = refs[:number], refs[number:-2], refs[-2:]
    ways = ((line + away < line_length, line + away), (line >= away, line - away))
    for way, (inside, target) in enumerate(ways):

        def use(x_refs, way=way, target=target):
            first = target * slots_line + pl.program_id(1) * count
            total = slot_sums(packed_ref, x_refs, place_ref[2], rank, first, count)
            if got:
                total += got[way][0].astype(jnp.float32)
            outs[way][0] = total.astype(jnp.bfloat16)

        @pl.when(inside)
        def _(use=use):
            by_group(x_refs, groups, use)


def own_kernel(groups, number, slots_line, count, rank, place_ref, packed_ref, *refs):
    x_refs, (right_ref, left_ref, out_ref) = refs[:number], refs[number:]

    def use(x_refs):
        first = place_ref[1] * slots_line + pl.program_id(1) * count
        total = slot_sums(packed_ref, x_refs, place_ref[2], rank, first, count)
        total += right_ref[0].astype(jnp.float32) + left_ref[0].astype(jnp.float32)
        out_ref[0] = (adapter_scale * total).astype(jnp.bfloat16)

    by_group(x_refs, groups, use)


def grad_a_step(place, packed, x_cols, half, got, away, groups, slots_line, rank):
    devices, depth, tokens = packed.shape
    width = x_cols[0].shape[-1] // 2
    local = devices // groups
    count = 8
    rows = count * rank
    number = len(x_cols)
    if number > 1:
        x_specs = [pl.BlockSpec((tokens, width), lambda g, s, place: (0, half))] * number
    else:
        if width % 128:
            x_cols, half = [x_cols[0][:, :, half * width : (half + 1) * width]], 0
        x_specs = [pl.BlockSpec((local, tokens, width), lambda g, s, place: (g, 0, half))]
    block = pl.BlockSpec((1, rows, width), lambda g, s, place: (g, s, 0))
    final = pl.BlockSpec((1, rows, width), lambda g, s, place: (g ^ place[0], s, 0))
    shape = jax.ShapeDtypeStruct((groups, slots_line * rank, width), jnp.bfloat16)
    ways = 1 if away == 0 else 2
    if away == 0:
        kernel = lambda *refs: own_kernel(groups, number, slots_line, count, rank, *refs)
    else:
        kernel = lambda *refs: send_kernel(groups, number, slots_line, count, rank, away, *refs)
    return call(
        kernel,
        place,
        (groups, slots_line // count),
        [pl.BlockSpec((local, depth, tokens), lambda g, s, place: (g ^ place[0], 0, 0))]
        + x_specs
        + [block] * len(got),
        final if away == 0 else [block, block],
        shape if away == 0 else [shape, shape],
        ways * 2 * devices * tokens * width * slots_line * rank,
        2 * devices * tokens * width + 2 * groups * slots_line * rank * width * (ways + len(got)),
        "grad_a_step" + str(away),
        (packed, *x_cols, *got),
    )


def in_line(slots, place_ref, total):
    slots -= place_ref[1] * (total // line_length)
    return jnp.where(slots < 0, slots + total, slots)


def put_together(pieces, a_ref):
    @pl.when(pl.program_id(0) == 0)
    def _():
        rows = pieces[0].shape[0]
        a_ref[:rows] = pieces[0][...]
        for k in range(1, line_length):
            left, right = pieces[line_length - k], pieces[line_length - 1 + k]
            a_ref[k * rows : (k + 1) * rows] = left[...] + right[...]


def low_kernel(chunk, rank, number, place_ref, packed_ref, *refs):
    x_refs, pieces, (low_ref, a_ref) = refs[:number], refs[number:-2], refs[-2:]
    put_together(pieces, a_ref)
    slots = packed_ref[0].astype(jnp.float32).T[:, rank + 1 : rank + 2].astype(jnp.int32)
    slots = in_line(slots, place_ref, a_ref.shape[0] // rank)
    tile = slots.shape[0]
    lane_slot = lax.broadcasted_iota(jnp.int32, (tile, chunk), 1) // rank

    def use(x):
        def step(c, low):
            part = pl.ds(pl.multiple_of(c * chunk, chunk), chunk)
            hidden = lax.dot_general(x, a_ref[part], NT, preferred_element_type=jnp.float32)
            hidden = jnp.where(lane_slot + c * (chunk // rank) == slots, hidden, 0.0)
            for k in range(chunk // (2 * rank)):
                low += hidden[:, k * 2 * rank : (k + 1) * 2 * rank]
            return low

        start = jnp.zeros((tile, 2 * rank), jnp.float32)
        low = repeat(a_ref.shape[0] // chunk, step, start).T
        low_ref[0] = low[:rank] + low[rank:]

    if number == 1:
        use(x_refs[0][0])
    else:
        for m in range(number):

            @pl.when(pl.program_id(0) == m)
            def _(m=m):
                use(x_refs[m][...])


def low_part(place, packed, x_cols, a_pieces, inner, rank):
    devices, depth, tokens = packed.shape
    width = x_cols[0].shape[-1]
    rows = a_pieces[0].shape[0]
    slots = line_length * rows
    number = len(x_cols)
    mate = lambda t, place: (t ^ (place[0] * inner + place[2]), 0, 0)
    if number > 1:
        x_specs = [pl.BlockSpec((tokens, width), lambda t, place: (0, 0))] * number
    else:
        x_specs = [pl.BlockSpec((1, tokens, width), lambda t, place: (t, 0, 0))]
    return call(
        lambda *refs: low_kernel(512, rank, number, *refs),
        place,
        (devices,),
        [pl.BlockSpec((1, depth, tokens), mate)]
        + x_specs
        + [pl.BlockSpec((rows, width), lambda t, place: (0, 0))] * len(a_pieces),
        pl.BlockSpec((1, rank, tokens), mate),
        jax.ShapeDtypeStruct((devices, rank, tokens), jnp.float32),
        2 * devices * tokens * width * slots,
        2 * (devices * tokens + slots) * width,
        "low_part",
        (packed, *x_cols, *a_pieces),
        [pltpu.VMEM((slots, width), jnp.bfloat16)],
    )


def out_kernel(chunk, rank, groups, place_ref, packed_ref, g_ref, *refs):
    number = 2 * line_length - 1
    a_pieces, w_pieces, (out_ref, a_ref, w_ref) = refs[:number], refs[number:-3], refs[-3:]
    put_together(a_pieces, a_ref)
    put_together(w_pieces, w_ref)
    rows = jnp.concatenate([p.astype(jnp.float32).T for p in packed_ref[...]], axis=0)
    back, slots = rows[:, :rank], rows[:, rank + 1 : rank + 2].astype(jnp.int32)
    total = a_ref.shape[0]
    slots = in_line(slots, place_ref, total // rank)
    tile = back.shape[0]
    repeated = jnp.concatenate([back] * (chunk // rank), axis=1)
    lane_slot = lax.broadcasted_iota(jnp.int32, (tile, chunk), 1) // rank

    def masked(c):
        keep = lane_slot + c * (chunk // rank) == slots
        return jnp.where(keep, repeated, 0.0).astype(jnp.bfloat16)

    if total // chunk <= 4:
        wide = jnp.concatenate([masked(c) for c in range(total // chunk)], axis=1)
        acc = jnp.dot(wide, a_ref[...], preferred_element_type=jnp.float32)
    else:

        def step(c, acc):
            block = a_ref[pl.ds(pl.multiple_of(c * chunk, chunk), chunk), :]
            return acc + jnp.dot(masked(c), block, preferred_element_type=jnp.float32)

        acc = repeat(total // chunk, step, jnp.zeros((tile, a_ref.shape[1]), jnp.float32))
    base = []
    count = w_pieces[0].shape[0]
    halves = line_length // groups
    for c in range(halves):
        at = (place_ref[0] * halves + c - place_ref[1] + line_length) % line_length
        w = w_ref[pl.ds(pl.multiple_of(at * count, count), count), :]
        base.append(lax.dot_general(g_ref[...], w, NT, preferred_element_type=jnp.float32))
    out = jnp.concatenate(base, axis=1) + adapter_scale * acc
    out_ref[...] = out.astype(out_ref.dtype).reshape(out_ref.shape)


def out_part(place, packed, g_all, w_pieces, a_pieces, groups, rank):
    devices, depth, tokens = packed.shape
    outs = g_all.shape[1]
    rows, width = a_pieces[0].shape
    slots = line_length * rows
    both = 2
    pieces = [*a_pieces, *w_pieces]
    return call(
        lambda *refs: out_kernel(512, rank, groups, *refs),
        place,
        (devices // both,),
        [
            pl.BlockSpec((both, depth, tokens), lambda t, place: (t, 0, 0)),
            pl.BlockSpec((both * tokens, outs), lambda t, place: (t, 0)),
        ]
        + [pl.BlockSpec(piece.shape, lambda t, place: (0, 0)) for piece in pieces],
        pl.BlockSpec((both, tokens, width), lambda t, place: (t, 0, 0)),
        jax.ShapeDtypeStruct((devices, tokens, width), jnp.bfloat16),
        2 * devices * tokens * width * (slots + outs),
        2 * devices * tokens * (width + outs) + 2 * slots * width,
        "out_part",
        (packed, g_all, *pieces),
        [
            pltpu.VMEM((slots, width), jnp.bfloat16),
            pltpu.VMEM((line_length * w_pieces[0].shape[0], outs), jnp.bfloat16),
        ],
    )


def body(x, g, tok, adapter_slot, w, a, b):
    groups, inner = lax.axis_size("groups"), lax.axis_size("inner")
    gi, li, ji = lax.axis_index("groups"), lax.axis_index("line"), lax.axis_index("inner")
    place = jnp.stack([gi, li, ji]).astype(jnp.int32)
    size = groups * inner
    devices = line_length * inner
    tokens, model = x.shape
    outs = g.shape[1]
    resident, _, rank = a.shape
    share = resident // groups
    count = inner * resident
    halves = line_length // groups
    width = model // size
    part = width // halves
    adapters = adapter_slot.shape[0]
    capacity = max(2, 2 * tokens // adapters)

    up = [(i, i + 1) for i in range(line_length - 1)]
    down = [(i + 1, i) for i in range(line_length - 1)]

    def hop(pieces, away):
        left, right = pieces
        return [
            lax.ppermute(left, "line", up[away - 1 :]),
            lax.ppermute(right, "line", down[: line_length - away]),
        ]

    w_hops = [hop((w, w), 1)]
    w_hops.append(hop(w_hops[0], 2))

    a_mine = split_columns(place, jnp.swapaxes(a, 1, 2), groups, halves, inner, part)
    a_own = lax.all_to_all(a_mine, plane, 0, 0, tiled=True).reshape(count * rank, width)

    def meet(m):
        return lax.ppermute(x_sends[m], plane, [(i, i ^ m) for i in range(size)])

    direct = size == 8 and part % 128 == 0
    x_cols = {}
    if direct:
        x_sends = split_pieces(place, x, groups, halves, inner, part)
        x_cols = {0: x_sends[0], 1: meet(1), 2: meet(2), 4: meet(4)}
    else:
        x_far = split_columns(place, x[None], groups, halves, inner, part)
        x_far = lax.all_to_all(x_far, plane, 0, 0, tiled=True)
        x_cols = {0: x_far[jnp.arange(size) ^ (gi * inner + ji)]}

    matches = tok == lax.broadcasted_iota(jnp.int32, (tokens, adapters), 1)
    slot = jnp.sum(jnp.where(matches, adapter_slot[None, :], 0), axis=1)
    running = jnp.cumsum(matches.astype(jnp.int32), axis=0)
    within = jnp.sum(jnp.where(matches, running - 1, 0), axis=1)
    position = slot * capacity + within
    at = lax.broadcasted_iota(jnp.int32, (adapters * capacity, tokens), 0) == position[None, :]
    at = at.astype(jnp.bfloat16)

    def route(rows):
        rows = rows.reshape(devices, resident * capacity, rows.shape[1])
        rows = lax.all_to_all(rows, row, 0, 0, tiled=True)
        return rows.reshape(devices, resident, capacity, rows.shape[2])

    g_send = jnp.dot(at, g, preferred_element_type=jnp.float32).astype(jnp.bfloat16)
    g_send, a_own, x_cols, w_hops = lax.optimization_barrier((g_send, a_own, x_cols, w_hops))
    w_hops.append(hop(w_hops[1], 3))
    g_rows = route(g_send)
    back = jnp.einsum("hjct,jrt->hjcr", g_rows, b, preferred_element_type=jnp.float32)
    back = back.astype(jnp.bfloat16).reshape(devices, resident * capacity, rank)
    hops = [hop((a_own, a_own), 1)]
    if direct:
        x_cols.update({3: meet(3), 5: meet(5)})
    back, x_cols = lax.optimization_barrier((back, x_cols))
    if direct:
        x_cols.update({6: meet(6), 7: meet(7)})
    back = lax.all_to_all(back, row, 0, 0, tiled=True).reshape(adapters * capacity, rank)
    back = lax.dot_general(
        back, at, (((0,), (0,)), ((), ())), preferred_element_type=jnp.float32
    ).astype(jnp.bfloat16)
    owner, res = slot // resident, slot % resident
    slot_a = (owner // inner) * count + ((res // share) * inner + owner % inner) * share + res % share
    names = jnp.stack([slot, slot_a] + [slot] * 14).astype(jnp.bfloat16)
    packed = jnp.concatenate([back, names], axis=0)
    packed, x_cols, hops, w_hops = lax.optimization_barrier((packed, x_cols, hops, w_hops))
    packed = jnp.broadcast_to(packed[None], (size,) + packed.shape)
    packed = lax.all_to_all(packed, plane, 0, 0, tiled=True)
    x_cols = [x_cols[m] for m in range(len(x_cols))]
    g_own, x_cols = lax.optimization_barrier((g, x_cols))
    g_all = lax.all_gather(g_own, plane, axis=0, tiled=True)

    hops.append(hop(hops[0], 2))

    def send(c, got, away):
        sums = grad_a_step(place, packed, x_cols, c, got, away, groups, count, rank)
        ahead = [(i, i + 1) for i in range(line_length - away)]
        behind = [(i, i - 1) for i in range(away, line_length)]
        moved = (lax.ppermute(sums[0], "line", ahead), lax.ppermute(sums[1], "line", behind))
        return moved, sums[0]

    def own(c, got):
        p = grad_a_step(place, packed, x_cols, c, got, 0, groups, count, rank)
        return p.reshape(size, resident * rank, part)

    first, done = send(0, (), 3)
    packed, done = lax.optimization_barrier((packed, done))
    second, done = send(1, (), 3)

    first, hops[1], done = lax.optimization_barrier((first, hops[1], done))
    hops.append(hop(hops[1], 3))
    first, done = send(0, first, 2)
    second, done = lax.optimization_barrier((second, done))
    second, done = send(1, second, 2)

    a_pieces = [a_own] + [h[0] for h in hops] + [h[1] for h in hops]
    w_pieces = [w] + [h[0] for h in w_hops] + [h[1] for h in w_hops]
    a_pieces, done = lax.optimization_barrier((a_pieces, done))
    out_cols = out_part(place, packed, g_all, w_pieces, a_pieces, groups, rank)
    first, out_cols = lax.optimization_barrier((first, out_cols))
    first, done = send(0, first, 1)
    out_back = lax.all_to_all(out_cols, plane, 0, 0, tiled=True)

    second, done = lax.optimization_barrier((second, done))
    second, done = send(1, second, 1)

    a_pieces, done = lax.optimization_barrier((a_pieces, done))
    low = low_part(place, packed, x_cols, a_pieces, inner, rank)
    low = lax.all_to_all(low, plane, 0, 0, tiled=True)
    first, out_back, done = lax.optimization_barrier((first, out_back, done))
    p_first = own(0, first)
    second, p_first = lax.optimization_barrier((second, p_first))
    p_second = own(1, second)
    p_first, low = lax.optimization_barrier((p_first, low))
    p_back = [lax.all_to_all(p, plane, 0, 0, tiled=True) for p in (p_first, p_second)]
    low = jnp.sum(low, axis=0).astype(jnp.bfloat16)
    low = lax.dot_general(at, low, NT, preferred_element_type=jnp.float32).astype(jnp.bfloat16)
    low = route(low)

    grad_b = jnp.einsum("hjcr,hjco->jro", low, g_rows, preferred_element_type=jnp.float32)
    grad_b = (adapter_scale * grad_b).astype(jnp.bfloat16)
    input_gradient = join_rows(place, out_back, groups, halves, inner, part)
    grad_a = join_slots(place, p_back, resident, groups, inner).swapaxes(1, 2)
    return input_gradient, grad_a, grad_b


def solution(mesh):
    groups, rows = mesh.shape["groups"], mesh.shape["row"]
    whole = ("groups", "line", "inner")
    split = Mesh(mesh.devices.reshape(groups, line_length, rows // line_length), whole)
    return jax.shard_map(
        body,
        mesh=split,
        in_specs=(
            P(whole, None),
            P(whole, None),
            P(whole, None),
            P(),
            P(row, None),
            P(row, None, None),
            P(row, None, None),
        ),
        out_specs=(P(whole, None), P(whole, None, None), P(whole, None, None)),
        check_vma=False,
    )
```

```python
import jax
import jax.numpy as jnp
from jax import lax
from jax.experimental import pallas as pl
from jax.experimental.pallas import tpu as pltpu
from jax.sharding import Mesh, PartitionSpec as P

adapter_scale = 2.0
line_length = 4
plane = ("groups", "inner")
row = ("line", "inner")
vmem_limit = 56 * 1024 * 1024
NT = (((1,), (1,)), ((), ()))


def call(kernel, place, grid, in_specs, out_specs, out_shape, flops, moved, name, args, scratch=()):
    return pl.pallas_call(
        kernel,
        grid_spec=pltpu.PrefetchScalarGridSpec(
            num_scalar_prefetch=1,
            grid=grid,
            in_specs=in_specs,
            out_specs=out_specs,
            scratch_shapes=scratch,
        ),
        out_shape=out_shape,
        compiler_params=pltpu.CompilerParams(vmem_limit_bytes=vmem_limit),
        cost_estimate=pl.CostEstimate(flops=flops, bytes_accessed=moved, transcendentals=0),
        name=name,
    )(place, *args)


def repeat(count, step, start):
    if count <= 4:
        for i in range(count):
            start = step(i, start)
        return start
    return lax.fori_loop(0, count, step, start)


def move(name, sources, in_blocks, in_maps, outs, out_blocks, out_maps, grid, kernel, place):
    moved = 0
    for shape in outs:
        size = 4
        for n in shape:
            size *= n
        moved += size
    return call(
        kernel,
        place,
        grid,
        [pl.BlockSpec(block, index) for block, index in zip(in_blocks, in_maps)],
        [pl.BlockSpec(block, index) for block, index in zip(out_blocks, out_maps)],
        [jax.ShapeDtypeStruct(shape, jnp.bfloat16) for shape in outs],
        0,
        moved,
        name,
        sources,
    )


def columns_of(q, c, halves, inner):
    return ((q // inner) * halves + c) * inner + q % inner


def split_columns(place, rows, groups, halves, inner, width):
    slots, rank, model = rows.shape
    size, share = groups * inner, max(1, slots // groups)
    group = lambda place: place[0] if slots >= groups else 0
    if width % 128:
        mine = lax.dynamic_slice_in_dim(rows, group(place) * share, share, 0)
        mine = mine.reshape(share * rank, groups, halves, inner, width)
        return mine.transpose(1, 3, 0, 2, 4).reshape(size, share * rank, halves * width)

    def kernel(place_ref, rows_ref, out_ref):
        for q in range(size):
            for c in range(halves):
                first = columns_of(q, c, halves, inner) * width
                out_ref[q, :, c * width : (c + 1) * width] = rows_ref[0, :, first : first + width]

    tile = min(rank, 64)
    steps = rank // tile
    return move(
        "split_columns", [rows], [(1, tile, model)],
        [lambda s, r, place: (group(place) * share + s, r, 0)],
        [(size, share * rank, halves * width)], [(size, tile, halves * width)],
        [lambda s, r, place: (0, s * steps + r, 0)], (share, steps), kernel, place,
    )[0]


def split_pieces(place, rows, groups, halves, inner, width):
    count, model = rows.shape
    size = groups * inner
    tile = min(count, 64)

    def kernel(place_ref, rows_ref, *out_refs):
        me = place_ref[0] * inner + place_ref[2]
        for m in range(size):
            for c in range(halves):
                first = pl.multiple_of(columns_of(me ^ m, c, halves, inner) * width, width)
                out_refs[m][:, c * width : (c + 1) * width] = rows_ref[:, pl.ds(first, width)]

    return move(
        "split_pieces", [rows], [(tile, model)], [lambda t, place: (t, 0)],
        [(count, halves * width)] * size, [(tile, halves * width)] * size,
        [lambda t, place: (t, 0)] * size, (count // tile,), kernel, place,
    )


def join_slots(place, parts, resident, groups, inner):
    size, rows, width = parts[0].shape
    halves, rank = len(parts), rows // resident
    if width % 128:
        parts = [p.reshape(groups, inner, rows, width) for p in parts]
        joined = jnp.stack(parts, axis=1).transpose(3, 0, 1, 2, 4)
        return joined.reshape(resident, rank, -1)

    def kernel(place_ref, *refs):
        for q in range(size):
            for c in range(halves):
                first = columns_of(q, c, halves, inner) * width
                refs[-1][0, :, first : first + width] = refs[c][q]

    return move(
        "join_slots", parts, [(size, rank, width)] * halves, [lambda r, place: (0, r, 0)] * halves,
        [(resident, rank, size * halves * width)], [(1, rank, size * halves * width)],
        [lambda r, place: (r, 0, 0)], (resident,), kernel, place,
    )[0]


def join_rows(place, rows, groups, halves, inner, part):
    size, tokens = rows.shape[:2]
    if part % 128:
        rows = rows.reshape(groups, inner, tokens, halves, part)
        return rows.transpose(2, 0, 3, 1, 4).reshape(tokens, -1)
    tile = min(tokens, 64)
    model = size * halves * part

    def kernel(place_ref, rows_ref, out_ref):
        for q in range(size):
            for c in range(halves):
                first = columns_of(q, c, halves, inner) * part
                out_ref[:, first : first + part] = rows_ref[q, :, c * part : (c + 1) * part]

    return move(
        "join_rows", [rows], [(size, tile, halves * part)], [lambda t, place: (0, t, 0)],
        [(tokens, model)], [(tile, model)], [lambda t, place: (t, 0)], (tokens // tile,),
        kernel, place,
    )[0]


def slot_sums(packed_ref, x_refs, me, rank, first, count):
    devices, _, tokens = packed_ref.shape
    width = x_refs[0].shape[-1]
    chunk = min(devices, 4)

    def step(c, total):
        columns = []
        for d in range(chunk):
            device = (c * chunk + d) ^ me
            back = packed_ref[device, :rank, :]
            slots = packed_ref[device, rank : rank + 1, :].astype(jnp.float32)
            rows = [
                back * (slots == (first + i).astype(jnp.float32)).astype(jnp.bfloat16)
                for i in range(count)
            ]
            columns.append(jnp.concatenate(rows, axis=0))
        if len(x_refs) > 1:
            x = jnp.concatenate([x_ref[...] for x_ref in x_refs], axis=0)
        else:
            x = x_refs[0][pl.ds(c * chunk, chunk)].reshape(chunk * tokens, width)
        return total + jnp.dot(
            jnp.concatenate(columns, axis=1), x, preferred_element_type=jnp.float32
        )

    return repeat(devices // chunk, step, jnp.zeros((count * rank, width), jnp.float32))


def by_group(x_refs, groups, use):
    if len(x_refs) == 1:
        use(x_refs)
        return
    local = len(x_refs) // groups
    for g in range(groups):

        @pl.when(pl.program_id(0) == g)
        def _(g=g):
            use(x_refs[g * local : (g + 1) * local])


def send_kernel(groups, number, slots_line, count, rank, away, place_ref, packed_ref, *refs):
    line = place_ref[1]
    ways_out = 2 if away == 1 else 1
    x_refs, got, outs = refs[:number], refs[number:-ways_out], refs[-ways_out:]
    ways = ((line + away < line_length, line + away), (line >= away, line - away))
    for way, (inside, target) in enumerate(ways):

        def use(x_refs, way=way, target=target):
            first = target * slots_line + pl.program_id(1) * count
            total = slot_sums(packed_ref, x_refs, place_ref[2], rank, first, count)
            if got:
                total += got[way % len(got)][0].astype(jnp.float32)
            outs[way % ways_out][0] = total.astype(jnp.bfloat16)

        @pl.when(inside)
        def _(use=use):
            by_group(x_refs, groups, use)


def own_kernel(groups, number, slots_line, count, rank, place_ref, packed_ref, *refs):
    x_refs, (right_ref, left_ref, out_ref) = refs[:number], refs[number:]

    def use(x_refs):
        first = place_ref[1] * slots_line + pl.program_id(1) * count
        total = slot_sums(packed_ref, x_refs, place_ref[2], rank, first, count)
        total += right_ref[0].astype(jnp.float32) + left_ref[0].astype(jnp.float32)
        out_ref[0] = (adapter_scale * total).astype(jnp.bfloat16)

    by_group(x_refs, groups, use)


def grad_a_step(place, packed, x_cols, half, got, away, groups, slots_line, rank):
    devices, depth, tokens = packed.shape
    width = x_cols[0].shape[-1] // 2
    local = devices // groups
    count = 8
    rows = count * rank
    number = len(x_cols)
    if number > 1:
        x_specs = [pl.BlockSpec((tokens, width), lambda g, s, place: (0, half))] * number
    else:
        if width % 128:
            x_cols, half = [x_cols[0][:, :, half * width : (half + 1) * width]], 0
        x_specs = [pl.BlockSpec((local, tokens, width), lambda g, s, place: (g, 0, half))]
    block = pl.BlockSpec((1, rows, width), lambda g, s, place: (g, s, 0))
    final = pl.BlockSpec((1, rows, width), lambda g, s, place: (g ^ place[0], s, 0))
    shape = jax.ShapeDtypeStruct((groups, slots_line * rank, width), jnp.bfloat16)
    ways = 2 if away == 1 else 1
    if away == 0:
        kernel = lambda *refs: own_kernel(groups, number, slots_line, count, rank, *refs)
    else:
        kernel = lambda *refs: send_kernel(groups, number, slots_line, count, rank, away, *refs)
    return call(
        kernel,
        place,
        (groups, slots_line // count),
        [pl.BlockSpec((local, depth, tokens), lambda g, s, place: (g ^ place[0], 0, 0))]
        + x_specs
        + [block] * len(got),
        final if away == 0 else [block] * ways,
        shape if away == 0 else [shape] * ways,
        ways * 2 * devices * tokens * width * slots_line * rank,
        2 * devices * tokens * width + 2 * groups * slots_line * rank * width * (ways + len(got)),
        "grad_a_step" + str(away),
        (packed, *x_cols, *got),
    )


def in_line(slots, place_ref, total):
    slots -= place_ref[1] * (total // line_length)
    return jnp.where(slots < 0, slots + total, slots)


def put_together(pieces, line, a_ref):
    @pl.when(pl.program_id(0) == 0)
    def _():
        rows = pieces[0].shape[0]
        a_ref[:rows] = pieces[0][...]
        for k in range(1, line_length):
            part = pl.ds(k * rows, rows)

            @pl.when(line + k < line_length)
            def _(k=k, part=part):
                a_ref[part] = pieces[line_length - 1 + k][...]

            @pl.when(line + k >= line_length)
            def _(k=k, part=part):
                a_ref[part] = pieces[line_length - k][...]


def low_kernel(chunk, rank, number, place_ref, packed_ref, *refs):
    x_refs, pieces, (low_ref, a_ref) = refs[:number], refs[number:-2], refs[-2:]
    put_together(pieces, place_ref[1], a_ref)
    slots = packed_ref[0].astype(jnp.float32).T[:, rank + 1 : rank + 2].astype(jnp.int32)
    slots = in_line(slots, place_ref, a_ref.shape[0] // rank)
    tile = slots.shape[0]
    lane_slot = lax.broadcasted_iota(jnp.int32, (tile, chunk), 1) // rank

    def use(x):
        def step(c, low):
            part = pl.ds(pl.multiple_of(c * chunk, chunk), chunk)
            hidden = lax.dot_general(x, a_ref[part], NT, preferred_element_type=jnp.float32)
            hidden = jnp.where(lane_slot + c * (chunk // rank) == slots, hidden, 0.0)
            for k in range(chunk // (2 * rank)):
                low += hidden[:, k * 2 * rank : (k + 1) * 2 * rank]
            return low

        start = jnp.zeros((tile, 2 * rank), jnp.float32)
        low = repeat(a_ref.shape[0] // chunk, step, start).T
        low_ref[0] = low[:rank] + low[rank:]

    if number == 1:
        use(x_refs[0][0])
    else:
        for m in range(number):

            @pl.when(pl.program_id(0) == m)
            def _(m=m):
                use(x_refs[m][...])


def low_part(place, packed, x_cols, a_pieces, inner, rank):
    devices, depth, tokens = packed.shape
    width = x_cols[0].shape[-1]
    rows = a_pieces[0].shape[0]
    slots = line_length * rows
    number = len(x_cols)
    mate = lambda t, place: (t ^ (place[0] * inner + place[2]), 0, 0)
    if number > 1:
        x_specs = [pl.BlockSpec((tokens, width), lambda t, place: (0, 0))] * number
    else:
        x_specs = [pl.BlockSpec((1, tokens, width), lambda t, place: (t, 0, 0))]
    return call(
        lambda *refs: low_kernel(512, rank, number, *refs),
        place,
        (devices,),
        [pl.BlockSpec((1, depth, tokens), mate)]
        + x_specs
        + [pl.BlockSpec((rows, width), lambda t, place: (0, 0))] * len(a_pieces),
        pl.BlockSpec((1, rank, tokens), mate),
        jax.ShapeDtypeStruct((devices, rank, tokens), jnp.float32),
        2 * devices * tokens * width * slots,
        2 * (devices * tokens + slots) * width,
        "low_part",
        (packed, *x_cols, *a_pieces),
        [pltpu.VMEM((slots, width), jnp.bfloat16)],
    )


def out_kernel(chunk, rank, groups, place_ref, packed_ref, g_ref, *refs):
    number = 2 * line_length - 1
    a_pieces, w_pieces, (out_ref, a_ref, w_ref) = refs[:number], refs[number:-3], refs[-3:]
    put_together(a_pieces, place_ref[1], a_ref)
    put_together(w_pieces, place_ref[1], w_ref)
    rows = jnp.concatenate([p.astype(jnp.float32).T for p in packed_ref[...]], axis=0)
    back, slots = rows[:, :rank], rows[:, rank + 1 : rank + 2].astype(jnp.int32)
    total = a_ref.shape[0]
    slots = in_line(slots, place_ref, total // rank)
    tile = back.shape[0]
    repeated = jnp.concatenate([back] * (chunk // rank), axis=1)
    lane_slot = lax.broadcasted_iota(jnp.int32, (tile, chunk), 1) // rank

    def masked(c):
        keep = lane_slot + c * (chunk // rank) == slots
        return jnp.where(keep, repeated, 0.0).astype(jnp.bfloat16)

    if total // chunk <= 4:
        wide = jnp.concatenate([masked(c) for c in range(total // chunk)], axis=1)
        acc = jnp.dot(wide, a_ref[...], preferred_element_type=jnp.float32)
    else:

        def step(c, acc):
            block = a_ref[pl.ds(pl.multiple_of(c * chunk, chunk), chunk), :]
            return acc + jnp.dot(masked(c), block, preferred_element_type=jnp.float32)

        acc = repeat(total // chunk, step, jnp.zeros((tile, a_ref.shape[1]), jnp.float32))
    base = []
    count = w_pieces[0].shape[0]
    halves = line_length // groups
    for c in range(halves):
        at = (place_ref[0] * halves + c - place_ref[1] + line_length) % line_length
        w = w_ref[pl.ds(pl.multiple_of(at * count, count), count), :]
        base.append(lax.dot_general(g_ref[...], w, NT, preferred_element_type=jnp.float32))
    out = jnp.concatenate(base, axis=1) + adapter_scale * acc
    out_ref[...] = out.astype(out_ref.dtype).reshape(out_ref.shape)


def out_part(place, packed, g_all, w_pieces, a_pieces, groups, rank):
    devices, depth, tokens = packed.shape
    outs = g_all.shape[1]
    rows, width = a_pieces[0].shape
    slots = line_length * rows
    both = 2
    pieces = [*a_pieces, *w_pieces]
    return call(
        lambda *refs: out_kernel(512, rank, groups, *refs),
        place,
        (devices // both,),
        [
            pl.BlockSpec((both, depth, tokens), lambda t, place: (t, 0, 0)),
            pl.BlockSpec((both * tokens, outs), lambda t, place: (t, 0)),
        ]
        + [pl.BlockSpec(piece.shape, lambda t, place: (0, 0)) for piece in pieces],
        pl.BlockSpec((both, tokens, width), lambda t, place: (t, 0, 0)),
        jax.ShapeDtypeStruct((devices, tokens, width), jnp.bfloat16),
        2 * devices * tokens * width * (slots + outs),
        2 * devices * tokens * (width + outs) + 2 * slots * width,
        "out_part",
        (packed, g_all, *pieces),
        [
            pltpu.VMEM((slots, width), jnp.bfloat16),
            pltpu.VMEM((line_length * w_pieces[0].shape[0], outs), jnp.bfloat16),
        ],
    )


def body(x, g, tok, adapter_slot, w, a, b):
    groups, inner = lax.axis_size("groups"), lax.axis_size("inner")
    gi, li, ji = lax.axis_index("groups"), lax.axis_index("line"), lax.axis_index("inner")
    place = jnp.stack([gi, li, ji]).astype(jnp.int32)
    size = groups * inner
    devices = line_length * inner
    tokens, model = x.shape
    outs = g.shape[1]
    resident, _, rank = a.shape
    share = resident // groups
    count = inner * resident
    halves = line_length // groups
    width = model // size
    part = width // halves
    adapters = adapter_slot.shape[0]
    capacity = max(2, 2 * tokens // adapters)

    up = [(i, i + 1) for i in range(line_length - 1)]
    down = [(i + 1, i) for i in range(line_length - 1)]

    def hop(pieces, away):
        left, right = pieces
        if away == line_length - 1:
            both = lax.ppermute(
                jnp.where(li == line_length - 2, left, right), "line", up[away - 1 :] + down[:1]
            )
            return [both, both]
        return [
            lax.ppermute(left, "line", up[away - 1 :]),
            lax.ppermute(right, "line", down[: line_length - away]),
        ]

    w_hops = [hop((w, w), 1)]
    w_hops.append(hop(w_hops[0], 2))

    a_mine = split_columns(place, jnp.swapaxes(a, 1, 2), groups, halves, inner, part)
    a_own = lax.all_to_all(a_mine, plane, 0, 0, tiled=True).reshape(count * rank, width)

    def meet(m):
        return lax.ppermute(x_sends[m], plane, [(i, i ^ m) for i in range(size)])

    direct = size == 8 and part % 128 == 0
    x_cols = {}
    if direct:
        x_sends = split_pieces(place, x, groups, halves, inner, part)
        x_cols = {0: x_sends[0], 1: meet(1), 2: meet(2), 4: meet(4)}
    else:
        x_far = split_columns(place, x[None], groups, halves, inner, part)
        x_far = lax.all_to_all(x_far, plane, 0, 0, tiled=True)
        x_cols = {0: x_far[jnp.arange(size) ^ (gi * inner + ji)]}

    matches = tok == lax.broadcasted_iota(jnp.int32, (tokens, adapters), 1)
    slot = jnp.sum(jnp.where(matches, adapter_slot[None, :], 0), axis=1)
    running = jnp.cumsum(matches.astype(jnp.int32), axis=0)
    within = jnp.sum(jnp.where(matches, running - 1, 0), axis=1)
    position = slot * capacity + within
    at = lax.broadcasted_iota(jnp.int32, (adapters * capacity, tokens), 0) == position[None, :]
    at = at.astype(jnp.bfloat16)

    def route(rows):
        rows = rows.reshape(devices, resident * capacity, rows.shape[1])
        rows = lax.all_to_all(rows, row, 0, 0, tiled=True)
        return rows.reshape(devices, resident, capacity, rows.shape[2])

    g_send = jnp.dot(at, g, preferred_element_type=jnp.float32).astype(jnp.bfloat16)
    g_send, a_own, x_cols, w_hops = lax.optimization_barrier((g_send, a_own, x_cols, w_hops))
    w_hops.append(hop(w_hops[1], 3))
    g_rows = route(g_send)
    back = jnp.einsum("hjct,jrt->hjcr", g_rows, b, preferred_element_type=jnp.float32)
    back = back.astype(jnp.bfloat16).reshape(devices, resident * capacity, rank)
    hops = [hop((a_own, a_own), 1)]
    if direct:
        x_cols.update({3: meet(3), 5: meet(5)})
    back, x_cols = lax.optimization_barrier((back, x_cols))
    if direct:
        x_cols.update({6: meet(6), 7: meet(7)})
    back = lax.all_to_all(back, row, 0, 0, tiled=True).reshape(adapters * capacity, rank)
    back = lax.dot_general(
        back, at, (((0,), (0,)), ((), ())), preferred_element_type=jnp.float32
    ).astype(jnp.bfloat16)
    owner, res = slot // resident, slot % resident
    slot_a = (owner // inner) * count + ((res // share) * inner + owner % inner) * share + res % share
    names = jnp.stack([slot, slot_a] + [slot] * 14).astype(jnp.bfloat16)
    packed = jnp.concatenate([back, names], axis=0)
    packed, x_cols, hops, w_hops = lax.optimization_barrier((packed, x_cols, hops, w_hops))
    packed = jnp.broadcast_to(packed[None], (size,) + packed.shape)
    packed = lax.all_to_all(packed, plane, 0, 0, tiled=True)
    x_cols = [x_cols[m] for m in range(len(x_cols))]
    g_own, x_cols = lax.optimization_barrier((g, x_cols))
    g_all = lax.all_gather(g_own, plane, axis=0, tiled=True)

    hops.append(hop(hops[0], 2))

    def send(c, got, away):
        sums = grad_a_step(place, packed, x_cols, c, got, away, groups, count, rank)
        ahead = [(i, i + 1) for i in range(line_length - away)]
        behind = [(i, i - 1) for i in range(away, line_length)]
        if away == line_length - 1:
            moved = (lax.ppermute(sums[0], "line", ahead + behind),)
        else:
            moved = (lax.ppermute(sums[0], "line", ahead), lax.ppermute(sums[-1], "line", behind))
        return moved, sums[0]

    def own(c, got):
        p = grad_a_step(place, packed, x_cols, c, got, 0, groups, count, rank)
        return p.reshape(size, resident * rank, part)

    first, done = send(0, (), 3)
    packed, done = lax.optimization_barrier((packed, done))
    second, done = send(1, (), 3)

    first, hops[1], done = lax.optimization_barrier((first, hops[1], done))
    hops.append(hop(hops[1], 3))
    first, done = send(0, first, 2)
    second, done = lax.optimization_barrier((second, done))
    second, done = send(1, second, 2)

    a_pieces = [a_own] + [h[0] for h in hops] + [h[1] for h in hops]
    w_pieces = [w] + [h[0] for h in w_hops] + [h[1] for h in w_hops]
    a_pieces, done = lax.optimization_barrier((a_pieces, done))
    out_cols = out_part(place, packed, g_all, w_pieces, a_pieces, groups, rank)
    first, out_cols = lax.optimization_barrier((first, out_cols))
    first, done = send(0, first, 1)
    out_back = lax.all_to_all(out_cols, plane, 0, 0, tiled=True)

    second, done = lax.optimization_barrier((second, done))
    second, done = send(1, second, 1)

    a_pieces, done = lax.optimization_barrier((a_pieces, done))
    low = low_part(place, packed, x_cols, a_pieces, inner, rank)
    low = lax.all_to_all(low, plane, 0, 0, tiled=True)
    first, out_back, done = lax.optimization_barrier((first, out_back, done))
    p_first = own(0, first)
    second, p_first = lax.optimization_barrier((second, p_first))
    p_second = own(1, second)
    p_first, low = lax.optimization_barrier((p_first, low))
    p_back = [lax.all_to_all(p, plane, 0, 0, tiled=True) for p in (p_first, p_second)]
    low = jnp.sum(low, axis=0).astype(jnp.bfloat16)
    low = lax.dot_general(at, low, NT, preferred_element_type=jnp.float32).astype(jnp.bfloat16)
    low, p_back = lax.optimization_barrier((low, p_back))
    low = route(low)
    grad_b = jnp.einsum("hjcr,hjco->jro", low, g_rows, preferred_element_type=jnp.float32)
    grad_b = (adapter_scale * grad_b).astype(jnp.bfloat16)
    input_gradient = join_rows(place, out_back, groups, halves, inner, part)
    grad_a = join_slots(place, p_back, resident, groups, inner).swapaxes(1, 2)
    return input_gradient, grad_a, grad_b


def solution(mesh):
    groups, rows = mesh.shape["groups"], mesh.shape["row"]
    whole = ("groups", "line", "inner")
    split = Mesh(mesh.devices.reshape(groups, line_length, rows // line_length), whole)
    return jax.shard_map(
        body,
        mesh=split,
        in_specs=(
            P(whole, None),
            P(whole, None),
            P(whole, None),
            P(),
            P(row, None),
            P(row, None, None),
            P(row, None, None),
        ),
        out_specs=(P(whole, None), P(whole, None, None), P(whole, None, None)),
        check_vma=False,
    )
```

```python
import jax
import jax.numpy as jnp
from jax import lax
from jax.experimental import pallas as pl
from jax.experimental.pallas import tpu as pltpu
from jax.sharding import Mesh, PartitionSpec as P

adapter_scale = 2.0
line_length = 4
plane = ("groups", "inner")
row = ("line", "inner")
vmem_limit = 56 * 1024 * 1024
NT = (((1,), (1,)), ((), ()))


def call(kernel, place, grid, in_specs, out_specs, out_shape, flops, moved, name, args, scratch=()):
    return pl.pallas_call(
        kernel,
        grid_spec=pltpu.PrefetchScalarGridSpec(
            num_scalar_prefetch=1,
            grid=grid,
            in_specs=in_specs,
            out_specs=out_specs,
            scratch_shapes=scratch,
        ),
        out_shape=out_shape,
        compiler_params=pltpu.CompilerParams(vmem_limit_bytes=vmem_limit),
        cost_estimate=pl.CostEstimate(flops=flops, bytes_accessed=moved, transcendentals=0),
        name=name,
    )(place, *args)


def repeat(count, step, start):
    if count <= 4:
        for i in range(count):
            start = step(i, start)
        return start
    return lax.fori_loop(0, count, step, start)


def move(name, sources, in_blocks, in_maps, outs, out_blocks, out_maps, grid, kernel, place):
    moved = 0
    for shape in outs:
        size = 4
        for n in shape:
            size *= n
        moved += size
    return call(
        kernel,
        place,
        grid,
        [pl.BlockSpec(block, index) for block, index in zip(in_blocks, in_maps)],
        [pl.BlockSpec(block, index) for block, index in zip(out_blocks, out_maps)],
        [jax.ShapeDtypeStruct(shape, jnp.bfloat16) for shape in outs],
        0,
        moved,
        name,
        sources,
    )


def columns_of(q, c, halves, inner):
    return ((q // inner) * halves + c) * inner + q % inner


def split_columns(place, rows, groups, halves, inner, width):
    slots, rank, model = rows.shape
    size, share = groups * inner, max(1, slots // groups)
    group = lambda place: place[0] if slots >= groups else 0
    if width % 128:
        mine = lax.dynamic_slice_in_dim(rows, group(place) * share, share, 0)
        mine = mine.reshape(share * rank, groups, halves, inner, width)
        return mine.transpose(1, 3, 0, 2, 4).reshape(size, share * rank, halves * width)

    def kernel(place_ref, rows_ref, out_ref):
        for q in range(size):
            for c in range(halves):
                first = columns_of(q, c, halves, inner) * width
                out_ref[q, :, c * width : (c + 1) * width] = rows_ref[0, :, first : first + width]

    tile = min(rank, 64)
    steps = rank // tile
    return move(
        "split_columns", [rows], [(1, tile, model)],
        [lambda s, r, place: (group(place) * share + s, r, 0)],
        [(size, share * rank, halves * width)], [(size, tile, halves * width)],
        [lambda s, r, place: (0, s * steps + r, 0)], (share, steps), kernel, place,
    )[0]


def split_pieces(place, rows, groups, halves, inner, width):
    count, model = rows.shape
    size = groups * inner
    tile = min(count, 64)

    def kernel(place_ref, rows_ref, *out_refs):
        me = place_ref[0] * inner + place_ref[2]
        for m in range(size):
            for c in range(halves):
                first = pl.multiple_of(columns_of(me ^ m, c, halves, inner) * width, width)
                out_refs[m][:, c * width : (c + 1) * width] = rows_ref[:, pl.ds(first, width)]

    return move(
        "split_pieces", [rows], [(tile, model)], [lambda t, place: (t, 0)],
        [(count, halves * width)] * size, [(tile, halves * width)] * size,
        [lambda t, place: (t, 0)] * size, (count // tile,), kernel, place,
    )


def join_slots(place, parts, resident, groups, inner):
    size, rows, width = parts[0].shape
    halves, rank = len(parts), rows // resident
    if width % 128:
        parts = [p.reshape(groups, inner, rows, width) for p in parts]
        joined = jnp.stack(parts, axis=1).transpose(3, 0, 1, 2, 4)
        return joined.reshape(resident, rank, -1)

    def kernel(place_ref, *refs):
        for q in range(size):
            for c in range(halves):
                first = columns_of(q, c, halves, inner) * width
                refs[-1][0, :, first : first + width] = refs[c][q]

    return move(
        "join_slots", parts, [(size, rank, width)] * halves, [lambda r, place: (0, r, 0)] * halves,
        [(resident, rank, size * halves * width)], [(1, rank, size * halves * width)],
        [lambda r, place: (r, 0, 0)], (resident,), kernel, place,
    )[0]


def join_rows(place, rows, groups, halves, inner, part):
    size, tokens = rows.shape[:2]
    if part % 128:
        rows = rows.reshape(groups, inner, tokens, halves, part)
        return rows.transpose(2, 0, 3, 1, 4).reshape(tokens, -1)
    tile = min(tokens, 64)
    model = size * halves * part

    def kernel(place_ref, rows_ref, out_ref):
        for q in range(size):
            for c in range(halves):
                first = columns_of(q, c, halves, inner) * part
                out_ref[:, first : first + part] = rows_ref[q, :, c * part : (c + 1) * part]

    return move(
        "join_rows", [rows], [(size, tile, halves * part)], [lambda t, place: (0, t, 0)],
        [(tokens, model)], [(tile, model)], [lambda t, place: (t, 0)], (tokens // tile,),
        kernel, place,
    )[0]


def slot_sums(packed_ref, x_refs, me, rank, first, count):
    devices, _, tokens = packed_ref.shape
    width = x_refs[0].shape[-1]
    chunk = min(devices, 4)

    def step(c, total):
        columns = []
        for d in range(chunk):
            device = (c * chunk + d) ^ me
            back = packed_ref[device, :rank, :]
            slots = packed_ref[device, rank : rank + 1, :].astype(jnp.float32)
            rows = [
                back * (slots == (first + i).astype(jnp.float32)).astype(jnp.bfloat16)
                for i in range(count)
            ]
            columns.append(jnp.concatenate(rows, axis=0))
        if len(x_refs) > 1:
            x = jnp.concatenate([x_ref[...] for x_ref in x_refs], axis=0)
        else:
            x = x_refs[0][pl.ds(c * chunk, chunk)].reshape(chunk * tokens, width)
        return total + jnp.dot(
            jnp.concatenate(columns, axis=1), x, preferred_element_type=jnp.float32
        )

    return repeat(devices // chunk, step, jnp.zeros((count * rank, width), jnp.float32))


def by_group(x_refs, groups, use):
    if len(x_refs) == 1:
        use(x_refs)
        return
    local = len(x_refs) // groups
    for g in range(groups):

        @pl.when(pl.program_id(0) == g)
        def _(g=g):
            use(x_refs[g * local : (g + 1) * local])


def send_kernel(groups, number, slots_line, count, rank, away, place_ref, packed_ref, *refs):
    line = place_ref[1]
    ways_out = 2 if away == 1 else 1
    x_refs, got, outs = refs[:number], refs[number:-ways_out], refs[-ways_out:]
    ways = ((line + away < line_length, line + away), (line >= away, line - away))
    for way, (inside, target) in enumerate(ways):

        def use(x_refs, way=way, target=target):
            first = target * slots_line + pl.program_id(1) * count
            total = slot_sums(packed_ref, x_refs, place_ref[2], rank, first, count)
            if got:
                total += got[way % len(got)][0].astype(jnp.float32)
            outs[way % ways_out][0] = total.astype(jnp.bfloat16)

        @pl.when(inside)
        def _(use=use):
            by_group(x_refs, groups, use)


def own_kernel(groups, number, slots_line, count, rank, place_ref, packed_ref, *refs):
    x_refs, (right_ref, left_ref, out_ref) = refs[:number], refs[number:]

    def use(x_refs):
        first = place_ref[1] * slots_line + pl.program_id(1) * count
        total = slot_sums(packed_ref, x_refs, place_ref[2], rank, first, count)
        total += right_ref[0].astype(jnp.float32) + left_ref[0].astype(jnp.float32)
        out_ref[0] = (adapter_scale * total).astype(jnp.bfloat16)

    by_group(x_refs, groups, use)


def grad_a_step(place, packed, x_cols, half, got, away, groups, slots_line, rank):
    devices, depth, tokens = packed.shape
    width = x_cols[0].shape[-1] // 2
    local = devices // groups
    count = 8
    rows = count * rank
    number = len(x_cols)
    if number > 1:
        x_specs = [pl.BlockSpec((tokens, width), lambda g, s, place: (0, half))] * number
    else:
        if width % 128:
            x_cols, half = [x_cols[0][:, :, half * width : (half + 1) * width]], 0
        x_specs = [pl.BlockSpec((local, tokens, width), lambda g, s, place: (g, 0, half))]
    block = pl.BlockSpec((1, rows, width), lambda g, s, place: (g, s, 0))
    final = pl.BlockSpec((1, rows, width), lambda g, s, place: (g ^ place[0], s, 0))
    shape = jax.ShapeDtypeStruct((groups, slots_line * rank, width), jnp.bfloat16)
    ways = 2 if away == 1 else 1
    if away == 0:
        kernel = lambda *refs: own_kernel(groups, number, slots_line, count, rank, *refs)
    else:
        kernel = lambda *refs: send_kernel(groups, number, slots_line, count, rank, away, *refs)
    return call(
        kernel,
        place,
        (groups, slots_line // count),
        [pl.BlockSpec((local, depth, tokens), lambda g, s, place: (g ^ place[0], 0, 0))]
        + x_specs
        + [block] * len(got),
        final if away == 0 else [block] * ways,
        shape if away == 0 else [shape] * ways,
        ways * 2 * devices * tokens * width * slots_line * rank,
        2 * devices * tokens * width + 2 * groups * slots_line * rank * width * (ways + len(got)),
        "grad_a_step" + str(away),
        (packed, *x_cols, *got),
    )


def in_line(slots, place_ref, total):
    slots -= place_ref[1] * (total // line_length)
    return jnp.where(slots < 0, slots + total, slots)


def put_together(pieces, line, a_ref):
    @pl.when(pl.program_id(0) == 0)
    def _():
        rows = pieces[0].shape[0]
        a_ref[:rows] = pieces[0][...]
        for k in range(1, line_length):
            part = pl.ds(k * rows, rows)

            @pl.when(line + k < line_length)
            def _(k=k, part=part):
                a_ref[part] = pieces[line_length - 1 + k][...]

            @pl.when(line + k >= line_length)
            def _(k=k, part=part):
                a_ref[part] = pieces[line_length - k][...]


def low_kernel(chunk, rank, number, place_ref, packed_ref, *refs):
    x_refs, pieces, (low_ref, a_ref) = refs[:number], refs[number:-2], refs[-2:]
    put_together(pieces, place_ref[1], a_ref)
    slots = packed_ref[0].astype(jnp.float32).T[:, rank + 1 : rank + 2].astype(jnp.int32)
    slots = in_line(slots, place_ref, a_ref.shape[0] // rank)
    tile = slots.shape[0]
    lane_slot = lax.broadcasted_iota(jnp.int32, (tile, chunk), 1) // rank

    def use(x):
        def step(c, low):
            part = pl.ds(pl.multiple_of(c * chunk, chunk), chunk)
            hidden = lax.dot_general(x, a_ref[part], NT, preferred_element_type=jnp.float32)
            hidden = jnp.where(lane_slot + c * (chunk // rank) == slots, hidden, 0.0)
            for k in range(chunk // (2 * rank)):
                low += hidden[:, k * 2 * rank : (k + 1) * 2 * rank]
            return low

        start = jnp.zeros((tile, 2 * rank), jnp.float32)
        low = repeat(a_ref.shape[0] // chunk, step, start).T
        low_ref[0] = low[:rank] + low[rank:]

    if number == 1:
        use(x_refs[0][0])
    else:
        for m in range(number):

            @pl.when(pl.program_id(0) == m)
            def _(m=m):
                use(x_refs[m][...])


def low_part(place, packed, x_cols, a_pieces, inner, rank):
    devices, depth, tokens = packed.shape
    width = x_cols[0].shape[-1]
    rows = a_pieces[0].shape[0]
    slots = line_length * rows
    number = len(x_cols)
    mate = lambda t, place: (t ^ (place[0] * inner + place[2]), 0, 0)
    if number > 1:
        x_specs = [pl.BlockSpec((tokens, width), lambda t, place: (0, 0))] * number
    else:
        x_specs = [pl.BlockSpec((1, tokens, width), lambda t, place: (t, 0, 0))]
    return call(
        lambda *refs: low_kernel(512, rank, number, *refs),
        place,
        (devices,),
        [pl.BlockSpec((1, depth, tokens), mate)]
        + x_specs
        + [pl.BlockSpec((rows, width), lambda t, place: (0, 0))] * len(a_pieces),
        pl.BlockSpec((1, rank, tokens), mate),
        jax.ShapeDtypeStruct((devices, rank, tokens), jnp.float32),
        2 * devices * tokens * width * slots,
        2 * (devices * tokens + slots) * width,
        "low_part",
        (packed, *x_cols, *a_pieces),
        [pltpu.VMEM((slots, width), jnp.bfloat16)],
    )


def out_kernel(chunk, rank, groups, place_ref, packed_ref, g_ref, *refs):
    number = 2 * line_length - 1
    a_pieces, w_pieces, (out_ref, a_ref, w_ref) = refs[:number], refs[number:-3], refs[-3:]
    put_together(a_pieces, place_ref[1], a_ref)
    put_together(w_pieces, place_ref[1], w_ref)
    rows = jnp.concatenate([p.astype(jnp.float32).T for p in packed_ref[...]], axis=0)
    back, slots = rows[:, :rank], rows[:, rank + 1 : rank + 2].astype(jnp.int32)
    total = a_ref.shape[0]
    slots = in_line(slots, place_ref, total // rank)
    tile = back.shape[0]
    repeated = jnp.concatenate([back] * (chunk // rank), axis=1)
    lane_slot = lax.broadcasted_iota(jnp.int32, (tile, chunk), 1) // rank

    def masked(c):
        keep = lane_slot + c * (chunk // rank) == slots
        return jnp.where(keep, repeated, 0.0).astype(jnp.bfloat16)

    if total // chunk <= 4:
        wide = jnp.concatenate([masked(c) for c in range(total // chunk)], axis=1)
        acc = jnp.dot(wide, a_ref[...], preferred_element_type=jnp.float32)
    else:

        def step(c, acc):
            block = a_ref[pl.ds(pl.multiple_of(c * chunk, chunk), chunk), :]
            return acc + jnp.dot(masked(c), block, preferred_element_type=jnp.float32)

        acc = repeat(total // chunk, step, jnp.zeros((tile, a_ref.shape[1]), jnp.float32))
    base = []
    count = w_pieces[0].shape[0]
    halves = line_length // groups
    for c in range(halves):
        at = (place_ref[0] * halves + c - place_ref[1] + line_length) % line_length
        w = w_ref[pl.ds(pl.multiple_of(at * count, count), count), :]
        base.append(lax.dot_general(g_ref[...], w, NT, preferred_element_type=jnp.float32))
    out = jnp.concatenate(base, axis=1) + adapter_scale * acc
    out_ref[...] = out.astype(out_ref.dtype).reshape(out_ref.shape)


def out_part(place, packed, g_all, w_pieces, a_pieces, groups, rank):
    devices, depth, tokens = packed.shape
    outs = g_all.shape[1]
    rows, width = a_pieces[0].shape
    slots = line_length * rows
    both = 2
    pieces = [*a_pieces, *w_pieces]
    return call(
        lambda *refs: out_kernel(512, rank, groups, *refs),
        place,
        (devices // both,),
        [
            pl.BlockSpec((both, depth, tokens), lambda t, place: (t, 0, 0)),
            pl.BlockSpec((both * tokens, outs), lambda t, place: (t, 0)),
        ]
        + [pl.BlockSpec(piece.shape, lambda t, place: (0, 0)) for piece in pieces],
        pl.BlockSpec((both, tokens, width), lambda t, place: (t, 0, 0)),
        jax.ShapeDtypeStruct((devices, tokens, width), jnp.bfloat16),
        2 * devices * tokens * width * (slots + outs),
        2 * devices * tokens * (width + outs) + 2 * slots * width,
        "out_part",
        (packed, g_all, *pieces),
        [
            pltpu.VMEM((slots, width), jnp.bfloat16),
            pltpu.VMEM((line_length * w_pieces[0].shape[0], outs), jnp.bfloat16),
        ],
    )


def body(x, g, tok, adapter_slot, w, a, b):
    groups, inner = lax.axis_size("groups"), lax.axis_size("inner")
    gi, li, ji = lax.axis_index("groups"), lax.axis_index("line"), lax.axis_index("inner")
    place = jnp.stack([gi, li, ji]).astype(jnp.int32)
    size = groups * inner
    devices = line_length * inner
    tokens, model = x.shape
    outs = g.shape[1]
    resident, _, rank = a.shape
    share = resident // groups
    count = inner * resident
    halves = line_length // groups
    width = model // size
    part = width // halves
    adapters = adapter_slot.shape[0]
    capacity = max(2, 2 * tokens // adapters)

    up = [(i, i + 1) for i in range(line_length - 1)]
    down = [(i + 1, i) for i in range(line_length - 1)]

    def hop(pieces, away):
        left, right = pieces
        if away == line_length - 1:
            both = lax.ppermute(
                jnp.where(li == line_length - 2, left, right), "line", up[away - 1 :] + down[:1]
            )
            return [both, both]
        return [
            lax.ppermute(left, "line", up[away - 1 :]),
            lax.ppermute(right, "line", down[: line_length - away]),
        ]

    w_hops = [hop((w, w), 1)]
    w_hops.append(hop(w_hops[0], 2))

    a_mine = split_columns(place, jnp.swapaxes(a, 1, 2), groups, halves, inner, part)
    a_own = lax.all_to_all(a_mine, plane, 0, 0, tiled=True).reshape(count * rank, width)

    def meet(m):
        return lax.ppermute(x_sends[m], plane, [(i, i ^ m) for i in range(size)])

    direct = size == 8 and part % 128 == 0
    x_cols = {}
    if direct:
        x_sends = split_pieces(place, x, groups, halves, inner, part)
        x_cols = {0: x_sends[0], 1: meet(1), 2: meet(2), 4: meet(4)}
    else:
        x_far = split_columns(place, x[None], groups, halves, inner, part)
        x_far = lax.all_to_all(x_far, plane, 0, 0, tiled=True)
        x_cols = {0: x_far[jnp.arange(size) ^ (gi * inner + ji)]}

    matches = tok == lax.broadcasted_iota(jnp.int32, (tokens, adapters), 1)
    slot = jnp.sum(jnp.where(matches, adapter_slot[None, :], 0), axis=1)
    running = jnp.cumsum(matches.astype(jnp.int32), axis=0)
    within = jnp.sum(jnp.where(matches, running - 1, 0), axis=1)
    position = slot * capacity + within
    at = lax.broadcasted_iota(jnp.int32, (adapters * capacity, tokens), 0) == position[None, :]
    at = at.astype(jnp.bfloat16)

    def route(rows):
        rows = rows.reshape(devices, resident * capacity, rows.shape[1])
        rows = lax.all_to_all(rows, row, 0, 0, tiled=True)
        return rows.reshape(devices, resident, capacity, rows.shape[2])

    g_send = jnp.dot(at, g, preferred_element_type=jnp.float32).astype(jnp.bfloat16)
    g_send, a_own, x_cols, w_hops = lax.optimization_barrier((g_send, a_own, x_cols, w_hops))
    w_hops.append(hop(w_hops[1], 3))
    g_rows = route(g_send)
    back = jnp.einsum("hjct,jrt->hjcr", g_rows, b, preferred_element_type=jnp.float32)
    back = back.astype(jnp.bfloat16).reshape(devices, resident * capacity, rank)
    hops = [hop((a_own, a_own), 1)]
    if direct:
        x_cols.update({3: meet(3), 5: meet(5)})
    back, x_cols = lax.optimization_barrier((back, x_cols))
    if direct:
        x_cols.update({6: meet(6), 7: meet(7)})
    back = lax.all_to_all(back, row, 0, 0, tiled=True).reshape(adapters * capacity, rank)
    back = lax.dot_general(
        back, at, (((0,), (0,)), ((), ())), preferred_element_type=jnp.float32
    ).astype(jnp.bfloat16)
    owner, res = slot // resident, slot % resident
    slot_a = (owner // inner) * count + ((res // share) * inner + owner % inner) * share + res % share
    names = jnp.stack([slot, slot_a] + [slot] * 14).astype(jnp.bfloat16)
    packed = jnp.concatenate([back, names], axis=0)
    packed, x_cols, hops, w_hops = lax.optimization_barrier((packed, x_cols, hops, w_hops))
    packed = jnp.broadcast_to(packed[None], (size,) + packed.shape)
    packed = lax.all_to_all(packed, plane, 0, 0, tiled=True)
    x_cols = [x_cols[m] for m in range(len(x_cols))]
    g_own, x_cols = lax.optimization_barrier((g, x_cols))
    g_all = lax.all_gather(g_own, plane, axis=0, tiled=True)

    hops.append(hop(hops[0], 2))

    def send(c, got, away):
        sums = grad_a_step(place, packed, x_cols, c, got, away, groups, count, rank)
        ahead = [(i, i + 1) for i in range(line_length - away)]
        behind = [(i, i - 1) for i in range(away, line_length)]
        if away == line_length - 1:
            moved = (lax.ppermute(sums[0], "line", ahead + behind),)
        else:
            moved = (lax.ppermute(sums[0], "line", ahead), lax.ppermute(sums[-1], "line", behind))
        return moved, sums[0]

    def own(c, got):
        p = grad_a_step(place, packed, x_cols, c, got, 0, groups, count, rank)
        return p.reshape(size, resident * rank, part)

    first, done = send(0, (), 3)
    packed, done = lax.optimization_barrier((packed, done))
    second, done = send(1, (), 3)

    first, hops[1], done = lax.optimization_barrier((first, hops[1], done))
    hops.append(hop(hops[1], 3))
    first, done = send(0, first, 2)
    second, done = lax.optimization_barrier((second, done))
    second, done = send(1, second, 2)

    a_pieces = [a_own] + [h[0] for h in hops] + [h[1] for h in hops]
    w_pieces = [w] + [h[0] for h in w_hops] + [h[1] for h in w_hops]
    a_pieces, done = lax.optimization_barrier((a_pieces, done))
    out_cols = out_part(place, packed, g_all, w_pieces, a_pieces, groups, rank)
    first, out_cols = lax.optimization_barrier((first, out_cols))
    first, done = send(0, first, 1)
    out_cols, done = lax.optimization_barrier((out_cols, done))
    out_back = lax.all_to_all(out_cols, plane, 0, 0, tiled=True)

    second, done = lax.optimization_barrier((second, done))
    second, done = send(1, second, 1)

    first, done = lax.optimization_barrier((first, done))
    p_first = own(0, first)

    a_pieces, p_first = lax.optimization_barrier((a_pieces, p_first))
    low = low_part(place, packed, x_cols, a_pieces, inner, rank)
    second, low = lax.optimization_barrier((second, low))
    p_second = own(1, second)
    p_first, out_back = lax.optimization_barrier((p_first, out_back))
    p_back = [lax.all_to_all(p_first, plane, 0, 0, tiled=True)]
    low, p_back[0] = lax.optimization_barrier((low, p_back[0]))
    low = lax.all_to_all(low, plane, 0, 0, tiled=True)
    p_second, low = lax.optimization_barrier((p_second, low))
    p_back.append(lax.all_to_all(p_second, plane, 0, 0, tiled=True))
    low = jnp.sum(low, axis=0).astype(jnp.bfloat16)
    low = lax.dot_general(at, low, NT, preferred_element_type=jnp.float32).astype(jnp.bfloat16)
    low, p_back = lax.optimization_barrier((low, p_back))
    low = route(low)
    grad_b = jnp.einsum("hjcr,hjco->jro", low, g_rows, preferred_element_type=jnp.float32)
    grad_b = (adapter_scale * grad_b).astype(jnp.bfloat16)
    input_gradient = join_rows(place, out_back, groups, halves, inner, part)
    grad_a = join_slots(place, p_back, resident, groups, inner).swapaxes(1, 2)
    return input_gradient, grad_a, grad_b


def solution(mesh):
    groups, rows = mesh.shape["groups"], mesh.shape["row"]
    whole = ("groups", "line", "inner")
    split = Mesh(mesh.devices.reshape(groups, line_length, rows // line_length), whole)
    return jax.shard_map(
        body,
        mesh=split,
        in_specs=(
            P(whole, None),
            P(whole, None),
            P(whole, None),
            P(),
            P(row, None),
            P(row, None, None),
            P(row, None, None),
        ),
        out_specs=(P(whole, None), P(whole, None, None), P(whole, None, None)),
        check_vma=False,
    )
```

```python
import jax
import jax.numpy as jnp
from jax import lax
from jax.experimental import pallas as pl
from jax.experimental.pallas import tpu as pltpu
from jax.sharding import Mesh, PartitionSpec as P

adapter_scale = 2.0
line_length = 4
plane = ("groups", "inner")
row = ("line", "inner")
vmem_limit = 56 * 1024 * 1024
NT = (((1,), (1,)), ((), ()))


def call(kernel, place, grid, in_specs, out_specs, out_shape, flops, moved, name, args, scratch=()):
    return pl.pallas_call(
        kernel,
        grid_spec=pltpu.PrefetchScalarGridSpec(
            num_scalar_prefetch=1,
            grid=grid,
            in_specs=in_specs,
            out_specs=out_specs,
            scratch_shapes=scratch,
        ),
        out_shape=out_shape,
        compiler_params=pltpu.CompilerParams(vmem_limit_bytes=vmem_limit),
        cost_estimate=pl.CostEstimate(flops=flops, bytes_accessed=moved, transcendentals=0),
        name=name,
    )(place, *args)


def repeat(count, step, start):
    if count <= 4:
        for i in range(count):
            start = step(i, start)
        return start
    return lax.fori_loop(0, count, step, start)


def move(name, sources, in_blocks, in_maps, outs, out_blocks, out_maps, grid, kernel, place):
    moved = 0
    for shape in outs:
        size = 4
        for n in shape:
            size *= n
        moved += size
    return call(
        kernel,
        place,
        grid,
        [pl.BlockSpec(block, index) for block, index in zip(in_blocks, in_maps)],
        [pl.BlockSpec(block, index) for block, index in zip(out_blocks, out_maps)],
        [jax.ShapeDtypeStruct(shape, jnp.bfloat16) for shape in outs],
        0,
        moved,
        name,
        sources,
    )


def columns_of(q, c, halves, inner):
    return ((q // inner) * halves + c) * inner + q % inner


def split_columns(place, rows, groups, halves, inner, width):
    slots, rank, model = rows.shape
    size, share = groups * inner, max(1, slots // groups)
    group = lambda place: place[0] if slots >= groups else 0
    if width % 128:
        mine = lax.dynamic_slice_in_dim(rows, group(place) * share, share, 0)
        mine = mine.reshape(share * rank, groups, halves, inner, width)
        return mine.transpose(1, 3, 0, 2, 4).reshape(size, share * rank, halves * width)

    def kernel(place_ref, rows_ref, out_ref):
        for q in range(size):
            for c in range(halves):
                first = columns_of(q, c, halves, inner) * width
                out_ref[q, :, c * width : (c + 1) * width] = rows_ref[0, :, first : first + width]

    tile = min(rank, 64)
    steps = rank // tile
    return move(
        "split_columns", [rows], [(1, tile, model)],
        [lambda s, r, place: (group(place) * share + s, r, 0)],
        [(size, share * rank, halves * width)], [(size, tile, halves * width)],
        [lambda s, r, place: (0, s * steps + r, 0)], (share, steps), kernel, place,
    )[0]


def split_pieces(place, rows, groups, halves, inner, width):
    count, model = rows.shape
    size = groups * inner
    tile = min(count, 64)

    def kernel(place_ref, rows_ref, *out_refs):
        me = place_ref[0] * inner + place_ref[2]
        for m in range(size):
            for c in range(halves):
                first = pl.multiple_of(columns_of(me ^ m, c, halves, inner) * width, width)
                out_refs[m][:, c * width : (c + 1) * width] = rows_ref[:, pl.ds(first, width)]

    return move(
        "split_pieces", [rows], [(tile, model)], [lambda t, place: (t, 0)],
        [(count, halves * width)] * size, [(tile, halves * width)] * size,
        [lambda t, place: (t, 0)] * size, (count // tile,), kernel, place,
    )


def join_slots(place, parts, resident, groups, inner):
    size, rows, width = parts[0].shape
    halves, rank = len(parts), rows // resident
    if width % 128:
        parts = [p.reshape(groups, inner, rows, width) for p in parts]
        joined = jnp.stack(parts, axis=1).transpose(3, 0, 1, 2, 4)
        return joined.reshape(resident, rank, -1)

    def kernel(place_ref, *refs):
        for q in range(size):
            for c in range(halves):
                first = columns_of(q, c, halves, inner) * width
                refs[-1][0, :, first : first + width] = refs[c][q]

    return move(
        "join_slots", parts, [(size, rank, width)] * halves, [lambda r, place: (0, r, 0)] * halves,
        [(resident, rank, size * halves * width)], [(1, rank, size * halves * width)],
        [lambda r, place: (r, 0, 0)], (resident,), kernel, place,
    )[0]


def join_rows(place, rows, groups, halves, inner, part):
    size, tokens = rows.shape[:2]
    if part % 128:
        rows = rows.reshape(groups, inner, tokens, halves, part)
        return rows.transpose(2, 0, 3, 1, 4).reshape(tokens, -1)
    tile = min(tokens, 64)
    model = size * halves * part

    def kernel(place_ref, rows_ref, out_ref):
        for q in range(size):
            for c in range(halves):
                first = columns_of(q, c, halves, inner) * part
                out_ref[:, first : first + part] = rows_ref[q, :, c * part : (c + 1) * part]

    return move(
        "join_rows", [rows], [(size, tile, halves * part)], [lambda t, place: (0, t, 0)],
        [(tokens, model)], [(tile, model)], [lambda t, place: (t, 0)], (tokens // tile,),
        kernel, place,
    )[0]


def slot_sums(packed_ref, x_refs, me, rank, first, count):
    devices, _, tokens = packed_ref.shape
    width = x_refs[0].shape[-1]
    chunk = min(devices, 4)

    def step(c, total):
        columns = []
        for d in range(chunk):
            device = (c * chunk + d) ^ me
            back = packed_ref[device, :rank, :]
            slots = packed_ref[device, rank : rank + 1, :].astype(jnp.float32)
            rows = [
                back * (slots == (first + i).astype(jnp.float32)).astype(jnp.bfloat16)
                for i in range(count)
            ]
            columns.append(jnp.concatenate(rows, axis=0))
        if len(x_refs) > 1:
            x = jnp.concatenate([x_ref[...] for x_ref in x_refs], axis=0)
        else:
            x = x_refs[0][pl.ds(c * chunk, chunk)].reshape(chunk * tokens, width)
        return total + jnp.dot(
            jnp.concatenate(columns, axis=1), x, preferred_element_type=jnp.float32
        )

    return repeat(devices // chunk, step, jnp.zeros((count * rank, width), jnp.float32))


def by_group(x_refs, groups, use):
    if len(x_refs) == 1:
        use(x_refs)
        return
    local = len(x_refs) // groups
    for g in range(groups):

        @pl.when(pl.program_id(0) == g)
        def _(g=g):
            use(x_refs[g * local : (g + 1) * local])


def send_kernel(groups, number, slots_line, count, rank, away, place_ref, packed_ref, *refs):
    line = place_ref[1]
    ways_out = 2 if away == 1 else 1
    x_refs, got, outs = refs[:number], refs[number:-ways_out], refs[-ways_out:]
    ways = ((line + away < line_length, line + away), (line >= away, line - away))
    for way, (inside, target) in enumerate(ways):

        def use(x_refs, way=way, target=target):
            first = target * slots_line + pl.program_id(1) * count
            total = slot_sums(packed_ref, x_refs, place_ref[2], rank, first, count)
            if got:
                total += got[way % len(got)][0].astype(jnp.float32)
            outs[way % ways_out][0] = total.astype(jnp.bfloat16)

        @pl.when(inside)
        def _(use=use):
            by_group(x_refs, groups, use)


def own_kernel(groups, number, slots_line, count, rank, place_ref, packed_ref, *refs):
    x_refs, (right_ref, left_ref, out_ref) = refs[:number], refs[number:]

    def use(x_refs):
        first = place_ref[1] * slots_line + pl.program_id(1) * count
        total = slot_sums(packed_ref, x_refs, place_ref[2], rank, first, count)
        total += right_ref[0].astype(jnp.float32) + left_ref[0].astype(jnp.float32)
        out_ref[0] = (adapter_scale * total).astype(jnp.bfloat16)

    by_group(x_refs, groups, use)


def grad_a_step(place, packed, x_cols, half, got, away, groups, slots_line, rank):
    devices, depth, tokens = packed.shape
    width = x_cols[0].shape[-1] // 2
    local = devices // groups
    count = 8
    rows = count * rank
    number = len(x_cols)
    if number > 1:
        x_specs = [pl.BlockSpec((tokens, width), lambda g, s, place: (0, half))] * number
    else:
        if width % 128:
            x_cols, half = [x_cols[0][:, :, half * width : (half + 1) * width]], 0
        x_specs = [pl.BlockSpec((local, tokens, width), lambda g, s, place: (g, 0, half))]
    block = pl.BlockSpec((1, rows, width), lambda g, s, place: (g, s, 0))
    final = pl.BlockSpec((1, rows, width), lambda g, s, place: (g ^ place[0], s, 0))
    shape = jax.ShapeDtypeStruct((groups, slots_line * rank, width), jnp.bfloat16)
    ways = 2 if away == 1 else 1
    if away == 0:
        kernel = lambda *refs: own_kernel(groups, number, slots_line, count, rank, *refs)
    else:
        kernel = lambda *refs: send_kernel(groups, number, slots_line, count, rank, away, *refs)
    return call(
        kernel,
        place,
        (groups, slots_line // count),
        [pl.BlockSpec((local, depth, tokens), lambda g, s, place: (g ^ place[0], 0, 0))]
        + x_specs
        + [block] * len(got),
        final if away == 0 else [block] * ways,
        shape if away == 0 else [shape] * ways,
        ways * 2 * devices * tokens * width * slots_line * rank,
        2 * devices * tokens * width + 2 * groups * slots_line * rank * width * (ways + len(got)),
        "grad_a_step" + str(away),
        (packed, *x_cols, *got),
    )


def in_line(slots, place_ref, total):
    slots -= place_ref[1] * (total // line_length)
    return jnp.where(slots < 0, slots + total, slots)


def put_together(pieces, line, a_ref):
    @pl.when(pl.program_id(0) == 0)
    def _():
        rows = pieces[0].shape[0]
        a_ref[:rows] = pieces[0][...]
        for k in range(1, line_length):
            part = pl.ds(k * rows, rows)

            @pl.when(line + k < line_length)
            def _(k=k, part=part):
                a_ref[part] = pieces[line_length - 1 + k][...]

            @pl.when(line + k >= line_length)
            def _(k=k, part=part):
                a_ref[part] = pieces[line_length - k][...]


def low_kernel(chunk, rank, number, place_ref, packed_ref, *refs):
    x_refs, pieces, (low_ref, a_ref) = refs[:number], refs[number:-2], refs[-2:]
    put_together(pieces, place_ref[1], a_ref)
    slots = packed_ref[0].astype(jnp.float32).T[:, rank + 1 : rank + 2].astype(jnp.int32)
    slots = in_line(slots, place_ref, a_ref.shape[0] // rank)
    tile = slots.shape[0]
    lane_slot = lax.broadcasted_iota(jnp.int32, (tile, chunk), 1) // rank

    def use(x):
        def step(c, low):
            part = pl.ds(pl.multiple_of(c * chunk, chunk), chunk)
            hidden = lax.dot_general(x, a_ref[part], NT, preferred_element_type=jnp.float32)
            hidden = jnp.where(lane_slot + c * (chunk // rank) == slots, hidden, 0.0)
            for k in range(chunk // (2 * rank)):
                low += hidden[:, k * 2 * rank : (k + 1) * 2 * rank]
            return low

        start = jnp.zeros((tile, 2 * rank), jnp.float32)
        low = repeat(a_ref.shape[0] // chunk, step, start).T
        low_ref[0] = low[:rank] + low[rank:]

    if number == 1:
        use(x_refs[0][0])
    else:
        for m in range(number):

            @pl.when(pl.program_id(0) == m)
            def _(m=m):
                use(x_refs[m][...])


def low_part(place, packed, x_cols, a_pieces, inner, rank):
    devices, depth, tokens = packed.shape
    width = x_cols[0].shape[-1]
    rows = a_pieces[0].shape[0]
    slots = line_length * rows
    number = len(x_cols)
    mate = lambda t, place: (t ^ (place[0] * inner + place[2]), 0, 0)
    if number > 1:
        x_specs = [pl.BlockSpec((tokens, width), lambda t, place: (0, 0))] * number
    else:
        x_specs = [pl.BlockSpec((1, tokens, width), lambda t, place: (t, 0, 0))]
    return call(
        lambda *refs: low_kernel(512, rank, number, *refs),
        place,
        (devices,),
        [pl.BlockSpec((1, depth, tokens), mate)]
        + x_specs
        + [pl.BlockSpec((rows, width), lambda t, place: (0, 0))] * len(a_pieces),
        pl.BlockSpec((1, rank, tokens), mate),
        jax.ShapeDtypeStruct((devices, rank, tokens), jnp.float32),
        2 * devices * tokens * width * slots,
        2 * (devices * tokens + slots) * width,
        "low_part",
        (packed, *x_cols, *a_pieces),
        [pltpu.VMEM((slots, width), jnp.bfloat16)],
    )


def out_kernel(chunk, rank, groups, place_ref, packed_ref, g_ref, *refs):
    number = 2 * line_length - 1
    a_pieces, w_pieces, (out_ref, a_ref, w_ref) = refs[:number], refs[number:-3], refs[-3:]
    put_together(a_pieces, place_ref[1], a_ref)
    put_together(w_pieces, place_ref[1], w_ref)
    rows = jnp.concatenate([p.astype(jnp.float32).T for p in packed_ref[...]], axis=0)
    back, slots = rows[:, :rank], rows[:, rank + 1 : rank + 2].astype(jnp.int32)
    total = a_ref.shape[0]
    slots = in_line(slots, place_ref, total // rank)
    tile = back.shape[0]
    repeated = jnp.concatenate([back] * (chunk // rank), axis=1)
    lane_slot = lax.broadcasted_iota(jnp.int32, (tile, chunk), 1) // rank

    def masked(c):
        keep = lane_slot + c * (chunk // rank) == slots
        return jnp.where(keep, repeated, 0.0).astype(jnp.bfloat16)

    if total // chunk <= 4:
        wide = jnp.concatenate([masked(c) for c in range(total // chunk)], axis=1)
        acc = jnp.dot(wide, a_ref[...], preferred_element_type=jnp.float32)
    else:

        def step(c, acc):
            block = a_ref[pl.ds(pl.multiple_of(c * chunk, chunk), chunk), :]
            return acc + jnp.dot(masked(c), block, preferred_element_type=jnp.float32)

        acc = repeat(total // chunk, step, jnp.zeros((tile, a_ref.shape[1]), jnp.float32))
    base = []
    count = w_pieces[0].shape[0]
    halves = line_length // groups
    for c in range(halves):
        at = (place_ref[0] * halves + c - place_ref[1] + line_length) % line_length
        w = w_ref[pl.ds(pl.multiple_of(at * count, count), count), :]
        base.append(lax.dot_general(g_ref[...], w, NT, preferred_element_type=jnp.float32))
    out = jnp.concatenate(base, axis=1) + adapter_scale * acc
    out_ref[...] = out.astype(out_ref.dtype).reshape(out_ref.shape)


def out_part(place, packed, g_all, w_pieces, a_pieces, groups, rank):
    devices, depth, tokens = packed.shape
    outs = g_all.shape[1]
    rows, width = a_pieces[0].shape
    slots = line_length * rows
    both = 2
    pieces = [*a_pieces, *w_pieces]
    return call(
        lambda *refs: out_kernel(512, rank, groups, *refs),
        place,
        (devices // both,),
        [
            pl.BlockSpec((both, depth, tokens), lambda t, place: (t, 0, 0)),
            pl.BlockSpec((both * tokens, outs), lambda t, place: (t, 0)),
        ]
        + [pl.BlockSpec(piece.shape, lambda t, place: (0, 0)) for piece in pieces],
        pl.BlockSpec((both, tokens, width), lambda t, place: (t, 0, 0)),
        jax.ShapeDtypeStruct((devices, tokens, width), jnp.bfloat16),
        2 * devices * tokens * width * (slots + outs),
        2 * devices * tokens * (width + outs) + 2 * slots * width,
        "out_part",
        (packed, g_all, *pieces),
        [
            pltpu.VMEM((slots, width), jnp.bfloat16),
            pltpu.VMEM((line_length * w_pieces[0].shape[0], outs), jnp.bfloat16),
        ],
    )


def body(x, g, tok, adapter_slot, w, a, b):
    groups, inner = lax.axis_size("groups"), lax.axis_size("inner")
    gi, li, ji = lax.axis_index("groups"), lax.axis_index("line"), lax.axis_index("inner")
    place = jnp.stack([gi, li, ji]).astype(jnp.int32)
    size = groups * inner
    devices = line_length * inner
    tokens, model = x.shape
    outs = g.shape[1]
    resident, _, rank = a.shape
    share = resident // groups
    count = inner * resident
    halves = line_length // groups
    width = model // size
    part = width // halves
    adapters = adapter_slot.shape[0]
    capacity = max(2, 2 * tokens // adapters)

    up = [(i, i + 1) for i in range(line_length - 1)]
    down = [(i + 1, i) for i in range(line_length - 1)]

    def hop(pieces, away):
        left, right = pieces
        if away == line_length - 1:
            both = lax.ppermute(
                jnp.where(li == line_length - 2, left, right), "line", up[away - 1 :] + down[:1]
            )
            return [both, both]
        return [
            lax.ppermute(left, "line", up[away - 1 :]),
            lax.ppermute(right, "line", down[: line_length - away]),
        ]

    w_hops = [hop((w, w), 1)]
    w_hops.append(hop(w_hops[0], 2))

    a_mine = split_columns(place, jnp.swapaxes(a, 1, 2), groups, halves, inner, part)
    a_own = lax.all_to_all(a_mine, plane, 0, 0, tiled=True).reshape(count * rank, width)

    def meet(m):
        return lax.ppermute(x_sends[m], plane, [(i, i ^ m) for i in range(size)])

    direct = size == 8 and part % 128 == 0
    x_cols = {}
    if direct:
        x_sends = split_pieces(place, x, groups, halves, inner, part)
        x_cols = {0: x_sends[0], 1: meet(1), 2: meet(2), 4: meet(4)}
    else:
        x_far = split_columns(place, x[None], groups, halves, inner, part)
        x_far = lax.all_to_all(x_far, plane, 0, 0, tiled=True)
        x_cols = {0: x_far[jnp.arange(size) ^ (gi * inner + ji)]}

    matches = tok == lax.broadcasted_iota(jnp.int32, (tokens, adapters), 1)
    slot = jnp.sum(jnp.where(matches, adapter_slot[None, :], 0), axis=1)
    running = jnp.cumsum(matches.astype(jnp.int32), axis=0)
    within = jnp.sum(jnp.where(matches, running - 1, 0), axis=1)
    position = slot * capacity + within
    at = lax.broadcasted_iota(jnp.int32, (adapters * capacity, tokens), 0) == position[None, :]
    at = at.astype(jnp.bfloat16)

    def route(rows):
        rows = rows.reshape(devices, resident * capacity, rows.shape[1])
        rows = lax.all_to_all(rows, row, 0, 0, tiled=True)
        return rows.reshape(devices, resident, capacity, rows.shape[2])

    g_send = jnp.dot(at, g, preferred_element_type=jnp.float32).astype(jnp.bfloat16)
    g_send, a_own, x_cols, w_hops = lax.optimization_barrier((g_send, a_own, x_cols, w_hops))
    w_hops.append(hop(w_hops[1], 3))
    g_rows = route(g_send)
    back = jnp.einsum("hjct,jrt->hjcr", g_rows, b, preferred_element_type=jnp.float32)
    back = back.astype(jnp.bfloat16).reshape(devices, resident * capacity, rank)
    hops = [hop((a_own, a_own), 1)]
    if direct:
        x_cols.update({3: meet(3), 5: meet(5)})
    back, x_cols = lax.optimization_barrier((back, x_cols))
    if direct:
        x_cols.update({6: meet(6), 7: meet(7)})
    back = lax.all_to_all(back, row, 0, 0, tiled=True).reshape(adapters * capacity, rank)
    back = lax.dot_general(
        back, at, (((0,), (0,)), ((), ())), preferred_element_type=jnp.float32
    ).astype(jnp.bfloat16)
    owner, res = slot // resident, slot % resident
    slot_a = (owner // inner) * count + ((res // share) * inner + owner % inner) * share + res % share
    names = jnp.stack([slot, slot_a] + [slot] * 14).astype(jnp.bfloat16)
    packed = jnp.concatenate([back, names], axis=0)
    packed, x_cols, hops, w_hops = lax.optimization_barrier((packed, x_cols, hops, w_hops))
    packed = jnp.broadcast_to(packed[None], (size,) + packed.shape)
    packed = lax.all_to_all(packed, plane, 0, 0, tiled=True)
    x_cols = [x_cols[m] for m in range(len(x_cols))]
    g_own, x_cols = lax.optimization_barrier((g, x_cols))
    g_all = lax.all_gather(g_own, plane, axis=0, tiled=True)

    hops.append(hop(hops[0], 2))

    def send(c, got, away):
        sums = grad_a_step(place, packed, x_cols, c, got, away, groups, count, rank)
        ahead = [(i, i + 1) for i in range(line_length - away)]
        behind = [(i, i - 1) for i in range(away, line_length)]
        if away == line_length - 1:
            moved = (lax.ppermute(sums[0], "line", ahead + behind),)
        else:
            moved = (lax.ppermute(sums[0], "line", ahead), lax.ppermute(sums[-1], "line", behind))
        return moved, sums[0]

    def own(c, got):
        p = grad_a_step(place, packed, x_cols, c, got, 0, groups, count, rank)
        return p.reshape(size, resident * rank, part)

    first, done = send(0, (), 3)
    packed, done = lax.optimization_barrier((packed, done))
    second, done = send(1, (), 3)

    first, hops[1], done = lax.optimization_barrier((first, hops[1], done))
    hops.append(hop(hops[1], 3))
    first, done = send(0, first, 2)
    second, done = lax.optimization_barrier((second, done))
    second, done = send(1, second, 2)

    a_pieces = [a_own] + [h[0] for h in hops] + [h[1] for h in hops]
    w_pieces = [w] + [h[0] for h in w_hops] + [h[1] for h in w_hops]
    a_pieces, done = lax.optimization_barrier((a_pieces, done))
    out_cols = out_part(place, packed, g_all, w_pieces, a_pieces, groups, rank)
    first, out_cols = lax.optimization_barrier((first, out_cols))
    first, done = send(0, first, 1)
    out_cols, done = lax.optimization_barrier((out_cols, done))
    out_back = lax.all_to_all(out_cols, plane, 0, 0, tiled=True)

    a_pieces, done = lax.optimization_barrier((a_pieces, done))
    low = low_part(place, packed, x_cols, a_pieces, inner, rank)
    second, low = lax.optimization_barrier((second, low))
    second, done = send(1, second, 1)
    first, done = lax.optimization_barrier((first, done))
    p_first = own(0, first)
    second, p_first = lax.optimization_barrier((second, p_first))
    p_second = own(1, second)
    low, out_back = lax.optimization_barrier((low, out_back))
    low = lax.all_to_all(low, plane, 0, 0, tiled=True)
    low = jnp.sum(low, axis=0).astype(jnp.bfloat16)
    low = lax.dot_general(at, low, NT, preferred_element_type=jnp.float32).astype(jnp.bfloat16)
    low = route(low)
    p_first, low = lax.optimization_barrier((p_first, low))
    p_back = [lax.all_to_all(p_first, plane, 0, 0, tiled=True)]
    p_second, p_back[0] = lax.optimization_barrier((p_second, p_back[0]))
    p_back.append(lax.all_to_all(p_second, plane, 0, 0, tiled=True))

    grad_b = jnp.einsum("hjcr,hjco->jro", low, g_rows, preferred_element_type=jnp.float32)
    grad_b = (adapter_scale * grad_b).astype(jnp.bfloat16)
    input_gradient = join_rows(place, out_back, groups, halves, inner, part)
    grad_a = join_slots(place, p_back, resident, groups, inner).swapaxes(1, 2)
    return input_gradient, grad_a, grad_b


def solution(mesh):
    groups, rows = mesh.shape["groups"], mesh.shape["row"]
    whole = ("groups", "line", "inner")
    split = Mesh(mesh.devices.reshape(groups, line_length, rows // line_length), whole)
    return jax.shard_map(
        body,
        mesh=split,
        in_specs=(
            P(whole, None),
            P(whole, None),
            P(whole, None),
            P(),
            P(row, None),
            P(row, None, None),
            P(row, None, None),
        ),
        out_specs=(P(whole, None), P(whole, None, None), P(whole, None, None)),
        check_vma=False,
    )
```

```python
import jax
import jax.numpy as jnp
from jax import lax
from jax.experimental import pallas as pl
from jax.experimental.pallas import tpu as pltpu
from jax.sharding import Mesh, PartitionSpec as P

adapter_scale = 2.0
line_length = 4
plane = ("groups", "inner")
row = ("line", "inner")
vmem_limit = 56 * 1024 * 1024
NT = (((1,), (1,)), ((), ()))


def call(kernel, place, grid, in_specs, out_specs, out_shape, flops, moved, name, args, scratch=()):
    return pl.pallas_call(
        kernel,
        grid_spec=pltpu.PrefetchScalarGridSpec(
            num_scalar_prefetch=1,
            grid=grid,
            in_specs=in_specs,
            out_specs=out_specs,
            scratch_shapes=scratch,
        ),
        out_shape=out_shape,
        compiler_params=pltpu.CompilerParams(vmem_limit_bytes=vmem_limit),
        cost_estimate=pl.CostEstimate(flops=flops, bytes_accessed=moved, transcendentals=0),
        name=name,
    )(place, *args)


def repeat(count, step, start):
    if count <= 4:
        for i in range(count):
            start = step(i, start)
        return start
    return lax.fori_loop(0, count, step, start)


def move(name, sources, in_blocks, in_maps, outs, out_blocks, out_maps, grid, kernel, place):
    moved = 0
    for shape in outs:
        size = 4
        for n in shape:
            size *= n
        moved += size
    return call(
        kernel,
        place,
        grid,
        [pl.BlockSpec(block, index) for block, index in zip(in_blocks, in_maps)],
        [pl.BlockSpec(block, index) for block, index in zip(out_blocks, out_maps)],
        [jax.ShapeDtypeStruct(shape, jnp.bfloat16) for shape in outs],
        0,
        moved,
        name,
        sources,
    )


def columns_of(q, c, halves, inner):
    return ((q // inner) * halves + c) * inner + q % inner


def split_columns(place, rows, groups, halves, inner, width):
    slots, rank, model = rows.shape
    size, share = groups * inner, max(1, slots // groups)
    group = lambda place: place[0] if slots >= groups else 0
    if width % 128:
        mine = lax.dynamic_slice_in_dim(rows, group(place) * share, share, 0)
        mine = mine.reshape(share * rank, groups, halves, inner, width)
        return mine.transpose(1, 3, 0, 2, 4).reshape(size, share * rank, halves * width)

    def kernel(place_ref, rows_ref, out_ref):
        for q in range(size):
            for c in range(halves):
                first = columns_of(q, c, halves, inner) * width
                out_ref[q, :, c * width : (c + 1) * width] = rows_ref[0, :, first : first + width]

    tile = min(rank, 64)
    steps = rank // tile
    return move(
        "split_columns", [rows], [(1, tile, model)],
        [lambda s, r, place: (group(place) * share + s, r, 0)],
        [(size, share * rank, halves * width)], [(size, tile, halves * width)],
        [lambda s, r, place: (0, s * steps + r, 0)], (share, steps), kernel, place,
    )[0]


def split_pieces(place, rows, groups, halves, inner, width):
    count, model = rows.shape
    size = groups * inner
    tile = min(count, 64)

    def kernel(place_ref, rows_ref, *out_refs):
        me = place_ref[0] * inner + place_ref[2]
        for m in range(size):
            for c in range(halves):
                first = pl.multiple_of(columns_of(me ^ m, c, halves, inner) * width, width)
                out_refs[m][:, c * width : (c + 1) * width] = rows_ref[:, pl.ds(first, width)]

    return move(
        "split_pieces", [rows], [(tile, model)], [lambda t, place: (t, 0)],
        [(count, halves * width)] * size, [(tile, halves * width)] * size,
        [lambda t, place: (t, 0)] * size, (count // tile,), kernel, place,
    )


def join_slots(place, parts, resident, groups, inner):
    size, rows, width = parts[0].shape
    halves, rank = len(parts), rows // resident
    if width % 128:
        parts = [p.reshape(groups, inner, rows, width) for p in parts]
        joined = jnp.stack(parts, axis=1).transpose(3, 0, 1, 2, 4)
        return joined.reshape(resident, rank, -1)

    def kernel(place_ref, *refs):
        for q in range(size):
            for c in range(halves):
                first = columns_of(q, c, halves, inner) * width
                refs[-1][0, :, first : first + width] = refs[c][q]

    return move(
        "join_slots", parts, [(size, rank, width)] * halves, [lambda r, place: (0, r, 0)] * halves,
        [(resident, rank, size * halves * width)], [(1, rank, size * halves * width)],
        [lambda r, place: (r, 0, 0)], (resident,), kernel, place,
    )[0]


def join_rows(place, rows, groups, halves, inner, part):
    size, tokens = rows.shape[:2]
    if part % 128:
        rows = rows.reshape(groups, inner, tokens, halves, part)
        return rows.transpose(2, 0, 3, 1, 4).reshape(tokens, -1)
    tile = min(tokens, 64)
    model = size * halves * part

    def kernel(place_ref, rows_ref, out_ref):
        for q in range(size):
            for c in range(halves):
                first = columns_of(q, c, halves, inner) * part
                out_ref[:, first : first + part] = rows_ref[q, :, c * part : (c + 1) * part]

    return move(
        "join_rows", [rows], [(size, tile, halves * part)], [lambda t, place: (0, t, 0)],
        [(tokens, model)], [(tile, model)], [lambda t, place: (t, 0)], (tokens // tile,),
        kernel, place,
    )[0]


def slot_sums(packed_ref, x_refs, me, rank, first, count):
    devices, _, tokens = packed_ref.shape
    width = x_refs[0].shape[-1]
    chunk = min(devices, 4)

    def step(c, total):
        columns = []
        for d in range(chunk):
            device = (c * chunk + d) ^ me
            back = packed_ref[device, :rank, :]
            slots = packed_ref[device, rank : rank + 1, :].astype(jnp.float32)
            rows = [
                back * (slots == (first + i).astype(jnp.float32)).astype(jnp.bfloat16)
                for i in range(count)
            ]
            columns.append(jnp.concatenate(rows, axis=0))
        if len(x_refs) > 1:
            x = jnp.concatenate([x_ref[...] for x_ref in x_refs], axis=0)
        else:
            x = x_refs[0][pl.ds(c * chunk, chunk)].reshape(chunk * tokens, width)
        return total + jnp.dot(
            jnp.concatenate(columns, axis=1), x, preferred_element_type=jnp.float32
        )

    return repeat(devices // chunk, step, jnp.zeros((count * rank, width), jnp.float32))


def by_group(x_refs, groups, use):
    if len(x_refs) == 1:
        use(x_refs)
        return
    local = len(x_refs) // groups
    for g in range(groups):

        @pl.when(pl.program_id(0) == g)
        def _(g=g):
            use(x_refs[g * local : (g + 1) * local])


def send_kernel(groups, number, slots_line, count, rank, away, place_ref, packed_ref, *refs):
    line = place_ref[1]
    x_refs, got, outs = refs[:number], refs[number:-2], refs[-2:]
    ways = ((line + away < line_length, line + away), (line >= away, line - away))
    for way, (inside, target) in enumerate(ways):

        def use(x_refs, way=way, target=target):
            first = target * slots_line + pl.program_id(1) * count
            total = slot_sums(packed_ref, x_refs, place_ref[2], rank, first, count)
            if got:
                total += got[way][0].astype(jnp.float32)
            outs[way][0] = total.astype(jnp.bfloat16)

        @pl.when(inside)
        def _(use=use):
            by_group(x_refs, groups, use)


def own_kernel(groups, number, slots_line, count, rank, place_ref, packed_ref, *refs):
    x_refs, (right_ref, left_ref, out_ref) = refs[:number], refs[number:]

    def use(x_refs):
        first = place_ref[1] * slots_line + pl.program_id(1) * count
        total = slot_sums(packed_ref, x_refs, place_ref[2], rank, first, count)
        total += right_ref[0].astype(jnp.float32) + left_ref[0].astype(jnp.float32)
        out_ref[0] = (adapter_scale * total).astype(jnp.bfloat16)

    by_group(x_refs, groups, use)


def grad_a_step(place, packed, x_cols, half, got, away, groups, slots_line, rank):
    devices, depth, tokens = packed.shape
    width = x_cols[0].shape[-1] // 2
    local = devices // groups
    count = 8
    rows = count * rank
    number = len(x_cols)
    if number > 1:
        x_specs = [pl.BlockSpec((tokens, width), lambda g, s, place: (0, half))] * number
    else:
        if width % 128:
            x_cols, half = [x_cols[0][:, :, half * width : (half + 1) * width]], 0
        x_specs = [pl.BlockSpec((local, tokens, width), lambda g, s, place: (g, 0, half))]
    block = pl.BlockSpec((1, rows, width), lambda g, s, place: (g, s, 0))
    final = pl.BlockSpec((1, rows, width), lambda g, s, place: (g ^ place[0], s, 0))
    shape = jax.ShapeDtypeStruct((groups, slots_line * rank, width), jnp.bfloat16)
    ways = 1 if away == 0 else 2
    if away == 0:
        kernel = lambda *refs: own_kernel(groups, number, slots_line, count, rank, *refs)
    else:
        kernel = lambda *refs: send_kernel(groups, number, slots_line, count, rank, away, *refs)
    return call(
        kernel,
        place,
        (groups, slots_line // count),
        [pl.BlockSpec((local, depth, tokens), lambda g, s, place: (g ^ place[0], 0, 0))]
        + x_specs
        + [block] * len(got),
        final if away == 0 else [block, block],
        shape if away == 0 else [shape, shape],
        ways * 2 * devices * tokens * width * slots_line * rank,
        2 * devices * tokens * width + 2 * groups * slots_line * rank * width * (ways + len(got)),
        "grad_a_step" + str(away),
        (packed, *x_cols, *got),
    )


def in_line(slots, place_ref, total):
    slots -= place_ref[1] * (total // line_length)
    return jnp.where(slots < 0, slots + total, slots)


def put_together(pieces, a_ref):
    @pl.when(pl.program_id(0) == 0)
    def _():
        rows = pieces[0].shape[0]
        a_ref[:rows] = pieces[0][...]
        for k in range(1, line_length):
            left, right = pieces[line_length - k], pieces[line_length - 1 + k]
            a_ref[k * rows : (k + 1) * rows] = left[...] + right[...]


def low_kernel(chunk, rank, number, place_ref, packed_ref, *refs):
    x_refs, pieces, (low_ref, a_ref) = refs[:number], refs[number:-2], refs[-2:]
    put_together(pieces, a_ref)
    slots = packed_ref[0].astype(jnp.float32).T[:, rank + 1 : rank + 2].astype(jnp.int32)
    slots = in_line(slots, place_ref, a_ref.shape[0] // rank)
    tile = slots.shape[0]
    lane_slot = lax.broadcasted_iota(jnp.int32, (tile, chunk), 1) // rank

    def use(x):
        def step(c, low):
            part = pl.ds(pl.multiple_of(c * chunk, chunk), chunk)
            hidden = lax.dot_general(x, a_ref[part], NT, preferred_element_type=jnp.float32)
            hidden = jnp.where(lane_slot + c * (chunk // rank) == slots, hidden, 0.0)
            for k in range(chunk // (2 * rank)):
                low += hidden[:, k * 2 * rank : (k + 1) * 2 * rank]
            return low

        start = jnp.zeros((tile, 2 * rank), jnp.float32)
        low = repeat(a_ref.shape[0] // chunk, step, start).T
        low_ref[0] = low[:rank] + low[rank:]

    if number == 1:
        use(x_refs[0][0])
    else:
        for m in range(number):

            @pl.when(pl.program_id(0) == m)
            def _(m=m):
                use(x_refs[m][...])


def low_part(place, packed, x_cols, a_pieces, inner, rank):
    devices, depth, tokens = packed.shape
    width = x_cols[0].shape[-1]
    rows = a_pieces[0].shape[0]
    slots = line_length * rows
    number = len(x_cols)
    mate = lambda t, place: (t ^ (place[0] * inner + place[2]), 0, 0)
    if number > 1:
        x_specs = [pl.BlockSpec((tokens, width), lambda t, place: (0, 0))] * number
    else:
        x_specs = [pl.BlockSpec((1, tokens, width), lambda t, place: (t, 0, 0))]
    return call(
        lambda *refs: low_kernel(512, rank, number, *refs),
        place,
        (devices,),
        [pl.BlockSpec((1, depth, tokens), mate)]
        + x_specs
        + [pl.BlockSpec((rows, width), lambda t, place: (0, 0))] * len(a_pieces),
        pl.BlockSpec((1, rank, tokens), mate),
        jax.ShapeDtypeStruct((devices, rank, tokens), jnp.float32),
        2 * devices * tokens * width * slots,
        2 * (devices * tokens + slots) * width,
        "low_part",
        (packed, *x_cols, *a_pieces),
        [pltpu.VMEM((slots, width), jnp.bfloat16)],
    )


def out_kernel(chunk, rank, groups, place_ref, packed_ref, g_ref, *refs):
    number = 2 * line_length - 1
    a_pieces, w_pieces, (out_ref, a_ref, w_ref) = refs[:number], refs[number:-3], refs[-3:]
    put_together(a_pieces, a_ref)
    put_together(w_pieces, w_ref)
    rows = jnp.concatenate([p.astype(jnp.float32).T for p in packed_ref[...]], axis=0)
    back, slots = rows[:, :rank], rows[:, rank + 1 : rank + 2].astype(jnp.int32)
    total = a_ref.shape[0]
    slots = in_line(slots, place_ref, total // rank)
    tile = back.shape[0]
    repeated = jnp.concatenate([back] * (chunk // rank), axis=1)
    lane_slot = lax.broadcasted_iota(jnp.int32, (tile, chunk), 1) // rank

    def masked(c):
        keep = lane_slot + c * (chunk // rank) == slots
        return jnp.where(keep, repeated, 0.0).astype(jnp.bfloat16)

    if total // chunk <= 4:
        wide = jnp.concatenate([masked(c) for c in range(total // chunk)], axis=1)
        acc = jnp.dot(wide, a_ref[...], preferred_element_type=jnp.float32)
    else:

        def step(c, acc):
            block = a_ref[pl.ds(pl.multiple_of(c * chunk, chunk), chunk), :]
            return acc + jnp.dot(masked(c), block, preferred_element_type=jnp.float32)

        acc = repeat(total // chunk, step, jnp.zeros((tile, a_ref.shape[1]), jnp.float32))
    base = []
    count = w_pieces[0].shape[0]
    halves = line_length // groups
    for c in range(halves):
        at = (place_ref[0] * halves + c - place_ref[1] + line_length) % line_length
        w = w_ref[pl.ds(pl.multiple_of(at * count, count), count), :]
        base.append(lax.dot_general(g_ref[...], w, NT, preferred_element_type=jnp.float32))
    out = jnp.concatenate(base, axis=1) + adapter_scale * acc
    out_ref[...] = out.astype(out_ref.dtype).reshape(out_ref.shape)


def out_part(place, packed, g_all, w_pieces, a_pieces, groups, rank):
    devices, depth, tokens = packed.shape
    outs = g_all.shape[1]
    rows, width = a_pieces[0].shape
    slots = line_length * rows
    both = 2
    pieces = [*a_pieces, *w_pieces]
    return call(
        lambda *refs: out_kernel(512, rank, groups, *refs),
        place,
        (devices // both,),
        [
            pl.BlockSpec((both, depth, tokens), lambda t, place: (t, 0, 0)),
            pl.BlockSpec((both * tokens, outs), lambda t, place: (t, 0)),
        ]
        + [pl.BlockSpec(piece.shape, lambda t, place: (0, 0)) for piece in pieces],
        pl.BlockSpec((both, tokens, width), lambda t, place: (t, 0, 0)),
        jax.ShapeDtypeStruct((devices, tokens, width), jnp.bfloat16),
        2 * devices * tokens * width * (slots + outs),
        2 * devices * tokens * (width + outs) + 2 * slots * width,
        "out_part",
        (packed, g_all, *pieces),
        [
            pltpu.VMEM((slots, width), jnp.bfloat16),
            pltpu.VMEM((line_length * w_pieces[0].shape[0], outs), jnp.bfloat16),
        ],
    )


def body(x, g, tok, adapter_slot, w, a, b):
    groups, inner = lax.axis_size("groups"), lax.axis_size("inner")
    gi, li, ji = lax.axis_index("groups"), lax.axis_index("line"), lax.axis_index("inner")
    place = jnp.stack([gi, li, ji]).astype(jnp.int32)
    size = groups * inner
    devices = line_length * inner
    tokens, model = x.shape
    outs = g.shape[1]
    resident, _, rank = a.shape
    share = resident // groups
    count = inner * resident
    halves = line_length // groups
    width = model // size
    part = width // halves
    adapters = adapter_slot.shape[0]
    capacity = max(2, 2 * tokens // adapters)

    up = [(i, i + 1) for i in range(line_length - 1)]
    down = [(i + 1, i) for i in range(line_length - 1)]

    def hop(pieces, away):
        left, right = pieces
        return [
            lax.ppermute(left, "line", up[away - 1 :]),
            lax.ppermute(right, "line", down[: line_length - away]),
        ]

    w_hops = [hop((w, w), 1)]
    w_hops.append(hop(w_hops[0], 2))

    a_mine = split_columns(place, jnp.swapaxes(a, 1, 2), groups, halves, inner, part)
    a_own = lax.all_to_all(a_mine, plane, 0, 0, tiled=True).reshape(count * rank, width)

    def meet(m):
        return lax.ppermute(x_sends[m], plane, [(i, i ^ m) for i in range(size)])

    direct = size == 8 and part % 128 == 0
    x_cols = {}
    if direct:
        x_sends = split_pieces(place, x, groups, halves, inner, part)
        x_cols = {0: x_sends[0], 1: meet(1), 2: meet(2), 4: meet(4)}
    else:
        x_far = split_columns(place, x[None], groups, halves, inner, part)
        x_far = lax.all_to_all(x_far, plane, 0, 0, tiled=True)
        x_cols = {0: x_far[jnp.arange(size) ^ (gi * inner + ji)]}

    matches = tok == lax.broadcasted_iota(jnp.int32, (tokens, adapters), 1)
    slot = jnp.sum(jnp.where(matches, adapter_slot[None, :], 0), axis=1)
    running = jnp.cumsum(matches.astype(jnp.int32), axis=0)
    within = jnp.sum(jnp.where(matches, running - 1, 0), axis=1)
    position = slot * capacity + within
    at = lax.broadcasted_iota(jnp.int32, (adapters * capacity, tokens), 0) == position[None, :]
    at = at.astype(jnp.bfloat16)

    def route(rows):
        rows = rows.reshape(devices, resident * capacity, rows.shape[1])
        rows = lax.all_to_all(rows, row, 0, 0, tiled=True)
        return rows.reshape(devices, resident, capacity, rows.shape[2])

    g_send = jnp.dot(at, g, preferred_element_type=jnp.float32).astype(jnp.bfloat16)
    g_send, a_own, x_cols, w_hops = lax.optimization_barrier((g_send, a_own, x_cols, w_hops))
    w_hops.append(hop(w_hops[1], 3))
    g_rows = route(g_send)
    back = jnp.einsum("hjct,jrt->hjcr", g_rows, b, preferred_element_type=jnp.float32)
    back = back.astype(jnp.bfloat16).reshape(devices, resident * capacity, rank)
    hops = [hop((a_own, a_own), 1)]
    if direct:
        x_cols.update({3: meet(3), 5: meet(5)})
    back, x_cols = lax.optimization_barrier((back, x_cols))
    if direct:
        x_cols.update({6: meet(6), 7: meet(7)})
    back = lax.all_to_all(back, row, 0, 0, tiled=True).reshape(adapters * capacity, rank)
    back = lax.dot_general(
        back, at, (((0,), (0,)), ((), ())), preferred_element_type=jnp.float32
    ).astype(jnp.bfloat16)
    owner, res = slot // resident, slot % resident
    slot_a = (owner // inner) * count + ((res // share) * inner + owner % inner) * share + res % share
    names = jnp.stack([slot, slot_a] + [slot] * 14).astype(jnp.bfloat16)
    packed = jnp.concatenate([back, names], axis=0)
    packed, x_cols, hops, w_hops = lax.optimization_barrier((packed, x_cols, hops, w_hops))
    packed = jnp.broadcast_to(packed[None], (size,) + packed.shape)
    packed = lax.all_to_all(packed, plane, 0, 0, tiled=True)
    x_cols = [x_cols[m] for m in range(len(x_cols))]
    g_own, x_cols = lax.optimization_barrier((g, x_cols))
    g_all = lax.all_gather(g_own, plane, axis=0, tiled=True)

    hops.append(hop(hops[0], 2))

    def send(c, got, away):
        sums = grad_a_step(place, packed, x_cols, c, got, away, groups, count, rank)
        ahead = [(i, i + 1) for i in range(line_length - away)]
        behind = [(i, i - 1) for i in range(away, line_length)]
        moved = (lax.ppermute(sums[0], "line", ahead), lax.ppermute(sums[1], "line", behind))
        return moved, sums[0]

    def own(c, got):
        p = grad_a_step(place, packed, x_cols, c, got, 0, groups, count, rank)
        return p.reshape(size, resident * rank, part)

    first, done = send(0, (), 3)
    packed, done = lax.optimization_barrier((packed, done))
    second, done = send(1, (), 3)

    first, hops[1], done = lax.optimization_barrier((first, hops[1], done))
    hops.append(hop(hops[1], 3))
    first, done = send(0, first, 2)
    second, done = lax.optimization_barrier((second, done))
    second, done = send(1, second, 2)

    a_pieces = [a_own] + [h[0] for h in hops] + [h[1] for h in hops]
    w_pieces = [w] + [h[0] for h in w_hops] + [h[1] for h in w_hops]
    a_pieces, done = lax.optimization_barrier((a_pieces, done))
    out_cols = out_part(place, packed, g_all, w_pieces, a_pieces, groups, rank)
    first, out_cols = lax.optimization_barrier((first, out_cols))
    first, done = send(0, first, 1)
    out_back = lax.all_to_all(out_cols, plane, 0, 0, tiled=True)

    a_pieces, done = lax.optimization_barrier((a_pieces, done))
    low = low_part(place, packed, x_cols, a_pieces, inner, rank)
    second, low = lax.optimization_barrier((second, low))
    second, done = send(1, second, 1)
    first, done = lax.optimization_barrier((first, done))
    p_back = [own(0, first)]
    low, out_back, done = lax.optimization_barrier((low, out_back, done))
    low = lax.all_to_all(low, plane, 0, 0, tiled=True)
    low, p_back[0] = lax.optimization_barrier((low, p_back[0]))
    p_back[0] = lax.all_to_all(p_back[0], plane, 0, 0, tiled=True)
    low = jnp.sum(low, axis=0).astype(jnp.bfloat16)
    low = lax.dot_general(at, low, NT, preferred_element_type=jnp.float32).astype(jnp.bfloat16)
    low, p_back[0] = lax.optimization_barrier((low, p_back[0]))
    low = route(low)
    p_second, low = lax.optimization_barrier((own(1, second), low))
    p_back.append(lax.all_to_all(p_second, plane, 0, 0, tiled=True))

    grad_b = jnp.einsum("hjcr,hjco->jro", low, g_rows, preferred_element_type=jnp.float32)
    grad_b = (adapter_scale * grad_b).astype(jnp.bfloat16)
    input_gradient = join_rows(place, out_back, groups, halves, inner, part)
    grad_a = join_slots(place, p_back, resident, groups, inner).swapaxes(1, 2)
    return input_gradient, grad_a, grad_b


def solution(mesh):
    groups, rows = mesh.shape["groups"], mesh.shape["row"]
    whole = ("groups", "line", "inner")
    split = Mesh(mesh.devices.reshape(groups, line_length, rows // line_length), whole)
    return jax.shard_map(
        body,
        mesh=split,
        in_specs=(
            P(whole, None),
            P(whole, None),
            P(whole, None),
            P(),
            P(row, None),
            P(row, None, None),
            P(row, None, None),
        ),
        out_specs=(P(whole, None), P(whole, None, None), P(whole, None, None)),
        check_vma=False,
    )
```

```python
import jax
import jax.numpy as jnp
from jax import lax
from jax.experimental import pallas as pl
from jax.experimental.pallas import tpu as pltpu
from jax.sharding import Mesh, PartitionSpec as P

adapter_scale = 2.0
line_length = 4
plane = ("groups", "inner")
row = ("line", "inner")
vmem_limit = 56 * 1024 * 1024
NT = (((1,), (1,)), ((), ()))


def call(kernel, place, grid, in_specs, out_specs, out_shape, flops, moved, name, args, scratch=()):
    return pl.pallas_call(
        kernel,
        grid_spec=pltpu.PrefetchScalarGridSpec(
            num_scalar_prefetch=1,
            grid=grid,
            in_specs=in_specs,
            out_specs=out_specs,
            scratch_shapes=scratch,
        ),
        out_shape=out_shape,
        compiler_params=pltpu.CompilerParams(vmem_limit_bytes=vmem_limit),
        cost_estimate=pl.CostEstimate(flops=flops, bytes_accessed=moved, transcendentals=0),
        name=name,
    )(place, *args)


def repeat(count, step, start):
    if count <= 4:
        for i in range(count):
            start = step(i, start)
        return start
    return lax.fori_loop(0, count, step, start)


def move(name, sources, in_blocks, in_maps, outs, out_blocks, out_maps, grid, kernel, place):
    moved = 0
    for shape in outs:
        size = 4
        for n in shape:
            size *= n
        moved += size
    return call(
        kernel,
        place,
        grid,
        [pl.BlockSpec(block, index) for block, index in zip(in_blocks, in_maps)],
        [pl.BlockSpec(block, index) for block, index in zip(out_blocks, out_maps)],
        [jax.ShapeDtypeStruct(shape, jnp.bfloat16) for shape in outs],
        0,
        moved,
        name,
        sources,
    )


def columns_of(q, c, halves, inner):
    return ((q // inner) * halves + c) * inner + q % inner


def split_columns(place, rows, groups, halves, inner, width):
    slots, rank, model = rows.shape
    size, share = groups * inner, max(1, slots // groups)
    group = lambda place: place[0] if slots >= groups else 0
    if width % 128:
        mine = lax.dynamic_slice_in_dim(rows, group(place) * share, share, 0)
        mine = mine.reshape(share * rank, groups, halves, inner, width)
        return mine.transpose(1, 3, 0, 2, 4).reshape(size, share * rank, halves * width)

    def kernel(place_ref, rows_ref, out_ref):
        for q in range(size):
            for c in range(halves):
                first = columns_of(q, c, halves, inner) * width
                out_ref[q, :, c * width : (c + 1) * width] = rows_ref[0, :, first : first + width]

    tile = min(rank, 64)
    steps = rank // tile
    return move(
        "split_columns", [rows], [(1, tile, model)],
        [lambda s, r, place: (group(place) * share + s, r, 0)],
        [(size, share * rank, halves * width)], [(size, tile, halves * width)],
        [lambda s, r, place: (0, s * steps + r, 0)], (share, steps), kernel, place,
    )[0]


def split_pieces(place, rows, groups, halves, inner, width):
    count, model = rows.shape
    size = groups * inner
    tile = min(count, 64)

    def kernel(place_ref, rows_ref, *out_refs):
        me = place_ref[0] * inner + place_ref[2]
        for m in range(size):
            for c in range(halves):
                first = pl.multiple_of(columns_of(me ^ m, c, halves, inner) * width, width)
                out_refs[m][:, c * width : (c + 1) * width] = rows_ref[:, pl.ds(first, width)]

    return move(
        "split_pieces", [rows], [(tile, model)], [lambda t, place: (t, 0)],
        [(count, halves * width)] * size, [(tile, halves * width)] * size,
        [lambda t, place: (t, 0)] * size, (count // tile,), kernel, place,
    )


def join_slots(place, parts, resident, groups, inner):
    size, rows, width = parts[0].shape
    halves, rank = len(parts), rows // resident
    if width % 128:
        parts = [p.reshape(groups, inner, rows, width) for p in parts]
        joined = jnp.stack(parts, axis=1).transpose(3, 0, 1, 2, 4)
        return joined.reshape(resident, rank, -1)

    def kernel(place_ref, *refs):
        for q in range(size):
            for c in range(halves):
                first = columns_of(q, c, halves, inner) * width
                refs[-1][0, :, first : first + width] = refs[c][q]

    return move(
        "join_slots", parts, [(size, rank, width)] * halves, [lambda r, place: (0, r, 0)] * halves,
        [(resident, rank, size * halves * width)], [(1, rank, size * halves * width)],
        [lambda r, place: (r, 0, 0)], (resident,), kernel, place,
    )[0]


def join_rows(place, rows, groups, halves, inner, part):
    size, tokens = rows.shape[:2]
    if part % 128:
        rows = rows.reshape(groups, inner, tokens, halves, part)
        return rows.transpose(2, 0, 3, 1, 4).reshape(tokens, -1)
    tile = min(tokens, 64)
    model = size * halves * part

    def kernel(place_ref, rows_ref, out_ref):
        for q in range(size):
            for c in range(halves):
                first = columns_of(q, c, halves, inner) * part
                out_ref[:, first : first + part] = rows_ref[q, :, c * part : (c + 1) * part]

    return move(
        "join_rows", [rows], [(size, tile, halves * part)], [lambda t, place: (0, t, 0)],
        [(tokens, model)], [(tile, model)], [lambda t, place: (t, 0)], (tokens // tile,),
        kernel, place,
    )[0]


def slot_sums(packed_ref, x_refs, me, rank, first, count):
    devices, _, tokens = packed_ref.shape
    width = x_refs[0].shape[-1]
    chunk = min(devices, 4)

    def step(c, total):
        columns = []
        for d in range(chunk):
            device = (c * chunk + d) ^ me
            back = packed_ref[device, :rank, :]
            slots = packed_ref[device, rank : rank + 1, :].astype(jnp.float32)
            rows = [
                back * (slots == (first + i).astype(jnp.float32)).astype(jnp.bfloat16)
                for i in range(count)
            ]
            columns.append(jnp.concatenate(rows, axis=0))
        if len(x_refs) > 1:
            x = jnp.concatenate([x_ref[...] for x_ref in x_refs], axis=0)
        else:
            x = x_refs[0][pl.ds(c * chunk, chunk)].reshape(chunk * tokens, width)
        return total + jnp.dot(
            jnp.concatenate(columns, axis=1), x, preferred_element_type=jnp.float32
        )

    return repeat(devices // chunk, step, jnp.zeros((count * rank, width), jnp.float32))


def by_group(x_refs, groups, use):
    if len(x_refs) == 1:
        use(x_refs)
        return
    local = len(x_refs) // groups
    for g in range(groups):

        @pl.when(pl.program_id(0) == g)
        def _(g=g):
            use(x_refs[g * local : (g + 1) * local])


def send_kernel(groups, number, slots_line, count, rank, away, place_ref, packed_ref, *refs):
    line = place_ref[1]
    x_refs, got, outs = refs[:number], refs[number:-2], refs[-2:]
    ways = ((line + away < line_length, line + away), (line >= away, line - away))
    for way, (inside, target) in enumerate(ways):

        def use(x_refs, way=way, target=target):
            first = target * slots_line + pl.program_id(1) * count
            total = slot_sums(packed_ref, x_refs, place_ref[2], rank, first, count)
            if got:
                total += got[way][0].astype(jnp.float32)
            outs[way][0] = total.astype(jnp.bfloat16)

        @pl.when(inside)
        def _(use=use):
            by_group(x_refs, groups, use)


def own_kernel(groups, number, slots_line, count, rank, place_ref, packed_ref, *refs):
    x_refs, (right_ref, left_ref, out_ref) = refs[:number], refs[number:]

    def use(x_refs):
        first = place_ref[1] * slots_line + pl.program_id(1) * count
        total = slot_sums(packed_ref, x_refs, place_ref[2], rank, first, count)
        total += right_ref[0].astype(jnp.float32) + left_ref[0].astype(jnp.float32)
        out_ref[0] = (adapter_scale * total).astype(jnp.bfloat16)

    by_group(x_refs, groups, use)


def grad_a_step(place, packed, x_cols, half, got, away, groups, slots_line, rank):
    devices, depth, tokens = packed.shape
    width = x_cols[0].shape[-1] // 2
    local = devices // groups
    count = 8
    rows = count * rank
    number = len(x_cols)
    if number > 1:
        x_specs = [pl.BlockSpec((tokens, width), lambda g, s, place: (0, half))] * number
    else:
        if width % 128:
            x_cols, half = [x_cols[0][:, :, half * width : (half + 1) * width]], 0
        x_specs = [pl.BlockSpec((local, tokens, width), lambda g, s, place: (g, 0, half))]
    block = pl.BlockSpec((1, rows, width), lambda g, s, place: (g, s, 0))
    final = pl.BlockSpec((1, rows, width), lambda g, s, place: (g ^ place[0], s, 0))
    shape = jax.ShapeDtypeStruct((groups, slots_line * rank, width), jnp.bfloat16)
    ways = 1 if away == 0 else 2
    if away == 0:
        kernel = lambda *refs: own_kernel(groups, number, slots_line, count, rank, *refs)
    else:
        kernel = lambda *refs: send_kernel(groups, number, slots_line, count, rank, away, *refs)
    return call(
        kernel,
        place,
        (groups, slots_line // count),
        [pl.BlockSpec((local, depth, tokens), lambda g, s, place: (g ^ place[0], 0, 0))]
        + x_specs
        + [block] * len(got),
        final if away == 0 else [block, block],
        shape if away == 0 else [shape, shape],
        ways * 2 * devices * tokens * width * slots_line * rank,
        2 * devices * tokens * width + 2 * groups * slots_line * rank * width * (ways + len(got)),
        "grad_a_step" + str(away),
        (packed, *x_cols, *got),
    )


def in_line(slots, place_ref, total):
    slots -= place_ref[1] * (total // line_length)
    return jnp.where(slots < 0, slots + total, slots)


def put_together(pieces, a_ref):
    @pl.when(pl.program_id(0) == 0)
    def _():
        rows = pieces[0].shape[0]
        a_ref[:rows] = pieces[0][...]
        for k in range(1, line_length):
            left, right = pieces[line_length - k], pieces[line_length - 1 + k]
            a_ref[k * rows : (k + 1) * rows] = left[...] + right[...]


def low_kernel(chunk, rank, number, place_ref, packed_ref, *refs):
    x_refs, pieces, (low_ref, a_ref) = refs[:number], refs[number:-2], refs[-2:]
    put_together(pieces, a_ref)
    slots = packed_ref[0].astype(jnp.float32).T[:, rank + 1 : rank + 2].astype(jnp.int32)
    slots = in_line(slots, place_ref, a_ref.shape[0] // rank)
    tile = slots.shape[0]
    lane_slot = lax.broadcasted_iota(jnp.int32, (tile, chunk), 1) // rank

    def use(x):
        def step(c, low):
            part = pl.ds(pl.multiple_of(c * chunk, chunk), chunk)
            hidden = lax.dot_general(x, a_ref[part], NT, preferred_element_type=jnp.float32)
            hidden = jnp.where(lane_slot + c * (chunk // rank) == slots, hidden, 0.0)
            for k in range(chunk // (2 * rank)):
                low += hidden[:, k * 2 * rank : (k + 1) * 2 * rank]
            return low

        start = jnp.zeros((tile, 2 * rank), jnp.float32)
        low = repeat(a_ref.shape[0] // chunk, step, start).T
        low_ref[0] = low[:rank] + low[rank:]

    if number == 1:
        use(x_refs[0][0])
    else:
        for m in range(number):

            @pl.when(pl.program_id(0) == m)
            def _(m=m):
                use(x_refs[m][...])


def low_part(place, packed, x_cols, a_pieces, inner, rank):
    devices, depth, tokens = packed.shape
    width = x_cols[0].shape[-1]
    rows = a_pieces[0].shape[0]
    slots = line_length * rows
    number = len(x_cols)
    mate = lambda t, place: (t ^ (place[0] * inner + place[2]), 0, 0)
    if number > 1:
        x_specs = [pl.BlockSpec((tokens, width), lambda t, place: (0, 0))] * number
    else:
        x_specs = [pl.BlockSpec((1, tokens, width), lambda t, place: (t, 0, 0))]
    return call(
        lambda *refs: low_kernel(512, rank, number, *refs),
        place,
        (devices,),
        [pl.BlockSpec((1, depth, tokens), mate)]
        + x_specs
        + [pl.BlockSpec((rows, width), lambda t, place: (0, 0))] * len(a_pieces),
        pl.BlockSpec((1, rank, tokens), mate),
        jax.ShapeDtypeStruct((devices, rank, tokens), jnp.float32),
        2 * devices * tokens * width * slots,
        2 * (devices * tokens + slots) * width,
        "low_part",
        (packed, *x_cols, *a_pieces),
        [pltpu.VMEM((slots, width), jnp.bfloat16)],
    )


def out_kernel(chunk, rank, groups, place_ref, packed_ref, g_ref, *refs):
    number = 2 * line_length - 1
    a_pieces, w_pieces, (out_ref, a_ref, w_ref) = refs[:number], refs[number:-3], refs[-3:]
    put_together(a_pieces, a_ref)
    put_together(w_pieces, w_ref)
    rows = jnp.concatenate([p.astype(jnp.float32).T for p in packed_ref[...]], axis=0)
    back, slots = rows[:, :rank], rows[:, rank + 1 : rank + 2].astype(jnp.int32)
    total = a_ref.shape[0]
    slots = in_line(slots, place_ref, total // rank)
    tile = back.shape[0]
    repeated = jnp.concatenate([back] * (chunk // rank), axis=1)
    lane_slot = lax.broadcasted_iota(jnp.int32, (tile, chunk), 1) // rank

    def masked(c):
        keep = lane_slot + c * (chunk // rank) == slots
        return jnp.where(keep, repeated, 0.0).astype(jnp.bfloat16)

    if total // chunk <= 4:
        wide = jnp.concatenate([masked(c) for c in range(total // chunk)], axis=1)
        acc = jnp.dot(wide, a_ref[...], preferred_element_type=jnp.float32)
    else:

        def step(c, acc):
            block = a_ref[pl.ds(pl.multiple_of(c * chunk, chunk), chunk), :]
            return acc + jnp.dot(masked(c), block, preferred_element_type=jnp.float32)

        acc = repeat(total // chunk, step, jnp.zeros((tile, a_ref.shape[1]), jnp.float32))
    base = []
    count = w_pieces[0].shape[0]
    halves = line_length // groups
    for c in range(halves):
        at = (place_ref[0] * halves + c - place_ref[1] + line_length) % line_length
        w = w_ref[pl.ds(pl.multiple_of(at * count, count), count), :]
        base.append(lax.dot_general(g_ref[...], w, NT, preferred_element_type=jnp.float32))
    out = jnp.concatenate(base, axis=1) + adapter_scale * acc
    out_ref[...] = out.astype(out_ref.dtype).reshape(out_ref.shape)


def out_part(place, packed, g_all, w_pieces, a_pieces, groups, rank):
    devices, depth, tokens = packed.shape
    outs = g_all.shape[1]
    rows, width = a_pieces[0].shape
    slots = line_length * rows
    both = 2
    pieces = [*a_pieces, *w_pieces]
    return call(
        lambda *refs: out_kernel(512, rank, groups, *refs),
        place,
        (devices // both,),
        [
            pl.BlockSpec((both, depth, tokens), lambda t, place: (t, 0, 0)),
            pl.BlockSpec((both * tokens, outs), lambda t, place: (t, 0)),
        ]
        + [pl.BlockSpec(piece.shape, lambda t, place: (0, 0)) for piece in pieces],
        pl.BlockSpec((both, tokens, width), lambda t, place: (t, 0, 0)),
        jax.ShapeDtypeStruct((devices, tokens, width), jnp.bfloat16),
        2 * devices * tokens * width * (slots + outs),
        2 * devices * tokens * (width + outs) + 2 * slots * width,
        "out_part",
        (packed, g_all, *pieces),
        [
            pltpu.VMEM((slots, width), jnp.bfloat16),
            pltpu.VMEM((line_length * w_pieces[0].shape[0], outs), jnp.bfloat16),
        ],
    )


def body(x, g, tok, adapter_slot, w, a, b):
    groups, inner = lax.axis_size("groups"), lax.axis_size("inner")
    gi, li, ji = lax.axis_index("groups"), lax.axis_index("line"), lax.axis_index("inner")
    place = jnp.stack([gi, li, ji]).astype(jnp.int32)
    size = groups * inner
    devices = line_length * inner
    tokens, model = x.shape
    outs = g.shape[1]
    resident, _, rank = a.shape
    share = resident // groups
    count = inner * resident
    halves = line_length // groups
    width = model // size
    part = width // halves
    adapters = adapter_slot.shape[0]
    capacity = max(2, 2 * tokens // adapters)

    up = [(i, i + 1) for i in range(line_length - 1)]
    down = [(i + 1, i) for i in range(line_length - 1)]

    def hop(pieces, away):
        left, right = pieces
        return [
            lax.ppermute(left, "line", up[away - 1 :]),
            lax.ppermute(right, "line", down[: line_length - away]),
        ]

    w_hops = [hop((w, w), 1)]
    w_hops.append(hop(w_hops[0], 2))

    a_mine = split_columns(place, jnp.swapaxes(a, 1, 2), groups, halves, inner, part)
    a_own = lax.all_to_all(a_mine, plane, 0, 0, tiled=True).reshape(count * rank, width)

    def meet(m):
        return lax.ppermute(x_sends[m], plane, [(i, i ^ m) for i in range(size)])

    direct = size == 8 and part % 128 == 0
    x_cols = {}
    if direct:
        x_sends = split_pieces(place, x, groups, halves, inner, part)
        x_cols = {0: x_sends[0], 1: meet(1), 2: meet(2), 4: meet(4)}
    else:
        x_far = split_columns(place, x[None], groups, halves, inner, part)
        x_far = lax.all_to_all(x_far, plane, 0, 0, tiled=True)
        x_cols = {0: x_far[jnp.arange(size) ^ (gi * inner + ji)]}

    matches = tok == lax.broadcasted_iota(jnp.int32, (tokens, adapters), 1)
    slot = jnp.sum(jnp.where(matches, adapter_slot[None, :], 0), axis=1)
    running = jnp.cumsum(matches.astype(jnp.int32), axis=0)
    within = jnp.sum(jnp.where(matches, running - 1, 0), axis=1)
    position = slot * capacity + within
    at = lax.broadcasted_iota(jnp.int32, (adapters * capacity, tokens), 0) == position[None, :]
    at = at.astype(jnp.bfloat16)

    def route(rows):
        rows = rows.reshape(devices, resident * capacity, rows.shape[1])
        rows = lax.all_to_all(rows, row, 0, 0, tiled=True)
        return rows.reshape(devices, resident, capacity, rows.shape[2])

    g_send = jnp.dot(at, g, preferred_element_type=jnp.float32).astype(jnp.bfloat16)
    g_send, a_own, x_cols, w_hops = lax.optimization_barrier((g_send, a_own, x_cols, w_hops))
    w_hops.append(hop(w_hops[1], 3))
    g_rows = route(g_send)
    back = jnp.einsum("hjct,jrt->hjcr", g_rows, b, preferred_element_type=jnp.float32)
    back = back.astype(jnp.bfloat16).reshape(devices, resident * capacity, rank)
    hops = [hop((a_own, a_own), 1)]
    if direct:
        x_cols.update({3: meet(3), 5: meet(5)})
    back, x_cols = lax.optimization_barrier((back, x_cols))
    if direct:
        x_cols.update({6: meet(6), 7: meet(7)})
    back = lax.all_to_all(back, row, 0, 0, tiled=True).reshape(adapters * capacity, rank)
    back = lax.dot_general(
        back, at, (((0,), (0,)), ((), ())), preferred_element_type=jnp.float32
    ).astype(jnp.bfloat16)
    owner, res = slot // resident, slot % resident
    slot_a = (owner // inner) * count + ((res // share) * inner + owner % inner) * share + res % share
    names = jnp.stack([slot, slot_a] + [slot] * 14).astype(jnp.bfloat16)
    packed = jnp.concatenate([back, names], axis=0)
    packed, x_cols, hops, w_hops = lax.optimization_barrier((packed, x_cols, hops, w_hops))
    packed = jnp.broadcast_to(packed[None], (size,) + packed.shape)
    packed = lax.all_to_all(packed, plane, 0, 0, tiled=True)
    x_cols = [x_cols[m] for m in range(len(x_cols))]
    g_own, x_cols = lax.optimization_barrier((g, x_cols))
    g_all = lax.all_gather(g_own, plane, axis=0, tiled=True)

    hops.append(hop(hops[0], 2))

    def send(c, got, away):
        sums = grad_a_step(place, packed, x_cols, c, got, away, groups, count, rank)
        ahead = [(i, i + 1) for i in range(line_length - away)]
        behind = [(i, i - 1) for i in range(away, line_length)]
        moved = (lax.ppermute(sums[0], "line", ahead), lax.ppermute(sums[1], "line", behind))
        return moved, sums[0]

    def own(c, got):
        p = grad_a_step(place, packed, x_cols, c, got, 0, groups, count, rank)
        return p.reshape(size, resident * rank, part)

    first, done = send(0, (), 3)
    packed, done = lax.optimization_barrier((packed, done))
    second, done = send(1, (), 3)

    first, hops[1], done = lax.optimization_barrier((first, hops[1], done))
    hops.append(hop(hops[1], 3))
    first, done = send(0, first, 2)
    second, done = lax.optimization_barrier((second, done))
    second, done = send(1, second, 2)

    a_pieces = [a_own] + [h[0] for h in hops] + [h[1] for h in hops]
    w_pieces = [w] + [h[0] for h in w_hops] + [h[1] for h in w_hops]
    a_pieces, done = lax.optimization_barrier((a_pieces, done))
    out_cols = out_part(place, packed, g_all, w_pieces, a_pieces, groups, rank)
    first, out_cols = lax.optimization_barrier((first, out_cols))
    first, done = send(0, first, 1)
    out_back = lax.all_to_all(out_cols, plane, 0, 0, tiled=True)

    a_pieces, done = lax.optimization_barrier((a_pieces, done))
    low = low_part(place, packed, x_cols, a_pieces, inner, rank)
    second, low = lax.optimization_barrier((second, low))
    second, done = send(1, second, 1)
    first, done = lax.optimization_barrier((first, done))
    p_first = own(0, first)
    second, p_first = lax.optimization_barrier((second, p_first))
    p_second = own(1, second)
    p_first, out_back = lax.optimization_barrier((p_first, out_back))
    p_back = [lax.all_to_all(p_first, plane, 0, 0, tiled=True)]
    low, p_back[0] = lax.optimization_barrier((low, p_back[0]))
    low = lax.all_to_all(low, plane, 0, 0, tiled=True)
    p_second, low = lax.optimization_barrier((p_second, low))
    p_back.append(lax.all_to_all(p_second, plane, 0, 0, tiled=True))
    low = jnp.sum(low, axis=0).astype(jnp.bfloat16)
    low = lax.dot_general(at, low, NT, preferred_element_type=jnp.float32).astype(jnp.bfloat16)
    low, p_back = lax.optimization_barrier((low, p_back))
    low = route(low)

    grad_b = jnp.einsum("hjcr,hjco->jro", low, g_rows, preferred_element_type=jnp.float32)
    grad_b = (adapter_scale * grad_b).astype(jnp.bfloat16)
    input_gradient = join_rows(place, out_back, groups, halves, inner, part)
    grad_a = join_slots(place, p_back, resident, groups, inner).swapaxes(1, 2)
    return input_gradient, grad_a, grad_b


def solution(mesh):
    groups, rows = mesh.shape["groups"], mesh.shape["row"]
    whole = ("groups", "line", "inner")
    split = Mesh(mesh.devices.reshape(groups, line_length, rows // line_length), whole)
    return jax.shard_map(
        body,
        mesh=split,
        in_specs=(
            P(whole, None),
            P(whole, None),
            P(whole, None),
            P(),
            P(row, None),
            P(row, None, None),
            P(row, None, None),
        ),
        out_specs=(P(whole, None), P(whole, None, None), P(whole, None, None)),
        check_vma=False,
    )
```

```python
import jax
import jax.numpy as jnp
from jax import lax
from jax.experimental import pallas as pl
from jax.experimental.pallas import tpu as pltpu
from jax.sharding import Mesh, PartitionSpec as P

adapter_scale = 2.0
line_length = 4
plane = ("groups", "inner")
row = ("line", "inner")
vmem_limit = 56 * 1024 * 1024
NT = (((1,), (1,)), ((), ()))


def call(kernel, place, grid, in_specs, out_specs, out_shape, flops, moved, name, args, scratch=()):
    return pl.pallas_call(
        kernel,
        grid_spec=pltpu.PrefetchScalarGridSpec(
            num_scalar_prefetch=1,
            grid=grid,
            in_specs=in_specs,
            out_specs=out_specs,
            scratch_shapes=scratch,
        ),
        out_shape=out_shape,
        compiler_params=pltpu.CompilerParams(vmem_limit_bytes=vmem_limit),
        cost_estimate=pl.CostEstimate(flops=flops, bytes_accessed=moved, transcendentals=0),
        name=name,
    )(place, *args)


def repeat(count, step, start):
    if count <= 4:
        for i in range(count):
            start = step(i, start)
        return start
    return lax.fori_loop(0, count, step, start)


def move(name, sources, in_blocks, in_maps, outs, out_blocks, out_maps, grid, kernel, place):
    moved = 0
    for shape in outs:
        size = 4
        for n in shape:
            size *= n
        moved += size
    return call(
        kernel,
        place,
        grid,
        [pl.BlockSpec(block, index) for block, index in zip(in_blocks, in_maps)],
        [pl.BlockSpec(block, index) for block, index in zip(out_blocks, out_maps)],
        [jax.ShapeDtypeStruct(shape, jnp.bfloat16) for shape in outs],
        0,
        moved,
        name,
        sources,
    )


def columns_of(q, c, halves, inner):
    return ((q // inner) * halves + c) * inner + q % inner


def split_columns(place, rows, groups, halves, inner, width):
    slots, rank, model = rows.shape
    size, share = groups * inner, max(1, slots // groups)
    group = lambda place: place[0] if slots >= groups else 0
    if width % 128:
        mine = lax.dynamic_slice_in_dim(rows, group(place) * share, share, 0)
        mine = mine.reshape(share * rank, groups, halves, inner, width)
        return mine.transpose(1, 3, 0, 2, 4).reshape(size, share * rank, halves * width)

    def kernel(place_ref, rows_ref, out_ref):
        for q in range(size):
            for c in range(halves):
                first = columns_of(q, c, halves, inner) * width
                out_ref[q, :, c * width : (c + 1) * width] = rows_ref[0, :, first : first + width]

    tile = min(rank, 64)
    steps = rank // tile
    return move(
        "split_columns", [rows], [(1, tile, model)],
        [lambda s, r, place: (group(place) * share + s, r, 0)],
        [(size, share * rank, halves * width)], [(size, tile, halves * width)],
        [lambda s, r, place: (0, s * steps + r, 0)], (share, steps), kernel, place,
    )[0]


def split_pieces(place, rows, groups, halves, inner, width):
    count, model = rows.shape
    size = groups * inner
    tile = min(count, 64)

    def kernel(place_ref, rows_ref, *out_refs):
        me = place_ref[0] * inner + place_ref[2]
        for m in range(size):
            for c in range(halves):
                first = pl.multiple_of(columns_of(me ^ m, c, halves, inner) * width, width)
                out_refs[m][:, c * width : (c + 1) * width] = rows_ref[:, pl.ds(first, width)]

    return move(
        "split_pieces", [rows], [(tile, model)], [lambda t, place: (t, 0)],
        [(count, halves * width)] * size, [(tile, halves * width)] * size,
        [lambda t, place: (t, 0)] * size, (count // tile,), kernel, place,
    )


def join_slots(place, parts, resident, groups, halves, inner):
    size, rows, width = parts.shape
    rows = rows // halves
    rank = rows // resident
    if width % 128:
        parts = [
            parts[:, c * rows : (c + 1) * rows].reshape(groups, inner, rows, width)
            for c in range(halves)
        ]
        joined = jnp.stack(parts, axis=1).transpose(3, 0, 1, 2, 4)
        return joined.reshape(resident, rank, -1)

    def kernel(place_ref, *refs):
        for q in range(size):
            for c in range(halves):
                first = columns_of(q, c, halves, inner) * width
                refs[-1][0, :, first : first + width] = refs[c][q]

    return move(
        "join_slots", [parts] * halves, [(size, rank, width)] * halves,
        [lambda r, place, c=c: (0, c * resident + r, 0) for c in range(halves)],
        [(resident, rank, size * halves * width)], [(1, rank, size * halves * width)],
        [lambda r, place: (r, 0, 0)], (resident,), kernel, place,
    )[0]


def join_rows(place, rows, groups, halves, inner, part):
    size, tokens = rows.shape[:2]
    if part % 128:
        rows = rows.reshape(groups, inner, tokens, halves, part)
        return rows.transpose(2, 0, 3, 1, 4).reshape(tokens, -1)
    tile = min(tokens, 64)
    model = size * halves * part

    def kernel(place_ref, rows_ref, out_ref):
        for q in range(size):
            for c in range(halves):
                first = columns_of(q, c, halves, inner) * part
                out_ref[:, first : first + part] = rows_ref[q, :, c * part : (c + 1) * part]

    return move(
        "join_rows", [rows], [(size, tile, halves * part)], [lambda t, place: (0, t, 0)],
        [(tokens, model)], [(tile, model)], [lambda t, place: (t, 0)], (tokens // tile,),
        kernel, place,
    )[0]


def slot_sums(packed_ref, x_refs, me, rank, first, count):
    devices, _, tokens = packed_ref.shape
    width = x_refs[0].shape[-1]
    chunk = min(devices, 4)

    def step(c, total):
        columns = []
        for d in range(chunk):
            device = (c * chunk + d) ^ me
            back = packed_ref[device, :rank, :]
            slots = packed_ref[device, rank : rank + 1, :].astype(jnp.float32)
            rows = [
                back * (slots == (first + i).astype(jnp.float32)).astype(jnp.bfloat16)
                for i in range(count)
            ]
            columns.append(jnp.concatenate(rows, axis=0))
        if len(x_refs) > 1:
            x = jnp.concatenate([x_ref[...] for x_ref in x_refs], axis=0)
        else:
            x = x_refs[0][pl.ds(c * chunk, chunk)].reshape(chunk * tokens, width)
        return total + jnp.dot(
            jnp.concatenate(columns, axis=1), x, preferred_element_type=jnp.float32
        )

    return repeat(devices // chunk, step, jnp.zeros((count * rank, width), jnp.float32))


def by_group(x_refs, groups, use):
    if len(x_refs) == 1:
        use(x_refs)
        return
    local = len(x_refs) // groups
    for g in range(groups):

        @pl.when(pl.program_id(0) == g)
        def _(g=g):
            use(x_refs[g * local : (g + 1) * local])


def send_kernel(groups, number, slots_line, count, rank, away, place_ref, packed_ref, *refs):
    line = place_ref[1]
    x_refs, got, outs = refs[:number], refs[number:-2], refs[-2:]
    ways = ((line + away < line_length, line + away), (line >= away, line - away))
    for way, (inside, target) in enumerate(ways):

        def use(x_refs, way=way, target=target):
            first = target * slots_line + pl.program_id(1) * count
            total = slot_sums(packed_ref, x_refs, place_ref[2], rank, first, count)
            if got:
                total += got[way][0].astype(jnp.float32)
            outs[way][0] = total.astype(jnp.bfloat16)

        @pl.when(inside)
        def _(use=use):
            by_group(x_refs, groups, use)


def own_kernel(groups, number, slots_line, count, rank, place_ref, packed_ref, *refs):
    x_refs, (right_ref, left_ref, out_ref) = refs[:number], refs[number:]

    def use(x_refs):
        first = place_ref[1] * slots_line + pl.program_id(1) * count
        total = slot_sums(packed_ref, x_refs, place_ref[2], rank, first, count)
        total += right_ref[0].astype(jnp.float32) + left_ref[0].astype(jnp.float32)
        out_ref[0] = (adapter_scale * total).astype(jnp.bfloat16)

    by_group(x_refs, groups, use)


def grad_a_step(place, packed, x_cols, half, got, away, groups, slots_line, rank):
    devices, depth, tokens = packed.shape
    width = x_cols[0].shape[-1] // 2
    local = devices // groups
    count = 8
    rows = count * rank
    number = len(x_cols)
    if number > 1:
        x_specs = [pl.BlockSpec((tokens, width), lambda g, s, place: (0, half))] * number
    else:
        if width % 128:
            x_cols, half = [x_cols[0][:, :, half * width : (half + 1) * width]], 0
        x_specs = [pl.BlockSpec((local, tokens, width), lambda g, s, place: (g, 0, half))]
    block = pl.BlockSpec((1, rows, width), lambda g, s, place: (g, s, 0))
    final = pl.BlockSpec((1, rows, width), lambda g, s, place: (g ^ place[0], s, 0))
    shape = jax.ShapeDtypeStruct((groups, slots_line * rank, width), jnp.bfloat16)
    ways = 1 if away == 0 else 2
    if away == 0:
        kernel = lambda *refs: own_kernel(groups, number, slots_line, count, rank, *refs)
    else:
        kernel = lambda *refs: send_kernel(groups, number, slots_line, count, rank, away, *refs)
    return call(
        kernel,
        place,
        (groups, slots_line // count),
        [pl.BlockSpec((local, depth, tokens), lambda g, s, place: (g ^ place[0], 0, 0))]
        + x_specs
        + [block] * len(got),
        final if away == 0 else [block, block],
        shape if away == 0 else [shape, shape],
        ways * 2 * devices * tokens * width * slots_line * rank,
        2 * devices * tokens * width + 2 * groups * slots_line * rank * width * (ways + len(got)),
        "grad_a_step" + str(away),
        (packed, *x_cols, *got),
    )


def in_line(slots, place_ref, total):
    slots -= place_ref[1] * (total // line_length)
    return jnp.where(slots < 0, slots + total, slots)


def put_together(pieces, a_ref):
    @pl.when(pl.program_id(0) == 0)
    def _():
        rows = pieces[0].shape[0]
        a_ref[:rows] = pieces[0][...]
        for k in range(1, line_length):
            left, right = pieces[line_length - k], pieces[line_length - 1 + k]
            a_ref[k * rows : (k + 1) * rows] = left[...] + right[...]


def low_kernel(chunk, rank, number, place_ref, packed_ref, *refs):
    x_refs, pieces, (low_ref, a_ref) = refs[:number], refs[number:-2], refs[-2:]
    put_together(pieces, a_ref)
    slots = packed_ref[0].astype(jnp.float32).T[:, rank + 1 : rank + 2].astype(jnp.int32)
    slots = in_line(slots, place_ref, a_ref.shape[0] // rank)
    tile = slots.shape[0]
    lane_slot = lax.broadcasted_iota(jnp.int32, (tile, chunk), 1) // rank

    def use(x):
        def step(c, low):
            part = pl.ds(pl.multiple_of(c * chunk, chunk), chunk)
            hidden = lax.dot_general(x, a_ref[part], NT, preferred_element_type=jnp.float32)
            hidden = jnp.where(lane_slot + c * (chunk // rank) == slots, hidden, 0.0)
            for k in range(chunk // (2 * rank)):
                low += hidden[:, k * 2 * rank : (k + 1) * 2 * rank]
            return low

        start = jnp.zeros((tile, 2 * rank), jnp.float32)
        low = repeat(a_ref.shape[0] // chunk, step, start).T
        low_ref[0] = low[:rank] + low[rank:]

    if number == 1:
        use(x_refs[0][0])
    else:
        for m in range(number):

            @pl.when(pl.program_id(0) == m)
            def _(m=m):
                use(x_refs[m][...])


def low_part(place, packed, x_cols, a_pieces, inner, rank):
    devices, depth, tokens = packed.shape
    width = x_cols[0].shape[-1]
    rows = a_pieces[0].shape[0]
    slots = line_length * rows
    number = len(x_cols)
    mate = lambda t, place: (t ^ (place[0] * inner + place[2]), 0, 0)
    if number > 1:
        x_specs = [pl.BlockSpec((tokens, width), lambda t, place: (0, 0))] * number
    else:
        x_specs = [pl.BlockSpec((1, tokens, width), lambda t, place: (t, 0, 0))]
    return call(
        lambda *refs: low_kernel(512, rank, number, *refs),
        place,
        (devices,),
        [pl.BlockSpec((1, depth, tokens), mate)]
        + x_specs
        + [pl.BlockSpec((rows, width), lambda t, place: (0, 0))] * len(a_pieces),
        pl.BlockSpec((1, rank, tokens), mate),
        jax.ShapeDtypeStruct((devices, rank, tokens), jnp.float32),
        2 * devices * tokens * width * slots,
        2 * (devices * tokens + slots) * width,
        "low_part",
        (packed, *x_cols, *a_pieces),
        [pltpu.VMEM((slots, width), jnp.bfloat16)],
    )


def out_kernel(chunk, rank, groups, place_ref, packed_ref, g_ref, *refs):
    number = 2 * line_length - 1
    a_pieces, w_pieces, (out_ref, a_ref, w_ref) = refs[:number], refs[number:-3], refs[-3:]
    put_together(a_pieces, a_ref)
    put_together(w_pieces, w_ref)
    rows = jnp.concatenate([p.astype(jnp.float32).T for p in packed_ref[...]], axis=0)
    back, slots = rows[:, :rank], rows[:, rank + 1 : rank + 2].astype(jnp.int32)
    total = a_ref.shape[0]
    slots = in_line(slots, place_ref, total // rank)
    tile = back.shape[0]
    repeated = jnp.concatenate([back] * (chunk // rank), axis=1)
    lane_slot = lax.broadcasted_iota(jnp.int32, (tile, chunk), 1) // rank

    def masked(c):
        keep = lane_slot + c * (chunk // rank) == slots
        return jnp.where(keep, repeated, 0.0).astype(jnp.bfloat16)

    if total // chunk <= 4:
        wide = jnp.concatenate([masked(c) for c in range(total // chunk)], axis=1)
        acc = jnp.dot(wide, a_ref[...], preferred_element_type=jnp.float32)
    else:

        def step(c, acc):
            block = a_ref[pl.ds(pl.multiple_of(c * chunk, chunk), chunk), :]
            return acc + jnp.dot(masked(c), block, preferred_element_type=jnp.float32)

        acc = repeat(total // chunk, step, jnp.zeros((tile, a_ref.shape[1]), jnp.float32))
    base = []
    count = w_pieces[0].shape[0]
    halves = line_length // groups
    for c in range(halves):
        at = (place_ref[0] * halves + c - place_ref[1] + line_length) % line_length
        w = w_ref[pl.ds(pl.multiple_of(at * count, count), count), :]
        base.append(lax.dot_general(g_ref[...], w, NT, preferred_element_type=jnp.float32))
    out = jnp.concatenate(base, axis=1) + adapter_scale * acc
    out_ref[...] = out.astype(out_ref.dtype).reshape(out_ref.shape)


def out_part(place, packed, g_all, w_pieces, a_pieces, groups, rank):
    devices, depth, tokens = packed.shape
    outs = g_all.shape[1]
    rows, width = a_pieces[0].shape
    slots = line_length * rows
    both = 2
    pieces = [*a_pieces, *w_pieces]
    return call(
        lambda *refs: out_kernel(512, rank, groups, *refs),
        place,
        (devices // both,),
        [
            pl.BlockSpec((both, depth, tokens), lambda t, place: (t, 0, 0)),
            pl.BlockSpec((both * tokens, outs), lambda t, place: (t, 0)),
        ]
        + [pl.BlockSpec(piece.shape, lambda t, place: (0, 0)) for piece in pieces],
        pl.BlockSpec((both, tokens, width), lambda t, place: (t, 0, 0)),
        jax.ShapeDtypeStruct((devices, tokens, width), jnp.bfloat16),
        2 * devices * tokens * width * (slots + outs),
        2 * devices * tokens * (width + outs) + 2 * slots * width,
        "out_part",
        (packed, g_all, *pieces),
        [
            pltpu.VMEM((slots, width), jnp.bfloat16),
            pltpu.VMEM((line_length * w_pieces[0].shape[0], outs), jnp.bfloat16),
        ],
    )


def body(x, g, tok, adapter_slot, w, a, b):
    groups, inner = lax.axis_size("groups"), lax.axis_size("inner")
    gi, li, ji = lax.axis_index("groups"), lax.axis_index("line"), lax.axis_index("inner")
    place = jnp.stack([gi, li, ji]).astype(jnp.int32)
    size = groups * inner
    devices = line_length * inner
    tokens, model = x.shape
    outs = g.shape[1]
    resident, _, rank = a.shape
    share = resident // groups
    count = inner * resident
    halves = line_length // groups
    width = model // size
    part = width // halves
    adapters = adapter_slot.shape[0]
    capacity = max(2, 2 * tokens // adapters)

    up = [(i, i + 1) for i in range(line_length - 1)]
    down = [(i + 1, i) for i in range(line_length - 1)]

    def hop(pieces, away):
        left, right = pieces
        return [
            lax.ppermute(left, "line", up[away - 1 :]),
            lax.ppermute(right, "line", down[: line_length - away]),
        ]

    w_hops = [hop((w, w), 1)]
    w_hops.append(hop(w_hops[0], 2))

    a_mine = split_columns(place, jnp.swapaxes(a, 1, 2), groups, halves, inner, part)
    a_own = lax.all_to_all(a_mine, plane, 0, 0, tiled=True).reshape(count * rank, width)

    def meet(m):
        return lax.ppermute(x_sends[m], plane, [(i, i ^ m) for i in range(size)])

    direct = size == 8 and part % 128 == 0
    x_cols = {}
    if direct:
        x_sends = split_pieces(place, x, groups, halves, inner, part)
        x_cols = {0: x_sends[0], 1: meet(1), 2: meet(2), 4: meet(4)}
    else:
        x_far = split_columns(place, x[None], groups, halves, inner, part)
        x_far = lax.all_to_all(x_far, plane, 0, 0, tiled=True)
        x_cols = {0: x_far[jnp.arange(size) ^ (gi * inner + ji)]}

    matches = tok == lax.broadcasted_iota(jnp.int32, (tokens, adapters), 1)
    slot = jnp.sum(jnp.where(matches, adapter_slot[None, :], 0), axis=1)
    running = jnp.cumsum(matches.astype(jnp.int32), axis=0)
    within = jnp.sum(jnp.where(matches, running - 1, 0), axis=1)
    position = slot * capacity + within
    at = lax.broadcasted_iota(jnp.int32, (adapters * capacity, tokens), 0) == position[None, :]
    at = at.astype(jnp.bfloat16)

    def route(rows):
        rows = rows.reshape(devices, resident * capacity, rows.shape[1])
        rows = lax.all_to_all(rows, row, 0, 0, tiled=True)
        return rows.reshape(devices, resident, capacity, rows.shape[2])

    g_send = jnp.dot(at, g, preferred_element_type=jnp.float32).astype(jnp.bfloat16)
    g_send, a_own, x_cols, w_hops = lax.optimization_barrier((g_send, a_own, x_cols, w_hops))
    w_hops.append(hop(w_hops[1], 3))
    g_rows = route(g_send)
    back = jnp.einsum("hjct,jrt->hjcr", g_rows, b, preferred_element_type=jnp.float32)
    back = back.astype(jnp.bfloat16).reshape(devices, resident * capacity, rank)
    hops = [hop((a_own, a_own), 1)]
    if direct:
        x_cols.update({3: meet(3), 5: meet(5)})
    back, x_cols = lax.optimization_barrier((back, x_cols))
    if direct:
        x_cols.update({6: meet(6), 7: meet(7)})
    back = lax.all_to_all(back, row, 0, 0, tiled=True).reshape(adapters * capacity, rank)
    back = lax.dot_general(
        back, at, (((0,), (0,)), ((), ())), preferred_element_type=jnp.float32
    ).astype(jnp.bfloat16)
    owner, res = slot // resident, slot % resident
    slot_a = (owner // inner) * count + ((res // share) * inner + owner % inner) * share + res % share
    names = jnp.stack([slot, slot_a] + [slot] * 14).astype(jnp.bfloat16)
    packed = jnp.concatenate([back, names], axis=0)
    packed, x_cols, hops, w_hops = lax.optimization_barrier((packed, x_cols, hops, w_hops))
    packed = jnp.broadcast_to(packed[None], (size,) + packed.shape)
    packed = lax.all_to_all(packed, plane, 0, 0, tiled=True)
    x_cols = [x_cols[m] for m in range(len(x_cols))]
    g_own, x_cols = lax.optimization_barrier((g, x_cols))
    g_all = lax.all_gather(g_own, plane, axis=0, tiled=True)

    hops.append(hop(hops[0], 2))

    def send(c, got, away):
        sums = grad_a_step(place, packed, x_cols, c, got, away, groups, count, rank)
        ahead = [(i, i + 1) for i in range(line_length - away)]
        behind = [(i, i - 1) for i in range(away, line_length)]
        moved = (lax.ppermute(sums[0], "line", ahead), lax.ppermute(sums[1], "line", behind))
        return moved, sums[0]

    def own(c, got):
        p = grad_a_step(place, packed, x_cols, c, got, 0, groups, count, rank)
        return p.reshape(size, resident * rank, part)

    first, done = send(0, (), 3)
    packed, done = lax.optimization_barrier((packed, done))
    second, done = send(1, (), 3)

    first, hops[1], done = lax.optimization_barrier((first, hops[1], done))
    hops.append(hop(hops[1], 3))
    first, done = send(0, first, 2)
    second, done = lax.optimization_barrier((second, done))
    second, done = send(1, second, 2)

    a_pieces = [a_own] + [h[0] for h in hops] + [h[1] for h in hops]
    w_pieces = [w] + [h[0] for h in w_hops] + [h[1] for h in w_hops]
    a_pieces, done = lax.optimization_barrier((a_pieces, done))
    out_cols = out_part(place, packed, g_all, w_pieces, a_pieces, groups, rank)
    first, out_cols = lax.optimization_barrier((first, out_cols))
    first, done = send(0, first, 1)
    out_back = lax.all_to_all(out_cols, plane, 0, 0, tiled=True)

    a_pieces, done = lax.optimization_barrier((a_pieces, done))
    low = low_part(place, packed, x_cols, a_pieces, inner, rank)
    second, low = lax.optimization_barrier((second, low))
    second, done = send(1, second, 1)
    first, done = lax.optimization_barrier((first, done))
    p_first = own(0, first)
    second, p_first = lax.optimization_barrier((second, p_first))
    p_second = own(1, second)
    low, out_back = lax.optimization_barrier((low, out_back))
    low = lax.all_to_all(low, plane, 0, 0, tiled=True)
    p_back = jnp.concatenate([p_first, p_second], axis=1)
    p_back, low = lax.optimization_barrier((p_back, low))
    p_back = lax.all_to_all(p_back, plane, 0, 0, tiled=True)
    low = jnp.sum(low, axis=0).astype(jnp.bfloat16)
    low = lax.dot_general(at, low, NT, preferred_element_type=jnp.float32).astype(jnp.bfloat16)
    low, p_back = lax.optimization_barrier((low, p_back))
    low = route(low)

    grad_b = jnp.einsum("hjcr,hjco->jro", low, g_rows, preferred_element_type=jnp.float32)
    grad_b = (adapter_scale * grad_b).astype(jnp.bfloat16)
    input_gradient = join_rows(place, out_back, groups, halves, inner, part)
    grad_a = join_slots(place, p_back, resident, groups, halves, inner).swapaxes(1, 2)
    return input_gradient, grad_a, grad_b


def solution(mesh):
    groups, rows = mesh.shape["groups"], mesh.shape["row"]
    whole = ("groups", "line", "inner")
    split = Mesh(mesh.devices.reshape(groups, line_length, rows // line_length), whole)
    return jax.shard_map(
        body,
        mesh=split,
        in_specs=(
            P(whole, None),
            P(whole, None),
            P(whole, None),
            P(),
            P(row, None),
            P(row, None, None),
            P(row, None, None),
        ),
        out_specs=(P(whole, None), P(whole, None, None), P(whole, None, None)),
        check_vma=False,
    )
```

```python
import jax
import jax.numpy as jnp
from jax import lax
from jax.experimental import pallas as pl
from jax.experimental.pallas import tpu as pltpu
from jax.sharding import Mesh, PartitionSpec as P

adapter_scale = 2.0
line_length = 4
plane = ("groups", "inner")
row = ("line", "inner")
vmem_limit = 56 * 1024 * 1024
NT = (((1,), (1,)), ((), ()))


def call(kernel, place, grid, in_specs, out_specs, out_shape, flops, moved, name, args, scratch=()):
    return pl.pallas_call(
        kernel,
        grid_spec=pltpu.PrefetchScalarGridSpec(
            num_scalar_prefetch=1,
            grid=grid,
            in_specs=in_specs,
            out_specs=out_specs,
            scratch_shapes=scratch,
        ),
        out_shape=out_shape,
        compiler_params=pltpu.CompilerParams(vmem_limit_bytes=vmem_limit),
        cost_estimate=pl.CostEstimate(flops=flops, bytes_accessed=moved, transcendentals=0),
        name=name,
    )(place, *args)


def repeat(count, step, start):
    if count <= 4:
        for i in range(count):
            start = step(i, start)
        return start
    return lax.fori_loop(0, count, step, start)


def move(name, sources, in_blocks, in_maps, outs, out_blocks, out_maps, grid, kernel, place):
    moved = 0
    for shape in outs:
        size = 4
        for n in shape:
            size *= n
        moved += size
    return call(
        kernel,
        place,
        grid,
        [pl.BlockSpec(block, index) for block, index in zip(in_blocks, in_maps)],
        [pl.BlockSpec(block, index) for block, index in zip(out_blocks, out_maps)],
        [jax.ShapeDtypeStruct(shape, jnp.bfloat16) for shape in outs],
        0,
        moved,
        name,
        sources,
    )


def columns_of(q, c, halves, inner):
    return ((q // inner) * halves + c) * inner + q % inner


def split_columns(place, rows, groups, halves, inner, width):
    slots, rank, model = rows.shape
    size, share = groups * inner, max(1, slots // groups)
    group = lambda place: place[0] if slots >= groups else 0
    if width % 128:
        mine = lax.dynamic_slice_in_dim(rows, group(place) * share, share, 0)
        mine = mine.reshape(share * rank, groups, halves, inner, width)
        return mine.transpose(1, 3, 0, 2, 4).reshape(size, share * rank, halves * width)

    def kernel(place_ref, rows_ref, out_ref):
        for q in range(size):
            for c in range(halves):
                first = columns_of(q, c, halves, inner) * width
                out_ref[q, :, c * width : (c + 1) * width] = rows_ref[0, :, first : first + width]

    tile = min(rank, 64)
    steps = rank // tile
    return move(
        "split_columns", [rows], [(1, tile, model)],
        [lambda s, r, place: (group(place) * share + s, r, 0)],
        [(size, share * rank, halves * width)], [(size, tile, halves * width)],
        [lambda s, r, place: (0, s * steps + r, 0)], (share, steps), kernel, place,
    )[0]


def split_pieces(place, rows, groups, halves, inner, width):
    count, model = rows.shape
    size = groups * inner
    tile = min(count, 64)

    def kernel(place_ref, rows_ref, *out_refs):
        me = place_ref[0] * inner + place_ref[2]
        for m in range(size):
            for c in range(halves):
                first = pl.multiple_of(columns_of(me ^ m, c, halves, inner) * width, width)
                out_refs[m][:, c * width : (c + 1) * width] = rows_ref[:, pl.ds(first, width)]

    return move(
        "split_pieces", [rows], [(tile, model)], [lambda t, place: (t, 0)],
        [(count, halves * width)] * size, [(tile, halves * width)] * size,
        [lambda t, place: (t, 0)] * size, (count // tile,), kernel, place,
    )


def join_slots(place, parts, resident, groups, halves, inner):
    size, rows, width = parts.shape
    rows = rows // halves
    rank = rows // resident
    if width % 128:
        parts = [
            parts[:, c * rows : (c + 1) * rows].reshape(groups, inner, rows, width)
            for c in range(halves)
        ]
        joined = jnp.stack(parts, axis=1).transpose(3, 0, 1, 2, 4)
        return joined.reshape(resident, rank, -1)

    def kernel(place_ref, *refs):
        for q in range(size):
            for c in range(halves):
                first = columns_of(q, c, halves, inner) * width
                refs[-1][0, :, first : first + width] = refs[c][q]

    return move(
        "join_slots", [parts] * halves, [(size, rank, width)] * halves,
        [lambda r, place, c=c: (0, c * resident + r, 0) for c in range(halves)],
        [(resident, rank, size * halves * width)], [(1, rank, size * halves * width)],
        [lambda r, place: (r, 0, 0)], (resident,), kernel, place,
    )[0]


def join_rows(place, rows, groups, halves, inner, part):
    size, tokens = rows.shape[:2]
    if part % 128:
        rows = rows.reshape(groups, inner, tokens, halves, part)
        return rows.transpose(2, 0, 3, 1, 4).reshape(tokens, -1)
    tile = min(tokens, 64)
    model = size * halves * part

    def kernel(place_ref, rows_ref, out_ref):
        for q in range(size):
            for c in range(halves):
                first = columns_of(q, c, halves, inner) * part
                out_ref[:, first : first + part] = rows_ref[q, :, c * part : (c + 1) * part]

    return move(
        "join_rows", [rows], [(size, tile, halves * part)], [lambda t, place: (0, t, 0)],
        [(tokens, model)], [(tile, model)], [lambda t, place: (t, 0)], (tokens // tile,),
        kernel, place,
    )[0]


def slot_sums(packed_ref, x_refs, me, rank, first, count):
    devices, _, tokens = packed_ref.shape
    width = x_refs[0].shape[-1]
    chunk = min(devices, 4)

    def step(c, total):
        columns = []
        for d in range(chunk):
            device = (c * chunk + d) ^ me
            back = packed_ref[device, :rank, :]
            slots = packed_ref[device, rank : rank + 1, :].astype(jnp.float32)
            rows = [
                back * (slots == (first + i).astype(jnp.float32)).astype(jnp.bfloat16)
                for i in range(count)
            ]
            columns.append(jnp.concatenate(rows, axis=0))
        if len(x_refs) > 1:
            x = jnp.concatenate([x_ref[...] for x_ref in x_refs], axis=0)
        else:
            x = x_refs[0][pl.ds(c * chunk, chunk)].reshape(chunk * tokens, width)
        return total + jnp.dot(
            jnp.concatenate(columns, axis=1), x, preferred_element_type=jnp.float32
        )

    return repeat(devices // chunk, step, jnp.zeros((count * rank, width), jnp.float32))


def by_group(x_refs, groups, use):
    if len(x_refs) == 1:
        use(x_refs)
        return
    local = len(x_refs) // groups
    for g in range(groups):

        @pl.when(pl.program_id(0) == g)
        def _(g=g):
            use(x_refs[g * local : (g + 1) * local])


def send_kernel(groups, number, slots_line, count, rank, away, place_ref, packed_ref, *refs):
    line = place_ref[1]
    x_refs, got, outs = refs[:number], refs[number:-2], refs[-2:]
    ways = ((line + away < line_length, line + away), (line >= away, line - away))
    for way, (inside, target) in enumerate(ways):

        def use(x_refs, way=way, target=target):
            first = target * slots_line + pl.program_id(1) * count
            total = slot_sums(packed_ref, x_refs, place_ref[2], rank, first, count)
            if got:
                total += got[way][0].astype(jnp.float32)
            outs[way][0] = total.astype(jnp.bfloat16)

        @pl.when(inside)
        def _(use=use):
            by_group(x_refs, groups, use)


def own_kernel(groups, number, slots_line, count, rank, place_ref, packed_ref, *refs):
    x_refs, (right_ref, left_ref, out_ref) = refs[:number], refs[number:]

    def use(x_refs):
        first = place_ref[1] * slots_line + pl.program_id(1) * count
        total = slot_sums(packed_ref, x_refs, place_ref[2], rank, first, count)
        total += right_ref[0].astype(jnp.float32) + left_ref[0].astype(jnp.float32)
        out_ref[0] = (adapter_scale * total).astype(jnp.bfloat16)

    by_group(x_refs, groups, use)


def grad_a_step(place, packed, x_cols, half, got, away, groups, slots_line, rank):
    devices, depth, tokens = packed.shape
    width = x_cols[0].shape[-1] // 2
    local = devices // groups
    count = 8
    rows = count * rank
    number = len(x_cols)
    if number > 1:
        x_specs = [pl.BlockSpec((tokens, width), lambda g, s, place: (0, half))] * number
    else:
        if width % 128:
            x_cols, half = [x_cols[0][:, :, half * width : (half + 1) * width]], 0
        x_specs = [pl.BlockSpec((local, tokens, width), lambda g, s, place: (g, 0, half))]
    block = pl.BlockSpec((1, rows, width), lambda g, s, place: (g, s, 0))
    final = pl.BlockSpec((1, rows, width), lambda g, s, place: (g ^ place[0], s, 0))
    shape = jax.ShapeDtypeStruct((groups, slots_line * rank, width), jnp.bfloat16)
    ways = 1 if away == 0 else 2
    if away == 0:
        kernel = lambda *refs: own_kernel(groups, number, slots_line, count, rank, *refs)
    else:
        kernel = lambda *refs: send_kernel(groups, number, slots_line, count, rank, away, *refs)
    return call(
        kernel,
        place,
        (groups, slots_line // count),
        [pl.BlockSpec((local, depth, tokens), lambda g, s, place: (g ^ place[0], 0, 0))]
        + x_specs
        + [block] * len(got),
        final if away == 0 else [block, block],
        shape if away == 0 else [shape, shape],
        ways * 2 * devices * tokens * width * slots_line * rank,
        2 * devices * tokens * width + 2 * groups * slots_line * rank * width * (ways + len(got)),
        "grad_a_step" + str(away),
        (packed, *x_cols, *got),
    )


def in_line(slots, place_ref, total):
    slots -= place_ref[1] * (total // line_length)
    return jnp.where(slots < 0, slots + total, slots)


def put_together(pieces, a_ref):
    @pl.when(pl.program_id(0) == 0)
    def _():
        rows = pieces[0].shape[0]
        a_ref[:rows] = pieces[0][...]
        for k in range(1, line_length):
            left, right = pieces[line_length - k], pieces[line_length - 1 + k]
            a_ref[k * rows : (k + 1) * rows] = left[...] + right[...]


def low_kernel(chunk, rank, number, place_ref, packed_ref, *refs):
    x_refs, pieces, (low_ref, a_ref) = refs[:number], refs[number:-2], refs[-2:]
    put_together(pieces, a_ref)
    slots = packed_ref[0].astype(jnp.float32).T[:, rank + 1 : rank + 2].astype(jnp.int32)
    slots = in_line(slots, place_ref, a_ref.shape[0] // rank)
    tile = slots.shape[0]
    lane_slot = lax.broadcasted_iota(jnp.int32, (tile, chunk), 1) // rank

    def use(x):
        def step(c, low):
            part = pl.ds(pl.multiple_of(c * chunk, chunk), chunk)
            hidden = lax.dot_general(x, a_ref[part], NT, preferred_element_type=jnp.float32)
            hidden = jnp.where(lane_slot + c * (chunk // rank) == slots, hidden, 0.0)
            for k in range(chunk // (2 * rank)):
                low += hidden[:, k * 2 * rank : (k + 1) * 2 * rank]
            return low

        start = jnp.zeros((tile, 2 * rank), jnp.float32)
        low = repeat(a_ref.shape[0] // chunk, step, start).T
        low_ref[0] = low[:rank] + low[rank:]

    if number == 1:
        use(x_refs[0][0])
    else:
        for m in range(number):

            @pl.when(pl.program_id(0) == m)
            def _(m=m):
                use(x_refs[m][...])


def low_part(place, packed, x_cols, a_pieces, inner, rank):
    devices, depth, tokens = packed.shape
    width = x_cols[0].shape[-1]
    rows = a_pieces[0].shape[0]
    slots = line_length * rows
    number = len(x_cols)
    mate = lambda t, place: (t ^ (place[0] * inner + place[2]), 0, 0)
    if number > 1:
        x_specs = [pl.BlockSpec((tokens, width), lambda t, place: (0, 0))] * number
    else:
        x_specs = [pl.BlockSpec((1, tokens, width), lambda t, place: (t, 0, 0))]
    return call(
        lambda *refs: low_kernel(512, rank, number, *refs),
        place,
        (devices,),
        [pl.BlockSpec((1, depth, tokens), mate)]
        + x_specs
        + [pl.BlockSpec((rows, width), lambda t, place: (0, 0))] * len(a_pieces),
        pl.BlockSpec((1, rank, tokens), mate),
        jax.ShapeDtypeStruct((devices, rank, tokens), jnp.float32),
        2 * devices * tokens * width * slots,
        2 * (devices * tokens + slots) * width,
        "low_part",
        (packed, *x_cols, *a_pieces),
        [pltpu.VMEM((slots, width), jnp.bfloat16)],
    )


def out_kernel(chunk, rank, groups, place_ref, packed_ref, g_ref, *refs):
    number = 2 * line_length - 1
    a_pieces, w_pieces, (out_ref, a_ref, w_ref) = refs[:number], refs[number:-3], refs[-3:]
    put_together(a_pieces, a_ref)
    put_together(w_pieces, w_ref)
    rows = jnp.concatenate([p.astype(jnp.float32).T for p in packed_ref[...]], axis=0)
    back, slots = rows[:, :rank], rows[:, rank + 1 : rank + 2].astype(jnp.int32)
    total = a_ref.shape[0]
    slots = in_line(slots, place_ref, total // rank)
    tile = back.shape[0]
    repeated = jnp.concatenate([back] * (chunk // rank), axis=1)
    lane_slot = lax.broadcasted_iota(jnp.int32, (tile, chunk), 1) // rank

    def masked(c):
        keep = lane_slot + c * (chunk // rank) == slots
        return jnp.where(keep, repeated, 0.0).astype(jnp.bfloat16)

    if total // chunk <= 4:
        wide = jnp.concatenate([masked(c) for c in range(total // chunk)], axis=1)
        acc = jnp.dot(wide, a_ref[...], preferred_element_type=jnp.float32)
    else:

        def step(c, acc):
            block = a_ref[pl.ds(pl.multiple_of(c * chunk, chunk), chunk), :]
            return acc + jnp.dot(masked(c), block, preferred_element_type=jnp.float32)

        acc = repeat(total // chunk, step, jnp.zeros((tile, a_ref.shape[1]), jnp.float32))
    base = []
    count = w_pieces[0].shape[0]
    halves = line_length // groups
    for c in range(halves):
        at = (place_ref[0] * halves + c - place_ref[1] + line_length) % line_length
        w = w_ref[pl.ds(pl.multiple_of(at * count, count), count), :]
        base.append(lax.dot_general(g_ref[...], w, NT, preferred_element_type=jnp.float32))
    out = jnp.concatenate(base, axis=1) + adapter_scale * acc
    out_ref[...] = out.astype(out_ref.dtype).reshape(out_ref.shape)


def out_part(place, packed, g_all, w_pieces, a_pieces, groups, rank):
    devices, depth, tokens = packed.shape
    outs = g_all.shape[1]
    rows, width = a_pieces[0].shape
    slots = line_length * rows
    both = 2
    pieces = [*a_pieces, *w_pieces]
    return call(
        lambda *refs: out_kernel(512, rank, groups, *refs),
        place,
        (devices // both,),
        [
            pl.BlockSpec((both, depth, tokens), lambda t, place: (t, 0, 0)),
            pl.BlockSpec((both * tokens, outs), lambda t, place: (t, 0)),
        ]
        + [pl.BlockSpec(piece.shape, lambda t, place: (0, 0)) for piece in pieces],
        pl.BlockSpec((both, tokens, width), lambda t, place: (t, 0, 0)),
        jax.ShapeDtypeStruct((devices, tokens, width), jnp.bfloat16),
        2 * devices * tokens * width * (slots + outs),
        2 * devices * tokens * (width + outs) + 2 * slots * width,
        "out_part",
        (packed, g_all, *pieces),
        [
            pltpu.VMEM((slots, width), jnp.bfloat16),
            pltpu.VMEM((line_length * w_pieces[0].shape[0], outs), jnp.bfloat16),
        ],
    )


def body(x, g, tok, adapter_slot, w, a, b):
    groups, inner = lax.axis_size("groups"), lax.axis_size("inner")
    gi, li, ji = lax.axis_index("groups"), lax.axis_index("line"), lax.axis_index("inner")
    place = jnp.stack([gi, li, ji]).astype(jnp.int32)
    size = groups * inner
    devices = line_length * inner
    tokens, model = x.shape
    outs = g.shape[1]
    resident, _, rank = a.shape
    share = resident // groups
    count = inner * resident
    halves = line_length // groups
    width = model // size
    part = width // halves
    adapters = adapter_slot.shape[0]
    capacity = max(2, 2 * tokens // adapters)

    up = [(i, i + 1) for i in range(line_length - 1)]
    down = [(i + 1, i) for i in range(line_length - 1)]

    def hop(pieces, away):
        left, right = pieces
        return [
            lax.ppermute(left, "line", up[away - 1 :]),
            lax.ppermute(right, "line", down[: line_length - away]),
        ]

    w_hops = [hop((w, w), 1)]
    w_hops.append(hop(w_hops[0], 2))

    a_mine = split_columns(place, jnp.swapaxes(a, 1, 2), groups, halves, inner, part)
    a_own = lax.all_to_all(a_mine, plane, 0, 0, tiled=True).reshape(count * rank, width)

    def meet(m):
        return lax.ppermute(x_sends[m], plane, [(i, i ^ m) for i in range(size)])

    direct = size == 8 and part % 128 == 0
    x_cols = {}
    if direct:
        x_sends = split_pieces(place, x, groups, halves, inner, part)
        x_cols = {0: x_sends[0], 1: meet(1), 2: meet(2), 4: meet(4)}
    else:
        x_far = split_columns(place, x[None], groups, halves, inner, part)
        x_far = lax.all_to_all(x_far, plane, 0, 0, tiled=True)
        x_cols = {0: x_far[jnp.arange(size) ^ (gi * inner + ji)]}

    matches = tok == lax.broadcasted_iota(jnp.int32, (tokens, adapters), 1)
    slot = jnp.sum(jnp.where(matches, adapter_slot[None, :], 0), axis=1)
    running = jnp.cumsum(matches.astype(jnp.int32), axis=0)
    within = jnp.sum(jnp.where(matches, running - 1, 0), axis=1)
    position = slot * capacity + within
    at = lax.broadcasted_iota(jnp.int32, (adapters * capacity, tokens), 0) == position[None, :]
    at = at.astype(jnp.bfloat16)

    def route(rows):
        rows = rows.reshape(devices, resident * capacity, rows.shape[1])
        rows = lax.all_to_all(rows, row, 0, 0, tiled=True)
        return rows.reshape(devices, resident, capacity, rows.shape[2])

    g_send = jnp.dot(at, g, preferred_element_type=jnp.float32).astype(jnp.bfloat16)
    g_send, a_own, x_cols, w_hops = lax.optimization_barrier((g_send, a_own, x_cols, w_hops))
    w_hops.append(hop(w_hops[1], 3))
    g_rows = route(g_send)
    back = jnp.einsum("hjct,jrt->hjcr", g_rows, b, preferred_element_type=jnp.float32)
    back = back.astype(jnp.bfloat16).reshape(devices, resident * capacity, rank)
    hops = [hop((a_own, a_own), 1)]
    if direct:
        x_cols.update({3: meet(3), 5: meet(5)})
    back, x_cols = lax.optimization_barrier((back, x_cols))
    if direct:
        x_cols.update({6: meet(6), 7: meet(7)})
    back = lax.all_to_all(back, row, 0, 0, tiled=True).reshape(adapters * capacity, rank)
    back = lax.dot_general(
        back, at, (((0,), (0,)), ((), ())), preferred_element_type=jnp.float32
    ).astype(jnp.bfloat16)
    owner, res = slot // resident, slot % resident
    slot_a = (owner // inner) * count + ((res // share) * inner + owner % inner) * share + res % share
    names = jnp.stack([slot, slot_a] + [slot] * 14).astype(jnp.bfloat16)
    packed = jnp.concatenate([back, names], axis=0)
    packed, x_cols, hops, w_hops = lax.optimization_barrier((packed, x_cols, hops, w_hops))
    packed = jnp.broadcast_to(packed[None], (size,) + packed.shape)
    packed = lax.all_to_all(packed, plane, 0, 0, tiled=True)
    x_cols = [x_cols[m] for m in range(len(x_cols))]
    g_own, x_cols = lax.optimization_barrier((g, x_cols))
    g_all = lax.all_gather(g_own, plane, axis=0, tiled=True)

    hops.append(hop(hops[0], 2))

    def send(c, got, away):
        sums = grad_a_step(place, packed, x_cols, c, got, away, groups, count, rank)
        ahead = [(i, i + 1) for i in range(line_length - away)]
        behind = [(i, i - 1) for i in range(away, line_length)]
        moved = (lax.ppermute(sums[0], "line", ahead), lax.ppermute(sums[1], "line", behind))
        return moved, sums[0]

    def own(c, got):
        p = grad_a_step(place, packed, x_cols, c, got, 0, groups, count, rank)
        return p.reshape(size, resident * rank, part)

    first, done = send(0, (), 3)
    packed, done = lax.optimization_barrier((packed, done))
    second, done = send(1, (), 3)

    first, hops[1], done = lax.optimization_barrier((first, hops[1], done))
    hops.append(hop(hops[1], 3))
    first, done = send(0, first, 2)
    second, done = lax.optimization_barrier((second, done))
    second, done = send(1, second, 2)

    a_pieces = [a_own] + [h[0] for h in hops] + [h[1] for h in hops]
    w_pieces = [w] + [h[0] for h in w_hops] + [h[1] for h in w_hops]
    a_pieces, done = lax.optimization_barrier((a_pieces, done))
    out_cols = out_part(place, packed, g_all, w_pieces, a_pieces, groups, rank)
    first, out_cols = lax.optimization_barrier((first, out_cols))
    first, done = send(0, first, 1)
    out_back = lax.all_to_all(out_cols, plane, 0, 0, tiled=True)

    a_pieces, done = lax.optimization_barrier((a_pieces, done))
    low = low_part(place, packed, x_cols, a_pieces, inner, rank)
    second, low = lax.optimization_barrier((second, low))
    second, done = send(1, second, 1)
    first, done = lax.optimization_barrier((first, done))
    p_first = own(0, first)
    second, p_first = lax.optimization_barrier((second, p_first))
    p_second = own(1, second)
    low, out_back = lax.optimization_barrier((low, out_back))
    low = lax.all_to_all(low, plane, 0, 0, tiled=True)
    low = jnp.sum(low, axis=0).astype(jnp.bfloat16)
    low = lax.dot_general(at, low, NT, preferred_element_type=jnp.float32).astype(jnp.bfloat16)
    low = route(low)
    p_back = jnp.concatenate([p_first, p_second], axis=1)
    p_back, low = lax.optimization_barrier((p_back, low))
    p_back = lax.all_to_all(p_back, plane, 0, 0, tiled=True)

    grad_b = jnp.einsum("hjcr,hjco->jro", low, g_rows, preferred_element_type=jnp.float32)
    grad_b = (adapter_scale * grad_b).astype(jnp.bfloat16)
    input_gradient = join_rows(place, out_back, groups, halves, inner, part)
    grad_a = join_slots(place, p_back, resident, groups, halves, inner).swapaxes(1, 2)
    return input_gradient, grad_a, grad_b


def solution(mesh):
    groups, rows = mesh.shape["groups"], mesh.shape["row"]
    whole = ("groups", "line", "inner")
    split = Mesh(mesh.devices.reshape(groups, line_length, rows // line_length), whole)
    return jax.shard_map(
        body,
        mesh=split,
        in_specs=(
            P(whole, None),
            P(whole, None),
            P(whole, None),
            P(),
            P(row, None),
            P(row, None, None),
            P(row, None, None),
        ),
        out_specs=(P(whole, None), P(whole, None, None), P(whole, None, None)),
        check_vma=False,
    )
```
